32 devices in a mesh: groups: 2 (over x), ctx: 8 (over z, y), exp: 2 (over core).
Axes of the slice: x: 2, y: 2, z: 4, core: 2. Of those that a mesh axis runs over, the one named last changes fastest.
Arguments:
- queries: bfloat16 [2048, 1536], P(('groups', 'ctx'), 'exp'), parts along dimension 0, may hold values from -8 to 8
- latent: bfloat16 [2048, 576], P(('groups', 'ctx')), parts along dimension 0, may hold values from -8 to 8
- residual: bfloat16 [2048, 2048], P(('groups', 'ctx')), parts along dimension 0, may hold values from -12 to 12
- seg_lengths: int32 [32], P('groups'), parts along dimension 0, may hold values from 1 to 256, 1024 in all
- span_order: int32 [32], P('groups'), parts along dimension 0, may hold values from 0 to 15, each once
- expert_ids: int32 [2048, 6], P(('groups', 'ctx')), parts along dimension 0, may hold values from 0 to 63, all different within a row; in each aligned block of 128 rows (0 to 127, 128 to 255, ...) at most 14 rows name the same one
- route_weights: float32 [2048, 6], P(('groups', 'ctx')), parts along dimension 0, may hold values from 0.1 to 1
- kv_up: bfloat16 [512, 2048], P(None, 'exp'), may hold values from -0.25 to 0.25
- out_proj: bfloat16 [1024, 2048], P('exp'), may hold values from -0.75 to 0.75
- norm_gain: bfloat16 [2048], replicated, may hold values from 0.099609375 to 1.8984375
- w_gate: bfloat16 [64, 2048, 1408], P('ctx', None, 'exp'), may hold values from -0.125 to 0.125
- w_up: bfloat16 [64, 2048, 1408], P('ctx', None, 'exp'), may hold values from -0.125 to 0.125
- w_down: bfloat16 [64, 1408, 2048], P('ctx', 'exp'), may hold values from -0.15625 to 0.15625
Outputs:
- layer_out: bfloat16 [2048, 2048], P(('groups', 'ctx'), 'exp'), parts along dimension 0
The draws below stay inside these ranges and needn't reach their ends.
There are 2 independent parts, one for each index of `groups`. The reference program is written for one: setup_inputs(seed, part) draws one part's arguments, and reference() takes and returns one part's arrays. A program takes and returns all parts, laid end to end along the dimension named above; an argument that names none is the same for every part. Nothing has to cross between parts.
Inputs may be any that keep to these rules, and one draw needn't show every extreme that they name: `seg_lengths`: the 16 lengths sum to 1024 and the longest is exactly 256. `span_order`: each block number appears once. `expert_ids`: each row names 6 different experts; within the rows of one index of ctx (aligned blocks of 128 rows) no expert is named by more than 14 rows, a bound that some block reaches.
All inputs are finite; a program needn't handle non-finite values.
Results may differ from the reference program's by a relative error of at most 0.018.
Values may be sent and summed in bfloat16 or wider, within the bound.
No kernel may reach another device: no remote copies, remote signals or barrier semaphores. Data moves between devices by JAX's collectives and lax.ppermute only.
A program may use at most 192 MiB of HBM per device.

```python
import math
import jax
import jax.numpy as jnp
import numpy as np
from jax import lax

D = 2048
HEADS = 8
NOPE = 128
ROPE = 64
VHEAD = 128
LAT = 512
EXPERTS = 64
TOP = 6
FF = 1408
SEGS = 16
SPAN = 64
TOKENS = 1024
MAXLEN = 256
MOST = 14
N_CTX = 8


def draw_queries(key, part):
    mine = jax.random.fold_in(key, 23)
    shape = (TOKENS, HEADS, NOPE + ROPE)
    base = jnp.clip(jax.random.normal(mine, shape, jnp.float32), -6.0, 6.0)
    return base.reshape(TOKENS, HEADS * (NOPE + ROPE)).astype(jnp.bfloat16)


def draw_latent(key, part):
    mine = jax.random.fold_in(key, 11)
    shape = (TOKENS, LAT + ROPE)
    base = jnp.clip(jax.random.normal(mine, shape, jnp.float32), -6.0, 6.0)
    return base.astype(jnp.bfloat16)


def draw_residual(key, part):
    key = jax.random.fold_in(key, 37)
    row_key, column_key, value_key = jax.random.split(key, 3)
    row_scale = jnp.exp(jax.random.uniform(row_key, (TOKENS, 1), jnp.float32, math.log(0.1), 0.0))
    ramp = jnp.exp(math.log(3.0) * jnp.arange(D, dtype=jnp.float32) / (D - 1))
    column_scale = 0.3 * ramp * jnp.exp(jax.random.uniform(column_key, (D,), jnp.float32, 0.0, math.log(10.0 / 3.0)))
    entries = jnp.clip(jax.random.normal(value_key, (TOKENS, D), jnp.float32), -4.0, 4.0)
    return (entries * row_scale * column_scale[None, :]).astype(jnp.bfloat16)


def levels(key, shape, cuts, smallest, largest):
    gain, own = 1.0, jax.random.fold_in(key, 6)
    for dim, blocks in cuts:
        draws = jnp.exp(jax.random.uniform(jax.random.fold_in(own, dim), (blocks,), jnp.float32, smallest / len(cuts), largest / len(cuts)))
        gain = gain * jnp.repeat(draws, shape[dim] // blocks).reshape([-1 if axis == dim else 1 for axis in range(len(shape))])
    return gain


def profile(amount, total, reach, slope):
    portions = [(1 << 20) // math.isqrt(rank ** slope) + 1 for rank in range(2, amount + 1)]
    rest, holding = total - reach - (amount - 1), [1] * (amount - 1)
    while rest > 0:
        movable = [i for i in range(amount - 1) if holding[i] < reach]
        pool, left = sum([portions[i] for i in movable]), rest
        for i in movable:
            extra = min(reach - holding[i], max(1, left * portions[i] // pool), rest)
            holding[i] = holding[i] + extra
            rest = rest - extra
    return np.array([reach] + holding)


def uneven_parts(rng, number_of, total, limit, skew):
    if number_of == 2:
        one = jax.random.randint(rng, (), max(1, total - limit), min(limit, total - 1) + 1)
        return jnp.stack([one, total - one])
    sizes = jnp.asarray(profile(number_of, total, limit, skew), jnp.int32)
    twos = (number_of - 1) // 2
    donor, taker = sizes[1:1 + 2 * twos:2], sizes[2:2 + 2 * twos:2]
    margin = jnp.minimum(donor - 1, limit - taker)
    passed = jax.random.randint(jax.random.fold_in(rng, 1), (twos,), 0, 1 << 20) % (margin + 1)
    sizes = sizes.at[1:1 + 2 * twos:2].set(donor - passed).at[2:2 + 2 * twos:2].set(taker + passed)
    return sizes[jax.random.permutation(jax.random.fold_in(rng, 2), number_of)]


def routed_block(rng, own, number, rows, count, top, reach, lean):
    order = jax.random.permutation(rng, count)
    heavy_load, ordinary = portions_of(count, rows * top, reach, lean, True), portions_of(count, rows * top, reach, lean, False)
    places = jnp.arange(count)

    def named(tallies, rotation):
        used = int((tallies > 0).sum())
        fixed = max(1, used // 4)
        moved = fixed + (places - fixed + rotation * (used - fixed)) % max(1, count - fixed)
        return jnp.zeros((count,), jnp.int32).at[order[jnp.where(places < fixed, places, moved)]].set(jnp.asarray(tallies, jnp.int32))

    tallies = jnp.where(number % 4 == 0, named(heavy_load, number // 4), named(ordinary, number - number // 4 - 1))
    mixed = jax.random.permutation(jax.random.fold_in(own, 3), count)
    giver, receiver = mixed[0:count // 2 * 2:2], mixed[1:count // 2 * 2:2]
    room = jnp.minimum(tallies[giver] - 1, reach - tallies[receiver]) // 2
    room = jnp.where((giver == order[0]) | (receiver == order[0]) | (tallies[receiver] == 0), 0, jnp.maximum(room, 0))
    moved = jax.random.randint(jax.random.fold_in(own, 4), (count // 2,), 0, 1 << 20) % (room + 1)
    tallies = tallies.at[giver].add(-moved).at[receiver].add(moved)
    labels = jnp.searchsorted(jnp.cumsum(tallies), jnp.arange(rows * top), side="right").astype(jnp.int32)
    listing = labels.reshape(top, rows).T
    listing = listing[jax.random.permutation(jax.random.fold_in(own, 1), rows)]
    rotation = jax.random.randint(jax.random.fold_in(own, 2), (rows, 1), 0, top)
    return jnp.take_along_axis(listing, (jnp.arange(top)[None, :] + rotation) % top, axis=1)


def portions_of(count, total, bound, slope, full):
    portions = [(1 << 20) // math.isqrt(rank ** slope) + 1 for rank in range(1, count + 1)]
    largest = bound if full else min(bound, max(-(-total // count), total * portions[0] // sum(portions)))
    least = 1 if total - largest >= count - 1 else 0
    holding, spare = [largest] + [least] * (count - 1), total - largest - least * (count - 1)
    while spare > 0:
        free = [i for i in range(1, count) if holding[i] < largest] or [i for i in range(1, count) if holding[i] < bound]
        pool, budget = sum([portions[i] for i in free]), spare
        for i in free:
            extra = min(bound - holding[i], max(1, budget * portions[i] // pool), spare)
            holding[i] = holding[i] + extra
            spare = spare - extra
    return np.array(holding)


def noise(key, shape, width, bound, pieces=(), kind=jnp.bfloat16):
    result = jax.random.normal(key, shape, jnp.float32) * width
    if len(pieces) > 0:
        result = levels(key, shape, pieces, -0.22, 0.18) * result
    return jnp.clip(result, min=-bound, max=bound).astype(kind)


def setup_inputs(seed: int = 0, part: int = 0) -> dict:
    splits = jax.random.split(jax.random.key(seed), 14)
    part_keys = jax.random.split(jax.random.fold_in(splits[13], part), 14)
    queries = draw_queries(jax.random.fold_in(jax.random.fold_in(splits[13], part), 71), part)
    latent = draw_latent(jax.random.fold_in(jax.random.fold_in(splits[13], part), 71), part)
    residual = draw_residual(jax.random.fold_in(jax.random.fold_in(splits[13], part), 71), part)
    seg_lengths = uneven_parts(part_keys[3], SEGS, TOKENS, MAXLEN, 2).astype(jnp.int32)
    span_order = jax.random.permutation(part_keys[4], 2 * N_CTX).astype(jnp.int32)
    expert_ids_keys = jax.random.split(jax.random.fold_in(part_keys[5], 1), TOKENS // (2 * SPAN))
    expert_ids_turns = jax.random.permutation(jax.random.fold_in(part_keys[5], 3), TOKENS // (2 * SPAN))
    expert_ids = jax.vmap(lambda own, number: routed_block(jax.random.fold_in(part_keys[5], 2), own, number, 2 * SPAN, EXPERTS, TOP, MOST, 2))(expert_ids_keys, expert_ids_turns).reshape((TOKENS, TOP))
    route_weights = jnp.clip(0.1 + 0.9 * jax.random.uniform(part_keys[6], (TOKENS, TOP), jnp.float32) ** levels(part_keys[6], (TOKENS, TOP), ((0, 8),), -0.2, 0.2), 0.1, 1.0)
    kv_up = noise(splits[7], (LAT, HEADS * (NOPE + VHEAD)), LAT ** -0.5, 0.25, ((1, 2),))
    out_proj = noise(splits[8], (HEADS * VHEAD, D), (VHEAD // 2) ** -0.5, 0.75, ((0, 2),))
    norm_gain = jnp.clip(1.0 + 0.18 * jax.random.normal(splits[9], (D,), jnp.float32), 0.099609375, 1.8984375).astype(jnp.bfloat16)
    w_gate = noise(splits[10], (EXPERTS, D, FF), D ** -0.5, 0.125, ((0, 8), (2, 2)))
    w_up = noise(splits[11], (EXPERTS, D, FF), D ** -0.5, 0.125, ((0, 8), (2, 2)))
    w_down = noise(splits[12], (EXPERTS, FF, D), FF ** -0.5, 0.15625, ((0, 8), (1, 2)))
    return dict(queries=queries, latent=latent, residual=residual, seg_lengths=seg_lengths, span_order=span_order, expert_ids=expert_ids, route_weights=route_weights, kv_up=kv_up, out_proj=out_proj, norm_gain=norm_gain, w_gate=w_gate, w_up=w_up, w_down=w_down)


def rounded(value):
    return lax.optimization_barrier(value.astype(jnp.bfloat16)).astype(jnp.float32)

def place_rows(span_order, seg_lengths, row_ids):
    position = span_order[row_ids // SPAN].astype(jnp.int32) * SPAN + row_ids % SPAN
    seg_ends = jnp.cumsum(seg_lengths).astype(jnp.int32)
    segment = lax.optimization_barrier(jnp.sum((position[:, None] >= seg_ends[None, :]).astype(jnp.int32), axis=1))
    return (position.astype(jnp.int32), segment.astype(jnp.int32))

def reference(queries, latent, residual, seg_lengths, span_order, expert_ids, route_weights, kv_up, out_proj, norm_gain, w_gate, w_up, w_down):
    row_ids = jnp.arange(TOKENS).astype(jnp.int32)
    position, segment = place_rows(span_order, seg_lengths, row_ids)
    keyval = jnp.dot(latent[:, :LAT], kv_up, preferred_element_type=jnp.float32).astype(jnp.bfloat16)
    keyval = keyval.reshape(TOKENS, HEADS, NOPE + VHEAD)
    key_nope = keyval[:, :, :NOPE].astype(jnp.float32)
    values = keyval[:, :, NOPE:].astype(jnp.float32)
    key_rope = latent[:, LAT:].astype(jnp.float32)
    query_all = queries.reshape(TOKENS, HEADS, NOPE + ROPE).astype(jnp.float32)
    scale = 1.0 / math.sqrt(NOPE + ROPE)
    block_rows = 2 * SPAN

    def attend(block_index):
        start = (block_index * block_rows).astype(jnp.int32)
        query_block = lax.dynamic_slice_in_dim(query_all, start, block_rows, 0)
        query_pos = lax.dynamic_slice_in_dim(position, start, block_rows, 0)
        query_seg = lax.dynamic_slice_in_dim(segment, start, block_rows, 0)
        scores = jnp.einsum('rhn,khn->hrk', query_block[:, :, :NOPE], key_nope)
        scores = (scores + jnp.einsum('rhn,kn->hrk', query_block[:, :, NOPE:], key_rope)) * scale
        visible = (segment[None, :] == query_seg[:, None]) & (position[None, :] <= query_pos[:, None])
        scores = jnp.where(visible[None], scores, -1e+30)
        highest = lax.optimization_barrier(jnp.max(scores, axis=2, keepdims=True))
        weights = jnp.where(visible[None], jnp.exp(scores - highest), 0.0)
        weight_sum = lax.optimization_barrier(jnp.sum(weights, axis=2, keepdims=True))
        mixed = jnp.einsum('hrk,khv->hrv', rounded(weights), values) / weight_sum
        return mixed.astype(jnp.bfloat16)
    attended = lax.map(attend, jnp.arange(TOKENS // block_rows).astype(jnp.int32))
    attended = attended.transpose(0, 2, 1, 3).reshape(TOKENS, HEADS * VHEAD)
    split_heads = HEADS // 2 * VHEAD
    first = rounded(jnp.dot(attended[:, :split_heads], out_proj[:split_heads], preferred_element_type=jnp.float32))
    second = rounded(jnp.dot(attended[:, split_heads:], out_proj[split_heads:], preferred_element_type=jnp.float32))
    middle = (residual.astype(jnp.float32) + (first + second)).astype(jnp.bfloat16)
    middle_f = middle.astype(jnp.float32)
    inverse = lax.rsqrt(lax.optimization_barrier(jnp.mean(middle_f * middle_f, axis=1, keepdims=True)) + 1e-06)
    normed = (middle_f * inverse * norm_gain.astype(jnp.float32)[None, :]).astype(jnp.bfloat16)
    blocks = TOKENS // block_rows
    flat_experts = expert_ids.reshape(blocks, block_rows * TOP).astype(jnp.int32)
    onehot = (flat_experts[:, :, None] == jnp.arange(EXPERTS).astype(jnp.int32)[None, None, :]).astype(jnp.int32)
    slots = lax.optimization_barrier(jnp.sum((jnp.cumsum(onehot, axis=1) - onehot) * onehot, axis=2)).astype(jnp.int32)
    sources = jnp.broadcast_to(jnp.arange(blocks).astype(jnp.int32)[:, None], flat_experts.shape)
    tokens_of = jnp.repeat(row_ids, TOP).reshape(blocks, block_rows * TOP)
    lookup_rows = jnp.full((EXPERTS, blocks, MOST), TOKENS, jnp.int32).at[flat_experts, sources, slots].set(tokens_of)
    padded = jnp.concatenate([normed, jnp.zeros((1, D), jnp.bfloat16)], axis=0)
    half_units = FF // 2

    def expert(index):
        picked = padded[lookup_rows[index].reshape(blocks * MOST)]
        gate = jnp.dot(picked, w_gate[index], preferred_element_type=jnp.float32)
        upper = jnp.dot(picked, w_up[index], preferred_element_type=jnp.float32)
        hidden = (jax.nn.silu(gate) * upper).astype(jnp.bfloat16)
        down = w_down[index]
        low = rounded(jnp.dot(hidden[:, :half_units], down[:half_units], preferred_element_type=jnp.float32))
        high = rounded(jnp.dot(hidden[:, half_units:], down[half_units:], preferred_element_type=jnp.float32))
        return (low + high).astype(jnp.bfloat16)
    outputs = lax.map(expert, jnp.arange(EXPERTS).astype(jnp.int32))
    gathered = outputs[flat_experts, sources * MOST + slots].reshape(TOKENS, TOP, D)
    mixture = jnp.zeros((TOKENS, D), jnp.float32)
    for slot_k in range(TOP):
        mixture = mixture + route_weights[:, slot_k:slot_k + 1].astype(jnp.float32) * gathered[:, slot_k].astype(jnp.float32)
    return (middle_f + mixture).astype(jnp.bfloat16)
```

```python
import functools
import math

import jax
import jax.numpy as jnp
from jax import lax
from jax.experimental import pallas as pl
from jax.experimental.pallas import tpu as pltpu
from jax.sharding import PartitionSpec as P

NOPE = 128
ROPE = 64
VHEAD = 128
LAT = 512
EXPERTS = 64
TOP = 6
SLOTS = 16
WIDE = 640
VMEM_LIMIT = 56 * 1024 * 1024
SWAP = [(0, 1), (1, 0)]
FEW = 8


def grid_of(count):
    fast = 2 ** (int(math.log2(count)) // 2)
    return (count // fast, fast)


def shift_slow(value, step, count):
    slow, fast = grid_of(count)
    perm = [(i, (i // fast + step) % slow * fast + i % fast) for i in range(count)]
    return lax.ppermute(value, "ctx", perm)


def shift_fast(value, step, count):
    fast = grid_of(count)[1]
    perm = [(i, i // fast * fast + (i % fast + step) % fast) for i in range(count)]
    return lax.ppermute(value, "ctx", perm)


def swap(value):
    return lax.ppermute(value, "exp", SWAP)


def each(send, pieces, count):
    if count <= FEW:
        return [send(piece) for piece in pieces]
    return list(send(jnp.stack(pieces)))


def spread(block, count):
    slow, fast = grid_of(count)
    line = [block] + [shift_slow(block, s, count) for s in range(1, slow)]
    found = list(line)
    for r in range(1, fast):
        found += each(lambda piece: shift_fast(piece, r, count), line, count)
    return found


def collect(parts, count):
    slow, fast = grid_of(count)
    sums = [part.astype(jnp.float32) for part in parts[:slow]]
    for r in range(1, fast):
        arrived = each(lambda piece: shift_fast(piece, -r, count), parts[r * slow : (r + 1) * slow], count)
        sums = [total + piece.astype(jnp.float32) for total, piece in zip(sums, arrived)]
    arrived = [shift_slow(sums[s].astype(jnp.bfloat16), -s, count) for s in range(1, slow)]
    total = sums[0]
    for piece in arrived:
        total = total + piece.astype(jnp.float32)
    return total


def owner_of(place, me, count):
    slow, fast = grid_of(count)
    r, s = place // slow, place % slow
    return (me // fast + slow - s) % slow * fast + (me % fast + fast - r) % fast


def attend_kernel(count, blocks, info, q_ref, mine_ref, other_ref, up_ref, proj_ref, out_ref, m_ref, l_ref, acc_ref):
    step = pl.program_id(0)
    me, side = info[0], info[1]
    segs = 16
    span = mine_ref.shape[1]
    heads, rows, _ = q_ref.shape

    @pl.when(step == 0)
    def _():
        m_ref[...] = jnp.full_like(m_ref, -1e30)
        l_ref[...] = jnp.zeros_like(l_ref)
        acc_ref[...] = jnp.zeros_like(acc_ref)

    row = lax.broadcasted_iota(jnp.int32, (rows, 1), 0)
    first = info[2 + segs + 2 * me] * span
    second = info[2 + segs + 2 * me + 1] * span
    qpos = jnp.where(row < span, first + row, second + row - span)
    low = jnp.zeros((rows, 1), jnp.int32)
    start = jnp.int32(0)
    for m in range(segs):
        low = jnp.where(qpos >= start, start, low)
        start = start + info[2 + m]
    keys = blocks * span
    lane = lax.broadcasted_iota(jnp.int32, (1, keys), 1)
    within, which = lane % span, lane // span
    kpos_parts = []
    for half in (side, 1 - side):
        base = jnp.zeros((1, keys), jnp.int32)
        for j in range(blocks):
            src = owner_of(step * blocks + j, me, count)
            base = jnp.where(which == j, info[2 + segs + 2 * src + half] * span, base)
        kpos_parts.append(base + within)
    kpos = jnp.concatenate(kpos_parts, axis=1)
    visible = (kpos >= low) & (kpos <= qpos)

    lat = jnp.concatenate([mine_ref[...].reshape(keys, WIDE), other_ref[...].reshape(keys, WIDE)], axis=0)
    keyval = jnp.dot(lat[:, :LAT], up_ref[...], preferred_element_type=jnp.float32).astype(jnp.bfloat16)
    rope = lat[:, LAT : LAT + ROPE]
    scale = 1.0 / math.sqrt(NOPE + ROPE)
    for h in range(heads):
        base = h * (NOPE + VHEAD)
        key = jnp.concatenate([keyval[:, base : base + NOPE], rope], axis=1)
        scores = lax.dot_general(q_ref[h], key, (((1,), (1,)), ((), ())), preferred_element_type=jnp.float32)
        scores = jnp.where(visible, scores * scale, -1e30)
        best = m_ref[h]
        fresh = jnp.maximum(best, jnp.max(scores, axis=1, keepdims=True))
        weights = jnp.where(visible, jnp.exp(scores - fresh), 0.0)
        shrink = jnp.exp(best - fresh)
        m_ref[h] = fresh
        l_ref[h] = l_ref[h] * shrink + jnp.sum(weights, axis=1, keepdims=True)
        mixed = jnp.dot(
            weights.astype(jnp.bfloat16), keyval[:, base + NOPE : base + NOPE + VHEAD], preferred_element_type=jnp.float32
        )
        acc_ref[h] = acc_ref[h] * shrink + mixed

    @pl.when(step == pl.num_programs(0) - 1)
    def _():
        attended = [(acc_ref[h] / l_ref[h]).astype(jnp.bfloat16) for h in range(heads)]
        out = jnp.dot(jnp.concatenate(attended, axis=1), proj_ref[...], preferred_element_type=jnp.float32)
        out_ref[...] = out.astype(jnp.bfloat16)


def attend(info, q, mine, other, kv_up, out_proj, count):
    heads, rows, depth = q.shape
    blocks = math.gcd(count, 8)
    span = mine.shape[1]
    whole2 = lambda i, *_: (0, 0)
    whole3 = lambda i, *_: (0, 0, 0)
    lat_spec = pl.BlockSpec((blocks, span, WIDE), lambda i, *_: (i, 0, 0))
    return pl.pallas_call(
        functools.partial(attend_kernel, count, blocks),
        grid_spec=pltpu.PrefetchScalarGridSpec(
            num_scalar_prefetch=1,
            grid=(count // blocks,),
            in_specs=[
                pl.BlockSpec(q.shape, whole3),
                lat_spec,
                lat_spec,
                pl.BlockSpec(kv_up.shape, whole2),
                pl.BlockSpec(out_proj.shape, whole2),
            ],
            out_specs=pl.BlockSpec((rows, out_proj.shape[1]), whole2),
            scratch_shapes=[
                pltpu.VMEM((heads, rows, 1), jnp.float32),
                pltpu.VMEM((heads, rows, 1), jnp.float32),
                pltpu.VMEM((heads, rows, VHEAD), jnp.float32),
            ],
        ),
        out_shape=jax.ShapeDtypeStruct((rows, out_proj.shape[1]), jnp.bfloat16),
        compiler_params=pltpu.CompilerParams(vmem_limit_bytes=VMEM_LIMIT),
        name="attend",
    )(info, q, mine, other, kv_up, out_proj)


def norm_kernel(info, residual_ref, here_ref, there_ref, gain_ref, middle_ref, normed_ref):
    side = info[1]
    half = middle_ref.shape[1]
    total = here_ref[...].astype(jnp.float32) + there_ref[...].astype(jnp.float32)
    middle = (residual_ref[...].astype(jnp.float32) + total).astype(jnp.bfloat16)
    wide = middle.astype(jnp.float32)
    inverse = lax.rsqrt(jnp.mean(wide * wide, axis=1, keepdims=True) + 1e-06)
    normed = wide * inverse * gain_ref[...].astype(jnp.float32)
    middle_ref[...] = jnp.where(side == 0, wide[:, :half], wide[:, half:]).astype(jnp.bfloat16)
    normed_ref[...] = jnp.where(side == 0, normed[:, :half], normed[:, half:]).astype(jnp.bfloat16)


def norm(info, residual, here, there, gain):
    rows, width = residual.shape
    half = jax.ShapeDtypeStruct((rows, width // 2), jnp.bfloat16)
    full = pl.BlockSpec((rows, width), lambda i, *_: (0, 0))
    part = pl.BlockSpec((rows, width // 2), lambda i, *_: (0, 0))
    return pl.pallas_call(
        norm_kernel,
        grid_spec=pltpu.PrefetchScalarGridSpec(
            num_scalar_prefetch=1,
            grid=(1,),
            in_specs=[full, full, full, pl.BlockSpec((1, width), lambda i, *_: (0, 0))],
            out_specs=[part, part],
        ),
        out_shape=[half, half],
        compiler_params=pltpu.CompilerParams(vmem_limit_bytes=VMEM_LIMIT),
        name="norm",
    )(info, residual, here, there, gain.reshape(1, width))


def up_kernel(info, mine_ref, other_ref, gm_ref, go_ref, um_ref, uo_ref, scale_ref, out_ref):
    rows = out_ref.shape[1]
    mine = mine_ref[...].reshape(rows, mine_ref.shape[3])
    other = other_ref[...].reshape(rows, other_ref.shape[3])
    gate = jnp.dot(mine, gm_ref[0], preferred_element_type=jnp.float32)
    gate = gate + jnp.dot(other, go_ref[0], preferred_element_type=jnp.float32)
    upper = jnp.dot(mine, um_ref[0], preferred_element_type=jnp.float32)
    upper = upper + jnp.dot(other, uo_ref[0], preferred_element_type=jnp.float32)
    hidden = gate / (1.0 + jnp.exp(-gate)) * upper * scale_ref[0]
    out_ref[0] = hidden.astype(jnp.bfloat16)


def up(info, mine, other, w_gate, w_up, scale):
    count, here, slots, half = mine.shape
    hidden = w_gate.shape[2]
    rows = count * slots
    rows_spec = pl.BlockSpec((count, 1, slots, half), lambda e, info: (0, e, 0, 0))
    mine_spec = pl.BlockSpec((1, half, hidden), lambda e, info: (e, info[1], 0))
    other_spec = pl.BlockSpec((1, half, hidden), lambda e, info: (e, 1 - info[1], 0))
    return pl.pallas_call(
        up_kernel,
        grid_spec=pltpu.PrefetchScalarGridSpec(
            num_scalar_prefetch=1,
            grid=(here,),
            in_specs=[
                rows_spec,
                rows_spec,
                mine_spec,
                other_spec,
                mine_spec,
                other_spec,
                pl.BlockSpec((1, rows, 1), lambda e, info: (e, 0, 0)),
            ],
            out_specs=pl.BlockSpec((1, rows, hidden), lambda e, info: (e, 0, 0)),
        ),
        out_shape=jax.ShapeDtypeStruct((here, rows, hidden), jnp.bfloat16),
        compiler_params=pltpu.CompilerParams(vmem_limit_bytes=VMEM_LIMIT),
        name="expert_up",
    )(info, mine, other, w_gate, w_gate, w_up, w_up, scale)


def down_kernel(info, hidden_ref, w_ref, combine_ref, out_ref, held):
    expert = pl.program_id(0)
    count, here, slots, half = held.shape
    result = jnp.dot(hidden_ref[0], w_ref[0], preferred_element_type=jnp.float32).astype(jnp.bfloat16)
    held[:, pl.ds(expert, 1)] = result.reshape(count, 1, slots, half)

    @pl.when(expert == pl.num_programs(0) - 1)
    def _():
        def place(c, _):
            rows = held[c].reshape(here * slots, half)
            out_ref[c] = jnp.dot(combine_ref[c], rows, preferred_element_type=jnp.float32).astype(jnp.bfloat16)
            return 0

        lax.fori_loop(0, count, place, 0)


def down(info, hidden, w_down, combine, flip):
    here, rows, units = hidden.shape
    count, local, _ = combine.shape
    half = w_down.shape[2] // 2
    return pl.pallas_call(
        down_kernel,
        grid_spec=pltpu.PrefetchScalarGridSpec(
            num_scalar_prefetch=1,
            grid=(here,),
            in_specs=[
                pl.BlockSpec((1, rows, units), lambda e, info: (e, 0, 0)),
                pl.BlockSpec((1, units, half), lambda e, info: (e, 0, 1 - info[1] if flip else info[1])),
                pl.BlockSpec(combine.shape, lambda e, info: (0, 0, 0)),
            ],
            out_specs=pl.BlockSpec((count, local, half), lambda e, info: (0, 0, 0)),
            scratch_shapes=[pltpu.VMEM((count, here, rows // count, half), jnp.bfloat16)],
        ),
        out_shape=jax.ShapeDtypeStruct((count, local, half), jnp.bfloat16),
        compiler_params=pltpu.CompilerParams(vmem_limit_bytes=VMEM_LIMIT),
        name="expert_down",
    )(info, hidden, w_down, combine)


def body(
    queries,
    latent,
    residual,
    seg_lengths,
    span_order,
    expert_ids,
    route_weights,
    kv_up,
    out_proj,
    norm_gain,
    w_gate,
    w_up,
    w_down,
):
    local_rows, width = residual.shape
    span = local_rows // 2
    heads = kv_up.shape[1] // (NOPE + VHEAD)
    count = lax.axis_size("ctx")
    here = EXPERTS // count
    me, side = lax.axis_index("ctx"), lax.axis_index("exp")
    info = jnp.concatenate([jnp.stack([me, side]).astype(jnp.int32), seg_lengths, span_order])

    high = route_weights.astype(jnp.bfloat16)
    lower = (route_weights - high.astype(jnp.float32)).astype(jnp.bfloat16)
    base = latent.shape[1]
    packed = jnp.concatenate(
        [
            latent,
            expert_ids.astype(jnp.bfloat16),
            high,
            lower,
            jnp.zeros((local_rows, WIDE - base - 3 * TOP), jnp.bfloat16),
        ],
        axis=1,
    )
    found = spread(lax.dynamic_slice_in_dim(packed, side * span, span, 0), count)
    mine = jnp.stack(found)
    other = jnp.stack(each(swap, found, count))

    q = queries.reshape(local_rows, heads, NOPE + ROPE).transpose(1, 0, 2)
    partial = attend(info, q, mine, other, kv_up, out_proj, count)
    middle, normed = norm(info, residual, partial, swap(partial), norm_gain)

    facts_mine, facts_other = mine[:, :, base : base + 3 * TOP], other[:, :, base : base + 3 * TOP]
    facts = jnp.concatenate(
        [jnp.where(side == 0, facts_mine, facts_other), jnp.where(side == 0, facts_other, facts_mine)], axis=1
    ).astype(jnp.float32)
    ids, share = facts[:, :, :TOP], facts[:, :, TOP : 2 * TOP] + facts[:, :, 2 * TOP :]
    own = (me * here + jnp.arange(here, dtype=jnp.int32)).astype(jnp.float32)
    hit = ids[:, :, :, None] == own
    hot = jnp.any(hit, axis=2)
    share = jnp.sum(jnp.where(hit, share[:, :, :, None], 0.0), axis=2)
    token = jnp.arange(local_rows, dtype=jnp.int32)
    before = (token[:, None] > token[None, :]).astype(jnp.bfloat16)
    rank = jnp.einsum("tu,cue->cte", before, hot.astype(jnp.bfloat16), preferred_element_type=jnp.float32)
    rank = jnp.where(hot, rank, -1.0)
    slot = jnp.arange(SLOTS, dtype=jnp.int32).astype(jnp.float32)
    combine = rank[:, :, :, None] == slot
    scale = jnp.sum(jnp.where(combine, share[:, :, :, None], 0.0), axis=1)
    scale = scale.transpose(1, 0, 2).reshape(here, count * SLOTS, 1)
    combine = combine.astype(jnp.bfloat16).reshape(count, local_rows, here * SLOTS)

    got = spread(normed, count)
    got_other = jnp.stack(each(swap, got, count))
    got = jnp.stack(got)

    def pick(rows):
        picked = jnp.einsum("cts,ctd->csd", combine, rows, preferred_element_type=jnp.float32)
        return picked.astype(jnp.bfloat16).reshape(count, here, SLOTS, rows.shape[2])

    hidden = up(info, pick(got), pick(got_other), w_gate, w_up, scale)
    away = down(info, hidden, w_down, combine, True)
    away = swap(away)
    kept = down(info, hidden, w_down, combine, False)
    sums = (kept.astype(jnp.float32) + away.astype(jnp.float32)).astype(jnp.bfloat16)
    mixture = collect([sums[c] for c in range(count)], count)
    return (middle.astype(jnp.float32) + mixture).astype(jnp.bfloat16)


def solution(mesh):
    in_specs = (
        P(("groups", "ctx"), "exp"),
        P(("groups", "ctx"), None),
        P(("groups", "ctx"), None),
        P("groups"),
        P("groups"),
        P(("groups", "ctx"), None),
        P(("groups", "ctx"), None),
        P(None, "exp"),
        P("exp", None),
        P(),
        P("ctx", None, "exp"),
        P("ctx", None, "exp"),
        P("ctx", "exp", None),
    )
    out_specs = P(("groups", "ctx"), "exp")
    return jax.shard_map(body, mesh=mesh, in_specs=in_specs, out_specs=out_specs, check_vma=False)
```

```python
import functools
import math

import jax
import jax.numpy as jnp
from jax import lax
from jax.experimental import pallas as pl
from jax.experimental.pallas import tpu as pltpu
from jax.sharding import PartitionSpec as P

NOPE = 128
ROPE = 64
VHEAD = 128
LAT = 512
EXPERTS = 64
TOP = 6
SLOTS = 16
WIDE = 640
VMEM_LIMIT = 56 * 1024 * 1024
SWAP = [(0, 1), (1, 0)]
FEW = 8


def grid_of(count):
    fast = 2 ** (int(math.log2(count)) // 2)
    return (count // fast, fast)


def shift_slow(value, step, count):
    slow, fast = grid_of(count)
    perm = [(i, (i // fast + step) % slow * fast + i % fast) for i in range(count)]
    return lax.ppermute(value, "ctx", perm)


def shift_fast(value, step, count):
    fast = grid_of(count)[1]
    perm = [(i, i // fast * fast + (i % fast + step) % fast) for i in range(count)]
    return lax.ppermute(value, "ctx", perm)


def swap(value):
    return lax.ppermute(value, "exp", SWAP)


def each(send, pieces, count):
    if count <= FEW:
        return [send(piece) for piece in pieces]
    return list(send(jnp.stack(list(pieces))))


def spread(block, count):
    slow, fast = grid_of(count)
    line = [block]
    for _ in range(1, slow):
        line.append(shift_slow(line[-1], 1, count))
    found = list(line)
    for r in range(1, fast):
        found += each(lambda piece: shift_fast(piece, r, count), line, count)
    return found


def summed(pieces):
    total = pieces[0].astype(jnp.float32)
    for piece in pieces[1:]:
        total = total + piece.astype(jnp.float32)
    return total


def collect(kept, away, count):
    slow, fast = grid_of(count)
    terms = [[kept[s], away[s]] for s in range(slow)]
    for r in range(1, fast):
        here = range(r * slow, (r + 1) * slow)
        parts = [summed([kept[c], away[c]]).astype(jnp.bfloat16) for c in here]
        for s, piece in enumerate(each(lambda piece: shift_fast(piece, -r, count), parts, count)):
            terms[s].append(piece)
    sums = [summed(pieces) for pieces in terms]
    arrived = [shift_slow(sums[s].astype(jnp.bfloat16), -s, count) for s in range(1, slow)]
    return summed([sums[0]] + arrived)


def owner_of(place, me, count):
    slow, fast = grid_of(count)
    r, s = place // slow, place % slow
    return (me // fast + slow - s) % slow * fast + (me % fast + fast - r) % fast


def attend_kernel(count, blocks, info, q_ref, mine_ref, other_ref, up_ref, proj_ref, out_ref, m_ref, l_ref, acc_ref):
    step = pl.program_id(0)
    me, side = info[0], info[1]
    segs = 16
    span = mine_ref.shape[1]
    heads, rows, _ = q_ref.shape

    @pl.when(step == 0)
    def _():
        m_ref[...] = jnp.full_like(m_ref, -1e30)
        l_ref[...] = jnp.zeros_like(l_ref)
        acc_ref[...] = jnp.zeros_like(acc_ref)

    row = lax.broadcasted_iota(jnp.int32, (rows, 1), 0)
    first = info[2 + segs + 2 * me] * span
    second = info[2 + segs + 2 * me + 1] * span
    qpos = jnp.where(row < span, first + row, second + row - span)
    low = jnp.zeros((rows, 1), jnp.int32)
    start = jnp.int32(0)
    for m in range(segs):
        low = jnp.where(qpos >= start, start, low)
        start = start + info[2 + m]
    keys = blocks * span
    lane = lax.broadcasted_iota(jnp.int32, (1, keys), 1)
    within, which = lane % span, lane // span
    kpos_parts = []
    for half in (side, 1 - side):
        base = jnp.zeros((1, keys), jnp.int32)
        for j in range(blocks):
            src = owner_of(step * blocks + j, me, count)
            base = jnp.where(which == j, info[2 + segs + 2 * src + half] * span, base)
        kpos_parts.append(base + within)
    kpos = jnp.concatenate(kpos_parts, axis=1)
    visible = (kpos >= low) & (kpos <= qpos)

    lat = jnp.concatenate([mine_ref[...].reshape(keys, WIDE), other_ref[...].reshape(keys, WIDE)], axis=0)
    keyval = jnp.dot(lat[:, :LAT], up_ref[...], preferred_element_type=jnp.float32).astype(jnp.bfloat16)
    rope = lat[:, LAT : LAT + ROPE]
    scale = 1.0 / math.sqrt(NOPE + ROPE)
    for h in range(heads):
        base = h * (NOPE + VHEAD)
        key = jnp.concatenate([keyval[:, base : base + NOPE], rope], axis=1)
        scores = lax.dot_general(q_ref[h], key, (((1,), (1,)), ((), ())), preferred_element_type=jnp.float32)
        scores = jnp.where(visible, scores * scale, -1e30)
        best = m_ref[h]
        fresh = jnp.maximum(best, jnp.max(scores, axis=1, keepdims=True))
        weights = jnp.where(visible, jnp.exp(scores - fresh), 0.0)
        shrink = jnp.exp(best - fresh)
        m_ref[h] = fresh
        l_ref[h] = l_ref[h] * shrink + jnp.sum(weights, axis=1, keepdims=True)
        mixed = jnp.dot(
            weights.astype(jnp.bfloat16), keyval[:, base + NOPE : base + NOPE + VHEAD], preferred_element_type=jnp.float32
        )
        acc_ref[h] = acc_ref[h] * shrink + mixed

    @pl.when(step == pl.num_programs(0) - 1)
    def _():
        attended = [(acc_ref[h] / l_ref[h]).astype(jnp.bfloat16) for h in range(heads)]
        out = jnp.dot(jnp.concatenate(attended, axis=1), proj_ref[...], preferred_element_type=jnp.float32)
        out_ref[...] = out.astype(jnp.bfloat16)


def attend(info, q, mine, other, kv_up, out_proj, count):
    heads, rows, depth = q.shape
    blocks = math.gcd(count, 8)
    span = mine.shape[1]
    whole2 = lambda i, *_: (0, 0)
    whole3 = lambda i, *_: (0, 0, 0)
    lat_spec = pl.BlockSpec((blocks, span, WIDE), lambda i, *_: (i, 0, 0))
    return pl.pallas_call(
        functools.partial(attend_kernel, count, blocks),
        grid_spec=pltpu.PrefetchScalarGridSpec(
            num_scalar_prefetch=1,
            grid=(count // blocks,),
            in_specs=[
                pl.BlockSpec(q.shape, whole3),
                lat_spec,
                lat_spec,
                pl.BlockSpec(kv_up.shape, whole2),
                pl.BlockSpec(out_proj.shape, whole2),
            ],
            out_specs=pl.BlockSpec((rows, out_proj.shape[1]), whole2),
            scratch_shapes=[
                pltpu.VMEM((heads, rows, 1), jnp.float32),
                pltpu.VMEM((heads, rows, 1), jnp.float32),
                pltpu.VMEM((heads, rows, VHEAD), jnp.float32),
            ],
        ),
        out_shape=jax.ShapeDtypeStruct((rows, out_proj.shape[1]), jnp.bfloat16),
        compiler_params=pltpu.CompilerParams(vmem_limit_bytes=VMEM_LIMIT),
        name="attend",
    )(info, q, mine, other, kv_up, out_proj)


def norm_kernel(info, residual_ref, here_ref, there_ref, gain_ref, middle_ref, normed_ref):
    side = info[1]
    half = middle_ref.shape[1]
    total = here_ref[...].astype(jnp.float32) + there_ref[...].astype(jnp.float32)
    middle = (residual_ref[...].astype(jnp.float32) + total).astype(jnp.bfloat16)
    wide = middle.astype(jnp.float32)
    inverse = lax.rsqrt(jnp.mean(wide * wide, axis=1, keepdims=True) + 1e-06)
    normed = wide * inverse * gain_ref[...].astype(jnp.float32)
    middle_ref[...] = jnp.where(side == 0, wide[:, :half], wide[:, half:]).astype(jnp.bfloat16)
    normed_ref[...] = jnp.where(side == 0, normed[:, :half], normed[:, half:]).astype(jnp.bfloat16)


def norm(info, residual, here, there, gain):
    rows, width = residual.shape
    half = jax.ShapeDtypeStruct((rows, width // 2), jnp.bfloat16)
    full = pl.BlockSpec((rows, width), lambda i, *_: (0, 0))
    part = pl.BlockSpec((rows, width // 2), lambda i, *_: (0, 0))
    return pl.pallas_call(
        norm_kernel,
        grid_spec=pltpu.PrefetchScalarGridSpec(
            num_scalar_prefetch=1,
            grid=(1,),
            in_specs=[full, full, full, pl.BlockSpec((1, width), lambda i, *_: (0, 0))],
            out_specs=[part, part],
        ),
        out_shape=[half, half],
        compiler_params=pltpu.CompilerParams(vmem_limit_bytes=VMEM_LIMIT),
        name="norm",
    )(info, residual, here, there, gain.reshape(1, width))


def pack_kernel(info, latent_ref, facts_ref, out_ref):
    rows = jnp.concatenate([latent_ref[...].astype(jnp.float32), facts_ref[...]], axis=0)
    span = out_ref.shape[0]
    tokens = rows.T.astype(jnp.bfloat16)
    out_ref[...] = jnp.where(info[1] == 0, tokens[:span], tokens[span:])


def pack(info, latent, expert_ids, route_weights):
    local_rows, base = latent.shape
    weights = route_weights.T
    high = lax.reduce_precision(weights, 8, 7)
    pad = jnp.zeros((WIDE - base - 3 * TOP, local_rows), jnp.float32)
    facts = jnp.concatenate([expert_ids.T.astype(jnp.float32), high, weights - high, pad], axis=0)
    return pl.pallas_call(
        pack_kernel,
        grid_spec=pltpu.PrefetchScalarGridSpec(
            num_scalar_prefetch=1,
            grid=(1,),
            in_specs=[
                pl.BlockSpec((base, local_rows), lambda i, *_: (0, 0)),
                pl.BlockSpec(facts.shape, lambda i, *_: (0, 0)),
            ],
            out_specs=pl.BlockSpec((local_rows // 2, WIDE), lambda i, *_: (0, 0)),
        ),
        out_shape=jax.ShapeDtypeStruct((local_rows // 2, WIDE), jnp.bfloat16),
        compiler_params=pltpu.CompilerParams(vmem_limit_bytes=VMEM_LIMIT),
        name="pack",
    )(info, latent.T, facts)


def expert_rows(rows, gate_ref, up_ref, down_ref, scale_ref):
    by_columns = (((1,), (1,)), ((), ()))
    gate = lax.dot_general(rows, gate_ref[0], by_columns, preferred_element_type=jnp.float32)
    upper = lax.dot_general(rows, up_ref[0], by_columns, preferred_element_type=jnp.float32)
    hidden = (gate / (1.0 + jnp.exp(-gate)) * upper * scale_ref[0]).astype(jnp.bfloat16)
    return jnp.dot(hidden, down_ref[0], preferred_element_type=jnp.float32).astype(jnp.bfloat16)


def plain_kernel(info, rows_ref, gate_ref, up_ref, down_ref, scale_ref, out_ref):
    out_ref[0] = expert_rows(rows_ref[0], gate_ref, up_ref, down_ref, scale_ref)


def fused_kernel(count, info, *refs):
    mine, other = refs[:count], refs[count : 2 * count]
    pick_ref, combine_ref, gate_ref, up_ref, down_ref, scale_ref = refs[2 * count : 2 * count + 6]
    kept, away = refs[2 * count + 6 : 3 * count + 6], refs[3 * count + 6 : 4 * count + 6]
    picked, held = refs[4 * count + 6 :]
    expert = pl.program_id(0)
    here = picked.shape[0]
    half = picked.shape[2] // 2
    side = info[1]
    near = pl.ds(pl.multiple_of(side * half, half), half)
    far = pl.ds(pl.multiple_of((1 - side) * half, half), half)

    @pl.when(expert == 0)
    def _():
        for c in range(count):
            for columns, block in ((near, mine[c]), (far, other[c])):
                rows = jnp.dot(pick_ref[c], block[...], preferred_element_type=jnp.float32).astype(jnp.bfloat16)
                for e in range(here):
                    picked[e, c * SLOTS : (c + 1) * SLOTS, columns] = rows[e * SLOTS : (e + 1) * SLOTS]

    result = expert_rows(picked[expert], gate_ref, up_ref, down_ref, scale_ref)
    place = pl.ds(pl.multiple_of(expert * SLOTS, SLOTS), SLOTS)
    for c in range(count):
        held[c, place, :] = result[c * SLOTS : (c + 1) * SLOTS]

    @pl.when(expert == here - 1)
    def _():
        for c in range(count):
            for columns, out in ((far, away[c]), (near, kept[c])):
                total = jnp.dot(combine_ref[c], held[c, :, columns], preferred_element_type=jnp.float32)
                out[...] = total.astype(jnp.bfloat16)


def expert_specs(w_gate, rows):
    hidden, width = w_gate.shape[1:]
    weight = pl.BlockSpec((1, hidden, width), lambda e, info: (e, 0, 0))
    return [weight, weight, weight, pl.BlockSpec((1, rows, 1), lambda e, info: (e, 0, 0))]


def experts_plain(info, picked, w_gate, w_up, w_down, scale):
    here, rows, width = picked.shape
    rows_spec = pl.BlockSpec((1, rows, width), lambda e, info: (e, 0, 0))
    return pl.pallas_call(
        plain_kernel,
        grid_spec=pltpu.PrefetchScalarGridSpec(
            num_scalar_prefetch=1,
            grid=(here,),
            in_specs=[rows_spec] + expert_specs(w_gate, rows),
            out_specs=rows_spec,
        ),
        out_shape=jax.ShapeDtypeStruct(picked.shape, jnp.bfloat16),
        compiler_params=pltpu.CompilerParams(vmem_limit_bytes=VMEM_LIMIT),
        name="experts",
    )(info, picked, w_gate, w_up, w_down, scale)


def experts_fused(info, mine, other, pick, combine, w_gate, w_up, w_down, scale):
    count, (local, half) = len(mine), mine[0].shape
    here, rows, _ = scale.shape
    whole = pl.BlockSpec((local, half), lambda e, info: (0, 0))
    outs = pl.pallas_call(
        functools.partial(fused_kernel, count),
        grid_spec=pltpu.PrefetchScalarGridSpec(
            num_scalar_prefetch=1,
            grid=(here,),
            in_specs=[whole] * (2 * count)
            + [pl.BlockSpec(pick.shape, lambda e, info: (0, 0, 0)), pl.BlockSpec(combine.shape, lambda e, info: (0, 0, 0))]
            + expert_specs(w_gate, rows),
            out_specs=[whole] * (2 * count),
            scratch_shapes=[
                pltpu.VMEM((here, rows, 2 * half), jnp.bfloat16),
                pltpu.VMEM((count, here * SLOTS, 2 * half), jnp.bfloat16),
            ],
        ),
        out_shape=[jax.ShapeDtypeStruct((local, half), jnp.bfloat16)] * (2 * count),
        compiler_params=pltpu.CompilerParams(vmem_limit_bytes=VMEM_LIMIT),
        name="experts",
    )(info, *mine, *other, pick, combine, w_gate, w_up, w_down, scale)
    return outs[:count], outs[count:]


def body(
    queries,
    latent,
    residual,
    seg_lengths,
    span_order,
    expert_ids,
    route_weights,
    kv_up,
    out_proj,
    norm_gain,
    w_gate,
    w_up,
    w_down,
):
    local_rows, width = residual.shape
    span = local_rows // 2
    heads = kv_up.shape[1] // (NOPE + VHEAD)
    count = lax.axis_size("ctx")
    here = EXPERTS // count
    me, side = lax.axis_index("ctx"), lax.axis_index("exp")
    info = jnp.concatenate([jnp.stack([me, side]).astype(jnp.int32), seg_lengths, span_order])

    base = latent.shape[1]
    found = spread(pack(info, latent, expert_ids, route_weights), count)
    mine = jnp.stack(found)
    other = jnp.stack(each(swap, found, count))

    q = queries.reshape(local_rows, heads, NOPE + ROPE).transpose(1, 0, 2)
    partial = attend(info, q, mine, other, kv_up, out_proj, count)
    middle, normed = norm(info, residual, partial, swap(partial), norm_gain)

    facts_mine, facts_other = mine[:, :, base : base + 3 * TOP], other[:, :, base : base + 3 * TOP]
    facts = jnp.concatenate(
        [jnp.where(side == 0, facts_mine, facts_other), jnp.where(side == 0, facts_other, facts_mine)], axis=1
    ).astype(jnp.float32)
    ids, share = facts[:, :, :TOP], facts[:, :, TOP : 2 * TOP] + facts[:, :, 2 * TOP :]
    own = (me * here + jnp.arange(here, dtype=jnp.int32)).astype(jnp.float32)
    hit = ids[:, :, :, None] == own
    hot = jnp.any(hit, axis=2)
    share = jnp.sum(jnp.where(hit, share[:, :, :, None], 0.0), axis=2)
    token = jnp.arange(local_rows, dtype=jnp.int32)
    before = (token[:, None] > token[None, :]).astype(jnp.bfloat16)
    rank = jnp.einsum("tu,cue->cte", before, hot.astype(jnp.bfloat16), preferred_element_type=jnp.float32)
    rank = jnp.where(hot, rank, -1.0)
    slot = jnp.arange(SLOTS, dtype=jnp.int32).astype(jnp.float32)
    combine = rank[:, :, :, None] == slot
    scale = jnp.sum(jnp.where(combine, share[:, :, :, None], 0.0), axis=1)
    scale = scale.transpose(1, 0, 2).reshape(here, count * SLOTS, 1)
    combine = combine.astype(jnp.bfloat16).reshape(count, local_rows, here * SLOTS)
    pick = combine.transpose(0, 2, 1)

    got = spread(normed, count)
    got_other = each(swap, got, count)
    w_gate, w_up = w_gate.transpose(0, 2, 1), w_up.transpose(0, 2, 1)
    if count <= FEW:
        kept, away = experts_fused(info, got, got_other, pick, combine, w_gate, w_up, w_down, scale)
    else:
        near, far = jnp.stack(got), jnp.stack(got_other)
        full = jnp.concatenate([jnp.where(side == 0, near, far), jnp.where(side == 0, far, near)], axis=2)
        picked = jnp.einsum("cst,ctd->csd", pick, full, preferred_element_type=jnp.float32).astype(jnp.bfloat16)
        picked = picked.reshape(count, here, SLOTS, width).transpose(1, 0, 2, 3).reshape(here, count * SLOTS, width)
        result = experts_plain(info, picked, w_gate, w_up, w_down, scale)
        result = result.reshape(here, count, SLOTS, width).transpose(1, 0, 2, 3).reshape(count, here * SLOTS, width)
        total = jnp.einsum("cts,csd->ctd", combine, result, preferred_element_type=jnp.float32).astype(jnp.bfloat16)
        left, right = jnp.split(total, 2, axis=2)
        kept, away = jnp.where(side == 0, left, right), jnp.where(side == 0, right, left)
    away = each(swap, away, count)
    mixture = collect(kept, away, count)
    return (middle.astype(jnp.float32) + mixture).astype(jnp.bfloat16)


def solution(mesh):
    in_specs = (
        P(("groups", "ctx"), "exp"),
        P(("groups", "ctx"), None),
        P(("groups", "ctx"), None),
        P("groups"),
        P("groups"),
        P(("groups", "ctx"), None),
        P(("groups", "ctx"), None),
        P(None, "exp"),
        P("exp", None),
        P(),
        P("ctx", None, "exp"),
        P("ctx", None, "exp"),
        P("ctx", "exp", None),
    )
    out_specs = P(("groups", "ctx"), "exp")
    return jax.shard_map(body, mesh=mesh, in_specs=in_specs, out_specs=out_specs, check_vma=False)
```

```python
import functools
import math

import jax
import jax.numpy as jnp
from jax import lax
from jax.experimental import pallas as pl
from jax.experimental.pallas import tpu as pltpu
from jax.sharding import PartitionSpec as P

NOPE = 128
ROPE = 64
VHEAD = 128
LAT = 512
EXPERTS = 64
TOP = 6
SLOTS = 16
WIDE = 640
VMEM_LIMIT = 56 * 1024 * 1024
SWAP = [(0, 1), (1, 0)]
FEW = 8


def grid_of(count):
    fast = 2 ** (int(math.log2(count)) // 2)
    return (count // fast, fast)


def shift_slow(value, step, count):
    slow, fast = grid_of(count)
    perm = [(i, (i // fast + step) % slow * fast + i % fast) for i in range(count)]
    return lax.ppermute(value, "ctx", perm)


def shift_fast(value, step, count):
    fast = grid_of(count)[1]
    perm = [(i, i // fast * fast + (i % fast + step) % fast) for i in range(count)]
    return lax.ppermute(value, "ctx", perm)


def swap(value):
    return lax.ppermute(value, "exp", SWAP)


def each(send, pieces, count):
    if count <= FEW:
        return [send(piece) for piece in pieces]
    return list(send(jnp.stack(list(pieces))))


def ring(block, count):
    line = [block]
    for _ in range(1, grid_of(count)[0]):
        line.append(shift_slow(line[-1], 1, count))
    return line


def direct(block, count):
    return [block] + [shift_slow(block, s, count) for s in range(1, grid_of(count)[0])]


def across(line, count):
    found = list(line)
    for r in range(1, grid_of(count)[1]):
        found += each(lambda piece: shift_fast(piece, r, count), line, count)
    return found


def summed(pieces):
    total = pieces[0].astype(jnp.float32)
    for piece in pieces[1:]:
        total = total + piece.astype(jnp.float32)
    return total


def collect(near, swapped, combine, count):
    slow, fast = grid_of(count)

    def part(c):
        rows = (near[c].astype(jnp.float32) + swapped[c].astype(jnp.float32)).astype(jnp.bfloat16)
        return jnp.dot(combine[c], rows, preferred_element_type=jnp.float32)

    terms = [[] for _ in range(slow)]
    for r in range(1, fast):
        parts = [part(r * slow + s).astype(jnp.bfloat16) for s in reversed(range(slow))]
        arrived = each(lambda piece: shift_fast(piece, -r, count), parts, count)
        for s, piece in zip(reversed(range(slow)), arrived):
            terms[s].append(piece)
    sums = [summed([part(s)] + terms[s]) for s in range(slow)]
    arrived = [shift_slow(sums[s].astype(jnp.bfloat16), -s, count) for s in range(1, slow)]
    return summed([sums[0]] + arrived)


def owner_of(place, me, count):
    slow, fast = grid_of(count)
    r, s = place // slow, place % slow
    return (me // fast + slow - s) % slow * fast + (me % fast + fast - r) % fast


def attend_kernel(count, blocks, where, lengths, order, q_ref, mine_ref, other_ref, up_ref, proj_ref, out_ref, m_ref, l_ref, acc_ref):
    step = pl.program_id(0)
    me, side = where[0], where[1]
    segs = lengths.shape[0]
    span = mine_ref.shape[1]
    heads, rows, _ = q_ref.shape

    @pl.when(step == 0)
    def _():
        m_ref[...] = jnp.full_like(m_ref, -1e30)
        l_ref[...] = jnp.zeros_like(l_ref)
        acc_ref[...] = jnp.zeros_like(acc_ref)

    row = lax.broadcasted_iota(jnp.int32, (rows, 1), 0)
    first = order[2 * me] * span
    second = order[2 * me + 1] * span
    qpos = jnp.where(row < span, first + row, second + row - span)
    low = jnp.zeros((rows, 1), jnp.int32)
    start = jnp.int32(0)
    for m in range(segs):
        low = jnp.where(qpos >= start, start, low)
        start = start + lengths[m]
    keys = blocks * span
    lane = lax.broadcasted_iota(jnp.int32, (1, keys), 1)
    within, which = lane % span, lane // span
    kpos_parts = []
    for half in (side, 1 - side):
        base = jnp.zeros((1, keys), jnp.int32)
        for j in range(blocks):
            src = owner_of(step * blocks + j, me, count)
            base = jnp.where(which == j, order[2 * src + half] * span, base)
        kpos_parts.append(base + within)
    kpos = jnp.concatenate(kpos_parts, axis=1)
    visible = (kpos >= low) & (kpos <= qpos)

    lat = jnp.concatenate([mine_ref[...].reshape(keys, WIDE), other_ref[...].reshape(keys, WIDE)], axis=0)
    keyval = jnp.dot(lat[:, :LAT], up_ref[...], preferred_element_type=jnp.float32).astype(jnp.bfloat16)
    rope = lat[:, LAT : LAT + ROPE]
    scale = 1.0 / math.sqrt(NOPE + ROPE)
    for h in range(heads):
        base = h * (NOPE + VHEAD)
        key = jnp.concatenate([keyval[:, base : base + NOPE], rope], axis=1)
        scores = lax.dot_general(q_ref[h], key, (((1,), (1,)), ((), ())), preferred_element_type=jnp.float32)
        scores = jnp.where(visible, scores * scale, -1e30)
        best = m_ref[h]
        fresh = jnp.maximum(best, jnp.max(scores, axis=1, keepdims=True))
        weights = jnp.where(visible, jnp.exp(scores - fresh), 0.0)
        shrink = jnp.exp(best - fresh)
        m_ref[h] = fresh
        l_ref[h] = l_ref[h] * shrink + jnp.sum(weights, axis=1, keepdims=True)
        mixed = jnp.dot(
            weights.astype(jnp.bfloat16), keyval[:, base + NOPE : base + NOPE + VHEAD], preferred_element_type=jnp.float32
        )
        acc_ref[h] = acc_ref[h] * shrink + mixed

    @pl.when(step == pl.num_programs(0) - 1)
    def _():
        attended = [(acc_ref[h] / l_ref[h]).astype(jnp.bfloat16) for h in range(heads)]
        out = jnp.dot(jnp.concatenate(attended, axis=1), proj_ref[...], preferred_element_type=jnp.float32)
        out_ref[...] = out.astype(jnp.bfloat16)


def attend(where, lengths, order, q, mine, other, kv_up, out_proj, count):
    heads, rows, depth = q.shape
    blocks = math.gcd(count, 8)
    span = mine.shape[1]
    whole2 = lambda i, *_: (0, 0)
    whole3 = lambda i, *_: (0, 0, 0)
    lat_spec = pl.BlockSpec((blocks, span, WIDE), lambda i, *_: (i, 0, 0))
    return pl.pallas_call(
        functools.partial(attend_kernel, count, blocks),
        grid_spec=pltpu.PrefetchScalarGridSpec(
            num_scalar_prefetch=3,
            grid=(count // blocks,),
            in_specs=[
                pl.BlockSpec(q.shape, whole3),
                lat_spec,
                lat_spec,
                pl.BlockSpec(kv_up.shape, whole2),
                pl.BlockSpec(out_proj.shape, whole2),
            ],
            out_specs=pl.BlockSpec((rows, out_proj.shape[1]), whole2),
            scratch_shapes=[
                pltpu.VMEM((heads, rows, 1), jnp.float32),
                pltpu.VMEM((heads, rows, 1), jnp.float32),
                pltpu.VMEM((heads, rows, VHEAD), jnp.float32),
            ],
        ),
        out_shape=jax.ShapeDtypeStruct((rows, out_proj.shape[1]), jnp.bfloat16),
        compiler_params=pltpu.CompilerParams(vmem_limit_bytes=VMEM_LIMIT),
        name="attend",
    )(where, lengths, order, q, mine, other, kv_up, out_proj)


def norm_kernel(where, residual_ref, here_ref, there_ref, gain_ref, middle_ref, upper_ref, lower_ref):
    side = where[1]
    half = middle_ref.shape[1]
    total = here_ref[...].astype(jnp.float32) + there_ref[...].astype(jnp.float32)
    middle = (residual_ref[...].astype(jnp.float32) + total).astype(jnp.bfloat16)
    wide = middle.astype(jnp.float32)
    inverse = lax.rsqrt(jnp.mean(wide * wide, axis=1, keepdims=True) + 1e-06)
    normed = wide * inverse * gain_ref[...].astype(jnp.float32)
    middle_ref[...] = jnp.where(side == 0, wide[:, :half], wide[:, half:]).astype(jnp.bfloat16)
    normed = jnp.where(side == 0, normed[:, :half], normed[:, half:]).astype(jnp.bfloat16)
    span = upper_ref.shape[0]
    upper_ref[...] = normed[:span]
    lower_ref[...] = normed[span:]


def norm(where, residual, here, there, gain):
    rows, width = residual.shape
    half = lambda size: jax.ShapeDtypeStruct((size, width // 2), jnp.bfloat16)
    full = pl.BlockSpec((rows, width), lambda i, *_: (0, 0))
    part = lambda size: pl.BlockSpec((size, width // 2), lambda i, *_: (0, 0))
    return pl.pallas_call(
        norm_kernel,
        grid_spec=pltpu.PrefetchScalarGridSpec(
            num_scalar_prefetch=1,
            grid=(1,),
            in_specs=[full, full, full, pl.BlockSpec((1, width), lambda i, *_: (0, 0))],
            out_specs=[part(rows), part(rows // 2), part(rows // 2)],
        ),
        out_shape=[half(rows), half(rows // 2), half(rows // 2)],
        compiler_params=pltpu.CompilerParams(vmem_limit_bytes=VMEM_LIMIT),
        name="norm",
    )(where, residual, here, there, gain.reshape(1, width))


def pack_kernel(where, latent_ref, ids_ref, weights_ref, out_ref, rows):
    base, tokens = latent_ref.shape
    span = out_ref.shape[0]
    weights = weights_ref[...]
    high = weights.astype(jnp.bfloat16).astype(jnp.float32)
    rows[...] = jnp.zeros_like(rows)
    rows[0:TOP] = ids_ref[...].astype(jnp.float32)
    rows[TOP : 2 * TOP] = high
    rows[2 * TOP : 3 * TOP] = weights - high
    row = lax.broadcasted_iota(jnp.int32, (span, tokens), 0) + where[1] * span
    chosen = (row == lax.broadcasted_iota(jnp.int32, (span, tokens), 1)).astype(jnp.float32).astype(jnp.bfloat16)
    turn = lambda value: lax.dot_general(
        chosen, value, (((1,), (1,)), ((), ())), preferred_element_type=jnp.float32
    ).astype(jnp.bfloat16)
    every = jnp.concatenate([latent_ref[...], rows[...].astype(jnp.bfloat16)], axis=0)
    out_ref[...] = turn(every)


def pack(where, latent, expert_ids, route_weights):
    local_rows, base = latent.shape
    whole = lambda i, *_: (0, 0)
    return pl.pallas_call(
        pack_kernel,
        grid_spec=pltpu.PrefetchScalarGridSpec(
            num_scalar_prefetch=1,
            grid=(1,),
            in_specs=[
                pl.BlockSpec((base, local_rows), whole),
                pl.BlockSpec((TOP, local_rows), whole),
                pl.BlockSpec((TOP, local_rows), whole),
            ],
            out_specs=pl.BlockSpec((local_rows // 2, WIDE), whole),
            scratch_shapes=[pltpu.VMEM((WIDE - base, local_rows), jnp.float32)],
        ),
        out_shape=jax.ShapeDtypeStruct((local_rows // 2, WIDE), jnp.bfloat16),
        compiler_params=pltpu.CompilerParams(vmem_limit_bytes=VMEM_LIMIT),
        name="pack",
    )(where, latent.T, expert_ids.T, route_weights.T)


def expert_rows(rows, gate_ref, up_ref, down_ref, scale_ref):
    by_columns = (((1,), (1,)), ((), ()))
    gate = lax.dot_general(rows, gate_ref[0], by_columns, preferred_element_type=jnp.float32)
    upper = lax.dot_general(rows, up_ref[0], by_columns, preferred_element_type=jnp.float32)
    hidden = (gate / (1.0 + jnp.exp(-gate)) * upper * scale_ref[0]).astype(jnp.bfloat16)
    return jnp.dot(hidden, down_ref[0], preferred_element_type=jnp.float32).astype(jnp.bfloat16)


def plain_kernel(where, rows_ref, gate_ref, up_ref, down_ref, scale_ref, out_ref):
    out_ref[0] = expert_rows(rows_ref[0], gate_ref, up_ref, down_ref, scale_ref)


def fused_kernel(count, where, *refs):
    mine, other = refs[:count], refs[count : 2 * count]
    gate_ref, up_ref, down_ref, scale_ref = refs[2 * count : 2 * count + 4]
    kept, away = refs[2 * count + 4 : 3 * count + 4], refs[3 * count + 4 : 4 * count + 4]
    rows, result = refs[4 * count + 4 :]
    half = mine[0].shape[1]
    side = where[1]
    near = pl.ds(pl.multiple_of(side * half, half), half)
    far = pl.ds(pl.multiple_of((1 - side) * half, half), half)
    place = pl.ds(pl.multiple_of(pl.program_id(0) * SLOTS, SLOTS), SLOTS)
    for c in range(count):
        rows[c * SLOTS : (c + 1) * SLOTS, near] = mine[c][place, :]
        rows[c * SLOTS : (c + 1) * SLOTS, far] = other[c][place, :]
    result[...] = expert_rows(rows[...], gate_ref, up_ref, down_ref, scale_ref)
    for c in range(count):
        kept[c][place, :] = result[c * SLOTS : (c + 1) * SLOTS, near]
        away[c][place, :] = result[c * SLOTS : (c + 1) * SLOTS, far]


def expert_specs(w_gate, rows):
    hidden, width = w_gate.shape[1:]
    weight = pl.BlockSpec((1, hidden, width), lambda e, where: (e, 0, 0))
    return [weight, weight, weight, pl.BlockSpec((1, rows, 1), lambda e, where: (e, 0, 0))]


def experts_plain(where, picked, w_gate, w_up, w_down, scale):
    here, rows, width = picked.shape
    rows_spec = pl.BlockSpec((1, rows, width), lambda e, where: (e, 0, 0))
    return pl.pallas_call(
        plain_kernel,
        grid_spec=pltpu.PrefetchScalarGridSpec(
            num_scalar_prefetch=1,
            grid=(here,),
            in_specs=[rows_spec] + expert_specs(w_gate, rows),
            out_specs=rows_spec,
        ),
        out_shape=jax.ShapeDtypeStruct(picked.shape, jnp.bfloat16),
        compiler_params=pltpu.CompilerParams(vmem_limit_bytes=VMEM_LIMIT),
        name="experts",
    )(where, picked, w_gate, w_up, w_down, scale)


def experts_fused(where, mine, other, w_gate, w_up, w_down, scale):
    count, (slots, half) = len(mine), mine[0].shape
    here, rows, _ = scale.shape
    whole = pl.BlockSpec((slots, half), lambda e, where: (0, 0))
    outs = pl.pallas_call(
        functools.partial(fused_kernel, count),
        grid_spec=pltpu.PrefetchScalarGridSpec(
            num_scalar_prefetch=1,
            grid=(here,),
            in_specs=[whole] * (2 * count) + expert_specs(w_gate, rows),
            out_specs=[whole] * (2 * count),
            scratch_shapes=[pltpu.VMEM((rows, 2 * half), jnp.bfloat16)] * 2,
        ),
        out_shape=[jax.ShapeDtypeStruct((slots, half), jnp.bfloat16)] * (2 * count),
        compiler_params=pltpu.CompilerParams(vmem_limit_bytes=VMEM_LIMIT),
        name="experts",
    )(where, *mine, *other, w_gate, w_up, w_down, scale)
    return outs[:count], outs[count:]


def body(
    queries,
    latent,
    residual,
    seg_lengths,
    span_order,
    expert_ids,
    route_weights,
    kv_up,
    out_proj,
    norm_gain,
    w_gate,
    w_up,
    w_down,
):
    local_rows, width = residual.shape
    span = local_rows // 2
    heads = kv_up.shape[1] // (NOPE + VHEAD)
    count = lax.axis_size("ctx")
    here = EXPERTS // count
    me, side = lax.axis_index("ctx"), lax.axis_index("exp")
    where = jnp.stack([me, side]).astype(jnp.int32)

    base = latent.shape[1]
    found = across(direct(pack(where, latent, expert_ids, route_weights), count), count)
    mine = jnp.stack(found)
    other = jnp.stack(each(swap, found, count))

    q = queries.reshape(local_rows, heads, NOPE + ROPE).transpose(1, 0, 2)
    partial = attend(where, seg_lengths, span_order, q, mine, other, kv_up, out_proj, count)
    middle, upper, lower = norm(where, residual, partial, swap(partial), norm_gain)

    facts_mine, facts_other = mine[:, :, base : base + 3 * TOP], other[:, :, base : base + 3 * TOP]
    facts = jnp.concatenate(
        [jnp.where(side == 0, facts_mine, facts_other), jnp.where(side == 0, facts_other, facts_mine)], axis=1
    ).astype(jnp.float32)
    ids, share = facts[:, :, :TOP], facts[:, :, TOP : 2 * TOP] + facts[:, :, 2 * TOP :]
    own = (me * here + jnp.arange(here, dtype=jnp.int32)).astype(jnp.float32)
    hit = ids[:, :, :, None] == own
    hot = jnp.any(hit, axis=2)
    share = jnp.sum(jnp.where(hit, share[:, :, :, None], 0.0), axis=2)
    token = jnp.arange(local_rows, dtype=jnp.int32)
    before = (token[:, None] > token[None, :]).astype(jnp.bfloat16)
    rank = jnp.einsum("tu,cue->cte", before, hot.astype(jnp.bfloat16), preferred_element_type=jnp.float32)
    rank = jnp.where(hot, rank, -1.0)
    slot = jnp.arange(SLOTS, dtype=jnp.int32).astype(jnp.float32)
    combine = rank[:, :, :, None] == slot
    scale = jnp.sum(jnp.where(combine, share[:, :, :, None], 0.0), axis=1)
    scale = scale.transpose(1, 0, 2).reshape(here, count * SLOTS, 1)
    combine = combine.astype(jnp.bfloat16).reshape(count, local_rows, here * SLOTS)
    pick = combine.transpose(0, 2, 1)

    lines = [ring(upper, count), ring(lower, count)]
    lines[0][1], pick, combine, scale = lax.optimization_barrier((lines[0][1], pick, combine, scale))
    halves = [across(line, count) for line in lines]
    got = [jnp.concatenate(pair, axis=0) for pair in zip(*halves)]
    got_other = each(swap, got, count)
    w_gate, w_up = w_gate.transpose(0, 2, 1), w_up.transpose(0, 2, 1)
    if count <= FEW:
        choose = lambda c, rows: jnp.dot(pick[c], rows, preferred_element_type=jnp.float32).astype(jnp.bfloat16)
        mine = [choose(c, got[c]) for c in range(count)]
        other = [choose(c, got_other[c]) for c in range(count)]
        kept, away = experts_fused(where, mine, other, w_gate, w_up, w_down, scale)
    else:
        near, far = jnp.stack(got), jnp.stack(got_other)
        full = jnp.concatenate([jnp.where(side == 0, near, far), jnp.where(side == 0, far, near)], axis=2)
        picked = jnp.einsum("cst,ctd->csd", pick, full, preferred_element_type=jnp.float32).astype(jnp.bfloat16)
        picked = picked.reshape(count, here, SLOTS, width).transpose(1, 0, 2, 3).reshape(here, count * SLOTS, width)
        result = experts_plain(where, picked, w_gate, w_up, w_down, scale)
        result = result.reshape(here, count, SLOTS, width).transpose(1, 0, 2, 3).reshape(count, here * SLOTS, width)
        left, right = jnp.split(result, 2, axis=2)
        kept, away = jnp.where(side == 0, left, right), jnp.where(side == 0, right, left)
    mixture = collect(kept, each(swap, away, count), combine, count)
    return (middle.astype(jnp.float32) + mixture).astype(jnp.bfloat16)


def solution(mesh):
    in_specs = (
        P(("groups", "ctx"), "exp"),
        P(("groups", "ctx"), None),
        P(("groups", "ctx"), None),
        P("groups"),
        P("groups"),
        P(("groups", "ctx"), None),
        P(("groups", "ctx"), None),
        P(None, "exp"),
        P("exp", None),
        P(),
        P("ctx", None, "exp"),
        P("ctx", None, "exp"),
        P("ctx", "exp", None),
    )
    out_specs = P(("groups", "ctx"), "exp")
    return jax.shard_map(body, mesh=mesh, in_specs=in_specs, out_specs=out_specs, check_vma=False)
```

```python
import functools
import math

import jax
import jax.numpy as jnp
import numpy as np
from jax import lax
from jax.experimental import pallas as pl
from jax.experimental.pallas import tpu as pltpu
from jax.sharding import PartitionSpec as P

NOPE = 128
ROPE = 64
VHEAD = 128
LAT = 512
EXPERTS = 64
TOP = 6
SLOTS = 16
WIDE = 640
VMEM_LIMIT = 56 * 1024 * 1024
SWAP = [(0, 1), (1, 0)]
FEW = 8


def cycle_of(count):
    fast = 2 ** (int(math.log2(count)) // 2)
    slow = count // fast
    cycle = [0]
    for i in range(slow):
        columns = range(1, fast)
        cycle += [i * fast + j for j in (columns if i % 2 == 0 else reversed(columns))]
    return cycle + [i * fast for i in reversed(range(1, slow))]


def step(value, ahead, count):
    cycle = cycle_of(count)
    return lax.ppermute(value, "ctx", [(cycle[p], cycle[(p + ahead) % count]) for p in range(count)])


def swap(value):
    return lax.ppermute(value, "exp", SWAP)


def summed(pieces):
    total = pieces[0].astype(jnp.float32)
    for piece in pieces[1:]:
        total = total + piece.astype(jnp.float32)
    return total


def sources_of(me, count):
    if count > FEW:
        return jnp.arange(count, dtype=jnp.int32)
    cycle = cycle_of(count)
    table = np.zeros((count, count), np.int32)
    for p in range(count):
        table[cycle[p]] = [cycle[p - d] for d in range(count)]
    return lax.dynamic_index_in_dim(jnp.asarray(table), me, keepdims=False)


def gather(block, count):
    if count > FEW:
        return list(lax.all_gather(block, "ctx"))
    middle = count // 2
    found = [None] * count
    found[0] = block
    for d in range(1, middle):
        found[d] = step(found[d - 1], 1, count)
        found[-d] = step(found[(1 - d) % count], -1, count)
    half = block.shape[0] // 2
    ahead, back = step(found[middle - 1][:half], 1, count), step(found[middle + 1][half:], -1, count)
    found[middle] = jnp.concatenate([ahead, back], axis=0)
    return found


def reduce(parts, count):
    if count > FEW:
        return lax.psum_scatter(jnp.stack([part() for part in parts]).astype(jnp.bfloat16), "ctx").astype(jnp.float32)
    middle = count // 2
    first = parts[middle]().astype(jnp.bfloat16)
    half = first.shape[0] // 2
    zero = jnp.zeros((half, first.shape[1]), jnp.bfloat16)
    ahead = jnp.concatenate([step(first[:half], 1, count), zero], axis=0)
    back = jnp.concatenate([zero, step(first[half:], -1, count)], axis=0)
    for d in range(middle - 1, 0, -1):
        ahead = step((parts[count - d]() + ahead.astype(jnp.float32)).astype(jnp.bfloat16), 1, count)
        back = step((parts[d]() + back.astype(jnp.float32)).astype(jnp.bfloat16), -1, count)
    return parts[0]() + ahead.astype(jnp.float32) + back.astype(jnp.float32)


def attend_kernel(blocks, where, sources, lengths, order, q_ref, mine_ref, other_ref, up_ref, proj_ref, out_ref, m_ref, l_ref, acc_ref):
    chunk = pl.program_id(0)
    me, side = where[0], where[1]
    segs = lengths.shape[0]
    span = mine_ref.shape[1]
    heads, rows, _ = q_ref.shape

    @pl.when(chunk == 0)
    def _():
        m_ref[...] = jnp.full_like(m_ref, -1e30)
        l_ref[...] = jnp.zeros_like(l_ref)
        acc_ref[...] = jnp.zeros_like(acc_ref)

    row = lax.broadcasted_iota(jnp.int32, (rows, 1), 0)
    first = order[2 * me] * span
    second = order[2 * me + 1] * span
    qpos = jnp.where(row < span, first + row, second + row - span)
    low = jnp.zeros((rows, 1), jnp.int32)
    start = jnp.int32(0)
    for m in range(segs):
        low = jnp.where(qpos >= start, start, low)
        start = start + lengths[m]
    keys = blocks * span
    lane = lax.broadcasted_iota(jnp.int32, (1, keys), 1)
    within, which = lane % span, lane // span
    kpos_parts = []
    for half in (side, 1 - side):
        base = jnp.zeros((1, keys), jnp.int32)
        for j in range(blocks):
            src = sources[chunk * blocks + j]
            base = jnp.where(which == j, order[2 * src + half] * span, base)
        kpos_parts.append(base + within)
    kpos = jnp.concatenate(kpos_parts, axis=1)
    visible = (kpos >= low) & (kpos <= qpos)

    lat = jnp.concatenate([mine_ref[...].reshape(keys, WIDE), other_ref[...].reshape(keys, WIDE)], axis=0)
    keyval = jnp.dot(lat[:, :LAT], up_ref[...], preferred_element_type=jnp.float32).astype(jnp.bfloat16)
    rope = lat[:, LAT : LAT + ROPE]
    scale = 1.0 / math.sqrt(NOPE + ROPE)
    for h in range(heads):
        base = h * (NOPE + VHEAD)
        key = jnp.concatenate([keyval[:, base : base + NOPE], rope], axis=1)
        scores = lax.dot_general(q_ref[h], key, (((1,), (1,)), ((), ())), preferred_element_type=jnp.float32)
        scores = jnp.where(visible, scores * scale, -1e30)
        best = m_ref[h]
        fresh = jnp.maximum(best, jnp.max(scores, axis=1, keepdims=True))
        weights = jnp.where(visible, jnp.exp(scores - fresh), 0.0)
        shrink = jnp.exp(best - fresh)
        m_ref[h] = fresh
        l_ref[h] = l_ref[h] * shrink + jnp.sum(weights, axis=1, keepdims=True)
        mixed = jnp.dot(
            weights.astype(jnp.bfloat16), keyval[:, base + NOPE : base + NOPE + VHEAD], preferred_element_type=jnp.float32
        )
        acc_ref[h] = acc_ref[h] * shrink + mixed

    @pl.when(chunk == pl.num_programs(0) - 1)
    def _():
        attended = [(acc_ref[h] / l_ref[h]).astype(jnp.bfloat16) for h in range(heads)]
        out = jnp.dot(jnp.concatenate(attended, axis=1), proj_ref[...], preferred_element_type=jnp.float32)
        out_ref[...] = out.astype(jnp.bfloat16)


def attend(where, sources, lengths, order, q, mine, other, kv_up, out_proj, count):
    heads, rows, depth = q.shape
    blocks = math.gcd(count, 8)
    span = mine.shape[1]
    whole2 = lambda i, *_: (0, 0)
    whole3 = lambda i, *_: (0, 0, 0)
    lat_spec = pl.BlockSpec((blocks, span, WIDE), lambda i, *_: (i, 0, 0))
    return pl.pallas_call(
        functools.partial(attend_kernel, blocks),
        grid_spec=pltpu.PrefetchScalarGridSpec(
            num_scalar_prefetch=4,
            grid=(count // blocks,),
            in_specs=[
                pl.BlockSpec(q.shape, whole3),
                lat_spec,
                lat_spec,
                pl.BlockSpec(kv_up.shape, whole2),
                pl.BlockSpec(out_proj.shape, whole2),
            ],
            out_specs=pl.BlockSpec((rows, out_proj.shape[1]), whole2),
            scratch_shapes=[
                pltpu.VMEM((heads, rows, 1), jnp.float32),
                pltpu.VMEM((heads, rows, 1), jnp.float32),
                pltpu.VMEM((heads, rows, VHEAD), jnp.float32),
            ],
        ),
        out_shape=jax.ShapeDtypeStruct((rows, out_proj.shape[1]), jnp.bfloat16),
        compiler_params=pltpu.CompilerParams(vmem_limit_bytes=VMEM_LIMIT),
        name="attend",
    )(where, sources, lengths, order, q, mine, other, kv_up, out_proj)


def norm_kernel(where, residual_ref, here_ref, there_ref, gain_ref, middle_ref, normed_ref):
    side = where[1]
    half = middle_ref.shape[1]
    total = here_ref[...].astype(jnp.float32) + there_ref[...].astype(jnp.float32)
    middle = (residual_ref[...].astype(jnp.float32) + total).astype(jnp.bfloat16)
    wide = middle.astype(jnp.float32)
    inverse = lax.rsqrt(jnp.mean(wide * wide, axis=1, keepdims=True) + 1e-06)
    normed = wide * inverse * gain_ref[...].astype(jnp.float32)
    middle_ref[...] = jnp.where(side == 0, wide[:, :half], wide[:, half:]).astype(jnp.bfloat16)
    normed_ref[...] = jnp.where(side == 0, normed[:, :half], normed[:, half:]).astype(jnp.bfloat16)


def norm(where, residual, here, there, gain):
    rows, width = residual.shape
    half = jax.ShapeDtypeStruct((rows, width // 2), jnp.bfloat16)
    full = pl.BlockSpec((rows, width), lambda i, *_: (0, 0))
    part = pl.BlockSpec((rows, width // 2), lambda i, *_: (0, 0))
    return pl.pallas_call(
        norm_kernel,
        grid_spec=pltpu.PrefetchScalarGridSpec(
            num_scalar_prefetch=1,
            grid=(1,),
            in_specs=[full, full, full, pl.BlockSpec((1, width), lambda i, *_: (0, 0))],
            out_specs=[part, part],
        ),
        out_shape=[half, half],
        compiler_params=pltpu.CompilerParams(vmem_limit_bytes=VMEM_LIMIT),
        name="norm",
    )(where, residual, here, there, gain.reshape(1, width))


def pack_kernel(where, latent_ref, ids_ref, weights_ref, out_ref, rows):
    base, tokens = latent_ref.shape
    span = out_ref.shape[0]
    weights = weights_ref[...]
    high = weights.astype(jnp.bfloat16).astype(jnp.float32)
    rows[...] = jnp.zeros_like(rows)
    rows[0:TOP] = ids_ref[...].astype(jnp.float32)
    rows[TOP : 2 * TOP] = high
    rows[2 * TOP : 3 * TOP] = weights - high
    row = lax.broadcasted_iota(jnp.int32, (span, tokens), 0) + where[1] * span
    chosen = (row == lax.broadcasted_iota(jnp.int32, (span, tokens), 1)).astype(jnp.float32).astype(jnp.bfloat16)
    turn = lambda value: lax.dot_general(
        chosen, value, (((1,), (1,)), ((), ())), preferred_element_type=jnp.float32
    ).astype(jnp.bfloat16)
    every = jnp.concatenate([latent_ref[...], rows[...].astype(jnp.bfloat16)], axis=0)
    out_ref[...] = turn(every)


def pack(where, latent, expert_ids, route_weights):
    local_rows, base = latent.shape
    whole = lambda i, *_: (0, 0)
    return pl.pallas_call(
        pack_kernel,
        grid_spec=pltpu.PrefetchScalarGridSpec(
            num_scalar_prefetch=1,
            grid=(1,),
            in_specs=[
                pl.BlockSpec((base, local_rows), whole),
                pl.BlockSpec((TOP, local_rows), whole),
                pl.BlockSpec((TOP, local_rows), whole),
            ],
            out_specs=pl.BlockSpec((local_rows // 2, WIDE), whole),
            scratch_shapes=[pltpu.VMEM((WIDE - base, local_rows), jnp.float32)],
        ),
        out_shape=jax.ShapeDtypeStruct((local_rows // 2, WIDE), jnp.bfloat16),
        compiler_params=pltpu.CompilerParams(vmem_limit_bytes=VMEM_LIMIT),
        name="pack",
    )(where, latent.T, expert_ids.T, route_weights.T)


def expert_rows(rows, gate_ref, up_ref, down_ref, scale_ref):
    by_columns = (((1,), (1,)), ((), ()))
    gate = lax.dot_general(gate_ref[0], rows, by_columns, preferred_element_type=jnp.float32)
    upper = lax.dot_general(up_ref[0], rows, by_columns, preferred_element_type=jnp.float32)
    hidden = (gate / (1.0 + jnp.exp(-gate)) * upper * scale_ref[0]).astype(jnp.bfloat16)
    by_rows = (((0,), (0,)), ((), ()))
    return lax.dot_general(hidden, down_ref[0], by_rows, preferred_element_type=jnp.float32).astype(jnp.bfloat16)


def plain_kernel(where, rows_ref, gate_ref, up_ref, down_ref, scale_ref, out_ref):
    out_ref[0] = expert_rows(rows_ref[0], gate_ref, up_ref, down_ref, scale_ref)


def fused_kernel(count, where, *refs):
    mine, other = refs[:count], refs[count : 2 * count]
    pick_ref, combine_ref, gate_ref, up_ref, down_ref, scale_ref = refs[2 * count : 2 * count + 6]
    kept, away = refs[2 * count + 6 : 3 * count + 6], refs[3 * count + 6 : 4 * count + 6]
    picked, held = refs[4 * count + 6 :]
    expert = pl.program_id(0)
    here = picked.shape[0]
    half = picked.shape[2] // 2
    side = where[1]
    near = pl.ds(pl.multiple_of(side * half, half), half)
    far = pl.ds(pl.multiple_of((1 - side) * half, half), half)

    @pl.when(expert == 0)
    def _():
        for c in range(count):
            for columns, block in ((near, mine[c]), (far, other[c])):
                rows = jnp.dot(pick_ref[c], block[...], preferred_element_type=jnp.float32).astype(jnp.bfloat16)
                for e in range(here):
                    picked[e, c * SLOTS : (c + 1) * SLOTS, columns] = rows[e * SLOTS : (e + 1) * SLOTS]

    result = expert_rows(picked[expert], gate_ref, up_ref, down_ref, scale_ref)
    place = pl.ds(pl.multiple_of(expert * SLOTS, SLOTS), SLOTS)
    for c in range(count):
        held[c, place, :] = result[c * SLOTS : (c + 1) * SLOTS]

    @pl.when(expert == here - 1)
    def _():
        for c in range(count):
            for columns, out in ((far, away[c]), (near, kept[c])):
                total = jnp.dot(combine_ref[c], held[c, :, columns], preferred_element_type=jnp.float32)
                out[...] = total.astype(jnp.bfloat16)


def expert_specs(w_gate, rows):
    hidden, width = w_gate.shape[1:]
    weight = pl.BlockSpec((1, hidden, width), lambda e, where: (e, 0, 0))
    return [weight, weight, weight, pl.BlockSpec((1, 1, rows), lambda e, where: (e, 0, 0))]


def experts_plain(where, picked, w_gate, w_up, w_down, scale):
    here, rows, width = picked.shape
    rows_spec = pl.BlockSpec((1, rows, width), lambda e, where: (e, 0, 0))
    return pl.pallas_call(
        plain_kernel,
        grid_spec=pltpu.PrefetchScalarGridSpec(
            num_scalar_prefetch=1,
            grid=(here,),
            in_specs=[rows_spec] + expert_specs(w_gate, rows),
            out_specs=rows_spec,
        ),
        out_shape=jax.ShapeDtypeStruct(picked.shape, jnp.bfloat16),
        compiler_params=pltpu.CompilerParams(vmem_limit_bytes=VMEM_LIMIT),
        name="experts",
    )(where, picked, w_gate, w_up, w_down, scale)


def experts_fused(where, mine, other, pick, combine, w_gate, w_up, w_down, scale):
    count, (local, half) = len(mine), mine[0].shape
    here, _, rows = scale.shape
    whole = pl.BlockSpec((local, half), lambda e, where: (0, 0))
    outs = pl.pallas_call(
        functools.partial(fused_kernel, count),
        grid_spec=pltpu.PrefetchScalarGridSpec(
            num_scalar_prefetch=1,
            grid=(here,),
            in_specs=[whole] * (2 * count)
            + [pl.BlockSpec(pick.shape, lambda e, where: (0, 0, 0)), pl.BlockSpec(combine.shape, lambda e, where: (0, 0, 0))]
            + expert_specs(w_gate, rows),
            out_specs=[whole] * (2 * count),
            scratch_shapes=[
                pltpu.VMEM((here, rows, 2 * half), jnp.bfloat16),
                pltpu.VMEM((count, here * SLOTS, 2 * half), jnp.bfloat16),
            ],
        ),
        out_shape=[jax.ShapeDtypeStruct((local, half), jnp.bfloat16)] * (2 * count),
        compiler_params=pltpu.CompilerParams(vmem_limit_bytes=VMEM_LIMIT),
        name="experts",
    )(where, *mine, *other, pick, combine, w_gate, w_up, w_down, scale)
    return outs[:count], outs[count:]


def body(
    queries,
    latent,
    residual,
    seg_lengths,
    span_order,
    expert_ids,
    route_weights,
    kv_up,
    out_proj,
    norm_gain,
    w_gate,
    w_up,
    w_down,
):
    local_rows, width = residual.shape
    span = local_rows // 2
    heads = kv_up.shape[1] // (NOPE + VHEAD)
    count = lax.axis_size("ctx")
    here = EXPERTS // count
    me, side = lax.axis_index("ctx"), lax.axis_index("exp")
    where = jnp.stack([me, side]).astype(jnp.int32)

    base = latent.shape[1]
    sources = sources_of(me, count)
    found = gather(pack(where, latent, expert_ids, route_weights), count)
    swap_all = lambda pieces: [swap(piece) for piece in pieces] if count <= FEW else list(swap(jnp.stack(pieces)))
    mine = jnp.stack(found)
    other = jnp.stack(swap_all(found))

    q = queries.reshape(local_rows, heads, NOPE + ROPE).transpose(1, 0, 2)
    partial = attend(where, sources, seg_lengths, span_order, q, mine, other, kv_up, out_proj, count)
    middle, normed = norm(where, residual, partial, swap(partial), norm_gain)

    facts_mine, facts_other = mine[:, :, base : base + 3 * TOP], other[:, :, base : base + 3 * TOP]
    facts = jnp.concatenate(
        [jnp.where(side == 0, facts_mine, facts_other), jnp.where(side == 0, facts_other, facts_mine)], axis=1
    ).astype(jnp.float32)
    ids, share = facts[:, :, :TOP], facts[:, :, TOP : 2 * TOP] + facts[:, :, 2 * TOP :]
    own = (me * here + jnp.arange(here, dtype=jnp.int32)).astype(jnp.float32)
    hit = ids[:, :, :, None] == own
    hot = jnp.any(hit, axis=2)
    share = jnp.sum(jnp.where(hit, share[:, :, :, None], 0.0), axis=2)
    token = jnp.arange(local_rows, dtype=jnp.int32)
    before = (token[:, None] > token[None, :]).astype(jnp.bfloat16)
    rank = jnp.einsum("tu,cue->cte", before, hot.astype(jnp.bfloat16), preferred_element_type=jnp.float32)
    rank = jnp.where(hot, rank, -1.0)
    slot = jnp.arange(SLOTS, dtype=jnp.int32).astype(jnp.float32)
    combine = rank[:, :, :, None] == slot
    scale = jnp.sum(jnp.where(combine, share[:, :, :, None], 0.0), axis=1)
    scale = scale.transpose(1, 0, 2).reshape(here, 1, count * SLOTS)
    combine = combine.astype(jnp.bfloat16).reshape(count, local_rows, here * SLOTS)
    pick = combine.transpose(0, 2, 1)

    got = gather(normed, count)
    got[1], pick, combine, scale = lax.optimization_barrier((got[1], pick, combine, scale))
    got_other = swap_all(got)
    w_gate, w_up = w_gate.transpose(0, 2, 1), w_up.transpose(0, 2, 1)
    if count <= FEW:
        kept, away = experts_fused(where, got, got_other, pick, combine, w_gate, w_up, w_down, scale)
    else:
        near, far = jnp.stack(got), jnp.stack(got_other)
        full = jnp.concatenate([jnp.where(side == 0, near, far), jnp.where(side == 0, far, near)], axis=2)
        picked = jnp.einsum("cst,ctd->csd", pick, full, preferred_element_type=jnp.float32).astype(jnp.bfloat16)
        picked = picked.reshape(count, here, SLOTS, width).transpose(1, 0, 2, 3).reshape(here, count * SLOTS, width)
        result = experts_plain(where, picked, w_gate, w_up, w_down, scale)
        result = result.reshape(here, count, SLOTS, width).transpose(1, 0, 2, 3).reshape(count, here * SLOTS, width)
        total = jnp.einsum("cts,csd->ctd", combine, result, preferred_element_type=jnp.float32).astype(jnp.bfloat16)
        left, right = jnp.split(total, 2, axis=2)
        kept, away = jnp.where(side == 0, left, right), jnp.where(side == 0, right, left)
    order = [(count // 2 + (d + 1) // 2 * (1 - d % 2 * 2)) % count for d in range(count)]
    swapped = dict(zip(order, swap_all([away[c] for c in order])))
    parts = [functools.partial(summed, [kept[c], swapped[c]]) for c in range(count)]
    return (middle.astype(jnp.float32) + reduce(parts, count)).astype(jnp.bfloat16)


def solution(mesh):
    in_specs = (
        P(("groups", "ctx"), "exp"),
        P(("groups", "ctx"), None),
        P(("groups", "ctx"), None),
        P("groups"),
        P("groups"),
        P(("groups", "ctx"), None),
        P(("groups", "ctx"), None),
        P(None, "exp"),
        P("exp", None),
        P(),
        P("ctx", None, "exp"),
        P("ctx", None, "exp"),
        P("ctx", "exp", None),
    )
    out_specs = P(("groups", "ctx"), "exp")
    return jax.shard_map(body, mesh=mesh, in_specs=in_specs, out_specs=out_specs, check_vma=False)
```

```python
import functools
import math

import jax
import jax.numpy as jnp
import numpy as np
from jax import lax
from jax.experimental import pallas as pl
from jax.experimental.pallas import tpu as pltpu
from jax.sharding import PartitionSpec as P

NOPE = 128
ROPE = 64
VHEAD = 128
LAT = 512
EXPERTS = 64
TOP = 6
SLOTS = 16
WIDE = 640
VMEM_LIMIT = 50 * 1024 * 1024
DEPTH = 3
PIECES = 2
SWAP = [(0, 1), (1, 0)]
FEW = 8


def cycle_of(count):
    fast = 2 ** (int(math.log2(count)) // 2)
    slow = count // fast
    cycle = [0]
    for i in range(slow):
        columns = range(1, fast)
        cycle += [i * fast + j for j in (columns if i % 2 == 0 else reversed(columns))]
    return cycle + [i * fast for i in reversed(range(1, slow))]


def step(value, ahead, count):
    cycle = cycle_of(count)
    return lax.ppermute(value, "ctx", [(cycle[p], cycle[(p + ahead) % count]) for p in range(count)])


def swap(value):
    return lax.ppermute(value, "exp", SWAP)


def summed(pieces):
    total = pieces[0].astype(jnp.float32)
    for piece in pieces[1:]:
        total = total + piece.astype(jnp.float32)
    return total


def sources_of(me, count):
    if count > FEW:
        return jnp.arange(count, dtype=jnp.int32)
    cycle = cycle_of(count)
    table = np.zeros((count, count), np.int32)
    for p in range(count):
        table[cycle[p]] = [cycle[p - d] for d in range(count)]
    return lax.dynamic_index_in_dim(jnp.asarray(table), me, keepdims=False)


def gather(block, count):
    if count > FEW:
        found = lax.all_gather(block, "ctx")
        return list(found), list(swap(found))
    middle = count // 2
    found, other = [None] * count, [None] * count
    found[0] = block
    other[0] = swap(block)
    for d in range(1, middle):
        for place, before, ahead in ((d, d - 1, 1), (count - d, (1 - d) % count, -1)):
            arrived = step(found[before], ahead, count)
            found[place], other[before] = lax.optimization_barrier((arrived, other[before]))
            other[place] = swap(found[place])
    half = block.shape[0] // 2
    ahead, back = step(found[middle - 1][:half], 1, count), step(found[middle + 1][half:], -1, count)
    found[middle] = jnp.concatenate([ahead, back], axis=0)
    other[middle] = swap(found[middle])
    return found, other


def reduce(parts, count):
    if count > FEW:
        return lax.psum_scatter(jnp.stack([part() for part in parts]).astype(jnp.bfloat16), "ctx").astype(jnp.float32)
    middle = count // 2
    first = parts[middle]().astype(jnp.bfloat16)
    half = first.shape[0] // 2
    zero = jnp.zeros((half, first.shape[1]), jnp.bfloat16)
    ahead = jnp.concatenate([step(first[:half], 1, count), zero], axis=0)
    back = jnp.concatenate([zero, step(first[half:], -1, count)], axis=0)
    for d in range(middle - 1, 0, -1):
        ahead = step((parts[count - d]() + ahead.astype(jnp.float32)).astype(jnp.bfloat16), 1, count)
        back = step((parts[d]() + back.astype(jnp.float32)).astype(jnp.bfloat16), -1, count)
    return parts[0]() + ahead.astype(jnp.float32) + back.astype(jnp.float32)


def attend_kernel(blocks, where, sources, lengths, order, q_ref, mine_ref, other_ref, up_ref, proj_ref, out_ref, m_ref, l_ref, acc_ref):
    chunk = pl.program_id(0)
    me, side = where[0], where[1]
    segs = lengths.shape[0]
    span = mine_ref.shape[1]
    heads, rows, _ = q_ref.shape

    @pl.when(chunk == 0)
    def _():
        m_ref[...] = jnp.full_like(m_ref, -1e30)
        l_ref[...] = jnp.zeros_like(l_ref)
        acc_ref[...] = jnp.zeros_like(acc_ref)

    row = lax.broadcasted_iota(jnp.int32, (rows, 1), 0)
    first = order[2 * me] * span
    second = order[2 * me + 1] * span
    qpos = jnp.where(row < span, first + row, second + row - span)
    low = jnp.zeros((rows, 1), jnp.int32)
    start = jnp.int32(0)
    for m in range(segs):
        low = jnp.where(qpos >= start, start, low)
        start = start + lengths[m]
    keys = blocks * span
    lane = lax.broadcasted_iota(jnp.int32, (1, keys), 1)
    within, which = lane % span, lane // span
    kpos_parts = []
    for half in (side, 1 - side):
        base = jnp.zeros((1, keys), jnp.int32)
        for j in range(blocks):
            src = sources[chunk * blocks + j]
            base = jnp.where(which == j, order[2 * src + half] * span, base)
        kpos_parts.append(base + within)
    kpos = jnp.concatenate(kpos_parts, axis=1)
    visible = (kpos >= low) & (kpos <= qpos)

    lat = jnp.concatenate([mine_ref[...].reshape(keys, WIDE), other_ref[...].reshape(keys, WIDE)], axis=0)
    keyval = jnp.dot(lat[:, :LAT], up_ref[...], preferred_element_type=jnp.float32).astype(jnp.bfloat16)
    rope = lat[:, LAT : LAT + ROPE]
    scale = 1.0 / math.sqrt(NOPE + ROPE)
    for h in range(heads):
        base = h * (NOPE + VHEAD)
        key = jnp.concatenate([keyval[:, base : base + NOPE], rope], axis=1)
        scores = lax.dot_general(q_ref[h], key, (((1,), (1,)), ((), ())), preferred_element_type=jnp.float32)
        scores = jnp.where(visible, scores * scale, -1e30)
        best = m_ref[h]
        fresh = jnp.maximum(best, jnp.max(scores, axis=1, keepdims=True))
        weights = jnp.where(visible, jnp.exp(scores - fresh), 0.0)
        shrink = jnp.exp(best - fresh)
        m_ref[h] = fresh
        l_ref[h] = l_ref[h] * shrink + jnp.sum(weights, axis=1, keepdims=True)
        mixed = jnp.dot(
            weights.astype(jnp.bfloat16), keyval[:, base + NOPE : base + NOPE + VHEAD], preferred_element_type=jnp.float32
        )
        acc_ref[h] = acc_ref[h] * shrink + mixed

    @pl.when(chunk == pl.num_programs(0) - 1)
    def _():
        attended = [(acc_ref[h] / l_ref[h]).astype(jnp.bfloat16) for h in range(heads)]
        out = jnp.dot(jnp.concatenate(attended, axis=1), proj_ref[...], preferred_element_type=jnp.float32)
        out_ref[...] = out.astype(jnp.bfloat16)


def attend(where, sources, lengths, order, q, mine, other, kv_up, out_proj, count):
    heads, rows, depth = q.shape
    blocks = math.gcd(count, 8)
    span = mine.shape[1]
    whole2 = lambda i, *_: (0, 0)
    whole3 = lambda i, *_: (0, 0, 0)
    lat_spec = pl.BlockSpec((blocks, span, WIDE), lambda i, *_: (i, 0, 0))
    return pl.pallas_call(
        functools.partial(attend_kernel, blocks),
        grid_spec=pltpu.PrefetchScalarGridSpec(
            num_scalar_prefetch=4,
            grid=(count // blocks,),
            in_specs=[
                pl.BlockSpec(q.shape, whole3),
                lat_spec,
                lat_spec,
                pl.BlockSpec(kv_up.shape, whole2),
                pl.BlockSpec(out_proj.shape, whole2),
            ],
            out_specs=pl.BlockSpec((rows, out_proj.shape[1]), whole2),
            scratch_shapes=[
                pltpu.VMEM((heads, rows, 1), jnp.float32),
                pltpu.VMEM((heads, rows, 1), jnp.float32),
                pltpu.VMEM((heads, rows, VHEAD), jnp.float32),
            ],
        ),
        out_shape=pltpu.VMEM((rows, out_proj.shape[1]), jnp.bfloat16),
        compiler_params=pltpu.CompilerParams(vmem_limit_bytes=VMEM_LIMIT),
        name="attend",
    )(where, sources, lengths, order, q, mine, other, kv_up, out_proj)


def norm_kernel(where, residual_ref, here_ref, there_ref, gain_ref, middle_ref, normed_ref):
    side = where[1]
    half = middle_ref.shape[1]
    total = here_ref[...].astype(jnp.float32) + there_ref[...].astype(jnp.float32)
    middle = (residual_ref[...].astype(jnp.float32) + total).astype(jnp.bfloat16)
    wide = middle.astype(jnp.float32)
    inverse = lax.rsqrt(jnp.mean(wide * wide, axis=1, keepdims=True) + 1e-06)
    normed = wide * inverse * gain_ref[...].astype(jnp.float32)
    middle_ref[...] = jnp.where(side == 0, wide[:, :half], wide[:, half:]).astype(jnp.bfloat16)
    normed_ref[...] = jnp.where(side == 0, normed[:, :half], normed[:, half:]).astype(jnp.bfloat16)


def norm(where, residual, here, there, gain):
    rows, width = residual.shape
    half = pltpu.VMEM((rows, width // 2), jnp.bfloat16)
    full = pl.BlockSpec((rows, width), lambda i, *_: (0, 0))
    part = pl.BlockSpec((rows, width // 2), lambda i, *_: (0, 0))
    return pl.pallas_call(
        norm_kernel,
        grid_spec=pltpu.PrefetchScalarGridSpec(
            num_scalar_prefetch=1,
            grid=(1,),
            in_specs=[full, full, full, pl.BlockSpec((1, width), lambda i, *_: (0, 0))],
            out_specs=[part, part],
        ),
        out_shape=[half, half],
        compiler_params=pltpu.CompilerParams(vmem_limit_bytes=VMEM_LIMIT),
        name="norm",
    )(where, residual, here, there, gain)


def pack_kernel(where, latent_ref, ids_ref, weights_ref, out_ref, rows):
    base, tokens = latent_ref.shape
    span = out_ref.shape[0]
    weights = weights_ref[...]
    high = weights.astype(jnp.bfloat16).astype(jnp.float32)
    rows[...] = jnp.zeros_like(rows)
    rows[0:TOP] = ids_ref[...].astype(jnp.float32)
    rows[TOP : 2 * TOP] = high
    rows[2 * TOP : 3 * TOP] = weights - high
    row = lax.broadcasted_iota(jnp.int32, (span, tokens), 0) + where[1] * span
    chosen = (row == lax.broadcasted_iota(jnp.int32, (span, tokens), 1)).astype(jnp.float32).astype(jnp.bfloat16)
    turn = lambda value: lax.dot_general(
        chosen, value, (((1,), (1,)), ((), ())), preferred_element_type=jnp.float32
    ).astype(jnp.bfloat16)
    every = jnp.concatenate([latent_ref[...], rows[...].astype(jnp.bfloat16)], axis=0)
    out_ref[...] = turn(every)


def pack(where, latent, expert_ids, route_weights):
    local_rows, base = latent.shape
    whole = lambda i, *_: (0, 0)
    return pl.pallas_call(
        pack_kernel,
        grid_spec=pltpu.PrefetchScalarGridSpec(
            num_scalar_prefetch=1,
            grid=(1,),
            in_specs=[
                pl.BlockSpec((base, local_rows), whole),
                pl.BlockSpec((TOP, local_rows), whole),
                pl.BlockSpec((TOP, local_rows), whole),
            ],
            out_specs=pl.BlockSpec((local_rows // 2, WIDE), whole),
            scratch_shapes=[pltpu.VMEM((WIDE - base, local_rows), jnp.float32)],
        ),
        out_shape=jax.ShapeDtypeStruct((local_rows // 2, WIDE), jnp.bfloat16),
        compiler_params=pltpu.CompilerParams(vmem_limit_bytes=VMEM_LIMIT),
        name="pack",
    )(where, latent.T, expert_ids.T, route_weights.T)


def expert_rows(rows, gate_ref, up_ref, down_ref, scale_ref):
    by_columns = (((1,), (1,)), ((), ()))
    gate = lax.dot_general(gate_ref[0], rows, by_columns, preferred_element_type=jnp.float32)
    upper = lax.dot_general(up_ref[0], rows, by_columns, preferred_element_type=jnp.float32)
    hidden = (gate / (1.0 + jnp.exp(-gate)) * upper * scale_ref[0]).astype(jnp.bfloat16)
    by_rows = (((0,), (0,)), ((), ()))
    return lax.dot_general(hidden, down_ref[0], by_rows, preferred_element_type=jnp.float32).astype(jnp.bfloat16)


def plain_kernel(where, rows_ref, gate_ref, up_ref, down_ref, scale_ref, out_ref):
    out_ref[0] = expert_rows(rows_ref[0], gate_ref, up_ref, down_ref, scale_ref)


def fused_kernel(count, where, *refs):
    mine, other = refs[:count], refs[count : 2 * count]
    pick_ref, combine_ref, scale_ref = refs[2 * count : 2 * count + 3]
    weights = refs[2 * count + 3 : 2 * count + 6]
    kept, away = refs[2 * count + 6 : 3 * count + 6], refs[3 * count + 6 : 4 * count + 6]
    picked, held = refs[4 * count + 6 : 4 * count + 8]
    buffers, sems = refs[4 * count + 8 : 4 * count + 11], refs[4 * count + 11]
    here = picked.shape[0]
    depth, units, _ = buffers[0].shape
    half = picked.shape[2] // 2
    side = where[1]
    near = pl.ds(pl.multiple_of(side * half, half), half)
    far = pl.ds(pl.multiple_of((1 - side) * half, half), half)
    piece = units // PIECES

    def copies(expert, slot):
        for w in range(3):
            for i in range(PIECES):
                rows = pl.ds(i * piece, piece)
                yield pltpu.make_async_copy(weights[w].at[expert, rows], buffers[w].at[slot, rows], sems.at[slot, w, i])

    for e in range(depth):
        for copy in copies(e, e):
            copy.start()

    for c in range(count):
        for columns, block in ((near, mine[c]), (far, other[c])):
            rows = jnp.dot(pick_ref[c], block[...], preferred_element_type=jnp.float32).astype(jnp.bfloat16)
            for e in range(here):
                picked[e, c * SLOTS : (c + 1) * SLOTS, columns] = rows[e * SLOTS : (e + 1) * SLOTS]

    def work(expert, _):
        slot = lax.rem(expert, depth)
        for copy in copies(expert, slot):
            copy.wait()
        one = pl.ds(slot, 1)
        result = expert_rows(picked[expert], *(buffer.at[one] for buffer in buffers), scale_ref.at[pl.ds(expert, 1)])
        place = pl.ds(pl.multiple_of(expert * SLOTS, SLOTS), SLOTS)
        for c in range(count):
            held[c, place, :] = result[c * SLOTS : (c + 1) * SLOTS]

        @pl.when(expert + depth < here)
        def _():
            for copy in copies(expert + depth, slot):
                copy.start()

        return 0

    lax.fori_loop(0, here, work, 0)
    for c in range(count):
        for columns, out in ((far, away[c]), (near, kept[c])):
            total = jnp.dot(combine_ref[c], held[c, :, columns], preferred_element_type=jnp.float32)
            out[...] = total.astype(jnp.bfloat16)


def expert_specs(w_gate, rows):
    hidden, width = w_gate.shape[1:]
    weight = pl.BlockSpec((1, hidden, width), lambda e, where: (e, 0, 0))
    return [weight, weight, weight, pl.BlockSpec((1, 1, rows), lambda e, where: (e, 0, 0))]


def experts_plain(where, picked, w_gate, w_up, w_down, scale):
    here, rows, width = picked.shape
    rows_spec = pl.BlockSpec((1, rows, width), lambda e, where: (e, 0, 0))
    return pl.pallas_call(
        plain_kernel,
        grid_spec=pltpu.PrefetchScalarGridSpec(
            num_scalar_prefetch=1,
            grid=(here,),
            in_specs=[rows_spec] + expert_specs(w_gate, rows),
            out_specs=rows_spec,
        ),
        out_shape=jax.ShapeDtypeStruct(picked.shape, jnp.bfloat16),
        compiler_params=pltpu.CompilerParams(vmem_limit_bytes=VMEM_LIMIT),
        name="experts",
    )(where, picked, w_gate, w_up, w_down, scale)


def experts_fused(where, mine, other, pick, combine, w_gate, w_up, w_down, scale):
    count, (local, half) = len(mine), mine[0].shape
    here, _, rows = scale.shape
    units = w_gate.shape[1]
    depth = min(DEPTH, here)
    whole = pl.BlockSpec(memory_space=pltpu.VMEM)
    outs = pl.pallas_call(
        functools.partial(fused_kernel, count),
        in_specs=[pl.BlockSpec(memory_space=pltpu.SMEM)]
        + [whole] * (2 * count + 3)
        + [pl.BlockSpec(memory_space=pl.ANY)] * 3,
        out_specs=[whole] * (2 * count),
        scratch_shapes=[
            pltpu.VMEM((here, rows, 2 * half), jnp.bfloat16),
            pltpu.VMEM((count, here * SLOTS, 2 * half), jnp.bfloat16),
        ]
        + [pltpu.VMEM((depth, units, 2 * half), jnp.bfloat16)] * 3
        + [pltpu.SemaphoreType.DMA((depth, 3, PIECES))],
        out_shape=[pltpu.VMEM((local, half), jnp.bfloat16)] * (2 * count),
        compiler_params=pltpu.CompilerParams(vmem_limit_bytes=VMEM_LIMIT),
        name="experts",
    )(where, *mine, *other, pick, combine, scale, w_gate, w_up, w_down)
    return outs[:count], outs[count:]


def body(
    queries,
    latent,
    residual,
    seg_lengths,
    span_order,
    expert_ids,
    route_weights,
    kv_up,
    out_proj,
    norm_gain,
    w_gate,
    w_up,
    w_down,
):
    local_rows, width = residual.shape
    span = local_rows // 2
    heads = kv_up.shape[1] // (NOPE + VHEAD)
    count = lax.axis_size("ctx")
    here = EXPERTS // count
    me, side = lax.axis_index("ctx"), lax.axis_index("exp")
    where = jnp.stack([me, side]).astype(jnp.int32)

    base = latent.shape[1]
    sources = sources_of(me, count)
    found, found_other = gather(pack(where, latent, expert_ids, route_weights), count)
    gain = norm_gain.reshape(1, width)
    found[1], gain = lax.optimization_barrier((found[1], gain))
    mine, other = jnp.stack(found), jnp.stack(found_other)

    q = queries.reshape(local_rows, heads, NOPE + ROPE).transpose(1, 0, 2)
    partial = attend(where, sources, seg_lengths, span_order, q, mine, other, kv_up, out_proj, count)
    middle, normed = norm(where, residual, partial, swap(partial), gain)

    facts_mine, facts_other = mine[:, :, base : base + 3 * TOP], other[:, :, base : base + 3 * TOP]
    facts = jnp.concatenate(
        [jnp.where(side == 0, facts_mine, facts_other), jnp.where(side == 0, facts_other, facts_mine)], axis=1
    ).astype(jnp.float32)
    ids, share = facts[:, :, :TOP], facts[:, :, TOP : 2 * TOP] + facts[:, :, 2 * TOP :]
    own = (me * here + jnp.arange(here, dtype=jnp.int32)).astype(jnp.float32)
    hit = ids[:, :, :, None] == own
    hot = jnp.any(hit, axis=2)
    share = jnp.sum(jnp.where(hit, share[:, :, :, None], 0.0), axis=2)
    token = jnp.arange(local_rows, dtype=jnp.int32)
    before = (token[:, None] > token[None, :]).astype(jnp.bfloat16)
    rank = jnp.einsum("tu,cue->cte", before, hot.astype(jnp.bfloat16), preferred_element_type=jnp.float32)
    rank = jnp.where(hot, rank, -1.0)
    slot = jnp.arange(SLOTS, dtype=jnp.int32).astype(jnp.float32)
    combine = rank[:, :, :, None] == slot
    scale = jnp.sum(jnp.where(combine, share[:, :, :, None], 0.0), axis=1)
    scale = scale.transpose(1, 0, 2).reshape(here, 1, count * SLOTS)
    combine = combine.astype(jnp.bfloat16).reshape(count, local_rows, here * SLOTS)
    pick = combine.transpose(0, 2, 1)

    got, got_other = gather(normed, count)
    got[1], pick, combine, scale = lax.optimization_barrier((got[1], pick, combine, scale))
    w_gate, w_up = w_gate.transpose(0, 2, 1), w_up.transpose(0, 2, 1)
    if count <= FEW:
        kept, away = experts_fused(where, got, got_other, pick, combine, w_gate, w_up, w_down, scale)
    else:
        near, far = jnp.stack(got), jnp.stack(got_other)
        full = jnp.concatenate([jnp.where(side == 0, near, far), jnp.where(side == 0, far, near)], axis=2)
        picked = jnp.einsum("cst,ctd->csd", pick, full, preferred_element_type=jnp.float32).astype(jnp.bfloat16)
        picked = picked.reshape(count, here, SLOTS, width).transpose(1, 0, 2, 3).reshape(here, count * SLOTS, width)
        result = experts_plain(where, picked, w_gate, w_up, w_down, scale)
        result = result.reshape(here, count, SLOTS, width).transpose(1, 0, 2, 3).reshape(count, here * SLOTS, width)
        total = jnp.einsum("cts,csd->ctd", combine, result, preferred_element_type=jnp.float32).astype(jnp.bfloat16)
        left, right = jnp.split(total, 2, axis=2)
        kept, away = jnp.where(side == 0, left, right), jnp.where(side == 0, right, left)
    swap_all = lambda pieces: [swap(piece) for piece in pieces] if count <= FEW else list(swap(jnp.stack(pieces)))
    order = [(count // 2 + (d + 1) // 2 * (1 - d % 2 * 2)) % count for d in range(count)]
    swapped = dict(zip(order, swap_all([away[c] for c in order])))
    parts = [functools.partial(summed, [kept[c], swapped[c]]) for c in range(count)]
    return (middle.astype(jnp.float32) + reduce(parts, count)).astype(jnp.bfloat16)


def solution(mesh):
    in_specs = (
        P(("groups", "ctx"), "exp"),
        P(("groups", "ctx"), None),
        P(("groups", "ctx"), None),
        P("groups"),
        P("groups"),
        P(("groups", "ctx"), None),
        P(("groups", "ctx"), None),
        P(None, "exp"),
        P("exp", None),
        P(),
        P("ctx", None, "exp"),
        P("ctx", None, "exp"),
        P("ctx", "exp", None),
    )
    out_specs = P(("groups", "ctx"), "exp")
    return jax.shard_map(body, mesh=mesh, in_specs=in_specs, out_specs=out_specs, check_vma=False)
```

```python
import functools
import math

import jax
import jax.numpy as jnp
import numpy as np
from jax import lax
from jax.experimental import pallas as pl
from jax.experimental.pallas import tpu as pltpu
from jax.sharding import PartitionSpec as P

NOPE = 128
ROPE = 64
VHEAD = 128
LAT = 512
EXPERTS = 64
TOP = 6
SLOTS = 16
WIDE = 640
MIB = 1024 * 1024
VMEM_LIMIT = 50 * MIB
STAGED = 2
DEPTH = 2
PIECES = 2
SWAP = [(0, 1), (1, 0)]
FEW = 8


def cycle_of(count):
    fast = 2 ** (int(math.log2(count)) // 2)
    slow = count // fast
    cycle = [0]
    for i in range(slow):
        columns = range(1, fast)
        cycle += [i * fast + j for j in (columns if i % 2 == 0 else reversed(columns))]
    return cycle + [i * fast for i in reversed(range(1, slow))]


def step(value, ahead, count):
    cycle = cycle_of(count)
    return lax.ppermute(value, "ctx", [(cycle[p], cycle[(p + ahead) % count]) for p in range(count)])


def swap(value):
    return lax.ppermute(value, "exp", SWAP)


def summed(pieces):
    total = pieces[0].astype(jnp.float32)
    for piece in pieces[1:]:
        total = total + piece.astype(jnp.float32)
    return total


def sources_of(me, count):
    if count > FEW:
        return jnp.arange(count, dtype=jnp.int32)
    cycle = cycle_of(count)
    table = np.zeros((count, count), np.int32)
    for p in range(count):
        table[cycle[p]] = [cycle[p - d] for d in range(count)]
    return lax.dynamic_index_in_dim(jnp.asarray(table), me, keepdims=False)


def gather(block, count, beside=()):
    if count > FEW:
        found = lax.all_gather(block, "ctx")
        return list(found), list(swap(found)), list(beside)
    middle = count // 2
    found, other, made = [None] * count, [None] * count, []
    found[0] = block
    other[0] = swap(block)
    for d in range(1, middle):
        for place, before, ahead in ((d, d - 1, 1), (count - d, (1 - d) % count, -1)):
            arrived = step(found[before], ahead, count)
            extra = beside[d - 1] if ahead == 1 and len(beside) >= d else ()
            found[place], other[before], extra = lax.optimization_barrier((arrived, other[before], extra))
            if ahead == 1:
                made.append(extra)
            other[place] = swap(found[place])
    half = block.shape[0] // 2
    ahead, back = step(found[middle - 1][:half], 1, count), step(found[middle + 1][half:], -1, count)
    found[middle] = jnp.concatenate([ahead, back], axis=0)
    other[middle] = swap(found[middle])
    return found, other, made[: len(beside)]


def reduce(parts, count):
    if count > FEW:
        return lax.psum_scatter(jnp.stack([part() for part in parts]).astype(jnp.bfloat16), "ctx").astype(jnp.float32)
    middle = count // 2
    first = parts[middle]().astype(jnp.bfloat16)
    half = first.shape[0] // 2
    zero = jnp.zeros((half, first.shape[1]), jnp.bfloat16)
    ahead = jnp.concatenate([step(first[:half], 1, count), zero], axis=0)
    back = jnp.concatenate([zero, step(first[half:], -1, count)], axis=0)
    for d in range(middle - 1, 0, -1):
        ahead = step((parts[count - d]() + ahead.astype(jnp.float32)).astype(jnp.bfloat16), 1, count)
        back = step((parts[d]() + back.astype(jnp.float32)).astype(jnp.bfloat16), -1, count)
    return parts[0]() + ahead.astype(jnp.float32) + back.astype(jnp.float32)


def attend_kernel(count, blocks, info, q_ref, mine_ref, other_ref, up_ref, proj_ref, out_ref, m_ref, l_ref, acc_ref):
    chunk = pl.program_id(0)
    side = info[1]
    sources = lambda c: info[2 + c]
    order = lambda j: info[2 + count + j]
    segs = info.shape[0] - 2 - 3 * count
    span = mine_ref.shape[1]
    heads, rows, _ = q_ref.shape

    @pl.when(chunk == 0)
    def _():
        m_ref[...] = jnp.full_like(m_ref, -1e30)
        l_ref[...] = jnp.zeros_like(l_ref)
        acc_ref[...] = jnp.zeros_like(acc_ref)

    row = lax.broadcasted_iota(jnp.int32, (rows, 1), 0)
    first = order(2 * sources(0)) * span
    second = order(2 * sources(0) + 1) * span
    qpos = jnp.where(row < span, first + row, second + row - span)
    low = jnp.zeros((rows, 1), jnp.int32)
    start = jnp.int32(0)
    for m in range(segs):
        low = jnp.where(qpos >= start, start, low)
        start = start + info[2 + 3 * count + m]
    keys = blocks * span
    lane = lax.broadcasted_iota(jnp.int32, (1, keys), 1)
    within, which = lane % span, lane // span
    kpos_parts = []
    for half in (side, 1 - side):
        base = jnp.zeros((1, keys), jnp.int32)
        for j in range(blocks):
            src = sources(chunk * blocks + j)
            base = jnp.where(which == j, order(2 * src + half) * span, base)
        kpos_parts.append(base + within)
    kpos = jnp.concatenate(kpos_parts, axis=1)
    visible = (kpos >= low) & (kpos <= qpos)

    lat = jnp.concatenate([mine_ref[...].reshape(keys, WIDE), other_ref[...].reshape(keys, WIDE)], axis=0)
    keyval = jnp.dot(lat[:, :LAT], up_ref[...], preferred_element_type=jnp.float32).astype(jnp.bfloat16)
    rope = lat[:, LAT : LAT + ROPE]
    scale = 1.0 / math.sqrt(NOPE + ROPE)
    for h in range(heads):
        base = h * (NOPE + VHEAD)
        key = jnp.concatenate([keyval[:, base : base + NOPE], rope], axis=1)
        scores = lax.dot_general(q_ref[h], key, (((1,), (1,)), ((), ())), preferred_element_type=jnp.float32)
        scores = jnp.where(visible, scores * scale, -1e30)
        best = m_ref[h]
        fresh = jnp.maximum(best, jnp.max(scores, axis=1, keepdims=True))
        weights = jnp.where(visible, jnp.exp(scores - fresh), 0.0)
        shrink = jnp.exp(best - fresh)
        m_ref[h] = fresh
        l_ref[h] = l_ref[h] * shrink + jnp.sum(weights, axis=1, keepdims=True)
        mixed = jnp.dot(
            weights.astype(jnp.bfloat16), keyval[:, base + NOPE : base + NOPE + VHEAD], preferred_element_type=jnp.float32
        )
        acc_ref[h] = acc_ref[h] * shrink + mixed

    @pl.when(chunk == pl.num_programs(0) - 1)
    def _():
        attended = [(acc_ref[h] / l_ref[h]).astype(jnp.bfloat16) for h in range(heads)]
        out = jnp.dot(jnp.concatenate(attended, axis=1), proj_ref[...], preferred_element_type=jnp.float32)
        out_ref[...] = out.astype(jnp.bfloat16)


def attend(info, q, mine, other, kv_up, out_proj, count):
    heads, rows, depth = q.shape
    blocks = math.gcd(count, 8)
    span = mine.shape[1]
    whole = pl.BlockSpec(memory_space=pltpu.VMEM)
    lat_spec = whole if blocks == count else pl.BlockSpec((blocks, span, WIDE), lambda i, *_: (i, 0, 0))
    return pl.pallas_call(
        functools.partial(attend_kernel, count, blocks),
        grid_spec=pltpu.PrefetchScalarGridSpec(
            num_scalar_prefetch=1,
            grid=(count // blocks,),
            in_specs=[whole, lat_spec, lat_spec, whole, whole],
            out_specs=whole,
            scratch_shapes=[
                pltpu.VMEM((heads, rows, 1), jnp.float32),
                pltpu.VMEM((heads, rows, 1), jnp.float32),
                pltpu.VMEM((heads, rows, VHEAD), jnp.float32),
            ],
        ),
        out_shape=pltpu.VMEM((rows, out_proj.shape[1]), jnp.bfloat16),
        compiler_params=pltpu.CompilerParams(vmem_limit_bytes=28 * MIB),
        name="attend",
    )(info, q, mine, other, kv_up, out_proj)


def stage_kernel(picks, *refs):
    here = len(picks)
    sems = refs[2 * here]
    copies = []
    for i, pick in enumerate(picks):
        source = refs[i] if pick is None else refs[i].at[pick]
        piece = source.shape[0] // PIECES
        for p in range(PIECES):
            rows = pl.ds(p * piece, piece)
            copies.append(pltpu.make_async_copy(source.at[rows], refs[here + i].at[rows], sems.at[i, p]))
    for copy in copies:
        copy.start()
    for copy in copies:
        copy.wait()


def stage(arrays, picks):
    shapes = [x.shape if pick is None else x.shape[1:] for x, pick in zip(arrays, picks)]
    return pl.pallas_call(
        functools.partial(stage_kernel, picks),
        in_specs=[pl.BlockSpec(memory_space=pltpu.HBM)] * len(arrays),
        out_specs=[pl.BlockSpec(memory_space=pltpu.VMEM)] * len(arrays),
        scratch_shapes=[pltpu.SemaphoreType.DMA((len(arrays), PIECES))],
        out_shape=[pltpu.VMEM(shape, x.dtype) for shape, x in zip(shapes, arrays)],
        compiler_params=pltpu.CompilerParams(vmem_limit_bytes=2 * MIB),
        name="stage",
    )(*(pltpu.with_memory_space_constraint(x, pltpu.HBM) for x in arrays))


def norm_kernel(where, residual_ref, here_ref, there_ref, gain_ref, middle_ref, normed_ref):
    side = where[1]
    half = middle_ref.shape[1]
    total = here_ref[...].astype(jnp.float32) + there_ref[...].astype(jnp.float32)
    middle = (residual_ref[...].astype(jnp.float32) + total).astype(jnp.bfloat16)
    wide = middle.astype(jnp.float32)
    inverse = lax.rsqrt(jnp.mean(wide * wide, axis=1, keepdims=True) + 1e-06)
    normed = wide * inverse * gain_ref[...].astype(jnp.float32)
    middle_ref[...] = jnp.where(side == 0, wide[:, :half], wide[:, half:]).astype(jnp.bfloat16)
    normed_ref[...] = jnp.where(side == 0, normed[:, :half], normed[:, half:]).astype(jnp.bfloat16)


def norm(where, residual, here, there, gain):
    rows, width = residual.shape
    half = pltpu.VMEM((rows, width // 2), jnp.bfloat16)
    whole = pl.BlockSpec(memory_space=pltpu.VMEM)
    return pl.pallas_call(
        norm_kernel,
        in_specs=[pl.BlockSpec(memory_space=pltpu.SMEM)] + [whole] * 4,
        out_specs=[whole, whole],
        out_shape=[half, half],
        compiler_params=pltpu.CompilerParams(vmem_limit_bytes=12 * MIB),
        name="norm",
    )(where, residual, here, there, gain)


def pack_kernel(where, *refs):
    copies = [pltpu.make_async_copy(refs[i], refs[4 + i], refs[8].at[i]) for i in range(3)]
    for copy in copies:
        copy.start()
    for copy in copies:
        copy.wait()
    out_ref, (latent_ref, ids_ref, weights_ref, rows) = refs[3], refs[4:8]
    base, tokens = latent_ref.shape
    span = out_ref.shape[0]
    weights = weights_ref[...]
    high = weights.astype(jnp.bfloat16).astype(jnp.float32)
    rows[...] = jnp.zeros_like(rows)
    rows[0:TOP] = ids_ref[...].astype(jnp.float32)
    rows[TOP : 2 * TOP] = high
    rows[2 * TOP : 3 * TOP] = weights - high
    row = lax.broadcasted_iota(jnp.int32, (span, tokens), 0) + where[1] * span
    chosen = (row == lax.broadcasted_iota(jnp.int32, (span, tokens), 1)).astype(jnp.float32).astype(jnp.bfloat16)
    turn = lambda value: lax.dot_general(
        chosen, value, (((1,), (1,)), ((), ())), preferred_element_type=jnp.float32
    ).astype(jnp.bfloat16)
    every = jnp.concatenate([latent_ref[...], rows[...].astype(jnp.bfloat16)], axis=0)
    out_ref[...] = turn(every)


def pack(where, latent, expert_ids, route_weights):
    local_rows, base = latent.shape
    arrays = (latent.T, expert_ids.T, route_weights.T)
    return pl.pallas_call(
        pack_kernel,
        in_specs=[pl.BlockSpec(memory_space=pltpu.SMEM)] + [pl.BlockSpec(memory_space=pltpu.HBM)] * 3,
        out_specs=pl.BlockSpec(memory_space=pltpu.VMEM),
        scratch_shapes=[pltpu.VMEM(x.shape, x.dtype) for x in arrays]
        + [pltpu.VMEM((WIDE - base, local_rows), jnp.float32), pltpu.SemaphoreType.DMA((3,))],
        out_shape=pltpu.VMEM((local_rows // 2, WIDE), jnp.bfloat16),
        compiler_params=pltpu.CompilerParams(vmem_limit_bytes=4 * MIB),
        name="pack",
    )(where, *(pltpu.with_memory_space_constraint(x, pltpu.HBM) for x in arrays))


def expert_rows(rows, gate_ref, up_ref, down_ref, scale):
    by_columns = (((1,), (1,)), ((), ()))
    gate = lax.dot_general(gate_ref[...], rows, by_columns, preferred_element_type=jnp.float32)
    upper = lax.dot_general(up_ref[...], rows, by_columns, preferred_element_type=jnp.float32)
    hidden = (gate / (1.0 + jnp.exp(-gate)) * upper * scale).astype(jnp.bfloat16)
    by_rows = (((0,), (0,)), ((), ()))
    return lax.dot_general(hidden, down_ref[...], by_rows, preferred_element_type=jnp.float32).astype(jnp.bfloat16)


def plain_kernel(where, rows_ref, gate_ref, up_ref, down_ref, scale_ref, out_ref):
    out_ref[0] = expert_rows(rows_ref[0], gate_ref.at[0], up_ref.at[0], down_ref.at[0], scale_ref[0])


def fused_kernel(count, staged, where, *refs):
    mine, other = refs[:count], refs[count : 2 * count]
    pick_ref, combine_ref, scale_ref = refs[2 * count : 2 * count + 3]
    at = 2 * count + 3
    early, at = [refs[at + 3 * i : at + 3 * i + 3] for i in range(staged)], at + 3 * staged
    weights, at = refs[at : at + 3], at + 3
    kept, away, at = refs[at : at + count], refs[at + count : at + 2 * count], at + 2 * count
    picked, buffers, sems = refs[at], refs[at + 1 : at + 4], refs[at + 4]
    here = picked.shape[0]
    depth, units, _ = buffers[0].shape
    half = picked.shape[2] // 2
    side = where[1]
    near = pl.ds(pl.multiple_of(side * half, half), half)
    far = pl.ds(pl.multiple_of((1 - side) * half, half), half)
    piece = units // PIECES

    def copies(expert, slot):
        for w in range(3):
            for i in range(PIECES):
                rows = pl.ds(i * piece, piece)
                yield pltpu.make_async_copy(weights[w].at[expert, rows], buffers[w].at[slot, rows], sems.at[slot, w, i])

    for i in range(min(depth, here - staged)):
        for copy in copies(staged + i, i):
            copy.start()

    for c in range(count):
        for columns, block in ((near, mine[c]), (far, other[c])):
            rows = jnp.dot(pick_ref[c], block[...], preferred_element_type=jnp.float32).astype(jnp.bfloat16)
            for e in range(here):
                picked[e, c * SLOTS : (c + 1) * SLOTS, columns] = rows[e * SLOTS : (e + 1) * SLOTS]

    for e in range(staged):
        picked[e] = expert_rows(picked[e], *early[e], scale_ref[e])

    def work(i, _):
        slot = lax.rem(i, depth)
        expert = staged + i
        for copy in copies(expert, slot):
            copy.wait()
        picked[expert] = expert_rows(picked[expert], *(buffer.at[slot] for buffer in buffers), scale_ref[expert])

        @pl.when(expert + depth < here)
        def _():
            for copy in copies(expert + depth, slot):
                copy.start()

        return 0

    lax.fori_loop(0, here - staged, work, 0)
    for c in range(count):
        for columns, out in ((far, away[c]), (near, kept[c])):
            rows = [picked[e, c * SLOTS : (c + 1) * SLOTS, columns] for e in range(here)]
            total = jnp.dot(combine_ref[c], jnp.concatenate(rows, axis=0), preferred_element_type=jnp.float32)
            out[...] = total.astype(jnp.bfloat16)


def expert_specs(w_gate, rows):
    hidden, width = w_gate.shape[1:]
    weight = pl.BlockSpec((1, hidden, width), lambda e, where: (e, 0, 0))
    return [weight, weight, weight, pl.BlockSpec((1, 1, rows), lambda e, where: (e, 0, 0))]


def experts_plain(where, picked, w_gate, w_up, w_down, scale):
    here, rows, width = picked.shape
    rows_spec = pl.BlockSpec((1, rows, width), lambda e, where: (e, 0, 0))
    return pl.pallas_call(
        plain_kernel,
        grid_spec=pltpu.PrefetchScalarGridSpec(
            num_scalar_prefetch=1,
            grid=(here,),
            in_specs=[rows_spec] + expert_specs(w_gate, rows),
            out_specs=rows_spec,
        ),
        out_shape=jax.ShapeDtypeStruct(picked.shape, jnp.bfloat16),
        compiler_params=pltpu.CompilerParams(vmem_limit_bytes=VMEM_LIMIT),
        name="experts",
    )(where, picked, w_gate, w_up, w_down, scale)


def experts_fused(where, mine, other, pick, combine, scale, early, w_gate, w_up, w_down):
    count, (local, half) = len(mine), mine[0].shape
    here, _, rows = scale.shape
    units = w_gate.shape[1]
    depth = min(DEPTH, here)
    whole = pl.BlockSpec(memory_space=pltpu.VMEM)
    outs = pl.pallas_call(
        functools.partial(fused_kernel, count, len(early)),
        in_specs=[pl.BlockSpec(memory_space=pltpu.SMEM)]
        + [whole] * (2 * count + 3 + 3 * len(early))
        + [pl.BlockSpec(memory_space=pltpu.HBM)] * 3,
        out_specs=[whole] * (2 * count),
        scratch_shapes=[pltpu.VMEM((here, rows, 2 * half), jnp.bfloat16)]
        + [pltpu.VMEM((depth, units, 2 * half), jnp.bfloat16)] * 3
        + [pltpu.SemaphoreType.DMA((depth, 3, PIECES))],
        out_shape=[pltpu.VMEM((local, half), jnp.bfloat16)] * (2 * count),
        compiler_params=pltpu.CompilerParams(vmem_limit_bytes=28 * MIB),
        name="experts",
    )(where, *mine, *other, pick, combine, scale, *sum(early, []),
      *(pltpu.with_memory_space_constraint(w, pltpu.HBM) for w in (w_gate, w_up, w_down)))
    return outs[:count], outs[count:]


def body(
    queries,
    latent,
    residual,
    seg_lengths,
    span_order,
    expert_ids,
    route_weights,
    kv_up,
    out_proj,
    norm_gain,
    w_gate,
    w_up,
    w_down,
):
    local_rows, width = residual.shape
    span = local_rows // 2
    heads = kv_up.shape[1] // (NOPE + VHEAD)
    count = lax.axis_size("ctx")
    here = EXPERTS // count
    me, side = lax.axis_index("ctx"), lax.axis_index("exp")
    where = jnp.stack([me, side]).astype(jnp.int32)

    base = latent.shape[1]
    w_gate, w_up = w_gate.transpose(0, 2, 1), w_up.transpose(0, 2, 1)
    packed = pack(where, latent, expert_ids, route_weights)
    info = jnp.concatenate([where, sources_of(me, count), span_order, seg_lengths])
    q = queries.reshape(local_rows, heads, NOPE + ROPE).transpose(1, 0, 2)
    gain = norm_gain.reshape(1, width)
    ready = stage((kv_up, out_proj, residual), (None, None, None)) if count <= FEW else (kv_up, out_proj, residual)
    found, found_other, made = gather(packed, count, [(info, q, gain), tuple(ready)])
    (info, q, gain), (kv_up, out_proj, residual) = made
    mine, other = jnp.stack(found), jnp.stack(found_other)
    partial = attend(info, q, mine, other, kv_up, out_proj, count)
    there = swap(partial)
    mine, other, partial = lax.optimization_barrier((mine, other, partial))
    middle, normed = norm(where, residual, partial, there, gain)

    facts_mine, facts_other = mine[:, :, base : base + 3 * TOP], other[:, :, base : base + 3 * TOP]
    facts = jnp.concatenate(
        [jnp.where(side == 0, facts_mine, facts_other), jnp.where(side == 0, facts_other, facts_mine)], axis=1
    ).astype(jnp.float32)
    ids, share = facts[:, :, :TOP], facts[:, :, TOP : 2 * TOP] + facts[:, :, 2 * TOP :]
    own = (me * here + jnp.arange(here, dtype=jnp.int32)).astype(jnp.float32)
    hit = ids[:, :, :, None] == own
    hot = jnp.any(hit, axis=2)
    share = jnp.sum(jnp.where(hit, share[:, :, :, None], 0.0), axis=2)
    token = jnp.arange(local_rows, dtype=jnp.int32)
    before = (token[:, None] > token[None, :]).astype(jnp.bfloat16)
    rank = jnp.einsum("tu,cue->cte", before, hot.astype(jnp.bfloat16), preferred_element_type=jnp.float32)
    rank = jnp.where(hot, rank, -1.0)
    slot = jnp.arange(SLOTS, dtype=jnp.int32).astype(jnp.float32)
    combine = rank[:, :, :, None] == slot
    scale = jnp.sum(jnp.where(combine, share[:, :, :, None], 0.0), axis=1)
    scale = scale.transpose(1, 0, 2).reshape(here, 1, count * SLOTS)
    combine = combine.astype(jnp.bfloat16).reshape(count, local_rows, here * SLOTS)
    pick = combine.transpose(0, 2, 1)

    early = [()] * STAGED if count > FEW else [stage((w_gate, w_up, w_down), (e, e, e)) for e in range(STAGED)]
    got, got_other, made = gather(normed, count, [(pick, combine, scale)] + [tuple(x) for x in early])
    (pick, combine, scale), early = made[0], [list(x) for x in made[1:]]
    if count <= FEW:
        kept, away = experts_fused(where, got, got_other, pick, combine, scale, early, w_gate, w_up, w_down)
    else:
        near, far = jnp.stack(got), jnp.stack(got_other)
        full = jnp.concatenate([jnp.where(side == 0, near, far), jnp.where(side == 0, far, near)], axis=2)
        picked = jnp.einsum("cst,ctd->csd", pick, full, preferred_element_type=jnp.float32).astype(jnp.bfloat16)
        picked = picked.reshape(count, here, SLOTS, width).transpose(1, 0, 2, 3).reshape(here, count * SLOTS, width)
        result = experts_plain(where, picked, w_gate, w_up, w_down, scale)
        result = result.reshape(here, count, SLOTS, width).transpose(1, 0, 2, 3).reshape(count, here * SLOTS, width)
        total = jnp.einsum("cts,csd->ctd", combine, result, preferred_element_type=jnp.float32).astype(jnp.bfloat16)
        left, right = jnp.split(total, 2, axis=2)
        kept, away = jnp.where(side == 0, left, right), jnp.where(side == 0, right, left)
    swap_all = lambda pieces: [swap(piece) for piece in pieces] if count <= FEW else list(swap(jnp.stack(pieces)))
    order = [(count // 2 + (d + 1) // 2 * (1 - d % 2 * 2)) % count for d in range(count)]
    swapped = dict(zip(order, swap_all([away[c] for c in order])))
    parts = [functools.partial(summed, [kept[c], swapped[c]]) for c in range(count)]
    return (middle.astype(jnp.float32) + reduce(parts, count)).astype(jnp.bfloat16)


def solution(mesh):
    in_specs = (
        P(("groups", "ctx"), "exp"),
        P(("groups", "ctx"), None),
        P(("groups", "ctx"), None),
        P("groups"),
        P("groups"),
        P(("groups", "ctx"), None),
        P(("groups", "ctx"), None),
        P(None, "exp"),
        P("exp", None),
        P(),
        P("ctx", None, "exp"),
        P("ctx", None, "exp"),
        P("ctx", "exp", None),
    )
    out_specs = P(("groups", "ctx"), "exp")
    return jax.shard_map(body, mesh=mesh, in_specs=in_specs, out_specs=out_specs, check_vma=False)
```

```python
import functools
import math

import jax
import jax.numpy as jnp
import numpy as np
from jax import lax
from jax.experimental import pallas as pl
from jax.experimental.pallas import tpu as pltpu
from jax.sharding import PartitionSpec as P

NOPE = 128
ROPE = 64
VHEAD = 128
LAT = 512
EXPERTS = 64
TOP = 6
SLOTS = 16
WIDE = 640
MIB = 1024 * 1024
VMEM_LIMIT = 50 * MIB
STREAMS = 2
DEPTH = 3
PIECES = 2
SWAP = [(0, 1), (1, 0)]
FEW = 8


def cycle_of(count):
    fast = 2 ** (int(math.log2(count)) // 2)
    slow = count // fast
    cycle = [0]
    for i in range(slow):
        columns = range(1, fast)
        cycle += [i * fast + j for j in (columns if i % 2 == 0 else reversed(columns))]
    return cycle + [i * fast for i in reversed(range(1, slow))]


def step(value, ahead, count):
    cycle = cycle_of(count)
    return lax.ppermute(value, "ctx", [(cycle[p], cycle[(p + ahead) % count]) for p in range(count)])


def swap(value):
    return lax.ppermute(value, "exp", SWAP)


def summed(pieces):
    total = pieces[0].astype(jnp.float32)
    for piece in pieces[1:]:
        total = total + piece.astype(jnp.float32)
    return total


def sources_of(me, count):
    if count > FEW:
        return jnp.arange(count, dtype=jnp.int32)
    cycle = cycle_of(count)
    table = np.zeros((count, count), np.int32)
    for p in range(count):
        table[cycle[p]] = [cycle[p - d] for d in range(count)]
    return lax.dynamic_index_in_dim(jnp.asarray(table), me, keepdims=False)


def gather(block, count, beside=()):
    if count > FEW:
        found = lax.all_gather(block, "ctx")
        return list(found), list(swap(found)), [run(*arguments) for run, arguments in beside]
    middle = count // 2
    found, other, made = [None] * count, [None] * count, []
    found[0] = block
    other[0] = swap(block)
    for d in range(1, middle):
        for place, before, ahead in ((d, d - 1, 1), (count - d, (1 - d) % count, -1)):
            arrived = step(found[before], ahead, count)
            extra = ()
            if ahead == 1 and len(beside) >= d:
                run, arguments = beside[d - 1]
                extra = run(*lax.optimization_barrier((found[before], arguments))[1])
            found[place], other[before], extra = lax.optimization_barrier((arrived, other[before], extra))
            if ahead == 1:
                made.append(extra)
            other[place] = swap(found[place])
    half = block.shape[0] // 2
    ahead, back = step(found[middle - 1][:half], 1, count), step(found[middle + 1][half:], -1, count)
    found[middle] = jnp.concatenate([ahead, back], axis=0)
    other[middle] = swap(found[middle])
    return found, other, made[: len(beside)]


def reduce(parts, count):
    if count > FEW:
        return lax.psum_scatter(jnp.stack([part() for part in parts]).astype(jnp.bfloat16), "ctx").astype(jnp.float32)
    middle = count // 2
    first = parts[middle]().astype(jnp.bfloat16)
    half = first.shape[0] // 2
    zero = jnp.zeros((half, first.shape[1]), jnp.bfloat16)
    ahead = jnp.concatenate([step(first[:half], 1, count), zero], axis=0)
    back = jnp.concatenate([zero, step(first[half:], -1, count)], axis=0)
    for d in range(middle - 1, 0, -1):
        ahead = step((parts[count - d]() + ahead.astype(jnp.float32)).astype(jnp.bfloat16), 1, count)
        back = step((parts[d]() + back.astype(jnp.float32)).astype(jnp.bfloat16), -1, count)
    return parts[0]() + ahead.astype(jnp.float32) + back.astype(jnp.float32)


def attend_kernel(count, blocks, info, q_ref, mine_ref, other_ref, up_ref, proj_ref, out_ref, m_ref, l_ref, acc_ref):
    chunk = pl.program_id(0)
    side = info[1]
    sources = lambda c: info[2 + c]
    order = lambda j: info[2 + count + j]
    segs = info.shape[0] - 2 - 3 * count
    span = mine_ref.shape[1]
    heads, rows, _ = q_ref.shape

    @pl.when(chunk == 0)
    def _():
        m_ref[...] = jnp.full_like(m_ref, -1e30)
        l_ref[...] = jnp.zeros_like(l_ref)
        acc_ref[...] = jnp.zeros_like(acc_ref)

    row = lax.broadcasted_iota(jnp.int32, (rows, 1), 0)
    first = order(2 * sources(0)) * span
    second = order(2 * sources(0) + 1) * span
    qpos = jnp.where(row < span, first + row, second + row - span)
    low = jnp.zeros((rows, 1), jnp.int32)
    start = jnp.int32(0)
    for m in range(segs):
        low = jnp.where(qpos >= start, start, low)
        start = start + info[2 + 3 * count + m]
    keys = blocks * span
    lane = lax.broadcasted_iota(jnp.int32, (1, keys), 1)
    within, which = lane % span, lane // span
    kpos_parts = []
    for half in (side, 1 - side):
        base = jnp.zeros((1, keys), jnp.int32)
        for j in range(blocks):
            src = sources(chunk * blocks + j)
            base = jnp.where(which == j, order(2 * src + half) * span, base)
        kpos_parts.append(base + within)
    kpos = jnp.concatenate(kpos_parts, axis=1)
    visible = (kpos >= low) & (kpos <= qpos)

    lat = jnp.concatenate([mine_ref[...].reshape(keys, WIDE), other_ref[...].reshape(keys, WIDE)], axis=0)
    keyval = jnp.dot(lat[:, :LAT], up_ref[...], preferred_element_type=jnp.float32).astype(jnp.bfloat16)
    rope = lat[:, LAT : LAT + ROPE]
    scale = 1.0 / math.sqrt(NOPE + ROPE)
    for h in range(heads):
        base = h * (NOPE + VHEAD)
        key = jnp.concatenate([keyval[:, base : base + NOPE], rope], axis=1)
        scores = lax.dot_general(q_ref[h], key, (((1,), (1,)), ((), ())), preferred_element_type=jnp.float32)
        scores = jnp.where(visible, scores * scale, -1e30)
        best = m_ref[h]
        fresh = jnp.maximum(best, jnp.max(scores, axis=1, keepdims=True))
        weights = jnp.where(visible, jnp.exp(scores - fresh), 0.0)
        shrink = jnp.exp(best - fresh)
        m_ref[h] = fresh
        l_ref[h] = l_ref[h] * shrink + jnp.sum(weights, axis=1, keepdims=True)
        mixed = jnp.dot(
            weights.astype(jnp.bfloat16), keyval[:, base + NOPE : base + NOPE + VHEAD], preferred_element_type=jnp.float32
        )
        acc_ref[h] = acc_ref[h] * shrink + mixed

    @pl.when(chunk == pl.num_programs(0) - 1)
    def _():
        attended = [(acc_ref[h] / l_ref[h]).astype(jnp.bfloat16) for h in range(heads)]
        out = jnp.dot(jnp.concatenate(attended, axis=1), proj_ref[...], preferred_element_type=jnp.float32)
        out_ref[...] = out.astype(jnp.bfloat16)


def attend(info, q, mine, other, kv_up, out_proj, count):
    heads, rows, depth = q.shape
    blocks = math.gcd(count, 8)
    span = mine.shape[1]
    whole = pl.BlockSpec(memory_space=pltpu.VMEM)
    lat_spec = whole if blocks == count else pl.BlockSpec((blocks, span, WIDE), lambda i, *_: (i, 0, 0))
    return pl.pallas_call(
        functools.partial(attend_kernel, count, blocks),
        grid_spec=pltpu.PrefetchScalarGridSpec(
            num_scalar_prefetch=1,
            grid=(count // blocks,),
            in_specs=[whole, lat_spec, lat_spec, whole, whole],
            out_specs=whole,
            scratch_shapes=[
                pltpu.VMEM((heads, rows, 1), jnp.float32),
                pltpu.VMEM((heads, rows, 1), jnp.float32),
                pltpu.VMEM((heads, rows, VHEAD), jnp.float32),
            ],
        ),
        out_shape=pltpu.VMEM((rows, out_proj.shape[1]), jnp.bfloat16),
        compiler_params=pltpu.CompilerParams(vmem_limit_bytes=28 * MIB),
        name="attend",
    )(info, q, mine, other, kv_up, out_proj)


def stage_kernel(picks, *refs):
    here = len(picks)
    sems = refs[2 * here]
    copies = []
    for i, pick in enumerate(picks):
        source = refs[i] if pick is None else refs[i].at[pick]
        piece = source.shape[0] // PIECES
        for p in range(PIECES):
            rows = pl.ds(p * piece, piece)
            copies.append(pltpu.make_async_copy(source.at[rows], refs[here + i].at[rows], sems.at[i, p]))
    for copy in copies:
        copy.start()
    for copy in copies:
        copy.wait()


def stage(arrays, picks):
    shapes = [x.shape if pick is None else x.shape[1:] for x, pick in zip(arrays, picks)]
    return pl.pallas_call(
        functools.partial(stage_kernel, picks),
        in_specs=[pl.BlockSpec(memory_space=pltpu.HBM)] * len(arrays),
        out_specs=[pl.BlockSpec(memory_space=pltpu.VMEM)] * len(arrays),
        scratch_shapes=[pltpu.SemaphoreType.DMA((len(arrays), PIECES))],
        out_shape=[pltpu.VMEM(shape, x.dtype) for shape, x in zip(shapes, arrays)],
        compiler_params=pltpu.CompilerParams(vmem_limit_bytes=2 * MIB),
        name="stage",
    )(*(pltpu.with_memory_space_constraint(x, pltpu.HBM) for x in arrays))


def norm_kernel(where, residual_ref, here_ref, there_ref, gain_ref, middle_ref, *normed_refs):
    side = where[1]
    half = middle_ref.shape[1]
    total = here_ref[...].astype(jnp.float32) + there_ref[...].astype(jnp.float32)
    middle = (residual_ref[...].astype(jnp.float32) + total).astype(jnp.bfloat16)
    wide = middle.astype(jnp.float32)
    inverse = lax.rsqrt(jnp.mean(wide * wide, axis=1, keepdims=True) + 1e-06)
    normed = wide * inverse * gain_ref[...].astype(jnp.float32)
    middle_ref[...] = jnp.where(side == 0, wide[:, :half], wide[:, half:]).astype(jnp.bfloat16)
    normed = jnp.where(side == 0, normed[:, :half], normed[:, half:]).astype(jnp.bfloat16)
    part = half // len(normed_refs)
    for h, ref in enumerate(normed_refs):
        ref[...] = normed[:, h * part : (h + 1) * part]


def norm(where, residual, here, there, gain):
    rows, width = residual.shape
    half = width // 2
    shapes = [(rows, half)] + [(rows, half // STREAMS)] * STREAMS
    whole = pl.BlockSpec(memory_space=pltpu.VMEM)
    return pl.pallas_call(
        norm_kernel,
        in_specs=[pl.BlockSpec(memory_space=pltpu.SMEM)] + [whole] * 4,
        out_specs=[whole] * len(shapes),
        out_shape=[pltpu.VMEM(shape, jnp.bfloat16) for shape in shapes],
        compiler_params=pltpu.CompilerParams(vmem_limit_bytes=12 * MIB),
        name="norm",
    )(where, residual, here, there, gain)


def pack_kernel(where, *refs):
    copies = [pltpu.make_async_copy(refs[i], refs[4 + i], refs[8].at[i]) for i in range(3)]
    for copy in copies:
        copy.start()
    for copy in copies:
        copy.wait()
    out_ref, (latent_ref, ids_ref, weights_ref, rows) = refs[3], refs[4:8]
    base, tokens = latent_ref.shape
    span = out_ref.shape[0]
    weights = weights_ref[...]
    high = weights.astype(jnp.bfloat16).astype(jnp.float32)
    rows[...] = jnp.zeros_like(rows)
    rows[0:TOP] = ids_ref[...].astype(jnp.float32)
    rows[TOP : 2 * TOP] = high
    rows[2 * TOP : 3 * TOP] = weights - high
    row = lax.broadcasted_iota(jnp.int32, (span, tokens), 0) + where[1] * span
    chosen = (row == lax.broadcasted_iota(jnp.int32, (span, tokens), 1)).astype(jnp.float32).astype(jnp.bfloat16)
    turn = lambda value: lax.dot_general(
        chosen, value, (((1,), (1,)), ((), ())), preferred_element_type=jnp.float32
    ).astype(jnp.bfloat16)
    every = jnp.concatenate([latent_ref[...], rows[...].astype(jnp.bfloat16)], axis=0)
    out_ref[...] = turn(every)


def pack(where, latent, expert_ids, route_weights):
    local_rows, base = latent.shape
    arrays = (latent.T, expert_ids.T, route_weights.T)
    return pl.pallas_call(
        pack_kernel,
        in_specs=[pl.BlockSpec(memory_space=pltpu.SMEM)] + [pl.BlockSpec(memory_space=pltpu.HBM)] * 3,
        out_specs=pl.BlockSpec(memory_space=pltpu.VMEM),
        scratch_shapes=[pltpu.VMEM(x.shape, x.dtype) for x in arrays]
        + [pltpu.VMEM((WIDE - base, local_rows), jnp.float32), pltpu.SemaphoreType.DMA((3,))],
        out_shape=pltpu.VMEM((local_rows // 2, WIDE), jnp.bfloat16),
        compiler_params=pltpu.CompilerParams(vmem_limit_bytes=4 * MIB),
        name="pack",
    )(where, *(pltpu.with_memory_space_constraint(x, pltpu.HBM) for x in arrays))


def expert_rows(rows, gate_ref, up_ref, down_ref, scale):
    by_columns = (((1,), (1,)), ((), ()))
    gate = lax.dot_general(gate_ref[...], rows, by_columns, preferred_element_type=jnp.float32)
    upper = lax.dot_general(up_ref[...], rows, by_columns, preferred_element_type=jnp.float32)
    hidden = (gate / (1.0 + jnp.exp(-gate)) * upper * scale).astype(jnp.bfloat16)
    by_rows = (((0,), (0,)), ((), ()))
    return lax.dot_general(hidden, down_ref[...], by_rows, preferred_element_type=jnp.float32).astype(jnp.bfloat16)


def plain_kernel(where, rows_ref, gate_ref, up_ref, down_ref, scale_ref, out_ref):
    out_ref[0] = expert_rows(rows_ref[0], gate_ref.at[0], up_ref.at[0], down_ref.at[0], scale_ref[0])


def fused_kernel(count, where, *refs):
    blocks = STREAMS * count
    mine, other = refs[:blocks], refs[blocks : 2 * blocks]
    combine_ref, scale_ref = refs[2 * blocks : 2 * blocks + 2]
    weights = refs[2 * blocks + 2 : 2 * blocks + 5]
    kept, away = refs[2 * blocks + 5 : 3 * blocks + 5], refs[3 * blocks + 5 : 4 * blocks + 5]
    picked, buffers, sems = refs[4 * blocks + 5], refs[4 * blocks + 6 : 4 * blocks + 9], refs[4 * blocks + 9]
    here = picked.shape[0]
    depth, units, _ = buffers[0].shape
    part = mine[0].shape[1]
    half = part * STREAMS
    side = where[1]
    piece = units // PIECES
    by_rows = (((0,), (0,)), ((), ()))

    def columns(side, h):
        return pl.ds(pl.multiple_of(side * half + h * part, part), part)

    def copies(expert, slot):
        for w in range(3):
            for i in range(PIECES):
                rows = pl.ds(i * piece, piece)
                yield pltpu.make_async_copy(weights[w].at[expert, rows], buffers[w].at[slot, rows], sems.at[slot, w, i])

    for e in range(depth):
        for copy in copies(e, e):
            copy.start()

    for c in range(count):
        for h in range(STREAMS):
            for place, block in ((columns(side, h), mine), (columns(1 - side, h), other)):
                rows = lax.dot_general(
                    combine_ref[c], block[h * count + c][...], by_rows, preferred_element_type=jnp.float32
                ).astype(jnp.bfloat16)
                for e in range(here):
                    picked[e, c * SLOTS : (c + 1) * SLOTS, place] = rows[e * SLOTS : (e + 1) * SLOTS]

    def work(expert, _):
        slot = lax.rem(expert, depth)
        for copy in copies(expert, slot):
            copy.wait()
        picked[expert] = expert_rows(picked[expert], *(buffer.at[slot] for buffer in buffers), scale_ref[expert])

        @pl.when(expert + depth < here)
        def _():
            for copy in copies(expert + depth, slot):
                copy.start()

        return 0

    lax.fori_loop(0, here, work, 0)
    for c in range(count):
        for h in range(STREAMS):
            for place, out in ((columns(1 - side, h), away), (columns(side, h), kept)):
                rows = [picked[e, c * SLOTS : (c + 1) * SLOTS, place] for e in range(here)]
                total = jnp.dot(combine_ref[c], jnp.concatenate(rows, axis=0), preferred_element_type=jnp.float32)
                out[h * count + c][...] = total.astype(jnp.bfloat16)


def expert_specs(w_gate, rows):
    hidden, width = w_gate.shape[1:]
    weight = pl.BlockSpec((1, hidden, width), lambda e, where: (e, 0, 0))
    return [weight, weight, weight, pl.BlockSpec((1, 1, rows), lambda e, where: (e, 0, 0))]


def experts_plain(where, picked, w_gate, w_up, w_down, scale):
    here, rows, width = picked.shape
    rows_spec = pl.BlockSpec((1, rows, width), lambda e, where: (e, 0, 0))
    return pl.pallas_call(
        plain_kernel,
        grid_spec=pltpu.PrefetchScalarGridSpec(
            num_scalar_prefetch=1,
            grid=(here,),
            in_specs=[rows_spec] + expert_specs(w_gate, rows),
            out_specs=rows_spec,
        ),
        out_shape=jax.ShapeDtypeStruct(picked.shape, jnp.bfloat16),
        compiler_params=pltpu.CompilerParams(vmem_limit_bytes=VMEM_LIMIT),
        name="experts",
    )(where, picked, w_gate, w_up, w_down, scale)


def experts_fused(where, mine, other, combine, scale, w_gate, w_up, w_down):
    count, (local, part) = len(mine[0]), mine[0][0].shape
    here, _, rows = scale.shape
    units = w_gate.shape[1]
    depth = min(DEPTH, here)
    blocks = STREAMS * count
    whole = pl.BlockSpec(memory_space=pltpu.VMEM)
    outs = pl.pallas_call(
        functools.partial(fused_kernel, count),
        in_specs=[pl.BlockSpec(memory_space=pltpu.SMEM)]
        + [whole] * (2 * blocks + 2)
        + [pl.BlockSpec(memory_space=pltpu.HBM)] * 3,
        out_specs=[whole] * (2 * blocks),
        scratch_shapes=[pltpu.VMEM((here, rows, w_gate.shape[2]), jnp.bfloat16)]
        + [pltpu.VMEM((depth, units, w_gate.shape[2]), jnp.bfloat16)] * 3
        + [pltpu.SemaphoreType.DMA((depth, 3, PIECES))],
        out_shape=[pltpu.VMEM((local, part), jnp.bfloat16)] * (2 * blocks),
        compiler_params=pltpu.CompilerParams(vmem_limit_bytes=38 * MIB),
        name="experts",
    )(where, *sum(mine, []), *sum(other, []), combine, scale,
      *(pltpu.with_memory_space_constraint(w, pltpu.HBM) for w in (w_gate, w_up, w_down)))
    lists = [outs[i * count : (i + 1) * count] for i in range(2 * STREAMS)]
    return lists[:STREAMS], lists[STREAMS:]


def body(
    queries,
    latent,
    residual,
    seg_lengths,
    span_order,
    expert_ids,
    route_weights,
    kv_up,
    out_proj,
    norm_gain,
    w_gate,
    w_up,
    w_down,
):
    local_rows, width = residual.shape
    span = local_rows // 2
    heads = kv_up.shape[1] // (NOPE + VHEAD)
    count = lax.axis_size("ctx")
    here = EXPERTS // count
    me, side = lax.axis_index("ctx"), lax.axis_index("exp")
    where = jnp.stack([me, side]).astype(jnp.int32)

    base = latent.shape[1]
    w_gate, w_up = w_gate.transpose(0, 2, 1), w_up.transpose(0, 2, 1)
    packed = pack(where, latent, expert_ids, route_weights)
    few = count <= FEW
    bring = lambda *arrays: stage(arrays, (None,) * len(arrays)) if few else arrays
    arrange = lambda x: x.reshape(local_rows, heads, NOPE + ROPE).transpose(1, 0, 2)
    scalars = lambda *arrays: jnp.concatenate([where, sources_of(me, count), *arrays])
    beside = [
        (arrange, (queries,)),
        (bring, (kv_up, out_proj, residual)),
        (lambda gain, *arrays: (gain.reshape(1, width), scalars(*arrays)), (norm_gain, span_order, seg_lengths)),
    ]
    found, found_other, made = gather(packed, count, beside)
    q, (kv_up, out_proj, residual), (gain, info) = made
    mine, other = jnp.stack(found), jnp.stack(found_other)
    partial = attend(info, q, mine, other, kv_up, out_proj, count)
    there = swap(partial)
    mine, other, partial = lax.optimization_barrier((mine, other, partial))
    middle, *normed = norm(where, residual, partial, there, gain)

    facts_mine, facts_other = mine[:, :, base : base + 3 * TOP], other[:, :, base : base + 3 * TOP]
    facts = jnp.concatenate(
        [jnp.where(side == 0, facts_mine, facts_other), jnp.where(side == 0, facts_other, facts_mine)], axis=1
    ).astype(jnp.float32)
    ids, share = facts[:, :, :TOP], facts[:, :, TOP : 2 * TOP] + facts[:, :, 2 * TOP :]
    own = (me * here + jnp.arange(here, dtype=jnp.int32)).astype(jnp.float32)
    hit = ids[:, :, :, None] == own
    hot = jnp.any(hit, axis=2)
    share = jnp.sum(jnp.where(hit, share[:, :, :, None], 0.0), axis=2)
    token = jnp.arange(local_rows, dtype=jnp.int32)
    before = (token[:, None] > token[None, :]).astype(jnp.bfloat16)
    rank = jnp.einsum("tu,cue->cte", before, hot.astype(jnp.bfloat16), preferred_element_type=jnp.float32)
    rank = jnp.where(hot, rank, -1.0)
    slot = jnp.arange(SLOTS, dtype=jnp.int32).astype(jnp.float32)
    combine = rank[:, :, :, None] == slot
    scale = jnp.sum(jnp.where(combine, share[:, :, :, None], 0.0), axis=1)
    scale = scale.transpose(1, 0, 2).reshape(here, 1, count * SLOTS)
    combine = combine.astype(jnp.bfloat16).reshape(count, local_rows, here * SLOTS)

    facts = [(lambda *x: x, (combine, scale))]
    streams = [gather(x, count, facts if h == 0 else ()) for h, x in enumerate(normed)]
    combine, scale = streams[0][2][0]
    near, far = [x[0] for x in streams], [x[1] for x in streams]
    if few:
        kept, away = experts_fused(where, near, far, combine, scale, w_gate, w_up, w_down)
    else:
        near, far = (jnp.concatenate([jnp.stack(x) for x in xs], axis=2) for xs in (near, far))
        full = jnp.concatenate([jnp.where(side == 0, near, far), jnp.where(side == 0, far, near)], axis=2)
        picked = jnp.einsum("cts,ctd->csd", combine, full, preferred_element_type=jnp.float32).astype(jnp.bfloat16)
        picked = picked.reshape(count, here, SLOTS, width).transpose(1, 0, 2, 3).reshape(here, count * SLOTS, width)
        result = experts_plain(where, picked, w_gate, w_up, w_down, scale)
        result = result.reshape(here, count, SLOTS, width).transpose(1, 0, 2, 3).reshape(count, here * SLOTS, width)
        total = jnp.einsum("cts,csd->ctd", combine, result, preferred_element_type=jnp.float32).astype(jnp.bfloat16)
        left, right = jnp.split(total, 2, axis=2)
        kept, away = jnp.where(side == 0, left, right), jnp.where(side == 0, right, left)
        kept, away = ([list(part) for part in jnp.split(x, STREAMS, axis=2)] for x in (kept, away))
    order = [(count // 2 + (d + 1) // 2 * (1 - d % 2 * 2)) % count for d in range(count)]
    swapped = [{} for _ in range(STREAMS)]
    if few:
        for c in order:
            for h in range(STREAMS):
                swapped[h][c] = swap(away[h][c])
    else:
        swapped = [dict(enumerate(swap(jnp.stack(part)))) for part in away]
    sums = [
        reduce([functools.partial(summed, [kept[h][c], swapped[h][c]]) for c in range(count)], count)
        for h in range(STREAMS)
    ]
    return (middle.astype(jnp.float32) + jnp.concatenate(sums, axis=1)).astype(jnp.bfloat16)


def solution(mesh):
    in_specs = (
        P(("groups", "ctx"), "exp"),
        P(("groups", "ctx"), None),
        P(("groups", "ctx"), None),
        P("groups"),
        P("groups"),
        P(("groups", "ctx"), None),
        P(("groups", "ctx"), None),
        P(None, "exp"),
        P("exp", None),
        P(),
        P("ctx", None, "exp"),
        P("ctx", None, "exp"),
        P("ctx", "exp", None),
    )
    out_specs = P(("groups", "ctx"), "exp")
    return jax.shard_map(body, mesh=mesh, in_specs=in_specs, out_specs=out_specs, check_vma=False)
```

```python
import functools
import math

import jax
import jax.numpy as jnp
import numpy as np
from jax import lax
from jax.experimental import pallas as pl
from jax.experimental.pallas import tpu as pltpu
from jax.sharding import PartitionSpec as P

NOPE = 128
ROPE = 64
VHEAD = 128
LAT = 512
EXPERTS = 64
TOP = 6
SLOTS = 16
WIDE = 640
MIB = 1024 * 1024
VMEM_LIMIT = 50 * MIB
STREAMS = 1
DEPTH = 3
PIECES = 2
SWAP = [(0, 1), (1, 0)]
FEW = 8


def cycle_of(count):
    fast = 2 ** (int(math.log2(count)) // 2)
    slow = count // fast
    cycle = [0]
    for i in range(slow):
        columns = range(1, fast)
        cycle += [i * fast + j for j in (columns if i % 2 == 0 else reversed(columns))]
    return cycle + [i * fast for i in reversed(range(1, slow))]


def step(value, ahead, count):
    cycle = cycle_of(count)
    return lax.ppermute(value, "ctx", [(cycle[p], cycle[(p + ahead) % count]) for p in range(count)])


def swap(value):
    return lax.ppermute(value, "exp", SWAP)


def summed(pieces):
    total = pieces[0].astype(jnp.float32)
    for piece in pieces[1:]:
        total = total + piece.astype(jnp.float32)
    return total


def sources_of(me, count):
    if count > FEW:
        return jnp.arange(count, dtype=jnp.int32)
    cycle = cycle_of(count)
    table = np.zeros((count, count), np.int32)
    for p in range(count):
        table[cycle[p]] = [cycle[p - d] for d in range(count)]
    return lax.dynamic_index_in_dim(jnp.asarray(table), me, keepdims=False)


def gather(block, count, beside=()):
    if count > FEW:
        found = lax.all_gather(block, "ctx")
        return list(found), list(swap(found)), [run(*arguments) for run, arguments in beside]
    middle = count // 2
    found, other, made = [None] * count, [None] * count, []
    found[0] = block
    other[0] = swap(block)
    for d in range(1, middle):
        for place, before, ahead in ((d, d - 1, 1), (count - d, (1 - d) % count, -1)):
            arrived = step(found[before], ahead, count)
            extra = ()
            if ahead == 1 and len(beside) >= d:
                run, arguments = beside[d - 1]
                extra = run(*lax.optimization_barrier((found[before], arguments))[1])
            found[place], other[before], extra = lax.optimization_barrier((arrived, other[before], extra))
            if ahead == 1:
                made.append(extra)
            other[place] = swap(found[place])
    half = block.shape[0] // 2
    ahead, back = step(found[middle - 1][:half], 1, count), step(found[middle + 1][half:], -1, count)
    found[middle] = jnp.concatenate([ahead, back], axis=0)
    other[middle] = swap(found[middle])
    return found, other, made[: len(beside)]


def reduce(parts, count):
    if count > FEW:
        return lax.psum_scatter(jnp.stack([part() for part in parts]).astype(jnp.bfloat16), "ctx").astype(jnp.float32)
    middle = count // 2
    first = parts[middle]().astype(jnp.bfloat16)
    half = first.shape[0] // 2
    zero = jnp.zeros((half, first.shape[1]), jnp.bfloat16)
    ahead = jnp.concatenate([step(first[:half], 1, count), zero], axis=0)
    back = jnp.concatenate([zero, step(first[half:], -1, count)], axis=0)
    for d in range(middle - 1, 0, -1):
        ahead = step((parts[count - d]() + ahead.astype(jnp.float32)).astype(jnp.bfloat16), 1, count)
        back = step((parts[d]() + back.astype(jnp.float32)).astype(jnp.bfloat16), -1, count)
    return parts[0]() + ahead.astype(jnp.float32) + back.astype(jnp.float32)


def attend_kernel(count, blocks, info, q_ref, *refs):
    up_ref, proj_ref, out_ref, m_ref, l_ref, acc_ref = refs[-6:]
    latents = refs[:-6]
    chunk = pl.program_id(0)
    side = info[1]
    sources = lambda c: info[2 + c]
    order = lambda j: info[2 + count + j]
    segs = info.shape[0] - 2 - 3 * count
    heads, rows, _ = q_ref.shape
    span = rows // 2

    @pl.when(chunk == 0)
    def _():
        m_ref[...] = jnp.full_like(m_ref, -1e30)
        l_ref[...] = jnp.zeros_like(l_ref)
        acc_ref[...] = jnp.zeros_like(acc_ref)

    row = lax.broadcasted_iota(jnp.int32, (rows, 1), 0)
    first = order(2 * sources(0)) * span
    second = order(2 * sources(0) + 1) * span
    qpos = jnp.where(row < span, first + row, second + row - span)
    low = jnp.zeros((rows, 1), jnp.int32)
    start = jnp.int32(0)
    for m in range(segs):
        low = jnp.where(qpos >= start, start, low)
        start = start + info[2 + 3 * count + m]
    keys = blocks * span
    lane = lax.broadcasted_iota(jnp.int32, (1, keys), 1)
    within, which = lane % span, lane // span
    kpos_parts = []
    for half in (side, 1 - side):
        base = jnp.zeros((1, keys), jnp.int32)
        for j in range(blocks):
            src = sources(chunk * blocks + j)
            base = jnp.where(which == j, order(2 * src + half) * span, base)
        kpos_parts.append(base + within)
    kpos = jnp.concatenate(kpos_parts, axis=1)
    visible = (kpos >= low) & (kpos <= qpos)

    lat = jnp.concatenate([ref[...].reshape(-1, WIDE) for ref in latents], axis=0)
    keyval = jnp.dot(lat[:, :LAT], up_ref[...], preferred_element_type=jnp.float32).astype(jnp.bfloat16)
    rope = lat[:, LAT : LAT + ROPE]
    scale = 1.0 / math.sqrt(NOPE + ROPE)
    for h in range(heads):
        base = h * (NOPE + VHEAD)
        key = jnp.concatenate([keyval[:, base : base + NOPE], rope], axis=1)
        scores = lax.dot_general(q_ref[h], key, (((1,), (1,)), ((), ())), preferred_element_type=jnp.float32)
        scores = jnp.where(visible, scores * scale, -1e30)
        best = m_ref[h]
        fresh = jnp.maximum(best, jnp.max(scores, axis=1, keepdims=True))
        weights = jnp.where(visible, jnp.exp(scores - fresh), 0.0)
        shrink = jnp.exp(best - fresh)
        m_ref[h] = fresh
        l_ref[h] = l_ref[h] * shrink + jnp.sum(weights, axis=1, keepdims=True)
        mixed = jnp.dot(
            weights.astype(jnp.bfloat16), keyval[:, base + NOPE : base + NOPE + VHEAD], preferred_element_type=jnp.float32
        )
        acc_ref[h] = acc_ref[h] * shrink + mixed

    @pl.when(chunk == pl.num_programs(0) - 1)
    def _():
        attended = [(acc_ref[h] / l_ref[h]).astype(jnp.bfloat16) for h in range(heads)]
        out = jnp.dot(jnp.concatenate(attended, axis=1), proj_ref[...], preferred_element_type=jnp.float32)
        out_ref[...] = out.astype(jnp.bfloat16)


def attend(info, q, mine, other, kv_up, out_proj, count):
    heads, rows, depth = q.shape
    blocks = math.gcd(count, 8)
    whole = pl.BlockSpec(memory_space=pltpu.VMEM)
    if blocks == count:
        latents, lat_spec = [*mine, *other], whole
    else:
        latents = [jnp.stack(mine), jnp.stack(other)]
        lat_spec = pl.BlockSpec((blocks, rows // 2, WIDE), lambda i, *_: (i, 0, 0))
    return pl.pallas_call(
        functools.partial(attend_kernel, count, blocks),
        grid_spec=pltpu.PrefetchScalarGridSpec(
            num_scalar_prefetch=1,
            grid=(count // blocks,),
            in_specs=[whole] + [lat_spec] * len(latents) + [whole, whole],
            out_specs=whole,
            scratch_shapes=[
                pltpu.VMEM((heads, rows, 1), jnp.float32),
                pltpu.VMEM((heads, rows, 1), jnp.float32),
                pltpu.VMEM((heads, rows, VHEAD), jnp.float32),
            ],
        ),
        out_shape=pltpu.VMEM((rows, out_proj.shape[1]), jnp.bfloat16),
        compiler_params=pltpu.CompilerParams(vmem_limit_bytes=28 * MIB),
        name="attend",
    )(info, q, *latents, kv_up, out_proj)


def route_kernel(count, where, *refs):
    mine, other, out_ref = refs[:count], refs[count : 2 * count], refs[2 * count]
    _, rows, width = out_ref.shape
    side, here = where[1], width // SLOTS
    base = LAT + ROPE
    lane = lax.broadcasted_iota(jnp.int32, (rows, width), 1)
    own = (where[0] * here + lane // SLOTS).astype(jnp.float32)
    slot = (lane % SLOTS).astype(jnp.float32)
    first = lax.broadcasted_iota(jnp.int32, (rows, rows), 0)
    before = (first > lax.broadcasted_iota(jnp.int32, (rows, rows), 1)).astype(jnp.float32).astype(jnp.bfloat16)
    for c in range(count):
        near, far = mine[c][:, LAT:].astype(jnp.float32), other[c][:, LAT:].astype(jnp.float32)
        left, right = jnp.where(side == 0, near, far), jnp.where(side == 0, far, near)
        facts = jnp.concatenate([left, right], axis=0)
        hot, share = jnp.zeros((rows, width), jnp.float32), jnp.zeros((rows, width), jnp.float32)
        for k in range(TOP):
            hit = facts[:, ROPE + k : ROPE + k + 1] == own
            hot = jnp.where(hit, 1.0, hot)
            share = jnp.where(hit, facts[:, ROPE + TOP + k : ROPE + TOP + k + 1], share)
        rank = jnp.dot(before, hot.astype(jnp.bfloat16), preferred_element_type=jnp.float32)
        out_ref[c] = jnp.where(rank == slot, share, 0.0).astype(jnp.bfloat16)


def route(where, mine, other, here):
    count, (span, _) = len(mine), mine[0].shape
    whole = pl.BlockSpec(memory_space=pltpu.VMEM)
    return pl.pallas_call(
        functools.partial(route_kernel, count),
        in_specs=[pl.BlockSpec(memory_space=pltpu.SMEM)] + [whole] * (2 * count),
        out_specs=whole,
        out_shape=pltpu.VMEM((count, 2 * span, here * SLOTS), jnp.bfloat16),
        compiler_params=pltpu.CompilerParams(vmem_limit_bytes=8 * MIB),
        name="route",
    )(where, *mine, *other)


def stage_kernel(picks, *refs):
    here = len(picks)
    sems = refs[2 * here]
    copies = []
    for i, pick in enumerate(picks):
        source = refs[i] if pick is None else refs[i].at[pick]
        piece = source.shape[0] // PIECES
        for p in range(PIECES):
            rows = pl.ds(p * piece, piece)
            copies.append(pltpu.make_async_copy(source.at[rows], refs[here + i].at[rows], sems.at[i, p]))
    for copy in copies:
        copy.start()
    for copy in copies:
        copy.wait()


def stage(arrays, picks):
    shapes = [x.shape if pick is None else x.shape[1:] for x, pick in zip(arrays, picks)]
    return pl.pallas_call(
        functools.partial(stage_kernel, picks),
        in_specs=[pl.BlockSpec(memory_space=pltpu.HBM)] * len(arrays),
        out_specs=[pl.BlockSpec(memory_space=pltpu.VMEM)] * len(arrays),
        scratch_shapes=[pltpu.SemaphoreType.DMA((len(arrays), PIECES))],
        out_shape=[pltpu.VMEM(shape, x.dtype) for shape, x in zip(shapes, arrays)],
        compiler_params=pltpu.CompilerParams(vmem_limit_bytes=2 * MIB),
        name="stage",
    )(*(pltpu.with_memory_space_constraint(x, pltpu.HBM) for x in arrays))


def norm_kernel(where, residual_ref, here_ref, there_ref, gain_ref, middle_ref, *normed_refs):
    side = where[1]
    half = middle_ref.shape[1]
    total = here_ref[...].astype(jnp.float32) + there_ref[...].astype(jnp.float32)
    middle = (residual_ref[...].astype(jnp.float32) + total).astype(jnp.bfloat16)
    wide = middle.astype(jnp.float32)
    inverse = lax.rsqrt(jnp.mean(wide * wide, axis=1, keepdims=True) + 1e-06)
    normed = wide * inverse * gain_ref[...].astype(jnp.float32)
    middle_ref[...] = jnp.where(side == 0, wide[:, :half], wide[:, half:]).astype(jnp.bfloat16)
    normed = jnp.where(side == 0, normed[:, :half], normed[:, half:]).astype(jnp.bfloat16)
    part = half // len(normed_refs)
    for h, ref in enumerate(normed_refs):
        ref[...] = normed[:, h * part : (h + 1) * part]


def norm(where, residual, here, there, gain):
    rows, width = residual.shape
    half = width // 2
    shapes = [(rows, half)] + [(rows, half // STREAMS)] * STREAMS
    whole = pl.BlockSpec(memory_space=pltpu.VMEM)
    return pl.pallas_call(
        norm_kernel,
        in_specs=[pl.BlockSpec(memory_space=pltpu.SMEM)] + [whole] * 4,
        out_specs=[whole] * len(shapes),
        out_shape=[pltpu.VMEM(shape, jnp.bfloat16) for shape in shapes],
        compiler_params=pltpu.CompilerParams(vmem_limit_bytes=12 * MIB),
        name="norm",
    )(where, residual, here, there, gain)


def pack_kernel(where, *refs):
    copies = [pltpu.make_async_copy(refs[i], refs[4 + i], refs[8].at[i]) for i in range(3)]
    for copy in copies:
        copy.start()
    for copy in copies:
        copy.wait()
    out_ref, (latent_ref, ids_ref, weights_ref, rows) = refs[3], refs[4:8]
    base, tokens = latent_ref.shape
    span = out_ref.shape[0]
    rows[...] = jnp.zeros_like(rows)
    rows[0:TOP] = ids_ref[...].astype(jnp.float32)
    rows[TOP : 2 * TOP] = weights_ref[...]
    row = lax.broadcasted_iota(jnp.int32, (span, tokens), 0) + where[1] * span
    chosen = (row == lax.broadcasted_iota(jnp.int32, (span, tokens), 1)).astype(jnp.float32).astype(jnp.bfloat16)
    turn = lambda value: lax.dot_general(
        chosen, value, (((1,), (1,)), ((), ())), preferred_element_type=jnp.float32
    ).astype(jnp.bfloat16)
    every = jnp.concatenate([latent_ref[...], rows[...].astype(jnp.bfloat16)], axis=0)
    out_ref[...] = turn(every)


def pack(where, latent, expert_ids, route_weights):
    local_rows, base = latent.shape
    arrays = (latent.T, expert_ids.T, route_weights.T)
    return pl.pallas_call(
        pack_kernel,
        in_specs=[pl.BlockSpec(memory_space=pltpu.SMEM)] + [pl.BlockSpec(memory_space=pltpu.HBM)] * 3,
        out_specs=pl.BlockSpec(memory_space=pltpu.VMEM),
        scratch_shapes=[pltpu.VMEM(x.shape, x.dtype) for x in arrays]
        + [pltpu.VMEM((WIDE - base, local_rows), jnp.float32), pltpu.SemaphoreType.DMA((3,))],
        out_shape=pltpu.VMEM((local_rows // 2, WIDE), jnp.bfloat16),
        compiler_params=pltpu.CompilerParams(vmem_limit_bytes=4 * MIB),
        name="pack",
    )(where, *(pltpu.with_memory_space_constraint(x, pltpu.HBM) for x in arrays))


def expert_rows(rows, gate_ref, up_ref, down_ref):
    by_columns = (((1,), (1,)), ((), ()))
    gate = lax.dot_general(gate_ref[...], rows, by_columns, preferred_element_type=jnp.float32)
    upper = lax.dot_general(up_ref[...], rows, by_columns, preferred_element_type=jnp.float32)
    hidden = (gate / (1.0 + jnp.exp(-gate)) * upper).astype(jnp.bfloat16)
    by_rows = (((0,), (0,)), ((), ()))
    return lax.dot_general(hidden, down_ref[...], by_rows, preferred_element_type=jnp.float32).astype(jnp.bfloat16)


def plain_kernel(where, rows_ref, gate_ref, up_ref, down_ref, out_ref):
    out_ref[0] = expert_rows(rows_ref[0], gate_ref.at[0], up_ref.at[0], down_ref.at[0])


def fused_kernel(count, where, *refs):
    blocks = STREAMS * count
    mine, other = refs[:blocks], refs[blocks : 2 * blocks]
    combine_ref = refs[2 * blocks]
    weights = refs[2 * blocks + 1 : 2 * blocks + 4]
    kept, away = refs[2 * blocks + 4 : 3 * blocks + 4], refs[3 * blocks + 4 : 4 * blocks + 4]
    picked, buffers, sems = refs[4 * blocks + 4], refs[4 * blocks + 5 : 4 * blocks + 8], refs[4 * blocks + 8]
    here = picked.shape[0]
    depth, units, _ = buffers[0].shape
    part = mine[0].shape[1]
    half = part * STREAMS
    side = where[1]
    piece = units // PIECES
    by_rows = (((0,), (0,)), ((), ()))

    def columns(side, h):
        return pl.ds(pl.multiple_of(side * half + h * part, part), part)

    def copies(expert, slot):
        for w in range(3):
            for i in range(PIECES):
                rows = pl.ds(i * piece, piece)
                yield pltpu.make_async_copy(weights[w].at[expert, rows], buffers[w].at[slot, rows], sems.at[slot, w, i])

    for e in range(depth):
        for copy in copies(e, e):
            copy.start()

    for c in range(count):
        pick = (combine_ref[c].astype(jnp.float32) > 0).astype(jnp.float32).astype(jnp.bfloat16)
        for h in range(STREAMS):
            for place, block in ((columns(side, h), mine), (columns(1 - side, h), other)):
                rows = lax.dot_general(
                    pick, block[h * count + c][...], by_rows, preferred_element_type=jnp.float32
                ).astype(jnp.bfloat16)
                for e in range(here):
                    picked[e, c * SLOTS : (c + 1) * SLOTS, place] = rows[e * SLOTS : (e + 1) * SLOTS]

    def work(expert, _):
        slot = lax.rem(expert, depth)
        for copy in copies(expert, slot):
            copy.wait()
        picked[expert] = expert_rows(picked[expert], *(buffer.at[slot] for buffer in buffers))

        @pl.when(expert + depth < here)
        def _():
            for copy in copies(expert + depth, slot):
                copy.start()

        return 0

    lax.fori_loop(0, here, work, 0)
    for c in range(count):
        for h in range(STREAMS):
            for place, out in ((columns(1 - side, h), away), (columns(side, h), kept)):
                rows = [picked[e, c * SLOTS : (c + 1) * SLOTS, place] for e in range(here)]
                total = jnp.dot(combine_ref[c], jnp.concatenate(rows, axis=0), preferred_element_type=jnp.float32)
                out[h * count + c][...] = total.astype(jnp.bfloat16)


def expert_specs(w_gate):
    hidden, width = w_gate.shape[1:]
    return [pl.BlockSpec((1, hidden, width), lambda e, where: (e, 0, 0))] * 3


def experts_plain(where, picked, w_gate, w_up, w_down):
    here, rows, width = picked.shape
    rows_spec = pl.BlockSpec((1, rows, width), lambda e, where: (e, 0, 0))
    return pl.pallas_call(
        plain_kernel,
        grid_spec=pltpu.PrefetchScalarGridSpec(
            num_scalar_prefetch=1,
            grid=(here,),
            in_specs=[rows_spec] + expert_specs(w_gate),
            out_specs=rows_spec,
        ),
        out_shape=jax.ShapeDtypeStruct(picked.shape, jnp.bfloat16),
        compiler_params=pltpu.CompilerParams(vmem_limit_bytes=VMEM_LIMIT),
        name="experts",
    )(where, picked, w_gate, w_up, w_down)


def experts_fused(where, mine, other, combine, w_gate, w_up, w_down):
    count, (local, part) = len(mine[0]), mine[0][0].shape
    here, units, _ = w_gate.shape
    rows = count * SLOTS
    depth = min(DEPTH, here)
    blocks = STREAMS * count
    whole = pl.BlockSpec(memory_space=pltpu.VMEM)
    outs = pl.pallas_call(
        functools.partial(fused_kernel, count),
        in_specs=[pl.BlockSpec(memory_space=pltpu.SMEM)]
        + [whole] * (2 * blocks + 1)
        + [pl.BlockSpec(memory_space=pltpu.HBM)] * 3,
        out_specs=[whole] * (2 * blocks),
        scratch_shapes=[pltpu.VMEM((here, rows, w_gate.shape[2]), jnp.bfloat16)]
        + [pltpu.VMEM((depth, units, w_gate.shape[2]), jnp.bfloat16)] * 3
        + [pltpu.SemaphoreType.DMA((depth, 3, PIECES))],
        out_shape=[pltpu.VMEM((local, part), jnp.bfloat16)] * (2 * blocks),
        compiler_params=pltpu.CompilerParams(vmem_limit_bytes=36 * MIB),
        name="experts",
    )(where, *sum(mine, []), *sum(other, []), combine,
      *(pltpu.with_memory_space_constraint(w, pltpu.HBM) for w in (w_gate, w_up, w_down)))
    lists = [outs[i * count : (i + 1) * count] for i in range(2 * STREAMS)]
    return lists[:STREAMS], lists[STREAMS:]


def body(
    queries,
    latent,
    residual,
    seg_lengths,
    span_order,
    expert_ids,
    route_weights,
    kv_up,
    out_proj,
    norm_gain,
    w_gate,
    w_up,
    w_down,
):
    local_rows, width = residual.shape
    span = local_rows // 2
    heads = kv_up.shape[1] // (NOPE + VHEAD)
    count = lax.axis_size("ctx")
    here = EXPERTS // count
    me, side = lax.axis_index("ctx"), lax.axis_index("exp")
    where = jnp.stack([me, side]).astype(jnp.int32)

    base = latent.shape[1]
    w_gate, w_up = w_gate.transpose(0, 2, 1), w_up.transpose(0, 2, 1)
    packed = pack(where, latent, expert_ids, route_weights)
    few = count <= FEW
    bring = lambda *arrays: stage(arrays, (None,) * len(arrays)) if few else arrays
    arrange = lambda x: x.reshape(local_rows, heads, NOPE + ROPE).transpose(1, 0, 2)
    scalars = lambda *arrays: jnp.concatenate([where, sources_of(me, count), *arrays])
    beside = [
        (arrange, (queries,)),
        (bring, (kv_up, out_proj, residual)),
        (lambda gain, *arrays: (gain.reshape(1, width), scalars(*arrays)), (norm_gain, span_order, seg_lengths)),
    ]
    found, found_other, made = gather(packed, count, beside)
    q, (kv_up, out_proj, residual), (gain, info) = made
    partial = attend(info, q, found, found_other, kv_up, out_proj, count)
    middle, *normed = norm(where, residual, partial, swap(partial), gain)

    def place_rows(*blocks):
        if few:
            return route(where, blocks[:count], blocks[count:], here)
        near, far = (jnp.stack(x)[:, :, base : base + 2 * TOP] for x in (blocks[:count], blocks[count:]))
        facts = jnp.concatenate([jnp.where(side == 0, near, far), jnp.where(side == 0, far, near)], axis=1)
        facts = facts.astype(jnp.float32)
        own = (me * here + jnp.arange(here, dtype=jnp.int32)).astype(jnp.float32)
        hit = facts[:, :, :TOP, None] == own
        hot = jnp.any(hit, axis=2)
        share = jnp.sum(jnp.where(hit, facts[:, :, TOP:, None], 0.0), axis=2)
        token = jnp.arange(local_rows, dtype=jnp.int32)
        before = (token[:, None] > token[None, :]).astype(jnp.bfloat16)
        rank = jnp.einsum("tu,cue->cte", before, hot.astype(jnp.bfloat16), preferred_element_type=jnp.float32)
        slot = jnp.arange(SLOTS, dtype=jnp.int32).astype(jnp.float32)
        combine = jnp.where(rank[:, :, :, None] == slot, share[:, :, :, None], 0.0)
        return combine.astype(jnp.bfloat16).reshape(count, local_rows, here * SLOTS)

    streams = [
        gather(x, count, [(place_rows, (*found, *found_other))] if h == 0 else ()) for h, x in enumerate(normed)
    ]
    combine = streams[0][2][0]
    near, far = [x[0] for x in streams], [x[1] for x in streams]
    if few:
        kept, away = experts_fused(where, near, far, combine, w_gate, w_up, w_down)
    else:
        near, far = (jnp.concatenate([jnp.stack(x) for x in xs], axis=2) for xs in (near, far))
        full = jnp.concatenate([jnp.where(side == 0, near, far), jnp.where(side == 0, far, near)], axis=2)
        pick = (combine > 0).astype(jnp.bfloat16)
        picked = jnp.einsum("cts,ctd->csd", pick, full, preferred_element_type=jnp.float32).astype(jnp.bfloat16)
        picked = picked.reshape(count, here, SLOTS, width).transpose(1, 0, 2, 3).reshape(here, count * SLOTS, width)
        result = experts_plain(where, picked, w_gate, w_up, w_down)
        result = result.reshape(here, count, SLOTS, width).transpose(1, 0, 2, 3).reshape(count, here * SLOTS, width)
        total = jnp.einsum("cts,csd->ctd", combine, result, preferred_element_type=jnp.float32).astype(jnp.bfloat16)
        left, right = jnp.split(total, 2, axis=2)
        kept, away = jnp.where(side == 0, left, right), jnp.where(side == 0, right, left)
        kept, away = ([list(part) for part in jnp.split(x, STREAMS, axis=2)] for x in (kept, away))
    order = [(count // 2 + (d + 1) // 2 * (1 - d % 2 * 2)) % count for d in range(count)]
    swapped = [{} for _ in range(STREAMS)]
    if few:
        for c in order:
            for h in range(STREAMS):
                swapped[h][c] = swap(away[h][c])
    else:
        swapped = [dict(enumerate(swap(jnp.stack(part)))) for part in away]
    sums = [
        reduce([functools.partial(summed, [kept[h][c], swapped[h][c]]) for c in range(count)], count)
        for h in range(STREAMS)
    ]
    return (middle.astype(jnp.float32) + jnp.concatenate(sums, axis=1)).astype(jnp.bfloat16)


def solution(mesh):
    in_specs = (
        P(("groups", "ctx"), "exp"),
        P(("groups", "ctx"), None),
        P(("groups", "ctx"), None),
        P("groups"),
        P("groups"),
        P(("groups", "ctx"), None),
        P(("groups", "ctx"), None),
        P(None, "exp"),
        P("exp", None),
        P(),
        P("ctx", None, "exp"),
        P("ctx", None, "exp"),
        P("ctx", "exp", None),
    )
    out_specs = P(("groups", "ctx"), "exp")
    return jax.shard_map(body, mesh=mesh, in_specs=in_specs, out_specs=out_specs, check_vma=False)
```

```python
import functools
import math

import jax
import jax.numpy as jnp
import numpy as np
from jax import lax
from jax.experimental import pallas as pl
from jax.experimental.pallas import tpu as pltpu
from jax.sharding import PartitionSpec as P

NOPE = 128
ROPE = 64
VHEAD = 128
LAT = 512
EXPERTS = 64
TOP = 6
SLOTS = 16
WIDE = 640
MIB = 1024 * 1024
VMEM_LIMIT = 50 * MIB
DEPTH = 3
PIECES = 2
SWAP = [(0, 1), (1, 0)]
FEW = 8


def cycle_of(count):
    fast = 2 ** (int(math.log2(count)) // 2)
    slow = count // fast
    cycle = [0]
    for i in range(slow):
        columns = range(1, fast)
        cycle += [i * fast + j for j in (columns if i % 2 == 0 else reversed(columns))]
    return cycle + [i * fast for i in reversed(range(1, slow))]


def swap(value):
    return lax.ppermute(value, "exp", SWAP)


def turn(value, count, cross=False):
    cycle = cycle_of(count)
    pairs = []
    for p in range(count):
        for core, ahead in ((0, 1), (1, -1)):
            pairs.append((cycle[p] * 2 + core, cycle[(p + ahead) % count] * 2 + (core ^ int(cross))))
    return lax.ppermute(value, ("ctx", "exp"), pairs)


def summed(pieces):
    total = pieces[0].astype(jnp.float32)
    for piece in pieces[1:]:
        total = total + piece.astype(jnp.float32)
    return total


def sources_of(me, side, count):
    if count > FEW:
        return jnp.arange(count, dtype=jnp.int32)
    cycle = cycle_of(count)
    middle = count // 2
    table = np.zeros((2 * count, count), np.int32)
    for p in range(count):
        for core, sign in ((0, 1), (1, -1)):
            ways = [sign * d for d in range(middle + 1)] + [-sign * d for d in range(1, middle)]
            table[cycle[p] * 2 + core] = [cycle[(p - way) % count] for way in ways]
    return lax.dynamic_index_in_dim(jnp.asarray(table), me * 2 + side, keepdims=False)


def gather(block, count, beside=()):
    if count > FEW:
        return list(lax.all_gather(block, "ctx")), [run(*arguments) for run, arguments in beside]
    middle = count // 2
    found, other, made = [block], [()], []
    for d in range(1, middle + 1):
        arrived, extra = turn(found[-1], count), ()
        if len(beside) >= d:
            run, arguments = beside[d - 1]
            extra = run(*lax.optimization_barrier((found[-1], arguments))[1])
        arrived, other[-1], extra = lax.optimization_barrier((arrived, other[-1], extra))
        made.append(extra)
        found.append(arrived)
        if d < middle:
            other.append(swap(arrived))
    return found + other[1:], made[: len(beside)]


def reduce(parts, opposite, own, side, count):
    middle = count // 2
    given = {d: swap(x) for d, x in [(middle, opposite[1])] + [(d, parts[d]) for d in range(middle - 1, 0, -1)]}
    first = turn(summed([opposite[0], given[middle]]).astype(jnp.bfloat16), count).astype(jnp.float32)
    nothing = jnp.zeros_like(first)
    running = jnp.concatenate([jnp.where(side == 0, first, nothing), jnp.where(side == 0, nothing, first)], axis=0)
    for d in range(middle - 1, 0, -1):
        total = summed([parts[middle + d], given[d]]) + running
        if d > 1:
            running = turn(total.astype(jnp.bfloat16), count).astype(jnp.float32)
    left, right = jnp.split(total.astype(jnp.bfloat16), 2, axis=1)
    near = turn(jnp.where(side == 0, left, right), count)
    far = turn(jnp.where(side == 0, right, left), count, cross=True)
    return summed([own[0], swap(own[1]), near, far])


def attend_kernel(count, blocks, info, q_ref, *refs):
    up_ref, proj_ref, out_ref, m_ref, l_ref, acc_ref = refs[-6:]
    latents = refs[:-6]
    chunk = pl.program_id(0)
    sources = lambda c: info[2 + c]
    order = lambda j: info[2 + count + j]
    segs = info.shape[0] - 2 - 3 * count
    heads, rows, _ = q_ref.shape
    span = rows // 2

    @pl.when(chunk == 0)
    def _():
        m_ref[...] = jnp.full_like(m_ref, -1e30)
        l_ref[...] = jnp.zeros_like(l_ref)
        acc_ref[...] = jnp.zeros_like(acc_ref)

    row = lax.broadcasted_iota(jnp.int32, (rows, 1), 0)
    first = order(2 * info[0]) * span
    second = order(2 * info[0] + 1) * span
    qpos = jnp.where(row < span, first + row, second + row - span)
    low = jnp.zeros((rows, 1), jnp.int32)
    start = jnp.int32(0)
    for m in range(segs):
        low = jnp.where(qpos >= start, start, low)
        start = start + info[2 + 3 * count + m]
    keys = blocks * rows
    lane = lax.broadcasted_iota(jnp.int32, (1, keys), 1)
    which = lane // span
    kpos = lane % span
    for j in range(blocks):
        source = sources(chunk * blocks + j)
        for i in range(2):
            kpos = jnp.where(which == 2 * j + i, order(2 * source + i) * span + lane % span, kpos)
    visible = (kpos >= low) & (kpos <= qpos)

    lat = jnp.concatenate([ref[...].reshape(-1, WIDE) for ref in latents], axis=0)
    keyval = jnp.dot(lat[:, :LAT], up_ref[...], preferred_element_type=jnp.float32).astype(jnp.bfloat16)
    rope = lat[:, LAT : LAT + ROPE]
    scale = 1.0 / math.sqrt(NOPE + ROPE)
    for h in range(heads):
        base = h * (NOPE + VHEAD)
        key = jnp.concatenate([keyval[:, base : base + NOPE], rope], axis=1)
        scores = lax.dot_general(q_ref[h], key, (((1,), (1,)), ((), ())), preferred_element_type=jnp.float32)
        scores = jnp.where(visible, scores * scale, -1e30)
        best = m_ref[h]
        fresh = jnp.maximum(best, jnp.max(scores, axis=1, keepdims=True))
        weights = jnp.where(visible, jnp.exp(scores - fresh), 0.0)
        shrink = jnp.exp(best - fresh)
        m_ref[h] = fresh
        l_ref[h] = l_ref[h] * shrink + jnp.sum(weights, axis=1, keepdims=True)
        mixed = jnp.dot(
            weights.astype(jnp.bfloat16), keyval[:, base + NOPE : base + NOPE + VHEAD], preferred_element_type=jnp.float32
        )
        acc_ref[h] = acc_ref[h] * shrink + mixed

    @pl.when(chunk == pl.num_programs(0) - 1)
    def _():
        attended = [(acc_ref[h] / l_ref[h]).astype(jnp.bfloat16) for h in range(heads)]
        out = jnp.dot(jnp.concatenate(attended, axis=1), proj_ref[...], preferred_element_type=jnp.float32)
        out_ref[...] = out.astype(jnp.bfloat16)


def attend(info, q, found, kv_up, out_proj, count):
    heads, rows, depth = q.shape
    blocks = math.gcd(count, 8)
    whole = pl.BlockSpec(memory_space=pltpu.VMEM)
    if blocks == count:
        latents, lat_spec = found, whole
    else:
        latents, lat_spec = [jnp.stack(found)], pl.BlockSpec((blocks, rows, WIDE), lambda i, *_: (i, 0, 0))
    return pl.pallas_call(
        functools.partial(attend_kernel, count, blocks),
        grid_spec=pltpu.PrefetchScalarGridSpec(
            num_scalar_prefetch=1,
            grid=(count // blocks,),
            in_specs=[whole] + [lat_spec] * len(latents) + [whole, whole],
            out_specs=whole,
            scratch_shapes=[
                pltpu.VMEM((heads, rows, 1), jnp.float32),
                pltpu.VMEM((heads, rows, 1), jnp.float32),
                pltpu.VMEM((heads, rows, VHEAD), jnp.float32),
            ],
        ),
        out_shape=pltpu.VMEM((rows, out_proj.shape[1]), jnp.bfloat16),
        compiler_params=pltpu.CompilerParams(vmem_limit_bytes=28 * MIB),
        name="attend",
    )(info, q, *latents, kv_up, out_proj)


def route_kernel(count, where, *refs):
    blocks, out_ref = refs[:count], refs[count]
    _, rows, width = out_ref.shape
    here = width // SLOTS
    lane = lax.broadcasted_iota(jnp.int32, (rows, width), 1)
    own = (where[0] * here + lane // SLOTS).astype(jnp.float32)
    slot = (lane % SLOTS).astype(jnp.float32)
    first = lax.broadcasted_iota(jnp.int32, (rows, rows), 0)
    before = (first > lax.broadcasted_iota(jnp.int32, (rows, rows), 1)).astype(jnp.float32).astype(jnp.bfloat16)
    for c in range(count):
        facts = blocks[c][:, LAT:].astype(jnp.float32)
        hot, share = jnp.zeros((rows, width), jnp.float32), jnp.zeros((rows, width), jnp.float32)
        for k in range(TOP):
            hit = facts[:, ROPE + k : ROPE + k + 1] == own
            hot = jnp.where(hit, 1.0, hot)
            share = jnp.where(hit, facts[:, ROPE + TOP + k : ROPE + TOP + k + 1], share)
        rank = jnp.dot(before, hot.astype(jnp.bfloat16), preferred_element_type=jnp.float32)
        out_ref[c] = jnp.where(rank == slot, share, 0.0).astype(jnp.bfloat16)


def route(where, found, here):
    count, (rows, _) = len(found), found[0].shape
    whole = pl.BlockSpec(memory_space=pltpu.VMEM)
    return pl.pallas_call(
        functools.partial(route_kernel, count),
        in_specs=[pl.BlockSpec(memory_space=pltpu.SMEM)] + [whole] * count,
        out_specs=whole,
        out_shape=pltpu.VMEM((count, rows, here * SLOTS), jnp.bfloat16),
        compiler_params=pltpu.CompilerParams(vmem_limit_bytes=8 * MIB),
        name="route",
    )(where, *found)


def stage_kernel(picks, *refs):
    here = len(picks)
    sems = refs[2 * here]
    copies = []
    for i, pick in enumerate(picks):
        source = refs[i] if pick is None else refs[i].at[pick]
        piece = source.shape[0] // PIECES
        for p in range(PIECES):
            rows = pl.ds(p * piece, piece)
            copies.append(pltpu.make_async_copy(source.at[rows], refs[here + i].at[rows], sems.at[i, p]))
    for copy in copies:
        copy.start()
    for copy in copies:
        copy.wait()


def stage(arrays, picks):
    shapes = [x.shape if pick is None else x.shape[1:] for x, pick in zip(arrays, picks)]
    return pl.pallas_call(
        functools.partial(stage_kernel, picks),
        in_specs=[pl.BlockSpec(memory_space=pltpu.HBM)] * len(arrays),
        out_specs=[pl.BlockSpec(memory_space=pltpu.VMEM)] * len(arrays),
        scratch_shapes=[pltpu.SemaphoreType.DMA((len(arrays), PIECES))],
        out_shape=[pltpu.VMEM(shape, x.dtype) for shape, x in zip(shapes, arrays)],
        compiler_params=pltpu.CompilerParams(vmem_limit_bytes=2 * MIB),
        name="stage",
    )(*(pltpu.with_memory_space_constraint(x, pltpu.HBM) for x in arrays))


def norm_kernel(where, residual_ref, here_ref, there_ref, gain_ref, middle_ref, normed_ref):
    half = middle_ref.shape[1]
    total = here_ref[...].astype(jnp.float32) + there_ref[...].astype(jnp.float32)
    middle = (residual_ref[...].astype(jnp.float32) + total).astype(jnp.bfloat16)
    wide = middle.astype(jnp.float32)
    inverse = lax.rsqrt(jnp.mean(wide * wide, axis=1, keepdims=True) + 1e-06)
    normed_ref[...] = (wide * inverse * gain_ref[...].astype(jnp.float32)).astype(jnp.bfloat16)
    middle_ref[...] = jnp.where(where[1] == 0, wide[:, :half], wide[:, half:]).astype(jnp.bfloat16)


def norm(where, residual, here, there, gain):
    rows, width = residual.shape
    whole = pl.BlockSpec(memory_space=pltpu.VMEM)
    return pl.pallas_call(
        norm_kernel,
        in_specs=[pl.BlockSpec(memory_space=pltpu.SMEM)] + [whole] * 4,
        out_specs=[whole] * 2,
        out_shape=[pltpu.VMEM(shape, jnp.bfloat16) for shape in ((rows, width // 2), (rows, width))],
        compiler_params=pltpu.CompilerParams(vmem_limit_bytes=12 * MIB),
        name="norm",
    )(where, residual, here, there, gain)


def pack_kernel(*refs):
    copies = [pltpu.make_async_copy(refs[i], refs[4 + i], refs[8].at[i]) for i in range(3)]
    for copy in copies:
        copy.start()
    for copy in copies:
        copy.wait()
    out_ref, (latent_ref, ids_ref, weights_ref, rows) = refs[3], refs[4:8]
    tokens = out_ref.shape[0]
    rows[...] = jnp.zeros_like(rows)
    rows[0:TOP] = ids_ref[...].astype(jnp.float32)
    rows[TOP : 2 * TOP] = weights_ref[...]
    row = lax.broadcasted_iota(jnp.int32, (tokens, tokens), 0)
    same = (row == lax.broadcasted_iota(jnp.int32, (tokens, tokens), 1)).astype(jnp.float32).astype(jnp.bfloat16)
    every = jnp.concatenate([latent_ref[...], rows[...].astype(jnp.bfloat16)], axis=0)
    turned = lax.dot_general(same, every, (((1,), (1,)), ((), ())), preferred_element_type=jnp.float32)
    out_ref[...] = turned.astype(jnp.bfloat16)


def pack(latent, expert_ids, route_weights):
    local_rows, base = latent.shape
    arrays = (latent.T, expert_ids.T, route_weights.T)
    return pl.pallas_call(
        pack_kernel,
        in_specs=[pl.BlockSpec(memory_space=pltpu.HBM)] * 3,
        out_specs=pl.BlockSpec(memory_space=pltpu.VMEM),
        scratch_shapes=[pltpu.VMEM(x.shape, x.dtype) for x in arrays]
        + [pltpu.VMEM((WIDE - base, local_rows), jnp.float32), pltpu.SemaphoreType.DMA((3,))],
        out_shape=pltpu.VMEM((local_rows, WIDE), jnp.bfloat16),
        compiler_params=pltpu.CompilerParams(vmem_limit_bytes=4 * MIB),
        name="pack",
    )(*(pltpu.with_memory_space_constraint(x, pltpu.HBM) for x in arrays))


def expert_rows(rows, gate_ref, up_ref, down_ref):
    by_columns = (((1,), (1,)), ((), ()))
    gate = lax.dot_general(gate_ref[...], rows, by_columns, preferred_element_type=jnp.float32)
    upper = lax.dot_general(up_ref[...], rows, by_columns, preferred_element_type=jnp.float32)
    hidden = (gate / (1.0 + jnp.exp(-gate)) * upper).astype(jnp.bfloat16)
    by_rows = (((0,), (0,)), ((), ()))
    return lax.dot_general(hidden, down_ref[...], by_rows, preferred_element_type=jnp.float32).astype(jnp.bfloat16)


def plain_kernel(where, rows_ref, gate_ref, up_ref, down_ref, out_ref):
    out_ref[0] = expert_rows(rows_ref[0], gate_ref.at[0], up_ref.at[0], down_ref.at[0])


def fused_kernel(count, where, *refs):
    blocks, combine_ref, weights = refs[:count], refs[count], refs[count + 1 : count + 4]
    outs, at = refs[count + 4 : 2 * count + 6], 2 * count + 6
    picked, buffers, sems = refs[at], refs[at + 1 : at + 4], refs[at + 4]
    here = picked.shape[0]
    depth, units, width = buffers[0].shape
    side = where[1]
    piece = units // PIECES
    middle = count // 2
    by_rows = (((0,), (0,)), ((), ()))

    def copies(expert, slot):
        for w in range(3):
            for i in range(PIECES):
                rows = pl.ds(i * piece, piece)
                yield pltpu.make_async_copy(weights[w].at[expert, rows], buffers[w].at[slot, rows], sems.at[slot, w, i])

    for e in range(depth):
        for copy in copies(e, e):
            copy.start()

    for c in range(count):
        pick = (combine_ref[c].astype(jnp.float32) > 0).astype(jnp.float32).astype(jnp.bfloat16)
        rows = lax.dot_general(pick, blocks[c][...], by_rows, preferred_element_type=jnp.float32).astype(jnp.bfloat16)
        for e in range(here):
            picked[e, c * SLOTS : (c + 1) * SLOTS] = rows[e * SLOTS : (e + 1) * SLOTS]

    def work(expert, _):
        slot = lax.rem(expert, depth)
        for copy in copies(expert, slot):
            copy.wait()
        picked[expert] = expert_rows(picked[expert], *(buffer.at[slot] for buffer in buffers))

        @pl.when(expert + depth < here)
        def _():
            for copy in copies(expert + depth, slot):
                copy.start()

        return 0

    lax.fori_loop(0, here, work, 0)

    def total(c):
        rows = jnp.concatenate([picked[e, c * SLOTS : (c + 1) * SLOTS] for e in range(here)], axis=0)
        return jnp.dot(combine_ref[c], rows, preferred_element_type=jnp.float32).astype(jnp.bfloat16)

    result = total(middle)
    half = result.shape[0] // 2
    upper, lower = result[:half], result[half:]
    outs[0][...] = jnp.where(side == 0, upper, lower)
    outs[1][...] = jnp.where(side == 0, lower, upper)
    result = total(0)
    left, right = result[:, : width // 2], result[:, width // 2 :]
    outs[2][...] = jnp.where(side == 0, left, right)
    outs[3][...] = jnp.where(side == 0, right, left)
    rest = [c for c in range(count) if c not in (0, middle)]
    for i, c in enumerate(rest):
        outs[4 + i][...] = total(c)


def expert_specs(w_gate):
    hidden, width = w_gate.shape[1:]
    return [pl.BlockSpec((1, hidden, width), lambda e, where: (e, 0, 0))] * 3


def experts_plain(where, picked, w_gate, w_up, w_down):
    here, rows, width = picked.shape
    rows_spec = pl.BlockSpec((1, rows, width), lambda e, where: (e, 0, 0))
    return pl.pallas_call(
        plain_kernel,
        grid_spec=pltpu.PrefetchScalarGridSpec(
            num_scalar_prefetch=1,
            grid=(here,),
            in_specs=[rows_spec] + expert_specs(w_gate),
            out_specs=rows_spec,
        ),
        out_shape=jax.ShapeDtypeStruct(picked.shape, jnp.bfloat16),
        compiler_params=pltpu.CompilerParams(vmem_limit_bytes=VMEM_LIMIT),
        name="experts",
    )(where, picked, w_gate, w_up, w_down)


def experts_fused(where, found, combine, w_gate, w_up, w_down):
    count, (local, width) = len(found), found[0].shape
    here, units, _ = w_gate.shape
    rows = count * SLOTS
    depth = min(DEPTH, here)
    middle = count // 2
    whole = pl.BlockSpec(memory_space=pltpu.VMEM)
    shapes = [(local // 2, width)] * 2 + [(local, width // 2)] * 2 + [(local, width)] * (count - 2)
    outs = pl.pallas_call(
        functools.partial(fused_kernel, count),
        in_specs=[pl.BlockSpec(memory_space=pltpu.SMEM)]
        + [whole] * (count + 1)
        + [pl.BlockSpec(memory_space=pltpu.HBM)] * 3,
        out_specs=[whole] * len(shapes),
        scratch_shapes=[pltpu.VMEM((here, rows, width), jnp.bfloat16)]
        + [pltpu.VMEM((depth, units, width), jnp.bfloat16)] * 3
        + [pltpu.SemaphoreType.DMA((depth, 3, PIECES))],
        out_shape=[pltpu.VMEM(shape, jnp.bfloat16) for shape in shapes],
        compiler_params=pltpu.CompilerParams(vmem_limit_bytes=36 * MIB),
        name="experts",
    )(where, *found, combine, *(pltpu.with_memory_space_constraint(w, pltpu.HBM) for w in (w_gate, w_up, w_down)))
    rest = [c for c in range(count) if c not in (0, middle)]
    return dict(zip(rest, outs[4:])), outs[:2], outs[2:4]


def body(
    queries,
    latent,
    residual,
    seg_lengths,
    span_order,
    expert_ids,
    route_weights,
    kv_up,
    out_proj,
    norm_gain,
    w_gate,
    w_up,
    w_down,
):
    local_rows, width = residual.shape
    span = local_rows // 2
    heads = kv_up.shape[1] // (NOPE + VHEAD)
    count = lax.axis_size("ctx")
    here = EXPERTS // count
    me, side = lax.axis_index("ctx"), lax.axis_index("exp")
    where = jnp.stack([me, side]).astype(jnp.int32)

    base = latent.shape[1]
    w_gate, w_up = w_gate.transpose(0, 2, 1), w_up.transpose(0, 2, 1)
    packed = pack(latent, expert_ids, route_weights)
    few = count <= FEW
    bring = lambda *arrays: stage(arrays, (None,) * len(arrays)) if few else arrays
    arrange = lambda x: x.reshape(local_rows, heads, NOPE + ROPE).transpose(1, 0, 2)
    scalars = lambda *arrays: jnp.concatenate([where, sources_of(me, side, count), *arrays])
    beside = [
        (arrange, (queries,)),
        (bring, (kv_up, out_proj, residual)),
        (lambda gain, *arrays: (gain.reshape(1, width), scalars(*arrays)), (norm_gain, span_order, seg_lengths)),
    ]
    found, made = gather(packed, count, beside)
    q, (kv_up, out_proj, residual), (gain, info) = made
    partial = attend(info, q, found, kv_up, out_proj, count)
    middle, normed = norm(where, residual, partial, swap(partial), gain)

    def place_rows(*blocks):
        if few:
            return route(where, blocks, here)
        facts = jnp.stack(blocks)[:, :, base : base + 2 * TOP].astype(jnp.float32)
        own = (me * here + jnp.arange(here, dtype=jnp.int32)).astype(jnp.float32)
        hit = facts[:, :, :TOP, None] == own
        hot = jnp.any(hit, axis=2)
        share = jnp.sum(jnp.where(hit, facts[:, :, TOP:, None], 0.0), axis=2)
        token = jnp.arange(local_rows, dtype=jnp.int32)
        before = (token[:, None] > token[None, :]).astype(jnp.bfloat16)
        rank = jnp.einsum("tu,cue->cte", before, hot.astype(jnp.bfloat16), preferred_element_type=jnp.float32)
        slot = jnp.arange(SLOTS, dtype=jnp.int32).astype(jnp.float32)
        combine = jnp.where(rank[:, :, :, None] == slot, share[:, :, :, None], 0.0)
        return combine.astype(jnp.bfloat16).reshape(count, local_rows, here * SLOTS)

    got, (combine,) = gather(normed, count, [(place_rows, tuple(found))])
    if few:
        parts, opposite, own = experts_fused(where, got, combine, w_gate, w_up, w_down)
        mixture = reduce(parts, opposite, own, side, count)
    else:
        pick = (combine > 0).astype(jnp.bfloat16)
        picked = jnp.einsum("cts,ctd->csd", pick, jnp.stack(got), preferred_element_type=jnp.float32).astype(jnp.bfloat16)
        picked = picked.reshape(count, here, SLOTS, width).transpose(1, 0, 2, 3).reshape(here, count * SLOTS, width)
        result = experts_plain(where, picked, w_gate, w_up, w_down)
        result = result.reshape(here, count, SLOTS, width).transpose(1, 0, 2, 3).reshape(count, here * SLOTS, width)
        total = jnp.einsum("cts,csd->ctd", combine, result, preferred_element_type=jnp.float32).astype(jnp.bfloat16)
        left, right = jnp.split(total, 2, axis=2)
        both = summed([jnp.where(side == 0, left, right), swap(jnp.where(side == 0, right, left))])
        mixture = lax.psum_scatter(both.astype(jnp.bfloat16), "ctx").astype(jnp.float32)
    return (middle.astype(jnp.float32) + mixture).astype(jnp.bfloat16)


def solution(mesh):
    in_specs = (
        P(("groups", "ctx"), "exp"),
        P(("groups", "ctx"), None),
        P(("groups", "ctx"), None),
        P("groups"),
        P("groups"),
        P(("groups", "ctx"), None),
        P(("groups", "ctx"), None),
        P(None, "exp"),
        P("exp", None),
        P(),
        P("ctx", None, "exp"),
        P("ctx", None, "exp"),
        P("ctx", "exp", None),
    )
    out_specs = P(("groups", "ctx"), "exp")
    return jax.shard_map(body, mesh=mesh, in_specs=in_specs, out_specs=out_specs, check_vma=False)
```

```python
import functools
import math

import jax
import jax.numpy as jnp
import numpy as np
from jax import lax
from jax.experimental import pallas as pl
from jax.experimental.pallas import tpu as pltpu
from jax.sharding import PartitionSpec as P

NOPE = 128
ROPE = 64
VHEAD = 128
LAT = 512
EXPERTS = 64
TOP = 6
SLOTS = 16
WIDE = 640
MIB = 1024 * 1024
VMEM_LIMIT = 50 * MIB
DEPTH = 3
PIECES = 2
SWAP = [(0, 1), (1, 0)]
PARTS = 2
FEW = 8


def cycle_of(count):
    fast = 2 ** (int(math.log2(count)) // 2)
    slow = count // fast
    cycle = [0]
    for i in range(slow):
        columns = range(1, fast)
        cycle += [i * fast + j for j in (columns if i % 2 == 0 else reversed(columns))]
    return cycle + [i * fast for i in reversed(range(1, slow))]


def swap(value):
    return lax.ppermute(value, "exp", SWAP)


def turn(value, count, cross=False):
    cycle = cycle_of(count)
    pairs = []
    for p in range(count):
        for core, ahead in ((0, 1), (1, -1)):
            pairs.append((cycle[p] * 2 + core, cycle[(p + ahead) % count] * 2 + (core ^ int(cross))))
    return lax.ppermute(value, ("ctx", "exp"), pairs)


def summed(pieces):
    total = pieces[0].astype(jnp.float32)
    for piece in pieces[1:]:
        total = total + piece.astype(jnp.float32)
    return total


def sources_of(me, side, count):
    if count > FEW:
        return jnp.arange(count, dtype=jnp.int32)
    cycle = cycle_of(count)
    middle = count // 2
    table = np.zeros((2 * count, count), np.int32)
    for p in range(count):
        for core, sign in ((0, 1), (1, -1)):
            ways = [sign * d for d in range(middle + 1)] + [-sign * d for d in range(1, middle)]
            table[cycle[p] * 2 + core] = [cycle[(p - way) % count] for way in ways]
    return lax.dynamic_index_in_dim(jnp.asarray(table), me * 2 + side, keepdims=False)


def gather(arrays, count, beside=()):
    if count > FEW:
        found = [lax.all_gather(block, "ctx") for block in arrays]
        return list(zip(*found)), [run(*arguments) for run, arguments in beside]
    middle = count // 2
    found, other, made = [tuple(arrays)], [()], []
    for d in range(1, middle + 1):
        arrived, extra = tuple(turn(x, count) for x in found[-1]), ()
        if len(beside) >= d:
            run, arguments = beside[d - 1]
            extra = run(*lax.optimization_barrier((found[-1], arguments))[1])
        arrived, other[-1], extra = lax.optimization_barrier((arrived, other[-1], extra))
        made.append(extra)
        found.append(arrived)
        if d < middle:
            other.append(tuple(swap(x) for x in arrived))
    return found + other[1:], made[: len(beside)]


def step(value, ahead, count):
    cycle = cycle_of(count)
    return lax.ppermute(value, "ctx", [(cycle[p], cycle[(p + ahead) % count]) for p in range(count)])


def reduce(parts, count):
    middle = count // 2
    first = parts[middle]().astype(jnp.bfloat16)
    half = first.shape[0] // 2
    zero = jnp.zeros((half, first.shape[1]), jnp.bfloat16)
    ahead = jnp.concatenate([step(first[:half], 1, count), zero], axis=0)
    back = jnp.concatenate([zero, step(first[half:], -1, count)], axis=0)
    for d in range(middle - 1, 0, -1):
        ahead = step((parts[count - d]() + ahead.astype(jnp.float32)).astype(jnp.bfloat16), 1, count)
        back = step((parts[d]() + back.astype(jnp.float32)).astype(jnp.bfloat16), -1, count)
    return parts[0]() + ahead.astype(jnp.float32) + back.astype(jnp.float32)


def order_of(count):
    return [(count // 2 + (d + 1) // 2 * (1 - d % 2 * 2)) % count for d in range(count)]


def attend_kernel(count, blocks, heads, info, *refs):
    latents, refs = refs[: len(refs) - 14], refs[len(refs) - 14 :]
    wanted, (out_ref, base_ref) = refs[:4], refs[4:6]
    held, sems, (m_ref, l_ref, acc_ref) = refs[6:10], refs[10], refs[11:14]
    q_ref, up_ref, proj_ref, residual_ref = held
    copies = [pltpu.make_async_copy(wanted[i], held[i], sems.at[i]) for i in range(4)]
    chunk = pl.program_id(0)
    sources = lambda c: info[2 + c]
    order = lambda j: info[2 + count + j]
    segs = info.shape[0] - 2 - 3 * count
    rows = q_ref.shape[0]
    span = rows // 2
    depth = q_ref.shape[1] // heads

    @pl.when(chunk == 0)
    def _():
        for copy in copies:
            copy.start()

    @pl.when(chunk == 0)
    def _():
        m_ref[...] = jnp.full_like(m_ref, -1e30)
        l_ref[...] = jnp.zeros_like(l_ref)
        acc_ref[...] = jnp.zeros_like(acc_ref)

    row = lax.broadcasted_iota(jnp.int32, (rows, 1), 0)
    first = order(2 * info[0]) * span
    second = order(2 * info[0] + 1) * span
    qpos = jnp.where(row < span, first + row, second + row - span)
    low = jnp.zeros((rows, 1), jnp.int32)
    start = jnp.int32(0)
    for m in range(segs):
        low = jnp.where(qpos >= start, start, low)
        start = start + info[2 + 3 * count + m]
    keys = blocks * rows
    lane = lax.broadcasted_iota(jnp.int32, (1, keys), 1)
    which = lane // span
    kpos = lane % span
    for j in range(blocks):
        source = sources(chunk * blocks + j)
        for i in range(2):
            kpos = jnp.where(which == 2 * j + i, order(2 * source + i) * span + lane % span, kpos)
    visible = (kpos >= low) & (kpos <= qpos)

    lat = jnp.concatenate([ref[...].reshape(-1, WIDE) for ref in latents], axis=0)

    @pl.when(chunk == 0)
    def _():
        copies[0].wait()
        copies[1].wait()

    keyval = jnp.dot(lat[:, :LAT], up_ref[...], preferred_element_type=jnp.float32).astype(jnp.bfloat16)
    rope = lat[:, LAT : LAT + ROPE]
    scale = 1.0 / math.sqrt(NOPE + ROPE)
    for h in range(heads):
        base = h * (NOPE + VHEAD)
        key = jnp.concatenate([keyval[:, base : base + NOPE], rope], axis=1)
        scores = lax.dot_general(q_ref[:, h * depth : (h + 1) * depth], key, (((1,), (1,)), ((), ())), preferred_element_type=jnp.float32)
        scores = jnp.where(visible, scores * scale, -1e30)
        best = m_ref[h]
        fresh = jnp.maximum(best, jnp.max(scores, axis=1, keepdims=True))
        weights = jnp.where(visible, jnp.exp(scores - fresh), 0.0)
        shrink = jnp.exp(best - fresh)
        m_ref[h] = fresh
        l_ref[h] = l_ref[h] * shrink + jnp.sum(weights, axis=1, keepdims=True)
        mixed = jnp.dot(
            weights.astype(jnp.bfloat16), keyval[:, base + NOPE : base + NOPE + VHEAD], preferred_element_type=jnp.float32
        )
        acc_ref[h] = acc_ref[h] * shrink + mixed

    @pl.when(chunk == pl.num_programs(0) - 1)
    def _():
        attended = [(acc_ref[h] / l_ref[h]).astype(jnp.bfloat16) for h in range(heads)]
        copies[2].wait()
        copies[3].wait()
        out = jnp.dot(jnp.concatenate(attended, axis=1), proj_ref[...], preferred_element_type=jnp.float32)
        out = out.astype(jnp.bfloat16)
        out_ref[...] = out
        base_ref[...] = residual_ref[...].astype(jnp.float32) + out.astype(jnp.float32)


def attend(info, found, queries, kv_up, out_proj, residual, count):
    rows, width = residual.shape
    heads = kv_up.shape[1] // (NOPE + VHEAD)
    blocks = math.gcd(count, 8)
    whole = pl.BlockSpec(memory_space=pltpu.VMEM)
    if blocks == count:
        latents, lat_spec = found, whole
    else:
        latents, lat_spec = [jnp.stack(found)], pl.BlockSpec((blocks, rows, WIDE), lambda i, *_: (i, 0, 0))
    wanted = (queries, kv_up, out_proj, residual)
    return pl.pallas_call(
        functools.partial(attend_kernel, count, blocks, heads),
        grid_spec=pltpu.PrefetchScalarGridSpec(
            num_scalar_prefetch=1,
            grid=(count // blocks,),
            in_specs=[lat_spec] * len(latents) + [pl.BlockSpec(memory_space=pltpu.HBM)] * 4,
            out_specs=[whole, whole],
            scratch_shapes=[pltpu.VMEM(x.shape, x.dtype) for x in wanted]
            + [
                pltpu.SemaphoreType.DMA((4,)),
                pltpu.VMEM((heads, rows, 1), jnp.float32),
                pltpu.VMEM((heads, rows, 1), jnp.float32),
                pltpu.VMEM((heads, rows, VHEAD), jnp.float32),
            ],
        ),
        out_shape=[pltpu.VMEM((rows, width), jnp.bfloat16), pltpu.VMEM((rows, width), jnp.float32)],
        compiler_params=pltpu.CompilerParams(vmem_limit_bytes=28 * MIB),
        name="attend",
    )(info, *latents, *(pltpu.with_memory_space_constraint(x, pltpu.HBM) for x in wanted))


def route_kernel(count, where, *refs):
    blocks, out_ref = refs[:count], refs[count]
    _, rows, width = out_ref.shape
    here = width // SLOTS
    lane = lax.broadcasted_iota(jnp.int32, (rows, width), 1)
    own = (where[0] * here + lane // SLOTS).astype(jnp.float32)
    slot = (lane % SLOTS).astype(jnp.float32)
    first = lax.broadcasted_iota(jnp.int32, (rows, rows), 0)
    before = (first > lax.broadcasted_iota(jnp.int32, (rows, rows), 1)).astype(jnp.float32).astype(jnp.bfloat16)
    for c in range(count):
        facts = blocks[c][:, LAT:].astype(jnp.float32)
        hot, share = jnp.zeros((rows, width), jnp.float32), jnp.zeros((rows, width), jnp.float32)
        for k in range(TOP):
            hit = facts[:, ROPE + k : ROPE + k + 1] == own
            hot = jnp.where(hit, 1.0, hot)
            share = jnp.where(hit, facts[:, ROPE + TOP + k : ROPE + TOP + k + 1], share)
        rank = jnp.dot(before, hot.astype(jnp.bfloat16), preferred_element_type=jnp.float32)
        out_ref[c] = jnp.where(rank == slot, share, 0.0).astype(jnp.bfloat16)


def route(where, found, here):
    count, (rows, _) = len(found), found[0].shape
    whole = pl.BlockSpec(memory_space=pltpu.VMEM)
    return pl.pallas_call(
        functools.partial(route_kernel, count),
        in_specs=[pl.BlockSpec(memory_space=pltpu.SMEM)] + [whole] * count,
        out_specs=whole,
        out_shape=pltpu.VMEM((count, rows, here * SLOTS), jnp.bfloat16),
        compiler_params=pltpu.CompilerParams(vmem_limit_bytes=8 * MIB),
        name="route",
    )(where, *found)


def norm_kernel(where, base_ref, there_ref, gain_ref, middle_ref, *normed_refs):
    half = middle_ref.shape[1]
    middle = (base_ref[...] + there_ref[...].astype(jnp.float32)).astype(jnp.bfloat16)
    wide = middle.astype(jnp.float32)
    inverse = lax.rsqrt(jnp.mean(wide * wide, axis=1, keepdims=True) + 1e-06)
    normed = (wide * inverse * gain_ref[...].astype(jnp.float32)).astype(jnp.bfloat16)
    part = normed_refs[0].shape[1]
    for h, ref in enumerate(normed_refs):
        ref[...] = normed[:, h * part : (h + 1) * part]
    middle_ref[...] = jnp.where(where[1] == 0, wide[:, :half], wide[:, half:]).astype(jnp.bfloat16)


def norm(where, base, there, gain):
    rows, width = base.shape
    whole = pl.BlockSpec(memory_space=pltpu.VMEM)
    shapes = [(rows, width // 2)] + [(rows, width // PARTS)] * PARTS
    return pl.pallas_call(
        norm_kernel,
        in_specs=[pl.BlockSpec(memory_space=pltpu.SMEM)] + [whole] * 3,
        out_specs=[whole] * len(shapes),
        out_shape=[pltpu.VMEM(shape, jnp.bfloat16) for shape in shapes],
        compiler_params=pltpu.CompilerParams(vmem_limit_bytes=12 * MIB),
        name="norm",
    )(where, base, there, gain)


def pack_kernel(*refs):
    copies = [pltpu.make_async_copy(refs[i], refs[4 + i], refs[8].at[i]) for i in range(3)]
    for copy in copies:
        copy.start()
    for copy in copies:
        copy.wait()
    out_ref, (latent_ref, ids_ref, weights_ref, rows) = refs[3], refs[4:8]
    tokens = out_ref.shape[0]
    rows[...] = jnp.zeros_like(rows)
    rows[0:TOP] = ids_ref[...].astype(jnp.float32)
    rows[TOP : 2 * TOP] = weights_ref[...]
    row = lax.broadcasted_iota(jnp.int32, (tokens, tokens), 0)
    same = (row == lax.broadcasted_iota(jnp.int32, (tokens, tokens), 1)).astype(jnp.float32).astype(jnp.bfloat16)
    every = jnp.concatenate([latent_ref[...], rows[...].astype(jnp.bfloat16)], axis=0)
    turned = lax.dot_general(same, every, (((1,), (1,)), ((), ())), preferred_element_type=jnp.float32)
    out_ref[...] = turned.astype(jnp.bfloat16)


def pack(latent, expert_ids, route_weights):
    local_rows, base = latent.shape
    arrays = (latent.T, expert_ids.T, route_weights.T)
    return pl.pallas_call(
        pack_kernel,
        in_specs=[pl.BlockSpec(memory_space=pltpu.HBM)] * 3,
        out_specs=pl.BlockSpec(memory_space=pltpu.VMEM),
        scratch_shapes=[pltpu.VMEM(x.shape, x.dtype) for x in arrays]
        + [pltpu.VMEM((WIDE - base, local_rows), jnp.float32), pltpu.SemaphoreType.DMA((3,))],
        out_shape=pltpu.VMEM((local_rows, WIDE), jnp.bfloat16),
        compiler_params=pltpu.CompilerParams(vmem_limit_bytes=4 * MIB),
        name="pack",
    )(*(pltpu.with_memory_space_constraint(x, pltpu.HBM) for x in arrays))


def expert_rows(rows, gate_ref, up_ref, down_ref):
    by_columns = (((1,), (1,)), ((), ()))
    gate = lax.dot_general(gate_ref[...], rows, by_columns, preferred_element_type=jnp.float32)
    upper = lax.dot_general(up_ref[...], rows, by_columns, preferred_element_type=jnp.float32)
    hidden = (gate / (1.0 + jnp.exp(-gate)) * upper).astype(jnp.bfloat16)
    by_rows = (((0,), (0,)), ((), ()))
    return lax.dot_general(hidden, down_ref[...], by_rows, preferred_element_type=jnp.float32).astype(jnp.bfloat16)


def plain_kernel(where, rows_ref, gate_ref, up_ref, down_ref, out_ref):
    out_ref[0] = expert_rows(rows_ref[0], gate_ref.at[0], up_ref.at[0], down_ref.at[0])


def fused_kernel(count, where, *refs):
    at = PARTS * count
    blocks, combine_ref, weights = refs[:at], refs[at], refs[at + 1 : at + 4]
    kept, away = refs[at + 4 : at + 4 + count], refs[at + 4 + count : at + 4 + 2 * count]
    at += 4 + 2 * count
    picked, buffers, sems = refs[at], refs[at + 1 : at + 4], refs[at + 4]
    here = picked.shape[0]
    depth, units, width = buffers[0].shape
    side = where[1]
    piece = units // PIECES
    middle = count // 2
    by_rows = (((0,), (0,)), ((), ()))

    def copies(expert, slot):
        for w in range(3):
            for i in range(PIECES):
                rows = pl.ds(i * piece, piece)
                yield pltpu.make_async_copy(weights[w].at[expert, rows], buffers[w].at[slot, rows], sems.at[slot, w, i])

    for e in range(depth):
        for copy in copies(e, e):
            copy.start()

    for c in range(count):
        pick = (combine_ref[c].astype(jnp.float32) > 0).astype(jnp.float32).astype(jnp.bfloat16)
        for h in range(PARTS):
            block = blocks[PARTS * c + h][...]
            rows = lax.dot_general(pick, block, by_rows, preferred_element_type=jnp.float32).astype(jnp.bfloat16)
            columns = pl.ds(h * block.shape[1], block.shape[1])
            for e in range(here):
                picked[e, c * SLOTS : (c + 1) * SLOTS, columns] = rows[e * SLOTS : (e + 1) * SLOTS]

    def work(expert, _):
        slot = lax.rem(expert, depth)
        for copy in copies(expert, slot):
            copy.wait()
        picked[expert] = expert_rows(picked[expert], *(buffer.at[slot] for buffer in buffers))

        @pl.when(expert + depth < here)
        def _():
            for copy in copies(expert + depth, slot):
                copy.start()

        return 0

    lax.fori_loop(0, here, work, 0)

    half = width // 2
    for d in order_of(count):
        forward = d if d <= middle else middle + count - d
        backward = forward if d in (0, middle) else (count - d if d > middle else middle + d)
        c = forward if forward == backward else jnp.where(side == 0, forward, backward)
        place = pl.ds(c * SLOTS if forward == backward else pl.multiple_of(c * SLOTS, SLOTS), SLOTS)
        for turned, out in ((1 - side, away[d]), (side, kept[d])):
            columns = pl.ds(pl.multiple_of(turned * half, half), half)
            rows = jnp.concatenate([picked[e, place, columns] for e in range(here)], axis=0)
            out[...] = jnp.dot(combine_ref[c], rows, preferred_element_type=jnp.float32).astype(jnp.bfloat16)


def expert_specs(w_gate):
    hidden, width = w_gate.shape[1:]
    return [pl.BlockSpec((1, hidden, width), lambda e, where: (e, 0, 0))] * 3


def experts_plain(where, picked, w_gate, w_up, w_down):
    here, rows, width = picked.shape
    rows_spec = pl.BlockSpec((1, rows, width), lambda e, where: (e, 0, 0))
    return pl.pallas_call(
        plain_kernel,
        grid_spec=pltpu.PrefetchScalarGridSpec(
            num_scalar_prefetch=1,
            grid=(here,),
            in_specs=[rows_spec] + expert_specs(w_gate),
            out_specs=rows_spec,
        ),
        out_shape=jax.ShapeDtypeStruct(picked.shape, jnp.bfloat16),
        compiler_params=pltpu.CompilerParams(vmem_limit_bytes=VMEM_LIMIT),
        name="experts",
    )(where, picked, w_gate, w_up, w_down)


def experts_fused(where, found, combine, w_gate, w_up, w_down):
    count, local = len(found), found[0][0].shape[0]
    here, units, width = w_gate.shape
    rows = count * SLOTS
    depth = min(DEPTH, here)
    whole = pl.BlockSpec(memory_space=pltpu.VMEM)
    outs = pl.pallas_call(
        functools.partial(fused_kernel, count),
        in_specs=[pl.BlockSpec(memory_space=pltpu.SMEM)]
        + [whole] * (PARTS * count + 1)
        + [pl.BlockSpec(memory_space=pltpu.HBM)] * 3,
        out_specs=[whole] * (2 * count),
        scratch_shapes=[pltpu.VMEM((here, rows, width), jnp.bfloat16)]
        + [pltpu.VMEM((depth, units, width), jnp.bfloat16)] * 3
        + [pltpu.SemaphoreType.DMA((depth, 3, PIECES))],
        out_shape=[pltpu.VMEM((local, width // 2), jnp.bfloat16)] * (2 * count),
        compiler_params=pltpu.CompilerParams(vmem_limit_bytes=36 * MIB),
        name="experts",
    )(where, *(x for block in found for x in block), combine,
      *(pltpu.with_memory_space_constraint(w, pltpu.HBM) for w in (w_gate, w_up, w_down)))
    return outs[:count], outs[count:]


def body(
    queries,
    latent,
    residual,
    seg_lengths,
    span_order,
    expert_ids,
    route_weights,
    kv_up,
    out_proj,
    norm_gain,
    w_gate,
    w_up,
    w_down,
):
    local_rows, width = residual.shape
    span = local_rows // 2
    count = lax.axis_size("ctx")
    here = EXPERTS // count
    me, side = lax.axis_index("ctx"), lax.axis_index("exp")
    where = jnp.stack([me, side]).astype(jnp.int32)

    base = latent.shape[1]
    w_gate, w_up = w_gate.transpose(0, 2, 1), w_up.transpose(0, 2, 1)
    packed = pack(latent, expert_ids, route_weights)
    few = count <= FEW
    scalars = lambda *arrays: jnp.concatenate([where, sources_of(me, side, count), *arrays])
    beside = [(scalars, (span_order, seg_lengths)), (lambda gain: gain.reshape(1, width), (norm_gain,))]
    found, (info, gain) = gather([packed], count, beside)
    found = [block for block, in found]
    partial, summand = attend(info, found, queries, kv_up, out_proj, residual, count)
    middle, *normed = norm(where, summand, swap(partial), gain)

    def place_rows(*blocks):
        if few:
            return route(where, blocks, here)
        facts = jnp.stack(blocks)[:, :, base : base + 2 * TOP].astype(jnp.float32)
        own = (me * here + jnp.arange(here, dtype=jnp.int32)).astype(jnp.float32)
        hit = facts[:, :, :TOP, None] == own
        hot = jnp.any(hit, axis=2)
        share = jnp.sum(jnp.where(hit, facts[:, :, TOP:, None], 0.0), axis=2)
        token = jnp.arange(local_rows, dtype=jnp.int32)
        before = (token[:, None] > token[None, :]).astype(jnp.bfloat16)
        rank = jnp.einsum("tu,cue->cte", before, hot.astype(jnp.bfloat16), preferred_element_type=jnp.float32)
        slot = jnp.arange(SLOTS, dtype=jnp.int32).astype(jnp.float32)
        combine = jnp.where(rank[:, :, :, None] == slot, share[:, :, :, None], 0.0)
        return combine.astype(jnp.bfloat16).reshape(count, local_rows, here * SLOTS)

    got, (combine,) = gather(normed, count, [(place_rows, tuple(found))])
    if few:
        kept, away = experts_fused(where, got, combine, w_gate, w_up, w_down)
        swapped = {d: swap(away[d]) for d in order_of(count)}
        parts = [functools.partial(summed, [kept[d], swapped[d]]) for d in range(count)]
        mixture = reduce(parts, count)
    else:
        pick = (combine > 0).astype(jnp.bfloat16)
        rows = jnp.stack([jnp.concatenate(block, axis=1) for block in got])
        picked = jnp.einsum("cts,ctd->csd", pick, rows, preferred_element_type=jnp.float32).astype(jnp.bfloat16)
        picked = picked.reshape(count, here, SLOTS, width).transpose(1, 0, 2, 3).reshape(here, count * SLOTS, width)
        result = experts_plain(where, picked, w_gate, w_up, w_down)
        result = result.reshape(here, count, SLOTS, width).transpose(1, 0, 2, 3).reshape(count, here * SLOTS, width)
        total = jnp.einsum("cts,csd->ctd", combine, result, preferred_element_type=jnp.float32).astype(jnp.bfloat16)
        left, right = jnp.split(total, 2, axis=2)
        both = summed([jnp.where(side == 0, left, right), swap(jnp.where(side == 0, right, left))])
        mixture = lax.psum_scatter(both.astype(jnp.bfloat16), "ctx").astype(jnp.float32)
    return (middle.astype(jnp.float32) + mixture).astype(jnp.bfloat16)


def solution(mesh):
    in_specs = (
        P(("groups", "ctx"), "exp"),
        P(("groups", "ctx"), None),
        P(("groups", "ctx"), None),
        P("groups"),
        P("groups"),
        P(("groups", "ctx"), None),
        P(("groups", "ctx"), None),
        P(None, "exp"),
        P("exp", None),
        P(),
        P("ctx", None, "exp"),
        P("ctx", None, "exp"),
        P("ctx", "exp", None),
    )
    out_specs = P(("groups", "ctx"), "exp")
    return jax.shard_map(body, mesh=mesh, in_specs=in_specs, out_specs=out_specs, check_vma=False)
```

```python
import functools
import math

import jax
import jax.numpy as jnp
import numpy as np
from jax import lax
from jax.experimental import pallas as pl
from jax.experimental.pallas import tpu as pltpu
from jax.sharding import PartitionSpec as P

NOPE = 128
ROPE = 64
VHEAD = 128
LAT = 512
EXPERTS = 64
TOP = 6
SLOTS = 16
WIDE = 640
MIB = 1024 * 1024
VMEM_LIMIT = 50 * MIB
DEPTH = 3
PIECES = 2
SWAP = [(0, 1), (1, 0)]
PARTS = 2
FEW = 8


def cycle_of(count):
    fast = 2 ** (int(math.log2(count)) // 2)
    slow = count // fast
    cycle = [0]
    for i in range(slow):
        columns = range(1, fast)
        cycle += [i * fast + j for j in (columns if i % 2 == 0 else reversed(columns))]
    return cycle + [i * fast for i in reversed(range(1, slow))]


def swap(value):
    return lax.ppermute(value, "exp", SWAP)


def turn(value, count, cross=False):
    cycle = cycle_of(count)
    pairs = []
    for p in range(count):
        for core, ahead in ((0, 1), (1, -1)):
            pairs.append((cycle[p] * 2 + core, cycle[(p + ahead) % count] * 2 + (core ^ int(cross))))
    return lax.ppermute(value, ("ctx", "exp"), pairs)


def summed(pieces):
    total = pieces[0].astype(jnp.float32)
    for piece in pieces[1:]:
        total = total + piece.astype(jnp.float32)
    return total


def sources_of(me, side, count):
    if count > FEW:
        return jnp.arange(count, dtype=jnp.int32)
    cycle = cycle_of(count)
    middle = count // 2
    table = np.zeros((2 * count, count), np.int32)
    for p in range(count):
        for core, sign in ((0, 1), (1, -1)):
            ways = [sign * d for d in range(middle + 1)] + [-sign * d for d in range(1, middle)]
            table[cycle[p] * 2 + core] = [cycle[(p - way) % count] for way in ways]
    return lax.dynamic_index_in_dim(jnp.asarray(table), me * 2 + side, keepdims=False)


def gather(block, count, beside=()):
    if count > FEW:
        return list(lax.all_gather(block, "ctx")), [run(*arguments) for run, arguments in beside]
    middle = count // 2
    found, other, made = [block], [()], []
    for d in range(1, middle + 1):
        arrived, extra = turn(found[-1], count), ()
        if len(beside) >= d:
            run, arguments = beside[d - 1]
            extra = run(*lax.optimization_barrier((found[-1], arguments))[1])
        arrived, other[-1], extra = lax.optimization_barrier((arrived, other[-1], extra))
        made.append(extra)
        found.append(arrived)
        if d < middle:
            other.append(swap(arrived))
    return found + other[1:], made[: len(beside)]


def reduce(parts, side, count):
    middle = count // 2
    near, far = 0, 1
    sums = [None, None]
    given = {}
    for d in range(middle, 0, -1):
        for stream in (near, far):
            mine = parts[1 - stream][d]
            given[stream, d] = swap(mine[1] if d == middle else mine)
    for stream in (near, far):
        first = summed([parts[stream][middle][0], given[stream, middle]]).astype(jnp.bfloat16)
        first = turn(first, count).astype(jnp.float32)
        nothing = jnp.zeros_like(first)
        running = jnp.concatenate([jnp.where(side == 0, first, nothing), jnp.where(side == 0, nothing, first)], axis=0)
        for d in range(middle - 1, 0, -1):
            total = (summed([parts[stream][middle + d], given[stream, d]]) + running).astype(jnp.bfloat16)
            running = turn(total, count, cross=d == 1 and stream == far).astype(jnp.float32)
        sums[stream] = running
    return summed([parts[near][0], swap(parts[far][0])]) + sums[near] + sums[far]


def attend_kernel(count, blocks, heads, info, *refs):
    latents, refs = refs[: len(refs) - 14], refs[len(refs) - 14 :]
    wanted, (out_ref, base_ref) = refs[:4], refs[4:6]
    held, sems, (m_ref, l_ref, acc_ref) = refs[6:10], refs[10], refs[11:14]
    q_ref, up_ref, proj_ref, residual_ref = held
    copies = [pltpu.make_async_copy(wanted[i], held[i], sems.at[i]) for i in range(4)]
    chunk = pl.program_id(0)
    sources = lambda c: info[2 + c]
    order = lambda j: info[2 + count + j]
    segs = info.shape[0] - 2 - 3 * count
    rows = q_ref.shape[0]
    span = rows // 2
    depth = q_ref.shape[1] // heads

    @pl.when(chunk == 0)
    def _():
        for copy in copies:
            copy.start()

    @pl.when(chunk == 0)
    def _():
        m_ref[...] = jnp.full_like(m_ref, -1e30)
        l_ref[...] = jnp.zeros_like(l_ref)
        acc_ref[...] = jnp.zeros_like(acc_ref)

    row = lax.broadcasted_iota(jnp.int32, (rows, 1), 0)
    first = order(2 * info[0]) * span
    second = order(2 * info[0] + 1) * span
    qpos = jnp.where(row < span, first + row, second + row - span)
    low = jnp.zeros((rows, 1), jnp.int32)
    start = jnp.int32(0)
    for m in range(segs):
        low = jnp.where(qpos >= start, start, low)
        start = start + info[2 + 3 * count + m]
    keys = blocks * rows
    lane = lax.broadcasted_iota(jnp.int32, (1, keys), 1)
    which = lane // span
    kpos = lane % span
    for j in range(blocks):
        source = sources(chunk * blocks + j)
        for i in range(2):
            kpos = jnp.where(which == 2 * j + i, order(2 * source + i) * span + lane % span, kpos)
    visible = (kpos >= low) & (kpos <= qpos)

    lat = jnp.concatenate([ref[...].reshape(-1, WIDE) for ref in latents], axis=0)

    @pl.when(chunk == 0)
    def _():
        copies[0].wait()
        copies[1].wait()

    keyval = jnp.dot(lat[:, :LAT], up_ref[...], preferred_element_type=jnp.float32).astype(jnp.bfloat16)
    rope = lat[:, LAT : LAT + ROPE]
    scale = 1.0 / math.sqrt(NOPE + ROPE)
    for h in range(heads):
        base = h * (NOPE + VHEAD)
        key = jnp.concatenate([keyval[:, base : base + NOPE], rope], axis=1)
        scores = lax.dot_general(q_ref[:, h * depth : (h + 1) * depth], key, (((1,), (1,)), ((), ())), preferred_element_type=jnp.float32)
        scores = jnp.where(visible, scores * scale, -1e30)
        best = m_ref[h]
        fresh = jnp.maximum(best, jnp.max(scores, axis=1, keepdims=True))
        weights = jnp.where(visible, jnp.exp(scores - fresh), 0.0)
        shrink = jnp.exp(best - fresh)
        m_ref[h] = fresh
        l_ref[h] = l_ref[h] * shrink + jnp.sum(weights, axis=1, keepdims=True)
        mixed = jnp.dot(
            weights.astype(jnp.bfloat16), keyval[:, base + NOPE : base + NOPE + VHEAD], preferred_element_type=jnp.float32
        )
        acc_ref[h] = acc_ref[h] * shrink + mixed

    @pl.when(chunk == pl.num_programs(0) - 1)
    def _():
        attended = [(acc_ref[h] / l_ref[h]).astype(jnp.bfloat16) for h in range(heads)]
        copies[2].wait()
        copies[3].wait()
        out = jnp.dot(jnp.concatenate(attended, axis=1), proj_ref[...], preferred_element_type=jnp.float32)
        out = out.astype(jnp.bfloat16)
        out_ref[...] = out
        base_ref[...] = residual_ref[...].astype(jnp.float32) + out.astype(jnp.float32)


def attend(info, found, queries, kv_up, out_proj, residual, count):
    rows, width = residual.shape
    heads = kv_up.shape[1] // (NOPE + VHEAD)
    blocks = math.gcd(count, 8)
    whole = pl.BlockSpec(memory_space=pltpu.VMEM)
    if blocks == count:
        latents, lat_spec = found, whole
    else:
        latents, lat_spec = [jnp.stack(found)], pl.BlockSpec((blocks, rows, WIDE), lambda i, *_: (i, 0, 0))
    wanted = (queries, kv_up, out_proj, residual)
    return pl.pallas_call(
        functools.partial(attend_kernel, count, blocks, heads),
        grid_spec=pltpu.PrefetchScalarGridSpec(
            num_scalar_prefetch=1,
            grid=(count // blocks,),
            in_specs=[lat_spec] * len(latents) + [pl.BlockSpec(memory_space=pltpu.HBM)] * 4,
            out_specs=[whole, whole],
            scratch_shapes=[pltpu.VMEM(x.shape, x.dtype) for x in wanted]
            + [
                pltpu.SemaphoreType.DMA((4,)),
                pltpu.VMEM((heads, rows, 1), jnp.float32),
                pltpu.VMEM((heads, rows, 1), jnp.float32),
                pltpu.VMEM((heads, rows, VHEAD), jnp.float32),
            ],
        ),
        out_shape=[pltpu.VMEM((rows, width), jnp.bfloat16), pltpu.VMEM((rows, width), jnp.float32)],
        compiler_params=pltpu.CompilerParams(vmem_limit_bytes=28 * MIB),
        name="attend",
    )(info, *latents, *(pltpu.with_memory_space_constraint(x, pltpu.HBM) for x in wanted))


def route_kernel(count, where, *refs):
    blocks, out_ref = refs[:count], refs[count]
    _, rows, width = out_ref.shape
    here = width // SLOTS
    lane = lax.broadcasted_iota(jnp.int32, (rows, width), 1)
    own = (where[0] * here + lane // SLOTS).astype(jnp.float32)
    slot = (lane % SLOTS).astype(jnp.float32)
    first = lax.broadcasted_iota(jnp.int32, (rows, rows), 0)
    before = (first > lax.broadcasted_iota(jnp.int32, (rows, rows), 1)).astype(jnp.float32).astype(jnp.bfloat16)
    for c in range(count):
        facts = blocks[c][:, LAT:].astype(jnp.float32)
        hot, share = jnp.zeros((rows, width), jnp.float32), jnp.zeros((rows, width), jnp.float32)
        for k in range(TOP):
            hit = facts[:, ROPE + k : ROPE + k + 1] == own
            hot = jnp.where(hit, 1.0, hot)
            share = jnp.where(hit, facts[:, ROPE + TOP + k : ROPE + TOP + k + 1], share)
        rank = jnp.dot(before, hot.astype(jnp.bfloat16), preferred_element_type=jnp.float32)
        out_ref[c] = jnp.where(rank == slot, share, 0.0).astype(jnp.bfloat16)


def route(where, found, here):
    count, (rows, _) = len(found), found[0].shape
    whole = pl.BlockSpec(memory_space=pltpu.VMEM)
    return pl.pallas_call(
        functools.partial(route_kernel, count),
        in_specs=[pl.BlockSpec(memory_space=pltpu.SMEM)] + [whole] * count,
        out_specs=whole,
        out_shape=pltpu.VMEM((count, rows, here * SLOTS), jnp.bfloat16),
        compiler_params=pltpu.CompilerParams(vmem_limit_bytes=8 * MIB),
        name="route",
    )(where, *found)


def norm_kernel(where, base_ref, there_ref, gain_ref, middle_ref, *normed_refs):
    half = middle_ref.shape[1]
    middle = (base_ref[...] + there_ref[...].astype(jnp.float32)).astype(jnp.bfloat16)
    wide = middle.astype(jnp.float32)
    inverse = lax.rsqrt(jnp.mean(wide * wide, axis=1, keepdims=True) + 1e-06)
    normed = (wide * inverse * gain_ref[...].astype(jnp.float32)).astype(jnp.bfloat16)
    part = normed_refs[0].shape[1]
    for h, ref in enumerate(normed_refs):
        ref[...] = normed[:, h * part : (h + 1) * part]
    middle_ref[...] = jnp.where(where[1] == 0, wide[:, :half], wide[:, half:]).astype(jnp.bfloat16)


def norm(where, base, there, gain):
    rows, width = base.shape
    whole = pl.BlockSpec(memory_space=pltpu.VMEM)
    shapes = [(rows, width // 2)] + [(rows, width // PARTS)] * PARTS
    return pl.pallas_call(
        norm_kernel,
        in_specs=[pl.BlockSpec(memory_space=pltpu.SMEM)] + [whole] * 3,
        out_specs=[whole] * len(shapes),
        out_shape=[pltpu.VMEM(shape, jnp.bfloat16) for shape in shapes],
        compiler_params=pltpu.CompilerParams(vmem_limit_bytes=12 * MIB),
        name="norm",
    )(where, base, there, gain)


def pack_kernel(*refs):
    copies = [pltpu.make_async_copy(refs[i], refs[4 + i], refs[8].at[i]) for i in range(3)]
    for copy in copies:
        copy.start()
    for copy in copies:
        copy.wait()
    out_ref, (latent_ref, ids_ref, weights_ref, rows) = refs[3], refs[4:8]
    tokens = out_ref.shape[0]
    rows[...] = jnp.zeros_like(rows)
    rows[0:TOP] = ids_ref[...].astype(jnp.float32)
    rows[TOP : 2 * TOP] = weights_ref[...]
    row = lax.broadcasted_iota(jnp.int32, (tokens, tokens), 0)
    same = (row == lax.broadcasted_iota(jnp.int32, (tokens, tokens), 1)).astype(jnp.float32).astype(jnp.bfloat16)
    every = jnp.concatenate([latent_ref[...], rows[...].astype(jnp.bfloat16)], axis=0)
    turned = lax.dot_general(same, every, (((1,), (1,)), ((), ())), preferred_element_type=jnp.float32)
    out_ref[...] = turned.astype(jnp.bfloat16)


def pack(latent, expert_ids, route_weights):
    local_rows, base = latent.shape
    arrays = (latent.T, expert_ids.T, route_weights.T)
    return pl.pallas_call(
        pack_kernel,
        in_specs=[pl.BlockSpec(memory_space=pltpu.HBM)] * 3,
        out_specs=pl.BlockSpec(memory_space=pltpu.VMEM),
        scratch_shapes=[pltpu.VMEM(x.shape, x.dtype) for x in arrays]
        + [pltpu.VMEM((WIDE - base, local_rows), jnp.float32), pltpu.SemaphoreType.DMA((3,))],
        out_shape=pltpu.VMEM((local_rows, WIDE), jnp.bfloat16),
        compiler_params=pltpu.CompilerParams(vmem_limit_bytes=4 * MIB),
        name="pack",
    )(*(pltpu.with_memory_space_constraint(x, pltpu.HBM) for x in arrays))


def expert_rows(rows, gate_ref, up_ref, down_ref):
    by_columns = (((1,), (1,)), ((), ()))
    gate = lax.dot_general(gate_ref[...], rows, by_columns, preferred_element_type=jnp.float32)
    upper = lax.dot_general(up_ref[...], rows, by_columns, preferred_element_type=jnp.float32)
    hidden = (gate / (1.0 + jnp.exp(-gate)) * upper).astype(jnp.bfloat16)
    by_rows = (((0,), (0,)), ((), ()))
    return lax.dot_general(hidden, down_ref[...], by_rows, preferred_element_type=jnp.float32).astype(jnp.bfloat16)


def plain_kernel(where, rows_ref, gate_ref, up_ref, down_ref, out_ref):
    out_ref[0] = expert_rows(rows_ref[0], gate_ref.at[0], up_ref.at[0], down_ref.at[0])


def fused_kernel(count, where, *refs):
    at = PARTS * count
    blocks, combine_ref, weights = refs[:at], refs[at], refs[at + 1 : at + 4]
    near, far = refs[at + 4 : at + 5 + count], refs[at + 5 + count : at + 6 + 2 * count]
    at += 6 + 2 * count
    picked, buffers, sems = refs[at], refs[at + 1 : at + 4], refs[at + 4]
    here = picked.shape[0]
    depth, units, width = buffers[0].shape
    side = where[1]
    piece = units // PIECES
    middle = count // 2
    by_rows = (((0,), (0,)), ((), ()))

    def copies(expert, slot):
        for w in range(3):
            for i in range(PIECES):
                rows = pl.ds(i * piece, piece)
                yield pltpu.make_async_copy(weights[w].at[expert, rows], buffers[w].at[slot, rows], sems.at[slot, w, i])

    for e in range(depth):
        for copy in copies(e, e):
            copy.start()

    for c in range(count):
        pick = (combine_ref[c].astype(jnp.float32) > 0).astype(jnp.float32).astype(jnp.bfloat16)
        for h in range(PARTS):
            block = blocks[PARTS * c + h][...]
            rows = lax.dot_general(pick, block, by_rows, preferred_element_type=jnp.float32).astype(jnp.bfloat16)
            columns = pl.ds(h * block.shape[1], block.shape[1])
            for e in range(here):
                picked[e, c * SLOTS : (c + 1) * SLOTS, columns] = rows[e * SLOTS : (e + 1) * SLOTS]

    def work(expert, _):
        slot = lax.rem(expert, depth)
        for copy in copies(expert, slot):
            copy.wait()
        picked[expert] = expert_rows(picked[expert], *(buffer.at[slot] for buffer in buffers))

        @pl.when(expert + depth < here)
        def _():
            for copy in copies(expert + depth, slot):
                copy.start()

        return 0

    lax.fori_loop(0, here, work, 0)

    half = width // 2
    for c in [middle] + list(range(middle)) + list(range(middle + 1, count)):
        for turned, outs in ((1 - side, far), (side, near)):
            columns = pl.ds(pl.multiple_of(turned * half, half), half)
            rows = jnp.concatenate([picked[e, c * SLOTS : (c + 1) * SLOTS, columns] for e in range(here)], axis=0)
            total = jnp.dot(combine_ref[c], rows, preferred_element_type=jnp.float32).astype(jnp.bfloat16)
            if c == middle:
                upper, lower = total[: total.shape[0] // 2], total[total.shape[0] // 2 :]
                outs[c][...] = jnp.where(side == 0, upper, lower)
                outs[count][...] = jnp.where(side == 0, lower, upper)
            else:
                outs[c][...] = total


def expert_specs(w_gate):
    hidden, width = w_gate.shape[1:]
    return [pl.BlockSpec((1, hidden, width), lambda e, where: (e, 0, 0))] * 3


def experts_plain(where, picked, w_gate, w_up, w_down):
    here, rows, width = picked.shape
    rows_spec = pl.BlockSpec((1, rows, width), lambda e, where: (e, 0, 0))
    return pl.pallas_call(
        plain_kernel,
        grid_spec=pltpu.PrefetchScalarGridSpec(
            num_scalar_prefetch=1,
            grid=(here,),
            in_specs=[rows_spec] + expert_specs(w_gate),
            out_specs=rows_spec,
        ),
        out_shape=jax.ShapeDtypeStruct(picked.shape, jnp.bfloat16),
        compiler_params=pltpu.CompilerParams(vmem_limit_bytes=VMEM_LIMIT),
        name="experts",
    )(where, picked, w_gate, w_up, w_down)


def experts_fused(where, found, combine, w_gate, w_up, w_down):
    count, local = len(found), found[0][0].shape[0]
    here, units, width = w_gate.shape
    rows = count * SLOTS
    depth = min(DEPTH, here)
    middle = count // 2
    sizes = [local // 2 if c in (middle, count) else local for c in range(count + 1)]
    whole = pl.BlockSpec(memory_space=pltpu.VMEM)
    outs = pl.pallas_call(
        functools.partial(fused_kernel, count),
        in_specs=[pl.BlockSpec(memory_space=pltpu.SMEM)]
        + [whole] * (PARTS * count + 1)
        + [pl.BlockSpec(memory_space=pltpu.HBM)] * 3,
        out_specs=[whole] * (2 * count + 2),
        scratch_shapes=[pltpu.VMEM((here, rows, width), jnp.bfloat16)]
        + [pltpu.VMEM((depth, units, width), jnp.bfloat16)] * 3
        + [pltpu.SemaphoreType.DMA((depth, 3, PIECES))],
        out_shape=[pltpu.VMEM((size, width // 2), jnp.bfloat16) for size in sizes] * 2,
        compiler_params=pltpu.CompilerParams(vmem_limit_bytes=36 * MIB),
        name="experts",
    )(where, *(x for block in found for x in block), combine,
      *(pltpu.with_memory_space_constraint(w, pltpu.HBM) for w in (w_gate, w_up, w_down)))
    parts = [list(outs[: count + 1]), list(outs[count + 1 :])]
    return [x[:middle] + [(x[middle], x[count])] + x[middle + 1 : count] for x in parts]


def body(
    queries,
    latent,
    residual,
    seg_lengths,
    span_order,
    expert_ids,
    route_weights,
    kv_up,
    out_proj,
    norm_gain,
    w_gate,
    w_up,
    w_down,
):
    local_rows, width = residual.shape
    span = local_rows // 2
    count = lax.axis_size("ctx")
    here = EXPERTS // count
    me, side = lax.axis_index("ctx"), lax.axis_index("exp")
    where = jnp.stack([me, side]).astype(jnp.int32)

    base = latent.shape[1]
    w_gate, w_up = w_gate.transpose(0, 2, 1), w_up.transpose(0, 2, 1)
    packed = pack(latent, expert_ids, route_weights)
    few = count <= FEW
    scalars = lambda *arrays: jnp.concatenate([where, sources_of(me, side, count), *arrays])
    beside = [(scalars, (span_order, seg_lengths)), (lambda gain: gain.reshape(1, width), (norm_gain,))]
    found, (info, gain) = gather(packed, count, beside)
    partial, summand = attend(info, found, queries, kv_up, out_proj, residual, count)
    middle, *normed = norm(where, summand, swap(partial), gain)

    def place_rows(*blocks):
        if few:
            return route(where, blocks, here)
        facts = jnp.stack(blocks)[:, :, base : base + 2 * TOP].astype(jnp.float32)
        own = (me * here + jnp.arange(here, dtype=jnp.int32)).astype(jnp.float32)
        hit = facts[:, :, :TOP, None] == own
        hot = jnp.any(hit, axis=2)
        share = jnp.sum(jnp.where(hit, facts[:, :, TOP:, None], 0.0), axis=2)
        token = jnp.arange(local_rows, dtype=jnp.int32)
        before = (token[:, None] > token[None, :]).astype(jnp.bfloat16)
        rank = jnp.einsum("tu,cue->cte", before, hot.astype(jnp.bfloat16), preferred_element_type=jnp.float32)
        slot = jnp.arange(SLOTS, dtype=jnp.int32).astype(jnp.float32)
        combine = jnp.where(rank[:, :, :, None] == slot, share[:, :, :, None], 0.0)
        return combine.astype(jnp.bfloat16).reshape(count, local_rows, here * SLOTS)

    streams = [gather(x, count, [(place_rows, tuple(found))] if h == 0 else ()) for h, x in enumerate(normed)]
    combine = streams[0][1][0]
    got = list(zip(*(blocks for blocks, _ in streams)))
    if few:
        mixture = reduce(experts_fused(where, got, combine, w_gate, w_up, w_down), side, count)
    else:
        pick = (combine > 0).astype(jnp.bfloat16)
        rows = jnp.stack([jnp.concatenate(block, axis=1) for block in got])
        picked = jnp.einsum("cts,ctd->csd", pick, rows, preferred_element_type=jnp.float32).astype(jnp.bfloat16)
        picked = picked.reshape(count, here, SLOTS, width).transpose(1, 0, 2, 3).reshape(here, count * SLOTS, width)
        result = experts_plain(where, picked, w_gate, w_up, w_down)
        result = result.reshape(here, count, SLOTS, width).transpose(1, 0, 2, 3).reshape(count, here * SLOTS, width)
        total = jnp.einsum("cts,csd->ctd", combine, result, preferred_element_type=jnp.float32).astype(jnp.bfloat16)
        left, right = jnp.split(total, 2, axis=2)
        both = summed([jnp.where(side == 0, left, right), swap(jnp.where(side == 0, right, left))])
        mixture = lax.psum_scatter(both.astype(jnp.bfloat16), "ctx").astype(jnp.float32)
    return (middle.astype(jnp.float32) + mixture).astype(jnp.bfloat16)


def solution(mesh):
    in_specs = (
        P(("groups", "ctx"), "exp"),
        P(("groups", "ctx"), None),
        P(("groups", "ctx"), None),
        P("groups"),
        P("groups"),
        P(("groups", "ctx"), None),
        P(("groups", "ctx"), None),
        P(None, "exp"),
        P("exp", None),
        P(),
        P("ctx", None, "exp"),
        P("ctx", None, "exp"),
        P("ctx", "exp", None),
    )
    out_specs = P(("groups", "ctx"), "exp")
    return jax.shard_map(body, mesh=mesh, in_specs=in_specs, out_specs=out_specs, check_vma=False)
```

```python
import functools
import math

import jax
import jax.numpy as jnp
import numpy as np
from jax import lax
from jax.experimental import pallas as pl
from jax.experimental.pallas import tpu as pltpu
from jax.sharding import PartitionSpec as P

NOPE = 128
ROPE = 64
VHEAD = 128
LAT = 512
EXPERTS = 64
TOP = 6
SLOTS = 16
WIDE = 640
MIB = 1024 * 1024
VMEM_LIMIT = 50 * MIB
HELD = 7
PIECES = 2
SWAP = [(0, 1), (1, 0)]
PARTS = 2
FEW = 8


def cycle_of(count):
    fast = 2 ** (int(math.log2(count)) // 2)
    slow = count // fast
    cycle = [0]
    for i in range(slow):
        columns = range(1, fast)
        cycle += [i * fast + j for j in (columns if i % 2 == 0 else reversed(columns))]
    return cycle + [i * fast for i in reversed(range(1, slow))]


def swap(value):
    return lax.ppermute(value, "exp", SWAP)


def turn(value, count, cross=False):
    cycle = cycle_of(count)
    pairs = []
    for p in range(count):
        for core, ahead in ((0, 1), (1, -1)):
            pairs.append((cycle[p] * 2 + core, cycle[(p + ahead) % count] * 2 + (core ^ int(cross))))
    return lax.ppermute(value, ("ctx", "exp"), pairs)


def summed(pieces):
    total = pieces[0].astype(jnp.float32)
    for piece in pieces[1:]:
        total = total + piece.astype(jnp.float32)
    return total


def sources_of(me, side, count):
    if count > FEW:
        return jnp.arange(count, dtype=jnp.int32)
    cycle = cycle_of(count)
    middle = count // 2
    table = np.zeros((2 * count, count), np.int32)
    for p in range(count):
        for core, sign in ((0, 1), (1, -1)):
            ways = [sign * d for d in range(middle + 1)] + [-sign * d for d in range(1, middle)]
            table[cycle[p] * 2 + core] = [cycle[(p - way) % count] for way in ways]
    return lax.dynamic_index_in_dim(jnp.asarray(table), me * 2 + side, keepdims=False)


def gather(block, count, beside=()):
    if count > FEW:
        return list(lax.all_gather(block, "ctx")), [run(*arguments) for run, arguments in beside]
    middle = count // 2
    found, other, made = [block], [()], []
    for d in range(1, middle + 1):
        arrived, extra = turn(found[-1], count), ()
        if len(beside) >= d:
            run, arguments = beside[d - 1]
            extra = run(*lax.optimization_barrier((found[-1], arguments))[1])
        arrived, other[-1], extra = lax.optimization_barrier((arrived, other[-1], extra))
        made.append(extra)
        found.append(arrived)
        if d < middle:
            other.append(swap(arrived))
    return found + other[1:], made[: len(beside)]


def reduce(parts, side, count):
    middle = count // 2
    near, far = 0, 1
    sums = [swap(parts[1 - stream][middle][1]) for stream in (near, far)]
    given = [swap(parts[1 - stream][middle - 1]) for stream in (near, far)]
    for stream in (near, far):
        first = summed([parts[stream][middle][0], sums[stream]]).astype(jnp.bfloat16)
        sums[stream] = turn(first, count)
    for d in range(middle - 1, 0, -1):
        for stream in (near, far):
            arrived = sums[stream]
            later = parts[1 - stream][d - 1] if d > 1 or stream == near else ()
            arrived, later = lax.optimization_barrier((arrived, later))
            running = arrived.astype(jnp.float32)
            if d == middle - 1:
                nothing = jnp.zeros_like(running)
                running = jnp.concatenate(
                    [jnp.where(side == 0, running, nothing), jnp.where(side == 0, nothing, running)], axis=0
                )
            total = (summed([parts[stream][middle + d], given[stream]]) + running).astype(jnp.bfloat16)
            sums[stream] = turn(total, count, cross=d == 1 and stream == far)
            if d > 1 or stream == near:
                given[stream] = swap(later)
    return summed([parts[near][0], given[near], sums[near], sums[far]])


def attend_kernel(count, blocks, heads, info, *refs):
    latents, refs = refs[: len(refs) - 14], refs[len(refs) - 14 :]
    wanted, (out_ref, base_ref) = refs[:4], refs[4:6]
    held, sems, (m_ref, l_ref, acc_ref) = refs[6:10], refs[10], refs[11:14]
    q_ref, up_ref, proj_ref, residual_ref = held
    copies = [pltpu.make_async_copy(wanted[i], held[i], sems.at[i]) for i in range(4)]
    chunk = pl.program_id(0)
    sources = lambda c: info[2 + c]
    order = lambda j: info[2 + count + j]
    segs = info.shape[0] - 2 - 3 * count
    rows = q_ref.shape[0]
    span = rows // 2
    depth = q_ref.shape[1] // heads

    @pl.when(chunk == 0)
    def _():
        for copy in copies:
            copy.start()

    @pl.when(chunk == 0)
    def _():
        m_ref[...] = jnp.full_like(m_ref, -1e30)
        l_ref[...] = jnp.zeros_like(l_ref)
        acc_ref[...] = jnp.zeros_like(acc_ref)

    row = lax.broadcasted_iota(jnp.int32, (rows, 1), 0)
    first = order(2 * info[0]) * span
    second = order(2 * info[0] + 1) * span
    qpos = jnp.where(row < span, first + row, second + row - span)
    low = jnp.zeros((rows, 1), jnp.int32)
    start = jnp.int32(0)
    for m in range(segs):
        low = jnp.where(qpos >= start, start, low)
        start = start + info[2 + 3 * count + m]
    keys = blocks * rows
    lane = lax.broadcasted_iota(jnp.int32, (1, keys), 1)
    which = lane // span
    kpos = lane % span
    for j in range(blocks):
        source = sources(chunk * blocks + j)
        for i in range(2):
            kpos = jnp.where(which == 2 * j + i, order(2 * source + i) * span + lane % span, kpos)
    visible = (kpos >= low) & (kpos <= qpos)

    lat = jnp.concatenate([ref[...].reshape(-1, WIDE) for ref in latents], axis=0)

    @pl.when(chunk == 0)
    def _():
        copies[0].wait()
        copies[1].wait()

    keyval = jnp.dot(lat[:, :LAT], up_ref[...], preferred_element_type=jnp.float32).astype(jnp.bfloat16)
    rope = lat[:, LAT : LAT + ROPE]
    scale = 1.0 / math.sqrt(NOPE + ROPE)
    for h in range(heads):
        base = h * (NOPE + VHEAD)
        key = jnp.concatenate([keyval[:, base : base + NOPE], rope], axis=1)
        scores = lax.dot_general(q_ref[:, h * depth : (h + 1) * depth], key, (((1,), (1,)), ((), ())), preferred_element_type=jnp.float32)
        scores = jnp.where(visible, scores * scale, -1e30)
        best = m_ref[h]
        fresh = jnp.maximum(best, jnp.max(scores, axis=1, keepdims=True))
        weights = jnp.where(visible, jnp.exp(scores - fresh), 0.0)
        shrink = jnp.exp(best - fresh)
        m_ref[h] = fresh
        l_ref[h] = l_ref[h] * shrink + jnp.sum(weights, axis=1, keepdims=True)
        mixed = jnp.dot(
            weights.astype(jnp.bfloat16), keyval[:, base + NOPE : base + NOPE + VHEAD], preferred_element_type=jnp.float32
        )
        acc_ref[h] = acc_ref[h] * shrink + mixed

    @pl.when(chunk == pl.num_programs(0) - 1)
    def _():
        attended = [(acc_ref[h] / l_ref[h]).astype(jnp.bfloat16) for h in range(heads)]
        copies[2].wait()
        copies[3].wait()
        out = jnp.dot(jnp.concatenate(attended, axis=1), proj_ref[...], preferred_element_type=jnp.float32)
        out = out.astype(jnp.bfloat16)
        out_ref[...] = out
        base_ref[...] = residual_ref[...].astype(jnp.float32) + out.astype(jnp.float32)


def attend(info, found, queries, kv_up, out_proj, residual, count):
    rows, width = residual.shape
    heads = kv_up.shape[1] // (NOPE + VHEAD)
    blocks = math.gcd(count, 8)
    whole = pl.BlockSpec(memory_space=pltpu.VMEM)
    if blocks == count:
        latents, lat_spec = found, whole
    else:
        latents, lat_spec = [jnp.stack(found)], pl.BlockSpec((blocks, rows, WIDE), lambda i, *_: (i, 0, 0))
    wanted = (queries, kv_up, out_proj, residual)
    return pl.pallas_call(
        functools.partial(attend_kernel, count, blocks, heads),
        grid_spec=pltpu.PrefetchScalarGridSpec(
            num_scalar_prefetch=1,
            grid=(count // blocks,),
            in_specs=[lat_spec] * len(latents) + [pl.BlockSpec(memory_space=pltpu.HBM)] * 4,
            out_specs=[whole, whole],
            scratch_shapes=[pltpu.VMEM(x.shape, x.dtype) for x in wanted]
            + [
                pltpu.SemaphoreType.DMA((4,)),
                pltpu.VMEM((heads, rows, 1), jnp.float32),
                pltpu.VMEM((heads, rows, 1), jnp.float32),
                pltpu.VMEM((heads, rows, VHEAD), jnp.float32),
            ],
        ),
        out_shape=[pltpu.VMEM((rows, width), jnp.bfloat16), pltpu.VMEM((rows, width), jnp.float32)],
        compiler_params=pltpu.CompilerParams(vmem_limit_bytes=28 * MIB),
        name="attend",
    )(info, *latents, *(pltpu.with_memory_space_constraint(x, pltpu.HBM) for x in wanted))


def route_kernel(count, where, *refs):
    blocks, out_ref = refs[:count], refs[count]
    _, rows, width = out_ref.shape
    here = width // SLOTS
    lane = lax.broadcasted_iota(jnp.int32, (rows, width), 1)
    own = (where[0] * here + lane // SLOTS).astype(jnp.float32)
    slot = (lane % SLOTS).astype(jnp.float32)
    first = lax.broadcasted_iota(jnp.int32, (rows, rows), 0)
    before = (first > lax.broadcasted_iota(jnp.int32, (rows, rows), 1)).astype(jnp.float32).astype(jnp.bfloat16)
    for c in range(count):
        facts = blocks[c][:, LAT:].astype(jnp.float32)
        hot, share = jnp.zeros((rows, width), jnp.float32), jnp.zeros((rows, width), jnp.float32)
        for k in range(TOP):
            hit = facts[:, ROPE + k : ROPE + k + 1] == own
            hot = jnp.where(hit, 1.0, hot)
            share = jnp.where(hit, facts[:, ROPE + TOP + k : ROPE + TOP + k + 1], share)
        rank = jnp.dot(before, hot.astype(jnp.bfloat16), preferred_element_type=jnp.float32)
        out_ref[c] = jnp.where(rank == slot, share, 0.0).astype(jnp.bfloat16)


def route(where, found, here):
    count, (rows, _) = len(found), found[0].shape
    whole = pl.BlockSpec(memory_space=pltpu.VMEM)
    return pl.pallas_call(
        functools.partial(route_kernel, count),
        in_specs=[pl.BlockSpec(memory_space=pltpu.SMEM)] + [whole] * count,
        out_specs=whole,
        out_shape=pltpu.VMEM((count, rows, here * SLOTS), jnp.bfloat16),
        compiler_params=pltpu.CompilerParams(vmem_limit_bytes=8 * MIB),
        name="route",
    )(where, *found)


def norm_kernel(where, base_ref, there_ref, gain_ref, middle_ref, *normed_refs):
    half = middle_ref.shape[1]
    middle = (base_ref[...] + there_ref[...].astype(jnp.float32)).astype(jnp.bfloat16)
    wide = middle.astype(jnp.float32)
    inverse = lax.rsqrt(jnp.mean(wide * wide, axis=1, keepdims=True) + 1e-06)
    normed = (wide * inverse * gain_ref[...].astype(jnp.float32)).astype(jnp.bfloat16)
    part = normed_refs[0].shape[1]
    for h, ref in enumerate(normed_refs):
        ref[...] = normed[:, h * part : (h + 1) * part]
    middle_ref[...] = jnp.where(where[1] == 0, wide[:, :half], wide[:, half:]).astype(jnp.bfloat16)


def norm(where, base, there, gain):
    rows, width = base.shape
    whole = pl.BlockSpec(memory_space=pltpu.VMEM)
    shapes = [(rows, width // 2)] + [(rows, width // PARTS)] * PARTS
    return pl.pallas_call(
        norm_kernel,
        in_specs=[pl.BlockSpec(memory_space=pltpu.SMEM)] + [whole] * 3,
        out_specs=[whole] * len(shapes),
        out_shape=[pltpu.VMEM(shape, jnp.bfloat16) for shape in shapes],
        compiler_params=pltpu.CompilerParams(vmem_limit_bytes=12 * MIB),
        name="norm",
    )(where, base, there, gain)


def pack_kernel(*refs):
    copies = [pltpu.make_async_copy(refs[i], refs[4 + i], refs[8].at[i]) for i in range(3)]
    for copy in copies:
        copy.start()
    for copy in copies:
        copy.wait()
    out_ref, (latent_ref, ids_ref, weights_ref, rows) = refs[3], refs[4:8]
    tokens = out_ref.shape[0]
    rows[...] = jnp.zeros_like(rows)
    rows[0:TOP] = ids_ref[...].astype(jnp.float32)
    rows[TOP : 2 * TOP] = weights_ref[...]
    row = lax.broadcasted_iota(jnp.int32, (tokens, tokens), 0)
    same = (row == lax.broadcasted_iota(jnp.int32, (tokens, tokens), 1)).astype(jnp.float32).astype(jnp.bfloat16)
    every = jnp.concatenate([latent_ref[...], rows[...].astype(jnp.bfloat16)], axis=0)
    turned = lax.dot_general(same, every, (((1,), (1,)), ((), ())), preferred_element_type=jnp.float32)
    out_ref[...] = turned.astype(jnp.bfloat16)


def pack(latent, expert_ids, route_weights):
    local_rows, base = latent.shape
    arrays = (latent.T, expert_ids.T, route_weights.T)
    return pl.pallas_call(
        pack_kernel,
        in_specs=[pl.BlockSpec(memory_space=pltpu.HBM)] * 3,
        out_specs=pl.BlockSpec(memory_space=pltpu.VMEM),
        scratch_shapes=[pltpu.VMEM(x.shape, x.dtype) for x in arrays]
        + [pltpu.VMEM((WIDE - base, local_rows), jnp.float32), pltpu.SemaphoreType.DMA((3,))],
        out_shape=pltpu.VMEM((local_rows, WIDE), jnp.bfloat16),
        compiler_params=pltpu.CompilerParams(vmem_limit_bytes=4 * MIB),
        name="pack",
    )(*(pltpu.with_memory_space_constraint(x, pltpu.HBM) for x in arrays))


def expert_hidden(rows, gate, up):
    by_columns = (((1,), (1,)), ((), ()))
    gate = lax.dot_general(gate, rows, by_columns, preferred_element_type=jnp.float32)
    upper = lax.dot_general(up, rows, by_columns, preferred_element_type=jnp.float32)
    return (gate / (1.0 + jnp.exp(-gate)) * upper).astype(jnp.bfloat16)


def expert_down(hidden, down):
    by_rows = (((0,), (0,)), ((), ()))
    return lax.dot_general(hidden, down, by_rows, preferred_element_type=jnp.float32).astype(jnp.bfloat16)


def plain_kernel(where, rows_ref, gate_ref, up_ref, down_ref, out_ref):
    out_ref[0] = expert_down(expert_hidden(rows_ref[0], gate_ref[0], up_ref[0]), down_ref[0])


def fused_kernel(count, where, *refs):
    at = PARTS * count
    blocks, combine_ref, weights = refs[:at], refs[at], refs[at + 1 : at + 4]
    near, far = refs[at + 4 : at + 5 + count], refs[at + 5 + count : at + 6 + 2 * count]
    at += 6 + 2 * count
    picked, buffer, sems = refs[at : at + 3]
    here = picked.shape[0]
    slots, units, width = buffer.shape
    side = where[1]
    piece = units // PIECES
    middle = count // 2
    by_rows = (((0,), (0,)), ((), ()))

    def copies(expert, w):
        slot = lax.rem(3 * expert + w, slots)
        for i in range(PIECES):
            rows = pl.ds(i * piece, piece)
            yield pltpu.make_async_copy(weights[w].at[expert, rows], buffer.at[slot, rows], sems.at[slot, i])

    def start(expert, w):
        for copy in copies(expert, w):
            copy.start()

    def arrived(expert, w):
        for copy in copies(expert, w):
            copy.wait()
        return buffer[lax.rem(3 * expert + w, slots)]

    for i in range(slots):
        start(i // 3, i % 3)

    for c in range(count):
        pick = (combine_ref[c].astype(jnp.float32) > 0).astype(jnp.float32).astype(jnp.bfloat16)
        for h in range(PARTS):
            block = blocks[PARTS * c + h][...]
            rows = lax.dot_general(pick, block, by_rows, preferred_element_type=jnp.float32).astype(jnp.bfloat16)
            columns = pl.ds(h * block.shape[1], block.shape[1])
            for e in range(here):
                picked[e, c * SLOTS : (c + 1) * SLOTS, columns] = rows[e * SLOTS : (e + 1) * SLOTS]

    def work(expert, _):
        hidden = expert_hidden(picked[expert], arrived(expert, 0), arrived(expert, 1))

        @pl.when(expert + slots // 3 < here)
        def _():
            start(expert + slots // 3, 1)
            start(expert + slots // 3, 2)

        picked[expert] = expert_down(hidden, arrived(expert, 2))

        @pl.when(expert + slots // 3 + 1 < here)
        def _():
            start(expert + slots // 3 + 1, 0)

        return 0

    lax.fori_loop(0, here, work, 0)

    half = width // 2
    for c in [middle] + list(range(middle)) + list(range(middle + 1, count)):
        for turned, outs in ((1 - side, far), (side, near)):
            columns = pl.ds(pl.multiple_of(turned * half, half), half)
            rows = jnp.concatenate([picked[e, c * SLOTS : (c + 1) * SLOTS, columns] for e in range(here)], axis=0)
            total = jnp.dot(combine_ref[c], rows, preferred_element_type=jnp.float32).astype(jnp.bfloat16)
            if c == middle:
                upper, lower = total[: total.shape[0] // 2], total[total.shape[0] // 2 :]
                outs[c][...] = jnp.where(side == 0, upper, lower)
                outs[count][...] = jnp.where(side == 0, lower, upper)
            else:
                outs[c][...] = total


def expert_specs(w_gate):
    hidden, width = w_gate.shape[1:]
    return [pl.BlockSpec((1, hidden, width), lambda e, where: (e, 0, 0))] * 3


def experts_plain(where, picked, w_gate, w_up, w_down):
    here, rows, width = picked.shape
    rows_spec = pl.BlockSpec((1, rows, width), lambda e, where: (e, 0, 0))
    return pl.pallas_call(
        plain_kernel,
        grid_spec=pltpu.PrefetchScalarGridSpec(
            num_scalar_prefetch=1,
            grid=(here,),
            in_specs=[rows_spec] + expert_specs(w_gate),
            out_specs=rows_spec,
        ),
        out_shape=jax.ShapeDtypeStruct(picked.shape, jnp.bfloat16),
        compiler_params=pltpu.CompilerParams(vmem_limit_bytes=VMEM_LIMIT),
        name="experts",
    )(where, picked, w_gate, w_up, w_down)


def experts_fused(where, found, combine, w_gate, w_up, w_down):
    count, local = len(found), found[0][0].shape[0]
    here, units, width = w_gate.shape
    rows = count * SLOTS
    middle = count // 2
    sizes = [local // 2 if c in (middle, count) else local for c in range(count + 1)]
    whole = pl.BlockSpec(memory_space=pltpu.VMEM)
    outs = pl.pallas_call(
        functools.partial(fused_kernel, count),
        in_specs=[pl.BlockSpec(memory_space=pltpu.SMEM)]
        + [whole] * (PARTS * count + 1)
        + [pl.BlockSpec(memory_space=pltpu.HBM)] * 3,
        out_specs=[whole] * (2 * count + 2),
        scratch_shapes=[pltpu.VMEM((here, rows, width), jnp.bfloat16)]
        + [pltpu.VMEM((HELD, units, width), jnp.bfloat16), pltpu.SemaphoreType.DMA((HELD, PIECES))],
        out_shape=[pltpu.VMEM((size, width // 2), jnp.bfloat16) for size in sizes] * 2,
        compiler_params=pltpu.CompilerParams(vmem_limit_bytes=29 * MIB),
        name="experts",
    )(where, *(x for block in found for x in block), combine,
      *(pltpu.with_memory_space_constraint(w, pltpu.HBM) for w in (w_gate, w_up, w_down)))
    parts = [list(outs[: count + 1]), list(outs[count + 1 :])]
    return [x[:middle] + [(x[middle], x[count])] + x[middle + 1 : count] for x in parts]


def body(
    queries,
    latent,
    residual,
    seg_lengths,
    span_order,
    expert_ids,
    route_weights,
    kv_up,
    out_proj,
    norm_gain,
    w_gate,
    w_up,
    w_down,
):
    local_rows, width = residual.shape
    span = local_rows // 2
    count = lax.axis_size("ctx")
    here = EXPERTS // count
    me, side = lax.axis_index("ctx"), lax.axis_index("exp")
    where = jnp.stack([me, side]).astype(jnp.int32)

    base = latent.shape[1]
    w_gate, w_up = w_gate.transpose(0, 2, 1), w_up.transpose(0, 2, 1)
    packed = pack(latent, expert_ids, route_weights)
    few = count <= FEW
    scalars = lambda *arrays: jnp.concatenate([where, sources_of(me, side, count), *arrays])
    beside = [(scalars, (span_order, seg_lengths)), (lambda gain: gain.reshape(1, width), (norm_gain,))]
    found, (info, gain) = gather(packed, count, beside)
    partial, summand = attend(info, found, queries, kv_up, out_proj, residual, count)
    def place_rows(*blocks):
        if few:
            return route(where, blocks, here)
        facts = jnp.stack(blocks)[:, :, base : base + 2 * TOP].astype(jnp.float32)
        own = (me * here + jnp.arange(here, dtype=jnp.int32)).astype(jnp.float32)
        hit = facts[:, :, :TOP, None] == own
        hot = jnp.any(hit, axis=2)
        share = jnp.sum(jnp.where(hit, facts[:, :, TOP:, None], 0.0), axis=2)
        token = jnp.arange(local_rows, dtype=jnp.int32)
        before = (token[:, None] > token[None, :]).astype(jnp.bfloat16)
        rank = jnp.einsum("tu,cue->cte", before, hot.astype(jnp.bfloat16), preferred_element_type=jnp.float32)
        slot = jnp.arange(SLOTS, dtype=jnp.int32).astype(jnp.float32)
        combine = jnp.where(rank[:, :, :, None] == slot, share[:, :, :, None], 0.0)
        return combine.astype(jnp.bfloat16).reshape(count, local_rows, here * SLOTS)

    there = swap(partial)
    blocks, _ = lax.optimization_barrier((tuple(found), partial))
    combine, there = lax.optimization_barrier((place_rows(*blocks), there))
    middle, *normed = norm(where, summand, there, gain)
    streams = [gather(x, count)[0] for x in normed]
    got = list(zip(*streams))
    if few:
        mixture = reduce(experts_fused(where, got, combine, w_gate, w_up, w_down), side, count)
    else:
        pick = (combine > 0).astype(jnp.bfloat16)
        rows = jnp.stack([jnp.concatenate(block, axis=1) for block in got])
        picked = jnp.einsum("cts,ctd->csd", pick, rows, preferred_element_type=jnp.float32).astype(jnp.bfloat16)
        picked = picked.reshape(count, here, SLOTS, width).transpose(1, 0, 2, 3).reshape(here, count * SLOTS, width)
        result = experts_plain(where, picked, w_gate, w_up, w_down)
        result = result.reshape(here, count, SLOTS, width).transpose(1, 0, 2, 3).reshape(count, here * SLOTS, width)
        total = jnp.einsum("cts,csd->ctd", combine, result, preferred_element_type=jnp.float32).astype(jnp.bfloat16)
        left, right = jnp.split(total, 2, axis=2)
        both = summed([jnp.where(side == 0, left, right), swap(jnp.where(side == 0, right, left))])
        mixture = lax.psum_scatter(both.astype(jnp.bfloat16), "ctx").astype(jnp.float32)
    return (middle.astype(jnp.float32) + mixture).astype(jnp.bfloat16)


def solution(mesh):
    in_specs = (
        P(("groups", "ctx"), "exp"),
        P(("groups", "ctx"), None),
        P(("groups", "ctx"), None),
        P("groups"),
        P("groups"),
        P(("groups", "ctx"), None),
        P(("groups", "ctx"), None),
        P(None, "exp"),
        P("exp", None),
        P(),
        P("ctx", None, "exp"),
        P("ctx", None, "exp"),
        P("ctx", "exp", None),
    )
    out_specs = P(("groups", "ctx"), "exp")
    return jax.shard_map(body, mesh=mesh, in_specs=in_specs, out_specs=out_specs, check_vma=False)
```

```python
import functools
import math

import jax
import jax.numpy as jnp
import numpy as np
from jax import lax
from jax.experimental import pallas as pl
from jax.experimental.pallas import tpu as pltpu
from jax.sharding import PartitionSpec as P

NOPE = 128
ROPE = 64
VHEAD = 128
LAT = 512
EXPERTS = 64
TOP = 6
SLOTS = 16
WIDE = 640
MIB = 1024 * 1024
VMEM_LIMIT = 50 * MIB
HELD = 7
PIECES = 2
SWAP = [(0, 1), (1, 0)]
FEW = 8


def cycle_of(count):
    fast = 2 ** (int(math.log2(count)) // 2)
    slow = count // fast
    cycle = [0]
    for i in range(slow):
        columns = range(1, fast)
        cycle += [i * fast + j for j in (columns if i % 2 == 0 else reversed(columns))]
    return cycle + [i * fast for i in reversed(range(1, slow))]


def swap(value):
    return lax.ppermute(value, "exp", SWAP)


def turn(value, count, cross=False):
    cycle = cycle_of(count)
    pairs = []
    for p in range(count):
        for core, ahead in ((0, 1), (1, -1)):
            pairs.append((cycle[p] * 2 + core, cycle[(p + ahead) % count] * 2 + (core ^ int(cross))))
    return lax.ppermute(value, ("ctx", "exp"), pairs)


def summed(pieces):
    total = pieces[0].astype(jnp.float32)
    for piece in pieces[1:]:
        total = total + piece.astype(jnp.float32)
    return total


def sources_of(me, side, count):
    if count > FEW:
        return jnp.arange(count, dtype=jnp.int32)
    cycle = cycle_of(count)
    middle = count // 2
    table = np.zeros((2 * count, count), np.int32)
    for p in range(count):
        for core, sign in ((0, 1), (1, -1)):
            ways = [sign * d for d in range(middle + 1)] + [-sign * d for d in range(1, middle)]
            table[cycle[p] * 2 + core] = [cycle[(p - way) % count] for way in ways]
    return lax.dynamic_index_in_dim(jnp.asarray(table), me * 2 + side, keepdims=False)


def gather(block, count, beside=()):
    if count > FEW:
        return list(lax.all_gather(block, "ctx")), [run(*arguments) for run, arguments in beside]
    middle = count // 2
    found, other, made = [block], [()], []
    for d in range(1, middle + 1):
        arrived, extra = turn(found[-1], count), ()
        if len(beside) >= d:
            run, arguments = beside[d - 1]
            extra = run(*lax.optimization_barrier((found[-1], arguments))[1])
        arrived, other[-1], extra = lax.optimization_barrier((arrived, other[-1], extra))
        made.append(extra)
        found.append(arrived)
        if d < middle:
            other.append(swap(arrived))
    return found + other[1:], made[: len(beside)]


def gather_columns(near, far, count):
    if count > FEW:
        return list(zip(lax.all_gather(near, "ctx"), lax.all_gather(far, "ctx")))
    middle = count // 2
    found, other = {0: [near], 1: [far]}, {0: [()], 1: [()]}
    for d in range(1, middle + 1):
        for stream in (0, 1) if d < middle else (0,):
            arrived = turn(found[stream][-1], count)
            arrived, other[stream][-1] = lax.optimization_barrier((arrived, other[stream][-1]))
            found[stream].append(arrived)
            other[stream].append(swap(arrived))
    here = [(found[0][d], found[1][d]) for d in range(middle)]
    there = [(other[1][d], other[0][d]) for d in range(1, middle)]
    return here + [(found[0][middle], other[0][middle])] + there


def reduce(parts, count):
    middle = count // 2
    given = [swap(parts[1][middle]), swap(parts[0][middle - 1])]
    running = [None, None]
    for d in range(middle, 0, -1):
        for stream in (0, 1) if d < middle else (0,):
            place = middle + d if d < middle else middle
            later = parts[1 - stream][d - 1] if d > 1 or stream == 0 else ()
            pieces = [parts[stream][place], given[stream]]
            if running[stream] is not None:
                running[stream], later = lax.optimization_barrier((running[stream], later))
                pieces.append(running[stream])
            running[stream] = turn(summed(pieces).astype(jnp.bfloat16), count, cross=d == 1 and stream == 1)
            if d > 1 or stream == 0:
                given[stream] = swap(later)
    return summed([parts[0][0], given[0], *running])


def attend_kernel(count, blocks, heads, info, *refs):
    latents, refs = refs[: len(refs) - 14], refs[len(refs) - 14 :]
    wanted, (out_ref, base_ref) = refs[:4], refs[4:6]
    held, sems, (m_ref, l_ref, acc_ref) = refs[6:10], refs[10], refs[11:14]
    q_ref, up_ref, proj_ref, residual_ref = held
    copies = [pltpu.make_async_copy(wanted[i], held[i], sems.at[i]) for i in range(4)]
    chunk = pl.program_id(0)
    sources = lambda c: info[2 + c]
    order = lambda j: info[2 + count + j]
    segs = info.shape[0] - 2 - 3 * count
    rows = q_ref.shape[0]
    span = rows // 2
    depth = q_ref.shape[1] // heads

    @pl.when(chunk == 0)
    def _():
        for copy in copies:
            copy.start()

    @pl.when(chunk == 0)
    def _():
        m_ref[...] = jnp.full_like(m_ref, -1e30)
        l_ref[...] = jnp.zeros_like(l_ref)
        acc_ref[...] = jnp.zeros_like(acc_ref)

    row = lax.broadcasted_iota(jnp.int32, (rows, 1), 0)
    first = order(2 * info[0]) * span
    second = order(2 * info[0] + 1) * span
    qpos = jnp.where(row < span, first + row, second + row - span)
    low = jnp.zeros((rows, 1), jnp.int32)
    start = jnp.int32(0)
    for m in range(segs):
        low = jnp.where(qpos >= start, start, low)
        start = start + info[2 + 3 * count + m]
    keys = blocks * rows
    lane = lax.broadcasted_iota(jnp.int32, (1, keys), 1)
    which = lane // span
    kpos = lane % span
    for j in range(blocks):
        source = sources(chunk * blocks + j)
        for i in range(2):
            kpos = jnp.where(which == 2 * j + i, order(2 * source + i) * span + lane % span, kpos)
    visible = (kpos >= low) & (kpos <= qpos)

    lat = jnp.concatenate([ref[...].reshape(-1, WIDE) for ref in latents], axis=0)

    @pl.when(chunk == 0)
    def _():
        copies[0].wait()
        copies[1].wait()

    keyval = jnp.dot(lat[:, :LAT], up_ref[...], preferred_element_type=jnp.float32).astype(jnp.bfloat16)
    rope = lat[:, LAT : LAT + ROPE]
    scale = 1.0 / math.sqrt(NOPE + ROPE)
    for h in range(heads):
        base = h * (NOPE + VHEAD)
        key = jnp.concatenate([keyval[:, base : base + NOPE], rope], axis=1)
        scores = lax.dot_general(q_ref[:, h * depth : (h + 1) * depth], key, (((1,), (1,)), ((), ())), preferred_element_type=jnp.float32)
        scores = jnp.where(visible, scores * scale, -1e30)
        best = m_ref[h]
        fresh = jnp.maximum(best, jnp.max(scores, axis=1, keepdims=True))
        weights = jnp.where(visible, jnp.exp(scores - fresh), 0.0)
        shrink = jnp.exp(best - fresh)
        m_ref[h] = fresh
        l_ref[h] = l_ref[h] * shrink + jnp.sum(weights, axis=1, keepdims=True)
        mixed = jnp.dot(
            weights.astype(jnp.bfloat16), keyval[:, base + NOPE : base + NOPE + VHEAD], preferred_element_type=jnp.float32
        )
        acc_ref[h] = acc_ref[h] * shrink + mixed

    @pl.when(chunk == pl.num_programs(0) - 1)
    def _():
        attended = [(acc_ref[h] / l_ref[h]).astype(jnp.bfloat16) for h in range(heads)]
        copies[2].wait()
        copies[3].wait()
        out = jnp.dot(jnp.concatenate(attended, axis=1), proj_ref[...], preferred_element_type=jnp.float32)
        out = out.astype(jnp.bfloat16)
        out_ref[...] = out
        base_ref[...] = residual_ref[...].astype(jnp.float32) + out.astype(jnp.float32)


def attend(info, found, queries, kv_up, out_proj, residual, count):
    rows, width = residual.shape
    heads = kv_up.shape[1] // (NOPE + VHEAD)
    blocks = math.gcd(count, 8)
    whole = pl.BlockSpec(memory_space=pltpu.VMEM)
    if blocks == count:
        latents, lat_spec = found, whole
    else:
        latents, lat_spec = [jnp.stack(found)], pl.BlockSpec((blocks, rows, WIDE), lambda i, *_: (i, 0, 0))
    wanted = (queries, kv_up, out_proj, residual)
    return pl.pallas_call(
        functools.partial(attend_kernel, count, blocks, heads),
        grid_spec=pltpu.PrefetchScalarGridSpec(
            num_scalar_prefetch=1,
            grid=(count // blocks,),
            in_specs=[lat_spec] * len(latents) + [pl.BlockSpec(memory_space=pltpu.HBM)] * 4,
            out_specs=[whole, whole],
            scratch_shapes=[pltpu.VMEM(x.shape, x.dtype) for x in wanted]
            + [
                pltpu.SemaphoreType.DMA((4,)),
                pltpu.VMEM((heads, rows, 1), jnp.float32),
                pltpu.VMEM((heads, rows, 1), jnp.float32),
                pltpu.VMEM((heads, rows, VHEAD), jnp.float32),
            ],
        ),
        out_shape=[pltpu.VMEM((rows, width), jnp.bfloat16), pltpu.VMEM((rows, width), jnp.float32)],
        compiler_params=pltpu.CompilerParams(vmem_limit_bytes=28 * MIB),
        name="attend",
    )(info, *latents, *(pltpu.with_memory_space_constraint(x, pltpu.HBM) for x in wanted))


def route_kernel(count, where, *refs):
    blocks, out_ref = refs[:count], refs[count]
    _, rows, width = out_ref.shape
    here = width // SLOTS
    lane = lax.broadcasted_iota(jnp.int32, (rows, width), 1)
    own = (where[0] * here + lane // SLOTS).astype(jnp.float32)
    slot = (lane % SLOTS).astype(jnp.float32)
    first = lax.broadcasted_iota(jnp.int32, (rows, rows), 0)
    before = (first > lax.broadcasted_iota(jnp.int32, (rows, rows), 1)).astype(jnp.float32).astype(jnp.bfloat16)
    for c in range(count):
        facts = blocks[c][:, LAT:].astype(jnp.float32)
        hot, share = jnp.zeros((rows, width), jnp.float32), jnp.zeros((rows, width), jnp.float32)
        for k in range(TOP):
            hit = facts[:, ROPE + k : ROPE + k + 1] == own
            hot = jnp.where(hit, 1.0, hot)
            share = jnp.where(hit, facts[:, ROPE + TOP + k : ROPE + TOP + k + 1], share)
        rank = jnp.dot(before, hot.astype(jnp.bfloat16), preferred_element_type=jnp.float32)
        out_ref[c] = jnp.where(rank == slot, share, 0.0).astype(jnp.bfloat16)


def route(where, found, here):
    count, (rows, _) = len(found), found[0].shape
    whole = pl.BlockSpec(memory_space=pltpu.VMEM)
    return pl.pallas_call(
        functools.partial(route_kernel, count),
        in_specs=[pl.BlockSpec(memory_space=pltpu.SMEM)] + [whole] * count,
        out_specs=whole,
        out_shape=pltpu.VMEM((count, rows, here * SLOTS), jnp.bfloat16),
        compiler_params=pltpu.CompilerParams(vmem_limit_bytes=8 * MIB),
        name="route",
    )(where, *found)


def norm_kernel(where, base_ref, there_ref, gain_ref, middle_ref, near_ref, far_ref):
    half = middle_ref.shape[1]
    middle = (base_ref[...] + there_ref[...].astype(jnp.float32)).astype(jnp.bfloat16)
    wide = middle.astype(jnp.float32)
    inverse = lax.rsqrt(jnp.mean(wide * wide, axis=1, keepdims=True) + 1e-06)
    normed = wide * inverse * gain_ref[...].astype(jnp.float32)
    first = where[1] == 0
    near_ref[...] = jnp.where(first, normed[:, :half], normed[:, half:]).astype(jnp.bfloat16)
    far_ref[...] = jnp.where(first, normed[:, half:], normed[:, :half]).astype(jnp.bfloat16)
    middle_ref[...] = jnp.where(first, wide[:, :half], wide[:, half:]).astype(jnp.bfloat16)


def norm(where, base, there, gain):
    rows, width = base.shape
    whole = pl.BlockSpec(memory_space=pltpu.VMEM)
    return pl.pallas_call(
        norm_kernel,
        in_specs=[pl.BlockSpec(memory_space=pltpu.SMEM)] + [whole] * 3,
        out_specs=[whole] * 3,
        out_shape=[pltpu.VMEM((rows, width // 2), jnp.bfloat16)] * 3,
        compiler_params=pltpu.CompilerParams(vmem_limit_bytes=12 * MIB),
        name="norm",
    )(where, base, there, gain)


def pack_kernel(*refs):
    copies = [pltpu.make_async_copy(refs[i], refs[4 + i], refs[8].at[i]) for i in range(3)]
    for copy in copies:
        copy.start()
    for copy in copies:
        copy.wait()
    out_ref, (latent_ref, ids_ref, weights_ref, rows) = refs[3], refs[4:8]
    tokens = out_ref.shape[0]
    rows[...] = jnp.zeros_like(rows)
    rows[0:TOP] = ids_ref[...].astype(jnp.float32)
    rows[TOP : 2 * TOP] = weights_ref[...]
    row = lax.broadcasted_iota(jnp.int32, (tokens, tokens), 0)
    same = (row == lax.broadcasted_iota(jnp.int32, (tokens, tokens), 1)).astype(jnp.float32).astype(jnp.bfloat16)
    every = jnp.concatenate([latent_ref[...], rows[...].astype(jnp.bfloat16)], axis=0)
    turned = lax.dot_general(same, every, (((1,), (1,)), ((), ())), preferred_element_type=jnp.float32)
    out_ref[...] = turned.astype(jnp.bfloat16)


def pack(latent, expert_ids, route_weights):
    local_rows, base = latent.shape
    arrays = (latent.T, expert_ids.T, route_weights.T)
    return pl.pallas_call(
        pack_kernel,
        in_specs=[pl.BlockSpec(memory_space=pltpu.HBM)] * 3,
        out_specs=pl.BlockSpec(memory_space=pltpu.VMEM),
        scratch_shapes=[pltpu.VMEM(x.shape, x.dtype) for x in arrays]
        + [pltpu.VMEM((WIDE - base, local_rows), jnp.float32), pltpu.SemaphoreType.DMA((3,))],
        out_shape=pltpu.VMEM((local_rows, WIDE), jnp.bfloat16),
        compiler_params=pltpu.CompilerParams(vmem_limit_bytes=4 * MIB),
        name="pack",
    )(*(pltpu.with_memory_space_constraint(x, pltpu.HBM) for x in arrays))


def expert_hidden(rows, gate, up):
    by_columns = (((1,), (1,)), ((), ()))
    gate = lax.dot_general(gate, rows, by_columns, preferred_element_type=jnp.float32)
    upper = lax.dot_general(up, rows, by_columns, preferred_element_type=jnp.float32)
    return (gate / (1.0 + jnp.exp(-gate)) * upper).astype(jnp.bfloat16)


def expert_down(hidden, down):
    by_rows = (((0,), (0,)), ((), ()))
    return lax.dot_general(hidden, down, by_rows, preferred_element_type=jnp.float32).astype(jnp.bfloat16)


def plain_kernel(where, rows_ref, gate_ref, up_ref, down_ref, out_ref):
    out_ref[0] = expert_down(expert_hidden(rows_ref[0], gate_ref[0], up_ref[0]), down_ref[0])


def fused_kernel(count, where, *refs):
    at = 2 * count
    blocks, combine_ref, weights = refs[:at], refs[at], refs[at + 1 : at + 4]
    near, far = refs[at + 4 : at + 4 + count], refs[at + 4 + count : at + 4 + 2 * count]
    at += 4 + 2 * count
    picked, buffer, sems = refs[at : at + 3]
    here = picked.shape[0]
    slots, units, width = buffer.shape
    half = width // 2
    side = where[1]
    columns = [pl.ds(pl.multiple_of(turned * half, half), half) for turned in (side, 1 - side)]
    piece = units // PIECES
    middle = count // 2
    by_rows = (((0,), (0,)), ((), ()))

    def copies(expert, w):
        slot = lax.rem(3 * expert + w, slots)
        for i in range(PIECES):
            rows = pl.ds(i * piece, piece)
            yield pltpu.make_async_copy(weights[w].at[expert, rows], buffer.at[slot, rows], sems.at[slot, i])

    def start(expert, w):
        for copy in copies(expert, w):
            copy.start()

    def arrived(expert, w):
        for copy in copies(expert, w):
            copy.wait()
        return buffer[lax.rem(3 * expert + w, slots)]

    for i in range(slots):
        start(i // 3, i % 3)

    for c in range(count):
        pick = (combine_ref[c].astype(jnp.float32) > 0).astype(jnp.float32).astype(jnp.bfloat16)
        for h in range(2):
            block = blocks[2 * c + h][...]
            rows = lax.dot_general(pick, block, by_rows, preferred_element_type=jnp.float32).astype(jnp.bfloat16)
            for e in range(here):
                picked[e, c * SLOTS : (c + 1) * SLOTS, columns[h]] = rows[e * SLOTS : (e + 1) * SLOTS]

    def work(expert, _):
        hidden = expert_hidden(picked[expert], arrived(expert, 0), arrived(expert, 1))

        @pl.when(expert + slots // 3 < here)
        def _():
            start(expert + slots // 3, 1)
            start(expert + slots // 3, 2)

        picked[expert] = expert_down(hidden, arrived(expert, 2))

        @pl.when(expert + slots // 3 + 1 < here)
        def _():
            start(expert + slots // 3 + 1, 0)

        return 0

    lax.fori_loop(0, here, work, 0)

    for c in [middle] + list(range(middle)) + list(range(middle + 1, count)):
        for h, outs in ((1, far), (0, near)):
            rows = jnp.concatenate([picked[e, c * SLOTS : (c + 1) * SLOTS, columns[h]] for e in range(here)], axis=0)
            outs[c][...] = jnp.dot(combine_ref[c], rows, preferred_element_type=jnp.float32).astype(jnp.bfloat16)


def expert_specs(w_gate):
    hidden, width = w_gate.shape[1:]
    return [pl.BlockSpec((1, hidden, width), lambda e, where: (e, 0, 0))] * 3


def experts_plain(where, picked, w_gate, w_up, w_down):
    here, rows, width = picked.shape
    rows_spec = pl.BlockSpec((1, rows, width), lambda e, where: (e, 0, 0))
    return pl.pallas_call(
        plain_kernel,
        grid_spec=pltpu.PrefetchScalarGridSpec(
            num_scalar_prefetch=1,
            grid=(here,),
            in_specs=[rows_spec] + expert_specs(w_gate),
            out_specs=rows_spec,
        ),
        out_shape=jax.ShapeDtypeStruct(picked.shape, jnp.bfloat16),
        compiler_params=pltpu.CompilerParams(vmem_limit_bytes=VMEM_LIMIT),
        name="experts",
    )(where, picked, w_gate, w_up, w_down)


def experts_fused(where, found, combine, w_gate, w_up, w_down):
    count, local = len(found), found[0][0].shape[0]
    here, units, width = w_gate.shape
    rows = count * SLOTS
    whole = pl.BlockSpec(memory_space=pltpu.VMEM)
    outs = pl.pallas_call(
        functools.partial(fused_kernel, count),
        in_specs=[pl.BlockSpec(memory_space=pltpu.SMEM)]
        + [whole] * (2 * count + 1)
        + [pl.BlockSpec(memory_space=pltpu.HBM)] * 3,
        out_specs=[whole] * (2 * count),
        scratch_shapes=[pltpu.VMEM((here, rows, width), jnp.bfloat16)]
        + [pltpu.VMEM((HELD, units, width), jnp.bfloat16), pltpu.SemaphoreType.DMA((HELD, PIECES))],
        out_shape=[pltpu.VMEM((local, width // 2), jnp.bfloat16)] * (2 * count),
        compiler_params=pltpu.CompilerParams(vmem_limit_bytes=29 * MIB),
        name="experts",
    )(where, *(x for block in found for x in block), combine,
      *(pltpu.with_memory_space_constraint(w, pltpu.HBM) for w in (w_gate, w_up, w_down)))
    return outs[:count], outs[count:]


def body(
    queries,
    latent,
    residual,
    seg_lengths,
    span_order,
    expert_ids,
    route_weights,
    kv_up,
    out_proj,
    norm_gain,
    w_gate,
    w_up,
    w_down,
):
    local_rows, width = residual.shape
    span = local_rows // 2
    count = lax.axis_size("ctx")
    here = EXPERTS // count
    me, side = lax.axis_index("ctx"), lax.axis_index("exp")
    where = jnp.stack([me, side]).astype(jnp.int32)

    base = latent.shape[1]
    w_gate, w_up = w_gate.transpose(0, 2, 1), w_up.transpose(0, 2, 1)
    packed = pack(latent, expert_ids, route_weights)
    few = count <= FEW
    scalars = lambda *arrays: jnp.concatenate([where, sources_of(me, side, count), *arrays])
    beside = [(scalars, (span_order, seg_lengths)), (lambda gain: gain.reshape(1, width), (norm_gain,))]
    found, (info, gain) = gather(packed, count, beside)
    partial, summand = attend(info, found, queries, kv_up, out_proj, residual, count)
    def place_rows(*blocks):
        if few:
            return route(where, blocks, here)
        facts = jnp.stack(blocks)[:, :, base : base + 2 * TOP].astype(jnp.float32)
        own = (me * here + jnp.arange(here, dtype=jnp.int32)).astype(jnp.float32)
        hit = facts[:, :, :TOP, None] == own
        hot = jnp.any(hit, axis=2)
        share = jnp.sum(jnp.where(hit, facts[:, :, TOP:, None], 0.0), axis=2)
        token = jnp.arange(local_rows, dtype=jnp.int32)
        before = (token[:, None] > token[None, :]).astype(jnp.bfloat16)
        rank = jnp.einsum("tu,cue->cte", before, hot.astype(jnp.bfloat16), preferred_element_type=jnp.float32)
        slot = jnp.arange(SLOTS, dtype=jnp.int32).astype(jnp.float32)
        combine = jnp.where(rank[:, :, :, None] == slot, share[:, :, :, None], 0.0)
        return combine.astype(jnp.bfloat16).reshape(count, local_rows, here * SLOTS)

    there = swap(partial)
    blocks, _ = lax.optimization_barrier((tuple(found), partial))
    combine, there = lax.optimization_barrier((place_rows(*blocks), there))
    middle, *normed = norm(where, summand, there, gain)
    got = gather_columns(*normed, count)
    if few:
        mixture = reduce(experts_fused(where, got, combine, w_gate, w_up, w_down), count)
    else:
        pick = (combine > 0).astype(jnp.bfloat16)
        near, far = (jnp.stack(x) for x in zip(*got))
        rows = jnp.concatenate([jnp.where(side == 0, near, far), jnp.where(side == 0, far, near)], axis=2)
        picked = jnp.einsum("cts,ctd->csd", pick, rows, preferred_element_type=jnp.float32).astype(jnp.bfloat16)
        picked = picked.reshape(count, here, SLOTS, width).transpose(1, 0, 2, 3).reshape(here, count * SLOTS, width)
        result = experts_plain(where, picked, w_gate, w_up, w_down)
        result = result.reshape(here, count, SLOTS, width).transpose(1, 0, 2, 3).reshape(count, here * SLOTS, width)
        total = jnp.einsum("cts,csd->ctd", combine, result, preferred_element_type=jnp.float32).astype(jnp.bfloat16)
        left, right = jnp.split(total, 2, axis=2)
        both = summed([jnp.where(side == 0, left, right), swap(jnp.where(side == 0, right, left))])
        mixture = lax.psum_scatter(both.astype(jnp.bfloat16), "ctx").astype(jnp.float32)
    return (middle.astype(jnp.float32) + mixture).astype(jnp.bfloat16)


def solution(mesh):
    in_specs = (
        P(("groups", "ctx"), "exp"),
        P(("groups", "ctx"), None),
        P(("groups", "ctx"), None),
        P("groups"),
        P("groups"),
        P(("groups", "ctx"), None),
        P(("groups", "ctx"), None),
        P(None, "exp"),
        P("exp", None),
        P(),
        P("ctx", None, "exp"),
        P("ctx", None, "exp"),
        P("ctx", "exp", None),
    )
    out_specs = P(("groups", "ctx"), "exp")
    return jax.shard_map(body, mesh=mesh, in_specs=in_specs, out_specs=out_specs, check_vma=False)
```

```python
import functools
import math

import jax
import jax.numpy as jnp
import numpy as np
from jax import lax
from jax.experimental import pallas as pl
from jax.experimental.pallas import tpu as pltpu
from jax.sharding import PartitionSpec as P

NOPE = 128
ROPE = 64
VHEAD = 128
LAT = 512
EXPERTS = 64
TOP = 6
SLOTS = 16
WIDE = 640
MIB = 1024 * 1024
VMEM_LIMIT = 50 * MIB
HELD = 7
PIECES = 2
SWAP = [(0, 1), (1, 0)]
FEW = 8


def cycle_of(count):
    fast = 2 ** (int(math.log2(count)) // 2)
    slow = count // fast
    cycle = [0]
    for i in range(slow):
        columns = range(1, fast)
        cycle += [i * fast + j for j in (columns if i % 2 == 0 else reversed(columns))]
    return cycle + [i * fast for i in reversed(range(1, slow))]


def swap(value):
    return lax.ppermute(value, "exp", SWAP)


def turn(value, count, cross=False):
    cycle = cycle_of(count)
    pairs = []
    for p in range(count):
        for core, ahead in ((0, 1), (1, -1)):
            pairs.append((cycle[p] * 2 + core, cycle[(p + ahead) % count] * 2 + (core ^ int(cross))))
    return lax.ppermute(value, ("ctx", "exp"), pairs)


def summed(pieces):
    total = pieces[0].astype(jnp.float32)
    for piece in pieces[1:]:
        total = total + piece.astype(jnp.float32)
    return total


def sources_of(me, side, count):
    if count > FEW:
        return jnp.arange(count, dtype=jnp.int32)
    cycle = cycle_of(count)
    middle = count // 2
    table = np.zeros((2 * count, count), np.int32)
    for p in range(count):
        for core, sign in ((0, 1), (1, -1)):
            ways = [sign * d for d in range(middle + 1)] + [-sign * d for d in range(1, middle)]
            table[cycle[p] * 2 + core] = [cycle[(p - way) % count] for way in ways]
    return lax.dynamic_index_in_dim(jnp.asarray(table), me * 2 + side, keepdims=False)


def gather(block, count, beside=()):
    if count > FEW:
        return list(lax.all_gather(block, "ctx")), [run(*arguments) for run, arguments in beside]
    middle = count // 2
    cycle = cycle_of(count)
    found, other, made = [block], [()], []
    opposite = lax.ppermute(block, "ctx", [(cycle[p], cycle[(p + middle) % count]) for p in range(count)])
    for d in range(1, middle):
        arrived, extra = turn(found[-1], count), ()
        if len(beside) >= d:
            run, arguments = beside[d - 1]
            extra = run(*lax.optimization_barrier((found[-1], arguments))[1])
        if d == 2:
            arrived, opposite = lax.optimization_barrier((arrived, opposite))
        arrived, other[-1], extra = lax.optimization_barrier((arrived, other[-1], extra))
        made.append(extra)
        found.append(arrived)
        other.append(swap(arrived))
    return found + [opposite] + other[1:], made[: len(beside)]


def gather_columns(near, far, count):
    if count > FEW:
        return list(zip(lax.all_gather(near, "ctx"), lax.all_gather(far, "ctx")))
    middle = count // 2
    found, other = {0: [near], 1: [far]}, {0: [()], 1: [()]}
    for d in range(1, middle + 1):
        for stream in (0, 1) if d < middle else (0,):
            arrived = turn(found[stream][-1], count)
            arrived, other[stream][-1] = lax.optimization_barrier((arrived, other[stream][-1]))
            found[stream].append(arrived)
            other[stream].append(swap(arrived))
    here = [(found[0][d], found[1][d]) for d in range(middle)]
    there = [(other[1][d], other[0][d]) for d in range(1, middle)]
    return here + [(found[0][middle], other[0][middle])] + there


def reduce(parts, count):
    middle = count // 2
    given = [swap(parts[1][middle]), swap(parts[0][middle - 1])]
    running = [None, None]
    for d in range(middle, 0, -1):
        for stream in (0, 1) if d < middle else (0,):
            place = middle + d if d < middle else middle
            later = parts[1 - stream][d - 1] if d > 1 or stream == 0 else ()
            pieces = [parts[stream][place], given[stream]]
            if running[stream] is not None:
                running[stream], later = lax.optimization_barrier((running[stream], later))
                pieces.append(running[stream])
            running[stream] = turn(summed(pieces).astype(jnp.bfloat16), count, cross=d == 1 and stream == 1)
            if d > 1 or stream == 0:
                given[stream] = swap(later)
    return summed([parts[0][0], given[0], *running])


def attend_kernel(count, blocks, heads, info, *refs):
    latents, up_ref, refs = refs[: len(refs) - 13], refs[len(refs) - 13], refs[len(refs) - 12 :]
    wanted, (out_ref, base_ref) = refs[:3], refs[3:5]
    held, sems, (m_ref, l_ref, acc_ref) = refs[5:8], refs[8], refs[9:12]
    q_ref, proj_ref, residual_ref = held
    copies = [pltpu.make_async_copy(wanted[i], held[i], sems.at[i]) for i in range(3)]
    chunk = pl.program_id(0)
    sources = lambda c: info[2 + c]
    order = lambda j: info[2 + count + j]
    segs = info.shape[0] - 2 - 3 * count
    rows = q_ref.shape[0]
    span = rows // 2
    depth = q_ref.shape[1] // heads

    @pl.when(chunk == 0)
    def _():
        for copy in copies:
            copy.start()

    @pl.when(chunk == 0)
    def _():
        m_ref[...] = jnp.full_like(m_ref, -1e30)
        l_ref[...] = jnp.zeros_like(l_ref)
        acc_ref[...] = jnp.zeros_like(acc_ref)

    row = lax.broadcasted_iota(jnp.int32, (rows, 1), 0)
    first = order(2 * info[0]) * span
    second = order(2 * info[0] + 1) * span
    qpos = jnp.where(row < span, first + row, second + row - span)
    low = jnp.zeros((rows, 1), jnp.int32)
    start = jnp.int32(0)
    for m in range(segs):
        low = jnp.where(qpos >= start, start, low)
        start = start + info[2 + 3 * count + m]
    keys = blocks * rows
    lane = lax.broadcasted_iota(jnp.int32, (1, keys), 1)
    which = lane // span
    kpos = lane % span
    for j in range(blocks):
        source = sources(chunk * blocks + j)
        for i in range(2):
            kpos = jnp.where(which == 2 * j + i, order(2 * source + i) * span + lane % span, kpos)
    visible = (kpos >= low) & (kpos <= qpos)

    lat = jnp.concatenate([ref[...].reshape(-1, WIDE) for ref in latents], axis=0)

    @pl.when(chunk == 0)
    def _():
        copies[0].wait()

    keyval = jnp.dot(lat[:, :LAT], up_ref[...], preferred_element_type=jnp.float32).astype(jnp.bfloat16)
    rope = lat[:, LAT : LAT + ROPE]
    scale = 1.0 / math.sqrt(NOPE + ROPE)
    for h in range(heads):
        base = h * (NOPE + VHEAD)
        key = jnp.concatenate([keyval[:, base : base + NOPE], rope], axis=1)
        scores = lax.dot_general(q_ref[:, h * depth : (h + 1) * depth], key, (((1,), (1,)), ((), ())), preferred_element_type=jnp.float32)
        scores = jnp.where(visible, scores * scale, -1e30)
        best = m_ref[h]
        fresh = jnp.maximum(best, jnp.max(scores, axis=1, keepdims=True))
        weights = jnp.where(visible, jnp.exp(scores - fresh), 0.0)
        shrink = jnp.exp(best - fresh)
        m_ref[h] = fresh
        l_ref[h] = l_ref[h] * shrink + jnp.sum(weights, axis=1, keepdims=True)
        mixed = jnp.dot(
            weights.astype(jnp.bfloat16), keyval[:, base + NOPE : base + NOPE + VHEAD], preferred_element_type=jnp.float32
        )
        acc_ref[h] = acc_ref[h] * shrink + mixed

    @pl.when(chunk == pl.num_programs(0) - 1)
    def _():
        attended = [(acc_ref[h] / l_ref[h]).astype(jnp.bfloat16) for h in range(heads)]
        copies[1].wait()
        copies[2].wait()
        out = jnp.dot(jnp.concatenate(attended, axis=1), proj_ref[...], preferred_element_type=jnp.float32)
        out = out.astype(jnp.bfloat16)
        out_ref[...] = out
        base_ref[...] = residual_ref[...].astype(jnp.float32) + out.astype(jnp.float32)


def attend(info, found, queries, kv_up, out_proj, residual, count):
    rows, width = residual.shape
    heads = kv_up.shape[1] // (NOPE + VHEAD)
    blocks = math.gcd(count, 8)
    whole = pl.BlockSpec(memory_space=pltpu.VMEM)
    if blocks == count:
        latents, lat_spec = found, whole
    else:
        latents, lat_spec = [jnp.stack(found)], pl.BlockSpec((blocks, rows, WIDE), lambda i, *_: (i, 0, 0))
    wanted = (queries, out_proj, residual)
    return pl.pallas_call(
        functools.partial(attend_kernel, count, blocks, heads),
        grid_spec=pltpu.PrefetchScalarGridSpec(
            num_scalar_prefetch=1,
            grid=(count // blocks,),
            in_specs=[lat_spec] * len(latents) + [whole] + [pl.BlockSpec(memory_space=pltpu.HBM)] * 3,
            out_specs=[whole, whole],
            scratch_shapes=[pltpu.VMEM(x.shape, x.dtype) for x in wanted]
            + [
                pltpu.SemaphoreType.DMA((3,)),
                pltpu.VMEM((heads, rows, 1), jnp.float32),
                pltpu.VMEM((heads, rows, 1), jnp.float32),
                pltpu.VMEM((heads, rows, VHEAD), jnp.float32),
            ],
        ),
        out_shape=[pltpu.VMEM((rows, width), jnp.bfloat16), pltpu.VMEM((rows, width), jnp.float32)],
        compiler_params=pltpu.CompilerParams(vmem_limit_bytes=28 * MIB),
        name="attend",
    )(info, *latents, kv_up, *(pltpu.with_memory_space_constraint(x, pltpu.HBM) for x in wanted))


def stage_kernel(source, out, sem):
    copy = pltpu.make_async_copy(source, out, sem)
    copy.start()
    copy.wait()


def stage(x):
    return pl.pallas_call(
        stage_kernel,
        in_specs=[pl.BlockSpec(memory_space=pltpu.HBM)],
        out_specs=pl.BlockSpec(memory_space=pltpu.VMEM),
        scratch_shapes=[pltpu.SemaphoreType.DMA],
        out_shape=pltpu.VMEM(x.shape, x.dtype),
        compiler_params=pltpu.CompilerParams(vmem_limit_bytes=2 * MIB),
        name="stage",
    )(pltpu.with_memory_space_constraint(x, pltpu.HBM))


def route_kernel(count, where, *refs):
    blocks, out_ref = refs[:count], refs[count]
    _, rows, width = out_ref.shape
    here = width // SLOTS
    lane = lax.broadcasted_iota(jnp.int32, (rows, width), 1)
    own = (where[0] * here + lane // SLOTS).astype(jnp.float32)
    slot = (lane % SLOTS).astype(jnp.float32)
    first = lax.broadcasted_iota(jnp.int32, (rows, rows), 0)
    before = (first > lax.broadcasted_iota(jnp.int32, (rows, rows), 1)).astype(jnp.float32).astype(jnp.bfloat16)
    for c in range(count):
        facts = blocks[c][:, LAT:].astype(jnp.float32)
        hot, share = jnp.zeros((rows, width), jnp.float32), jnp.zeros((rows, width), jnp.float32)
        for k in range(TOP):
            hit = facts[:, ROPE + k : ROPE + k + 1] == own
            hot = jnp.where(hit, 1.0, hot)
            share = jnp.where(hit, facts[:, ROPE + TOP + k : ROPE + TOP + k + 1], share)
        rank = jnp.dot(before, hot.astype(jnp.bfloat16), preferred_element_type=jnp.float32)
        out_ref[c] = jnp.where(rank == slot, share, 0.0).astype(jnp.bfloat16)


def route(where, found, here):
    count, (rows, _) = len(found), found[0].shape
    whole = pl.BlockSpec(memory_space=pltpu.VMEM)
    return pl.pallas_call(
        functools.partial(route_kernel, count),
        in_specs=[pl.BlockSpec(memory_space=pltpu.SMEM)] + [whole] * count,
        out_specs=whole,
        out_shape=pltpu.VMEM((count, rows, here * SLOTS), jnp.bfloat16),
        compiler_params=pltpu.CompilerParams(vmem_limit_bytes=8 * MIB),
        name="route",
    )(where, *found)


def norm_kernel(where, base_ref, there_ref, gain_ref, middle_ref, near_ref, far_ref):
    half = middle_ref.shape[1]
    middle = (base_ref[...] + there_ref[...].astype(jnp.float32)).astype(jnp.bfloat16)
    wide = middle.astype(jnp.float32)
    inverse = lax.rsqrt(jnp.mean(wide * wide, axis=1, keepdims=True) + 1e-06)
    normed = wide * inverse * gain_ref[...].astype(jnp.float32)
    first = where[1] == 0
    near_ref[...] = jnp.where(first, normed[:, :half], normed[:, half:]).astype(jnp.bfloat16)
    far_ref[...] = jnp.where(first, normed[:, half:], normed[:, :half]).astype(jnp.bfloat16)
    middle_ref[...] = jnp.where(first, wide[:, :half], wide[:, half:]).astype(jnp.bfloat16)


def norm(where, base, there, gain):
    rows, width = base.shape
    whole = pl.BlockSpec(memory_space=pltpu.VMEM)
    return pl.pallas_call(
        norm_kernel,
        in_specs=[pl.BlockSpec(memory_space=pltpu.SMEM)] + [whole] * 3,
        out_specs=[whole] * 3,
        out_shape=[pltpu.VMEM((rows, width // 2), jnp.bfloat16)] * 3,
        compiler_params=pltpu.CompilerParams(vmem_limit_bytes=12 * MIB),
        name="norm",
    )(where, base, there, gain)


def pack_kernel(*refs):
    copies = [pltpu.make_async_copy(refs[i], refs[4 + i], refs[8].at[i]) for i in range(3)]
    for copy in copies:
        copy.start()
    for copy in copies:
        copy.wait()
    out_ref, (latent_ref, ids_ref, weights_ref, rows) = refs[3], refs[4:8]
    tokens = out_ref.shape[0]
    rows[...] = jnp.zeros_like(rows)
    rows[0:TOP] = ids_ref[...].astype(jnp.float32)
    rows[TOP : 2 * TOP] = weights_ref[...]
    row = lax.broadcasted_iota(jnp.int32, (tokens, tokens), 0)
    same = (row == lax.broadcasted_iota(jnp.int32, (tokens, tokens), 1)).astype(jnp.float32).astype(jnp.bfloat16)
    every = jnp.concatenate([latent_ref[...], rows[...].astype(jnp.bfloat16)], axis=0)
    turned = lax.dot_general(same, every, (((1,), (1,)), ((), ())), preferred_element_type=jnp.float32)
    out_ref[...] = turned.astype(jnp.bfloat16)


def pack(latent, expert_ids, route_weights):
    local_rows, base = latent.shape
    arrays = (latent.T, expert_ids.T, route_weights.T)
    return pl.pallas_call(
        pack_kernel,
        in_specs=[pl.BlockSpec(memory_space=pltpu.HBM)] * 3,
        out_specs=pl.BlockSpec(memory_space=pltpu.VMEM),
        scratch_shapes=[pltpu.VMEM(x.shape, x.dtype) for x in arrays]
        + [pltpu.VMEM((WIDE - base, local_rows), jnp.float32), pltpu.SemaphoreType.DMA((3,))],
        out_shape=pltpu.VMEM((local_rows, WIDE), jnp.bfloat16),
        compiler_params=pltpu.CompilerParams(vmem_limit_bytes=4 * MIB),
        name="pack",
    )(*(pltpu.with_memory_space_constraint(x, pltpu.HBM) for x in arrays))


def expert_hidden(rows, gate, up):
    by_columns = (((1,), (1,)), ((), ()))
    gate = lax.dot_general(gate, rows, by_columns, preferred_element_type=jnp.float32)
    upper = lax.dot_general(up, rows, by_columns, preferred_element_type=jnp.float32)
    return (gate / (1.0 + jnp.exp(-gate)) * upper).astype(jnp.bfloat16)


def expert_down(hidden, down):
    by_rows = (((0,), (0,)), ((), ()))
    return lax.dot_general(hidden, down, by_rows, preferred_element_type=jnp.float32).astype(jnp.bfloat16)


def plain_kernel(where, rows_ref, gate_ref, up_ref, down_ref, out_ref):
    out_ref[0] = expert_down(expert_hidden(rows_ref[0], gate_ref[0], up_ref[0]), down_ref[0])


def fused_kernel(count, where, *refs):
    at = 2 * count
    blocks, combine_ref, weights = refs[:at], refs[at], refs[at + 1 : at + 4]
    near, far = refs[at + 4 : at + 4 + count], refs[at + 4 + count : at + 4 + 2 * count]
    at += 4 + 2 * count
    picked, buffer, sems = refs[at : at + 3]
    here = picked.shape[0]
    slots, units, width = buffer.shape
    half = width // 2
    side = where[1]
    columns = [pl.ds(pl.multiple_of(turned * half, half), half) for turned in (side, 1 - side)]
    piece = units // PIECES
    middle = count // 2
    by_rows = (((0,), (0,)), ((), ()))

    def copies(expert, w):
        slot = lax.rem(3 * expert + w, slots)
        for i in range(PIECES):
            rows = pl.ds(i * piece, piece)
            yield pltpu.make_async_copy(weights[w].at[expert, rows], buffer.at[slot, rows], sems.at[slot, i])

    def start(expert, w):
        for copy in copies(expert, w):
            copy.start()

    def arrived(expert, w):
        for copy in copies(expert, w):
            copy.wait()
        return buffer[lax.rem(3 * expert + w, slots)]

    for i in range(slots):
        start(i // 3, i % 3)

    for c in range(count):
        pick = (combine_ref[c].astype(jnp.float32) > 0).astype(jnp.float32).astype(jnp.bfloat16)
        for h in range(2):
            block = blocks[2 * c + h][...]
            rows = lax.dot_general(pick, block, by_rows, preferred_element_type=jnp.float32).astype(jnp.bfloat16)
            for e in range(here):
                picked[e, c * SLOTS : (c + 1) * SLOTS, columns[h]] = rows[e * SLOTS : (e + 1) * SLOTS]

    def work(expert, _):
        hidden = expert_hidden(picked[expert], arrived(expert, 0), arrived(expert, 1))

        @pl.when(expert + slots // 3 < here)
        def _():
            start(expert + slots // 3, 1)
            start(expert + slots // 3, 2)

        picked[expert] = expert_down(hidden, arrived(expert, 2))

        @pl.when(expert + slots // 3 + 1 < here)
        def _():
            start(expert + slots // 3 + 1, 0)

        return 0

    lax.fori_loop(0, here, work, 0)

    for c in [middle] + list(range(middle)) + list(range(middle + 1, count)):
        for h, outs in ((1, far), (0, near)):
            rows = jnp.concatenate([picked[e, c * SLOTS : (c + 1) * SLOTS, columns[h]] for e in range(here)], axis=0)
            outs[c][...] = jnp.dot(combine_ref[c], rows, preferred_element_type=jnp.float32).astype(jnp.bfloat16)


def expert_specs(w_gate):
    hidden, width = w_gate.shape[1:]
    return [pl.BlockSpec((1, hidden, width), lambda e, where: (e, 0, 0))] * 3


def experts_plain(where, picked, w_gate, w_up, w_down):
    here, rows, width = picked.shape
    rows_spec = pl.BlockSpec((1, rows, width), lambda e, where: (e, 0, 0))
    return pl.pallas_call(
        plain_kernel,
        grid_spec=pltpu.PrefetchScalarGridSpec(
            num_scalar_prefetch=1,
            grid=(here,),
            in_specs=[rows_spec] + expert_specs(w_gate),
            out_specs=rows_spec,
        ),
        out_shape=jax.ShapeDtypeStruct(picked.shape, jnp.bfloat16),
        compiler_params=pltpu.CompilerParams(vmem_limit_bytes=VMEM_LIMIT),
        name="experts",
    )(where, picked, w_gate, w_up, w_down)


def experts_fused(where, found, combine, w_gate, w_up, w_down):
    count, local = len(found), found[0][0].shape[0]
    here, units, width = w_gate.shape
    rows = count * SLOTS
    whole = pl.BlockSpec(memory_space=pltpu.VMEM)
    outs = pl.pallas_call(
        functools.partial(fused_kernel, count),
        in_specs=[pl.BlockSpec(memory_space=pltpu.SMEM)]
        + [whole] * (2 * count + 1)
        + [pl.BlockSpec(memory_space=pltpu.HBM)] * 3,
        out_specs=[whole] * (2 * count),
        scratch_shapes=[pltpu.VMEM((here, rows, width), jnp.bfloat16)]
        + [pltpu.VMEM((HELD, units, width), jnp.bfloat16), pltpu.SemaphoreType.DMA((HELD, PIECES))],
        out_shape=[pltpu.VMEM((local, width // 2), jnp.bfloat16)] * (2 * count),
        compiler_params=pltpu.CompilerParams(vmem_limit_bytes=29 * MIB),
        name="experts",
    )(where, *(x for block in found for x in block), combine,
      *(pltpu.with_memory_space_constraint(w, pltpu.HBM) for w in (w_gate, w_up, w_down)))
    return outs[:count], outs[count:]


def body(
    queries,
    latent,
    residual,
    seg_lengths,
    span_order,
    expert_ids,
    route_weights,
    kv_up,
    out_proj,
    norm_gain,
    w_gate,
    w_up,
    w_down,
):
    local_rows, width = residual.shape
    span = local_rows // 2
    count = lax.axis_size("ctx")
    here = EXPERTS // count
    me, side = lax.axis_index("ctx"), lax.axis_index("exp")
    where = jnp.stack([me, side]).astype(jnp.int32)

    base = latent.shape[1]
    w_gate, w_up = w_gate.transpose(0, 2, 1), w_up.transpose(0, 2, 1)
    packed = pack(latent, expert_ids, route_weights)
    few = count <= FEW
    scalars = lambda *arrays: jnp.concatenate([where, sources_of(me, side, count), *arrays])
    beside = [
        (scalars, (span_order, seg_lengths)),
        (lambda gain: gain.reshape(1, width), (norm_gain,)),
        (stage if few else lambda x: x, (kv_up,)),
    ]
    found, (info, gain, kv_up) = gather(packed, count, beside)
    partial, summand = attend(info, found, queries, kv_up, out_proj, residual, count)
    def place_rows(*blocks):
        if few:
            return route(where, blocks, here)
        facts = jnp.stack(blocks)[:, :, base : base + 2 * TOP].astype(jnp.float32)
        own = (me * here + jnp.arange(here, dtype=jnp.int32)).astype(jnp.float32)
        hit = facts[:, :, :TOP, None] == own
        hot = jnp.any(hit, axis=2)
        share = jnp.sum(jnp.where(hit, facts[:, :, TOP:, None], 0.0), axis=2)
        token = jnp.arange(local_rows, dtype=jnp.int32)
        before = (token[:, None] > token[None, :]).astype(jnp.bfloat16)
        rank = jnp.einsum("tu,cue->cte", before, hot.astype(jnp.bfloat16), preferred_element_type=jnp.float32)
        slot = jnp.arange(SLOTS, dtype=jnp.int32).astype(jnp.float32)
        combine = jnp.where(rank[:, :, :, None] == slot, share[:, :, :, None], 0.0)
        return combine.astype(jnp.bfloat16).reshape(count, local_rows, here * SLOTS)

    there = swap(partial)
    blocks, _ = lax.optimization_barrier((tuple(found), partial))
    combine, there = lax.optimization_barrier((place_rows(*blocks), there))
    middle, *normed = norm(where, summand, there, gain)
    got = gather_columns(*normed, count)
    if few:
        mixture = reduce(experts_fused(where, got, combine, w_gate, w_up, w_down), count)
    else:
        pick = (combine > 0).astype(jnp.bfloat16)
        near, far = (jnp.stack(x) for x in zip(*got))
        rows = jnp.concatenate([jnp.where(side == 0, near, far), jnp.where(side == 0, far, near)], axis=2)
        picked = jnp.einsum("cts,ctd->csd", pick, rows, preferred_element_type=jnp.float32).astype(jnp.bfloat16)
        picked = picked.reshape(count, here, SLOTS, width).transpose(1, 0, 2, 3).reshape(here, count * SLOTS, width)
        result = experts_plain(where, picked, w_gate, w_up, w_down)
        result = result.reshape(here, count, SLOTS, width).transpose(1, 0, 2, 3).reshape(count, here * SLOTS, width)
        total = jnp.einsum("cts,csd->ctd", combine, result, preferred_element_type=jnp.float32).astype(jnp.bfloat16)
        left, right = jnp.split(total, 2, axis=2)
        both = summed([jnp.where(side == 0, left, right), swap(jnp.where(side == 0, right, left))])
        mixture = lax.psum_scatter(both.astype(jnp.bfloat16), "ctx").astype(jnp.float32)
    return (middle.astype(jnp.float32) + mixture).astype(jnp.bfloat16)


def solution(mesh):
    in_specs = (
        P(("groups", "ctx"), "exp"),
        P(("groups", "ctx"), None),
        P(("groups", "ctx"), None),
        P("groups"),
        P("groups"),
        P(("groups", "ctx"), None),
        P(("groups", "ctx"), None),
        P(None, "exp"),
        P("exp", None),
        P(),
        P("ctx", None, "exp"),
        P("ctx", None, "exp"),
        P("ctx", "exp", None),
    )
    out_specs = P(("groups", "ctx"), "exp")
    return jax.shard_map(body, mesh=mesh, in_specs=in_specs, out_specs=out_specs, check_vma=False)
```

```python
import functools
import math

import jax
import jax.numpy as jnp
import numpy as np
from jax import lax
from jax.experimental import pallas as pl
from jax.experimental.pallas import tpu as pltpu
from jax.sharding import PartitionSpec as P

NOPE = 128
ROPE = 64
VHEAD = 128
LAT = 512
EXPERTS = 64
TOP = 6
SLOTS = 16
WIDE = 640
MIB = 1024 * 1024
VMEM_LIMIT = 50 * MIB
HELD = 7
PIECES = 2
SWAP = [(0, 1), (1, 0)]
FEW = 8


def cycle_of(count):
    fast = 2 ** (int(math.log2(count)) // 2)
    slow = count // fast
    cycle = [0]
    for i in range(slow):
        columns = range(1, fast)
        cycle += [i * fast + j for j in (columns if i % 2 == 0 else reversed(columns))]
    return cycle + [i * fast for i in reversed(range(1, slow))]


def swap(value):
    return lax.ppermute(value, "exp", SWAP)


def turn(value, count, cross=False):
    cycle = cycle_of(count)
    pairs = []
    for p in range(count):
        for core, ahead in ((0, 1), (1, -1)):
            pairs.append((cycle[p] * 2 + core, cycle[(p + ahead) % count] * 2 + (core ^ int(cross))))
    return lax.ppermute(value, ("ctx", "exp"), pairs)


def summed(pieces):
    total = pieces[0].astype(jnp.float32)
    for piece in pieces[1:]:
        total = total + piece.astype(jnp.float32)
    return total


def sources_of(me, side, count):
    if count > FEW:
        return jnp.arange(count, dtype=jnp.int32)
    cycle = cycle_of(count)
    middle = count // 2
    table = np.zeros((2 * count, count), np.int32)
    for p in range(count):
        for core, sign in ((0, 1), (1, -1)):
            ways = [sign * d for d in range(middle + 1)] + [-sign * d for d in range(1, middle)]
            table[cycle[p] * 2 + core] = [cycle[(p - way) % count] for way in ways]
    return lax.dynamic_index_in_dim(jnp.asarray(table), me * 2 + side, keepdims=False)


def gather(block, count, beside=()):
    if count > FEW:
        return list(lax.all_gather(block, "ctx")), [run(*arguments) for run, arguments in beside]
    middle = count // 2
    found, other, made = [block], [()], []
    for d in range(1, middle + 1):
        arrived, extra = turn(found[-1], count), ()
        if len(beside) >= d:
            run, arguments = beside[d - 1]
            extra = run(*lax.optimization_barrier((found[-1], arguments))[1])
        arrived, other[-1], extra = lax.optimization_barrier((arrived, other[-1], extra))
        made.append(extra)
        found.append(arrived)
        if d < middle:
            other.append(swap(arrived))
    return found + other[1:], made[: len(beside)]


def gather_columns(near, far, count):
    if count > FEW:
        return list(zip(lax.all_gather(near, "ctx"), lax.all_gather(far, "ctx")))
    middle = count // 2
    found, other = {0: [near], 1: [far]}, {0: [()], 1: [()]}
    for d in range(1, middle + 1):
        for stream in (0, 1) if d < middle else (0,):
            arrived = turn(found[stream][-1], count)
            arrived, other[stream][-1] = lax.optimization_barrier((arrived, other[stream][-1]))
            found[stream].append(arrived)
            other[stream].append(swap(arrived))
    here = [(found[0][d], found[1][d]) for d in range(middle)]
    there = [(other[1][d], other[0][d]) for d in range(1, middle)]
    return here + [(found[0][middle], other[0][middle])] + there


def reduce(parts, count):
    middle = count // 2
    given = [swap(parts[1][middle]), swap(parts[0][middle - 1])]
    running = [None, None]
    for d in range(middle, 0, -1):
        for stream in (0, 1) if d < middle else (0,):
            place = middle + d if d < middle else middle
            later = parts[1 - stream][d - 1] if d > 1 or stream == 0 else ()
            pieces = [parts[stream][place], given[stream]]
            if running[stream] is not None:
                running[stream], later = lax.optimization_barrier((running[stream], later))
                pieces.append(running[stream])
            running[stream] = turn(summed(pieces).astype(jnp.bfloat16), count, cross=d == 1 and stream == 1)
            if d > 1 or stream == 0:
                given[stream] = swap(later)
    return summed([parts[0][0], given[0], *running])


def attend_kernel(count, blocks, heads, info, *refs):
    latents, up_ref, refs = refs[: len(refs) - 13], refs[len(refs) - 13], refs[len(refs) - 12 :]
    wanted, (out_ref, base_ref) = refs[:3], refs[3:5]
    held, sems, (m_ref, l_ref, acc_ref) = refs[5:8], refs[8], refs[9:12]
    q_ref, proj_ref, residual_ref = held
    copies = [pltpu.make_async_copy(wanted[i], held[i], sems.at[i]) for i in range(3)]
    chunk = pl.program_id(0)
    sources = lambda c: info[2 + c]
    order = lambda j: info[2 + count + j]
    segs = info.shape[0] - 2 - 3 * count
    rows = q_ref.shape[0]
    span = rows // 2
    depth = q_ref.shape[1] // heads

    @pl.when(chunk == 0)
    def _():
        for copy in copies:
            copy.start()

    @pl.when(chunk == 0)
    def _():
        m_ref[...] = jnp.full_like(m_ref, -1e30)
        l_ref[...] = jnp.zeros_like(l_ref)
        acc_ref[...] = jnp.zeros_like(acc_ref)

    row = lax.broadcasted_iota(jnp.int32, (rows, 1), 0)
    first = order(2 * info[0]) * span
    second = order(2 * info[0] + 1) * span
    qpos = jnp.where(row < span, first + row, second + row - span)
    low = jnp.zeros((rows, 1), jnp.int32)
    start = jnp.int32(0)
    for m in range(segs):
        low = jnp.where(qpos >= start, start, low)
        start = start + info[2 + 3 * count + m]
    keys = blocks * rows
    lane = lax.broadcasted_iota(jnp.int32, (1, keys), 1)
    which = lane // span
    kpos = lane % span
    for j in range(blocks):
        source = sources(chunk * blocks + j)
        for i in range(2):
            kpos = jnp.where(which == 2 * j + i, order(2 * source + i) * span + lane % span, kpos)
    visible = (kpos >= low) & (kpos <= qpos)

    lat = jnp.concatenate([ref[...].reshape(-1, WIDE) for ref in latents], axis=0)

    @pl.when(chunk == 0)
    def _():
        copies[0].wait()

    keyval = jnp.dot(lat[:, :LAT], up_ref[...], preferred_element_type=jnp.float32).astype(jnp.bfloat16)
    rope = lat[:, LAT : LAT + ROPE]
    scale = 1.0 / math.sqrt(NOPE + ROPE)
    for h in range(heads):
        base = h * (NOPE + VHEAD)
        key = jnp.concatenate([keyval[:, base : base + NOPE], rope], axis=1)
        scores = lax.dot_general(q_ref[:, h * depth : (h + 1) * depth], key, (((1,), (1,)), ((), ())), preferred_element_type=jnp.float32)
        scores = jnp.where(visible, scores * scale, -1e30)
        best = m_ref[h]
        fresh = jnp.maximum(best, jnp.max(scores, axis=1, keepdims=True))
        weights = jnp.where(visible, jnp.exp(scores - fresh), 0.0)
        shrink = jnp.exp(best - fresh)
        m_ref[h] = fresh
        l_ref[h] = l_ref[h] * shrink + jnp.sum(weights, axis=1, keepdims=True)
        mixed = jnp.dot(
            weights.astype(jnp.bfloat16), keyval[:, base + NOPE : base + NOPE + VHEAD], preferred_element_type=jnp.float32
        )
        acc_ref[h] = acc_ref[h] * shrink + mixed

    @pl.when(chunk == pl.num_programs(0) - 1)
    def _():
        attended = [(acc_ref[h] / l_ref[h]).astype(jnp.bfloat16) for h in range(heads)]
        copies[1].wait()
        copies[2].wait()
        out = jnp.dot(jnp.concatenate(attended, axis=1), proj_ref[...], preferred_element_type=jnp.float32)
        out = out.astype(jnp.bfloat16)
        out_ref[...] = out
        base_ref[...] = residual_ref[...].astype(jnp.float32) + out.astype(jnp.float32)


def attend(info, found, queries, kv_up, out_proj, residual, count):
    rows, width = residual.shape
    heads = kv_up.shape[1] // (NOPE + VHEAD)
    blocks = math.gcd(count, 8)
    whole = pl.BlockSpec(memory_space=pltpu.VMEM)
    if blocks == count:
        latents, lat_spec = [half for block in found for half in block], whole
    else:
        found = [jnp.concatenate(block, axis=0) for block in found]
        latents, lat_spec = [jnp.stack(found)], pl.BlockSpec((blocks, rows, WIDE), lambda i, *_: (i, 0, 0))
    wanted = (queries, out_proj, residual)
    return pl.pallas_call(
        functools.partial(attend_kernel, count, blocks, heads),
        grid_spec=pltpu.PrefetchScalarGridSpec(
            num_scalar_prefetch=1,
            grid=(count // blocks,),
            in_specs=[lat_spec] * len(latents) + [whole] + [pl.BlockSpec(memory_space=pltpu.HBM)] * 3,
            out_specs=[whole, whole],
            scratch_shapes=[pltpu.VMEM(x.shape, x.dtype) for x in wanted]
            + [
                pltpu.SemaphoreType.DMA((3,)),
                pltpu.VMEM((heads, rows, 1), jnp.float32),
                pltpu.VMEM((heads, rows, 1), jnp.float32),
                pltpu.VMEM((heads, rows, VHEAD), jnp.float32),
            ],
        ),
        out_shape=[pltpu.VMEM((rows, width), jnp.bfloat16), pltpu.VMEM((rows, width), jnp.float32)],
        compiler_params=pltpu.CompilerParams(vmem_limit_bytes=28 * MIB),
        name="attend",
    )(info, *latents, kv_up, *(pltpu.with_memory_space_constraint(x, pltpu.HBM) for x in wanted))


def stage_kernel(source, out, sem):
    copy = pltpu.make_async_copy(source, out, sem)
    copy.start()
    copy.wait()


def stage(x):
    return pl.pallas_call(
        stage_kernel,
        in_specs=[pl.BlockSpec(memory_space=pltpu.HBM)],
        out_specs=pl.BlockSpec(memory_space=pltpu.VMEM),
        scratch_shapes=[pltpu.SemaphoreType.DMA],
        out_shape=pltpu.VMEM(x.shape, x.dtype),
        compiler_params=pltpu.CompilerParams(vmem_limit_bytes=2 * MIB),
        name="stage",
    )(pltpu.with_memory_space_constraint(x, pltpu.HBM))


def route_kernel(count, where, *refs):
    blocks, out_ref = refs[: 2 * count], refs[2 * count]
    _, rows, width = out_ref.shape
    here = width // SLOTS
    lane = lax.broadcasted_iota(jnp.int32, (rows, width), 1)
    own = (where[0] * here + lane // SLOTS).astype(jnp.float32)
    slot = (lane % SLOTS).astype(jnp.float32)
    first = lax.broadcasted_iota(jnp.int32, (rows, rows), 0)
    before = (first > lax.broadcasted_iota(jnp.int32, (rows, rows), 1)).astype(jnp.float32).astype(jnp.bfloat16)
    for c in range(count):
        facts = jnp.concatenate([blocks[2 * c + i][:, LAT:].astype(jnp.float32) for i in range(2)], axis=0)
        hot, share = jnp.zeros((rows, width), jnp.float32), jnp.zeros((rows, width), jnp.float32)
        for k in range(TOP):
            hit = facts[:, ROPE + k : ROPE + k + 1] == own
            hot = jnp.where(hit, 1.0, hot)
            share = jnp.where(hit, facts[:, ROPE + TOP + k : ROPE + TOP + k + 1], share)
        rank = jnp.dot(before, hot.astype(jnp.bfloat16), preferred_element_type=jnp.float32)
        out_ref[c] = jnp.where(rank == slot, share, 0.0).astype(jnp.bfloat16)


def route(where, found, here):
    count, (span, _) = len(found), found[0][0].shape
    whole = pl.BlockSpec(memory_space=pltpu.VMEM)
    return pl.pallas_call(
        functools.partial(route_kernel, count),
        in_specs=[pl.BlockSpec(memory_space=pltpu.SMEM)] + [whole] * (2 * count),
        out_specs=whole,
        out_shape=pltpu.VMEM((count, 2 * span, here * SLOTS), jnp.bfloat16),
        compiler_params=pltpu.CompilerParams(vmem_limit_bytes=8 * MIB),
        name="route",
    )(where, *(half for block in found for half in block))


def norm_kernel(where, base_ref, there_ref, gain_ref, middle_ref, near_ref, far_ref):
    half = middle_ref.shape[1]
    middle = (base_ref[...] + there_ref[...].astype(jnp.float32)).astype(jnp.bfloat16)
    wide = middle.astype(jnp.float32)
    inverse = lax.rsqrt(jnp.mean(wide * wide, axis=1, keepdims=True) + 1e-06)
    normed = wide * inverse * gain_ref[...].astype(jnp.float32)
    first = where[1] == 0
    near_ref[...] = jnp.where(first, normed[:, :half], normed[:, half:]).astype(jnp.bfloat16)
    far_ref[...] = jnp.where(first, normed[:, half:], normed[:, :half]).astype(jnp.bfloat16)
    middle_ref[...] = jnp.where(first, wide[:, :half], wide[:, half:]).astype(jnp.bfloat16)


def norm(where, base, there, gain):
    rows, width = base.shape
    whole = pl.BlockSpec(memory_space=pltpu.VMEM)
    return pl.pallas_call(
        norm_kernel,
        in_specs=[pl.BlockSpec(memory_space=pltpu.SMEM)] + [whole] * 3,
        out_specs=[whole] * 3,
        out_shape=[pltpu.VMEM((rows, width // 2), jnp.bfloat16)] * 3,
        compiler_params=pltpu.CompilerParams(vmem_limit_bytes=12 * MIB),
        name="norm",
    )(where, base, there, gain)


def pack_kernel(*refs):
    copies = [pltpu.make_async_copy(refs[i], refs[5 + i], refs[9].at[i]) for i in range(3)]
    for copy in copies:
        copy.start()
    for copy in copies:
        copy.wait()
    top_ref, bottom_ref, latent_ref, ids_ref, weights_ref, rows = refs[3:9]
    span = top_ref.shape[0]
    tokens = 2 * span
    rows[...] = jnp.zeros_like(rows)
    rows[0:TOP] = ids_ref[...].astype(jnp.float32)
    rows[TOP : 2 * TOP] = weights_ref[...]
    row = lax.broadcasted_iota(jnp.int32, (tokens, tokens), 0)
    same = (row == lax.broadcasted_iota(jnp.int32, (tokens, tokens), 1)).astype(jnp.float32).astype(jnp.bfloat16)
    every = jnp.concatenate([latent_ref[...], rows[...].astype(jnp.bfloat16)], axis=0)
    turned = lax.dot_general(same, every, (((1,), (1,)), ((), ())), preferred_element_type=jnp.float32)
    top_ref[...] = turned[:span].astype(jnp.bfloat16)
    bottom_ref[...] = turned[span:].astype(jnp.bfloat16)


def pack(latent, expert_ids, route_weights):
    local_rows, base = latent.shape
    arrays = (latent.T, expert_ids.T, route_weights.T)
    return pl.pallas_call(
        pack_kernel,
        in_specs=[pl.BlockSpec(memory_space=pltpu.HBM)] * 3,
        out_specs=[pl.BlockSpec(memory_space=pltpu.VMEM)] * 2,
        scratch_shapes=[pltpu.VMEM(x.shape, x.dtype) for x in arrays]
        + [pltpu.VMEM((WIDE - base, local_rows), jnp.float32), pltpu.SemaphoreType.DMA((3,))],
        out_shape=[pltpu.VMEM((local_rows // 2, WIDE), jnp.bfloat16)] * 2,
        compiler_params=pltpu.CompilerParams(vmem_limit_bytes=4 * MIB),
        name="pack",
    )(*(pltpu.with_memory_space_constraint(x, pltpu.HBM) for x in arrays))


def expert_hidden(rows, gate, up):
    by_columns = (((1,), (1,)), ((), ()))
    gate = lax.dot_general(gate, rows, by_columns, preferred_element_type=jnp.float32)
    upper = lax.dot_general(up, rows, by_columns, preferred_element_type=jnp.float32)
    return (gate / (1.0 + jnp.exp(-gate)) * upper).astype(jnp.bfloat16)


def expert_down(hidden, down):
    by_rows = (((0,), (0,)), ((), ()))
    return lax.dot_general(hidden, down, by_rows, preferred_element_type=jnp.float32).astype(jnp.bfloat16)


def plain_kernel(where, rows_ref, gate_ref, up_ref, down_ref, out_ref):
    out_ref[0] = expert_down(expert_hidden(rows_ref[0], gate_ref[0], up_ref[0]), down_ref[0])


def fused_kernel(count, where, *refs):
    at = 2 * count
    blocks, combine_ref, weights = refs[:at], refs[at], refs[at + 1 : at + 4]
    near, far = refs[at + 4 : at + 4 + count], refs[at + 4 + count : at + 4 + 2 * count]
    at += 4 + 2 * count
    picked, buffer, sems = refs[at : at + 3]
    here = picked.shape[0]
    slots, units, width = buffer.shape
    half = width // 2
    side = where[1]
    columns = [pl.ds(pl.multiple_of(turned * half, half), half) for turned in (side, 1 - side)]
    piece = units // PIECES
    middle = count // 2
    by_rows = (((0,), (0,)), ((), ()))

    def copies(expert, w):
        slot = lax.rem(3 * expert + w, slots)
        for i in range(PIECES):
            rows = pl.ds(i * piece, piece)
            yield pltpu.make_async_copy(weights[w].at[expert, rows], buffer.at[slot, rows], sems.at[slot, i])

    def start(expert, w):
        for copy in copies(expert, w):
            copy.start()

    def arrived(expert, w):
        for copy in copies(expert, w):
            copy.wait()
        return buffer[lax.rem(3 * expert + w, slots)]

    for i in range(slots):
        start(i // 3, i % 3)

    for c in range(count):
        pick = (combine_ref[c].astype(jnp.float32) > 0).astype(jnp.float32).astype(jnp.bfloat16)
        for h in range(2):
            block = blocks[2 * c + h][...]
            rows = lax.dot_general(pick, block, by_rows, preferred_element_type=jnp.float32).astype(jnp.bfloat16)
            for e in range(here):
                picked[e, c * SLOTS : (c + 1) * SLOTS, columns[h]] = rows[e * SLOTS : (e + 1) * SLOTS]

    def work(expert, _):
        hidden = expert_hidden(picked[expert], arrived(expert, 0), arrived(expert, 1))

        @pl.when(expert + slots // 3 < here)
        def _():
            start(expert + slots // 3, 1)
            start(expert + slots // 3, 2)

        picked[expert] = expert_down(hidden, arrived(expert, 2))

        @pl.when(expert + slots // 3 + 1 < here)
        def _():
            start(expert + slots // 3 + 1, 0)

        return 0

    lax.fori_loop(0, here, work, 0)

    for c in [middle] + list(range(middle)) + list(range(middle + 1, count)):
        for h, outs in ((1, far), (0, near)):
            rows = jnp.concatenate([picked[e, c * SLOTS : (c + 1) * SLOTS, columns[h]] for e in range(here)], axis=0)
            outs[c][...] = jnp.dot(combine_ref[c], rows, preferred_element_type=jnp.float32).astype(jnp.bfloat16)


def expert_specs(w_gate):
    hidden, width = w_gate.shape[1:]
    return [pl.BlockSpec((1, hidden, width), lambda e, where: (e, 0, 0))] * 3


def experts_plain(where, picked, w_gate, w_up, w_down):
    here, rows, width = picked.shape
    rows_spec = pl.BlockSpec((1, rows, width), lambda e, where: (e, 0, 0))
    return pl.pallas_call(
        plain_kernel,
        grid_spec=pltpu.PrefetchScalarGridSpec(
            num_scalar_prefetch=1,
            grid=(here,),
            in_specs=[rows_spec] + expert_specs(w_gate),
            out_specs=rows_spec,
        ),
        out_shape=jax.ShapeDtypeStruct(picked.shape, jnp.bfloat16),
        compiler_params=pltpu.CompilerParams(vmem_limit_bytes=VMEM_LIMIT),
        name="experts",
    )(where, picked, w_gate, w_up, w_down)


def experts_fused(where, found, combine, w_gate, w_up, w_down):
    count, local = len(found), found[0][0].shape[0]
    here, units, width = w_gate.shape
    rows = count * SLOTS
    whole = pl.BlockSpec(memory_space=pltpu.VMEM)
    outs = pl.pallas_call(
        functools.partial(fused_kernel, count),
        in_specs=[pl.BlockSpec(memory_space=pltpu.SMEM)]
        + [whole] * (2 * count + 1)
        + [pl.BlockSpec(memory_space=pltpu.HBM)] * 3,
        out_specs=[whole] * (2 * count),
        scratch_shapes=[pltpu.VMEM((here, rows, width), jnp.bfloat16)]
        + [pltpu.VMEM((HELD, units, width), jnp.bfloat16), pltpu.SemaphoreType.DMA((HELD, PIECES))],
        out_shape=[pltpu.VMEM((local, width // 2), jnp.bfloat16)] * (2 * count),
        compiler_params=pltpu.CompilerParams(vmem_limit_bytes=29 * MIB),
        name="experts",
    )(where, *(x for block in found for x in block), combine,
      *(pltpu.with_memory_space_constraint(w, pltpu.HBM) for w in (w_gate, w_up, w_down)))
    return outs[:count], outs[count:]


def body(
    queries,
    latent,
    residual,
    seg_lengths,
    span_order,
    expert_ids,
    route_weights,
    kv_up,
    out_proj,
    norm_gain,
    w_gate,
    w_up,
    w_down,
):
    local_rows, width = residual.shape
    span = local_rows // 2
    count = lax.axis_size("ctx")
    here = EXPERTS // count
    me, side = lax.axis_index("ctx"), lax.axis_index("exp")
    where = jnp.stack([me, side]).astype(jnp.int32)

    base = latent.shape[1]
    w_gate, w_up = w_gate.transpose(0, 2, 1), w_up.transpose(0, 2, 1)
    packed = pack(latent, expert_ids, route_weights)
    few = count <= FEW
    scalars = lambda *arrays: jnp.concatenate([where, sources_of(me, side, count), *arrays])
    beside = [
        (scalars, (span_order, seg_lengths)),
        (lambda gain: gain.reshape(1, width), (norm_gain,)),
        (stage if few else lambda x: x, (kv_up,)),
    ]
    streams = [gather(x, count, beside if h == 0 else ()) for h, x in enumerate(packed)]
    info, gain, kv_up = streams[0][1]
    found = list(zip(*(blocks for blocks, _ in streams)))
    partial, summand = attend(info, found, queries, kv_up, out_proj, residual, count)
    def place_rows(*blocks):
        if few:
            return route(where, blocks, here)
        facts = jnp.stack([jnp.concatenate(block, axis=0) for block in blocks])
        facts = facts[:, :, base : base + 2 * TOP].astype(jnp.float32)
        own = (me * here + jnp.arange(here, dtype=jnp.int32)).astype(jnp.float32)
        hit = facts[:, :, :TOP, None] == own
        hot = jnp.any(hit, axis=2)
        share = jnp.sum(jnp.where(hit, facts[:, :, TOP:, None], 0.0), axis=2)
        token = jnp.arange(local_rows, dtype=jnp.int32)
        before = (token[:, None] > token[None, :]).astype(jnp.bfloat16)
        rank = jnp.einsum("tu,cue->cte", before, hot.astype(jnp.bfloat16), preferred_element_type=jnp.float32)
        slot = jnp.arange(SLOTS, dtype=jnp.int32).astype(jnp.float32)
        combine = jnp.where(rank[:, :, :, None] == slot, share[:, :, :, None], 0.0)
        return combine.astype(jnp.bfloat16).reshape(count, local_rows, here * SLOTS)

    there = swap(partial)
    blocks, _ = lax.optimization_barrier((tuple(found), partial))
    combine, there = lax.optimization_barrier((place_rows(*blocks), there))
    middle, *normed = norm(where, summand, there, gain)
    got = gather_columns(*normed, count)
    if few:
        mixture = reduce(experts_fused(where, got, combine, w_gate, w_up, w_down), count)
    else:
        pick = (combine > 0).astype(jnp.bfloat16)
        near, far = (jnp.stack(x) for x in zip(*got))
        rows = jnp.concatenate([jnp.where(side == 0, near, far), jnp.where(side == 0, far, near)], axis=2)
        picked = jnp.einsum("cts,ctd->csd", pick, rows, preferred_element_type=jnp.float32).astype(jnp.bfloat16)
        picked = picked.reshape(count, here, SLOTS, width).transpose(1, 0, 2, 3).reshape(here, count * SLOTS, width)
        result = experts_plain(where, picked, w_gate, w_up, w_down)
        result = result.reshape(here, count, SLOTS, width).transpose(1, 0, 2, 3).reshape(count, here * SLOTS, width)
        total = jnp.einsum("cts,csd->ctd", combine, result, preferred_element_type=jnp.float32).astype(jnp.bfloat16)
        left, right = jnp.split(total, 2, axis=2)
        both = summed([jnp.where(side == 0, left, right), swap(jnp.where(side == 0, right, left))])
        mixture = lax.psum_scatter(both.astype(jnp.bfloat16), "ctx").astype(jnp.float32)
    return (middle.astype(jnp.float32) + mixture).astype(jnp.bfloat16)


def solution(mesh):
    in_specs = (
        P(("groups", "ctx"), "exp"),
        P(("groups", "ctx"), None),
        P(("groups", "ctx"), None),
        P("groups"),
        P("groups"),
        P(("groups", "ctx"), None),
        P(("groups", "ctx"), None),
        P(None, "exp"),
        P("exp", None),
        P(),
        P("ctx", None, "exp"),
        P("ctx", None, "exp"),
        P("ctx", "exp", None),
    )
    out_specs = P(("groups", "ctx"), "exp")
    return jax.shard_map(body, mesh=mesh, in_specs=in_specs, out_specs=out_specs, check_vma=False)
```

```python
import functools
import math

import jax
import jax.numpy as jnp
import numpy as np
from jax import lax
from jax.experimental import pallas as pl
from jax.experimental.pallas import tpu as pltpu
from jax.sharding import PartitionSpec as P

NOPE = 128
ROPE = 64
VHEAD = 128
LAT = 512
EXPERTS = 64
TOP = 6
SLOTS = 16
WIDE = 640
MIB = 1024 * 1024
VMEM_LIMIT = 50 * MIB
HELD = 7
PIECES = 2
SWAP = [(0, 1), (1, 0)]
FEW = 8


def cycle_of(count):
    fast = 2 ** (int(math.log2(count)) // 2)
    slow = count // fast
    cycle = [0]
    for i in range(slow):
        columns = range(1, fast)
        cycle += [i * fast + j for j in (columns if i % 2 == 0 else reversed(columns))]
    return cycle + [i * fast for i in reversed(range(1, slow))]


def swap(value):
    return lax.ppermute(value, "exp", SWAP)


def turn(value, count, cross=False):
    cycle = cycle_of(count)
    pairs = []
    for p in range(count):
        for core, ahead in ((0, 1), (1, -1)):
            pairs.append((cycle[p] * 2 + core, cycle[(p + ahead) % count] * 2 + (core ^ int(cross))))
    return lax.ppermute(value, ("ctx", "exp"), pairs)


def summed(pieces):
    total = pieces[0].astype(jnp.float32)
    for piece in pieces[1:]:
        total = total + piece.astype(jnp.float32)
    return total


def sources_table(count):
    if count > FEW:
        return jnp.tile(jnp.arange(count, dtype=jnp.int32), 2 * count)
    cycle = cycle_of(count)
    middle = count // 2
    table = np.zeros((2 * count, count), np.int32)
    for p in range(count):
        for core, sign in ((0, 1), (1, -1)):
            ways = [sign * d for d in range(middle + 1)] + [-sign * d for d in range(1, middle)]
            table[cycle[p] * 2 + core] = [cycle[(p - way) % count] for way in ways]
    return jnp.asarray(table.reshape(-1))


def gather(block, count, beside=()):
    if count > FEW:
        return list(lax.all_gather(block, "ctx")), [run(*arguments) for run, arguments in beside]
    middle = count // 2
    found, other, made = [block], [()], []
    for d in range(1, middle + 1):
        arrived, extra = turn(found[-1], count), ()
        if len(beside) >= d:
            run, arguments = beside[d - 1]
            extra = run(*lax.optimization_barrier((found[-1], arguments))[1])
        arrived, other[-1], extra = lax.optimization_barrier((arrived, other[-1], extra))
        made.append(extra)
        found.append(arrived)
        if d < middle:
            other.append(swap(arrived))
    return found + other[1:], made[: len(beside)]


def gather_columns(near, far, count):
    if count > FEW:
        return list(zip(lax.all_gather(near, "ctx"), lax.all_gather(far, "ctx")))
    middle = count // 2
    found, other = {0: [near], 1: [far]}, {0: [()], 1: [()]}
    for d in range(1, middle + 1):
        for stream in (0, 1) if d < middle else (0,):
            arrived = turn(found[stream][-1], count)
            arrived, other[stream][-1] = lax.optimization_barrier((arrived, other[stream][-1]))
            found[stream].append(arrived)
            other[stream].append(swap(arrived))
    here = [(found[0][d], found[1][d]) for d in range(middle)]
    there = [(other[1][d], other[0][d]) for d in range(1, middle)]
    return here + [(found[0][middle], other[0][middle])] + there


def reduce(parts, count):
    middle = count // 2
    given = [swap(parts[1][middle]), swap(parts[0][middle - 1])]
    running = [None, None]
    for d in range(middle, 0, -1):
        for stream in (0, 1) if d < middle else (0,):
            place = middle + d if d < middle else middle
            later = parts[1 - stream][d - 1] if d > 1 or stream == 0 else ()
            pieces = [parts[stream][place], given[stream]]
            if running[stream] is not None:
                running[stream], later = lax.optimization_barrier((running[stream], later))
                pieces.append(running[stream])
            running[stream] = turn(summed(pieces).astype(jnp.bfloat16), count, cross=d == 1 and stream == 1)
            if d > 1 or stream == 0:
                given[stream] = swap(later)
    return summed([parts[0][0], given[0], *running])


def attend_kernel(count, blocks, heads, where, *refs):
    latents, refs = refs[: len(refs) - 20], refs[len(refs) - 20 :]
    wanted, (out_ref, base_ref), held = refs[:7], refs[7:9], refs[9:16]
    sems, (m_ref, l_ref, acc_ref) = refs[16], refs[17:20]
    q_ref, up_ref, proj_ref, residual_ref, table, spans, lengths = held
    copies = [pltpu.make_async_copy(wanted[i], held[i], sems.at[i]) for i in range(7)]
    chunk = pl.program_id(0)
    sources = lambda c: table[(where[0] * 2 + where[1]) * count + c]
    order = lambda j: spans[j]
    segs = lengths.shape[0]
    rows = q_ref.shape[0]
    span = rows // 2
    depth = q_ref.shape[1] // heads

    @pl.when(chunk == 0)
    def _():
        for copy in copies:
            copy.start()

    @pl.when(chunk == 0)
    def _():
        m_ref[...] = jnp.full_like(m_ref, -1e30)
        l_ref[...] = jnp.zeros_like(l_ref)
        acc_ref[...] = jnp.zeros_like(acc_ref)

    lat = jnp.concatenate([ref[...].reshape(-1, WIDE) for ref in latents], axis=0)

    @pl.when(chunk == 0)
    def _():
        for i in (0, 1, 4, 5, 6):
            copies[i].wait()

    keyval = jnp.dot(lat[:, :LAT], up_ref[...], preferred_element_type=jnp.float32).astype(jnp.bfloat16)
    row = lax.broadcasted_iota(jnp.int32, (rows, 1), 0)
    first = order(2 * where[0]) * span
    second = order(2 * where[0] + 1) * span
    qpos = jnp.where(row < span, first + row, second + row - span)
    low = jnp.zeros((rows, 1), jnp.int32)
    start = jnp.int32(0)
    for m in range(segs):
        low = jnp.where(qpos >= start, start, low)
        start = start + lengths[m]
    keys = blocks * rows
    lane = lax.broadcasted_iota(jnp.int32, (1, keys), 1)
    which = lane // span
    kpos = lane % span
    for j in range(blocks):
        source = sources(chunk * blocks + j)
        for i in range(2):
            kpos = jnp.where(which == 2 * j + i, order(2 * source + i) * span + lane % span, kpos)
    visible = (kpos >= low) & (kpos <= qpos)

    rope = lat[:, LAT : LAT + ROPE]
    scale = 1.0 / math.sqrt(NOPE + ROPE)
    for h in range(heads):
        base = h * (NOPE + VHEAD)
        key = jnp.concatenate([keyval[:, base : base + NOPE], rope], axis=1)
        scores = lax.dot_general(q_ref[:, h * depth : (h + 1) * depth], key, (((1,), (1,)), ((), ())), preferred_element_type=jnp.float32)
        scores = jnp.where(visible, scores * scale, -1e30)
        best = m_ref[h]
        fresh = jnp.maximum(best, jnp.max(scores, axis=1, keepdims=True))
        weights = jnp.where(visible, jnp.exp(scores - fresh), 0.0)
        shrink = jnp.exp(best - fresh)
        m_ref[h] = fresh
        l_ref[h] = l_ref[h] * shrink + jnp.sum(weights, axis=1, keepdims=True)
        mixed = jnp.dot(
            weights.astype(jnp.bfloat16), keyval[:, base + NOPE : base + NOPE + VHEAD], preferred_element_type=jnp.float32
        )
        acc_ref[h] = acc_ref[h] * shrink + mixed

    @pl.when(chunk == pl.num_programs(0) - 1)
    def _():
        attended = [(acc_ref[h] / l_ref[h]).astype(jnp.bfloat16) for h in range(heads)]
        copies[2].wait()
        copies[3].wait()
        out = jnp.dot(jnp.concatenate(attended, axis=1), proj_ref[...], preferred_element_type=jnp.float32)
        out = out.astype(jnp.bfloat16)
        out_ref[...] = out
        base_ref[...] = residual_ref[...].astype(jnp.float32) + out.astype(jnp.float32)


def attend(where, scalars, found, queries, kv_up, out_proj, residual, count):
    rows, width = residual.shape
    heads = kv_up.shape[1] // (NOPE + VHEAD)
    blocks = math.gcd(count, 8)
    whole = pl.BlockSpec(memory_space=pltpu.VMEM)
    if blocks == count:
        latents, lat_spec = [half for block in found for half in block], whole
    else:
        found = [jnp.concatenate(block, axis=0) for block in found]
        latents, lat_spec = [jnp.stack(found)], pl.BlockSpec((blocks, rows, WIDE), lambda i, *_: (i, 0, 0))
    wanted = (queries, kv_up, out_proj, residual, *scalars)
    return pl.pallas_call(
        functools.partial(attend_kernel, count, blocks, heads),
        grid_spec=pltpu.PrefetchScalarGridSpec(
            num_scalar_prefetch=1,
            grid=(count // blocks,),
            in_specs=[lat_spec] * len(latents) + [pl.BlockSpec(memory_space=pltpu.HBM)] * 7,
            out_specs=[whole, whole],
            scratch_shapes=[pltpu.VMEM(x.shape, x.dtype) for x in wanted[:4]]
            + [pltpu.SMEM(x.shape, x.dtype) for x in scalars]
            + [
                pltpu.SemaphoreType.DMA((7,)),
                pltpu.VMEM((heads, rows, 1), jnp.float32),
                pltpu.VMEM((heads, rows, 1), jnp.float32),
                pltpu.VMEM((heads, rows, VHEAD), jnp.float32),
            ],
        ),
        out_shape=[pltpu.VMEM((rows, width), jnp.bfloat16), pltpu.VMEM((rows, width), jnp.float32)],
        compiler_params=pltpu.CompilerParams(vmem_limit_bytes=28 * MIB),
        name="attend",
    )(where, *latents, *(pltpu.with_memory_space_constraint(x, pltpu.HBM) for x in wanted))


def route_kernel(count, where, *refs):
    blocks, out_ref = refs[: 2 * count], refs[2 * count]
    _, rows, width = out_ref.shape
    here = width // SLOTS
    lane = lax.broadcasted_iota(jnp.int32, (rows, width), 1)
    own = (where[0] * here + lane // SLOTS).astype(jnp.float32)
    slot = (lane % SLOTS).astype(jnp.float32)
    first = lax.broadcasted_iota(jnp.int32, (rows, rows), 0)
    before = (first > lax.broadcasted_iota(jnp.int32, (rows, rows), 1)).astype(jnp.float32).astype(jnp.bfloat16)
    for c in range(count):
        facts = jnp.concatenate([blocks[2 * c + i][:, LAT:].astype(jnp.float32) for i in range(2)], axis=0)
        hot, share = jnp.zeros((rows, width), jnp.float32), jnp.zeros((rows, width), jnp.float32)
        for k in range(TOP):
            hit = facts[:, ROPE + k : ROPE + k + 1] == own
            hot = jnp.where(hit, 1.0, hot)
            share = jnp.where(hit, facts[:, ROPE + TOP + k : ROPE + TOP + k + 1], share)
        rank = jnp.dot(before, hot.astype(jnp.bfloat16), preferred_element_type=jnp.float32)
        out_ref[c] = jnp.where(rank == slot, share, 0.0).astype(jnp.bfloat16)


def route(where, found, here):
    count, (span, _) = len(found), found[0][0].shape
    whole = pl.BlockSpec(memory_space=pltpu.VMEM)
    return pl.pallas_call(
        functools.partial(route_kernel, count),
        in_specs=[pl.BlockSpec(memory_space=pltpu.SMEM)] + [whole] * (2 * count),
        out_specs=whole,
        out_shape=pltpu.VMEM((count, 2 * span, here * SLOTS), jnp.bfloat16),
        compiler_params=pltpu.CompilerParams(vmem_limit_bytes=8 * MIB),
        name="route",
    )(where, *(half for block in found for half in block))


def norm_kernel(where, base_ref, there_ref, gain_ref, middle_ref, near_ref, far_ref):
    half = middle_ref.shape[1]
    middle = (base_ref[...] + there_ref[...].astype(jnp.float32)).astype(jnp.bfloat16)
    wide = middle.astype(jnp.float32)
    inverse = lax.rsqrt(jnp.mean(wide * wide, axis=1, keepdims=True) + 1e-06)
    normed = wide * inverse * gain_ref[...].astype(jnp.float32)
    first = where[1] == 0
    near_ref[...] = jnp.where(first, normed[:, :half], normed[:, half:]).astype(jnp.bfloat16)
    far_ref[...] = jnp.where(first, normed[:, half:], normed[:, :half]).astype(jnp.bfloat16)
    middle_ref[...] = jnp.where(first, wide[:, :half], wide[:, half:]).astype(jnp.bfloat16)


def norm(where, base, there, gain):
    rows, width = base.shape
    whole = pl.BlockSpec(memory_space=pltpu.VMEM)
    return pl.pallas_call(
        norm_kernel,
        in_specs=[pl.BlockSpec(memory_space=pltpu.SMEM)] + [whole] * 3,
        out_specs=[whole] * 3,
        out_shape=[pltpu.VMEM((rows, width // 2), jnp.bfloat16)] * 3,
        compiler_params=pltpu.CompilerParams(vmem_limit_bytes=12 * MIB),
        name="norm",
    )(where, base, there, gain)


def pack_kernel(*refs):
    copies = [pltpu.make_async_copy(refs[i], refs[5 + i], refs[9].at[i]) for i in range(3)]
    for copy in copies:
        copy.start()
    for copy in copies:
        copy.wait()
    top_ref, bottom_ref, latent_ref, ids_ref, weights_ref, rows = refs[3:9]
    span = top_ref.shape[0]
    tokens = 2 * span
    rows[...] = jnp.zeros_like(rows)
    rows[0:TOP] = ids_ref[...].astype(jnp.float32)
    rows[TOP : 2 * TOP] = weights_ref[...]
    row = lax.broadcasted_iota(jnp.int32, (tokens, tokens), 0)
    same = (row == lax.broadcasted_iota(jnp.int32, (tokens, tokens), 1)).astype(jnp.float32).astype(jnp.bfloat16)
    every = jnp.concatenate([latent_ref[...], rows[...].astype(jnp.bfloat16)], axis=0)
    turned = lax.dot_general(same, every, (((1,), (1,)), ((), ())), preferred_element_type=jnp.float32)
    top_ref[...] = turned[:span].astype(jnp.bfloat16)
    bottom_ref[...] = turned[span:].astype(jnp.bfloat16)


def pack(latent, expert_ids, route_weights):
    local_rows, base = latent.shape
    arrays = (latent.T, expert_ids.T, route_weights.T)
    return pl.pallas_call(
        pack_kernel,
        in_specs=[pl.BlockSpec(memory_space=pltpu.HBM)] * 3,
        out_specs=[pl.BlockSpec(memory_space=pltpu.VMEM)] * 2,
        scratch_shapes=[pltpu.VMEM(x.shape, x.dtype) for x in arrays]
        + [pltpu.VMEM((WIDE - base, local_rows), jnp.float32), pltpu.SemaphoreType.DMA((3,))],
        out_shape=[pltpu.VMEM((local_rows // 2, WIDE), jnp.bfloat16)] * 2,
        compiler_params=pltpu.CompilerParams(vmem_limit_bytes=4 * MIB),
        name="pack",
    )(*(pltpu.with_memory_space_constraint(x, pltpu.HBM) for x in arrays))


def expert_hidden(rows, gate, up):
    by_columns = (((1,), (1,)), ((), ()))
    gate = lax.dot_general(gate, rows, by_columns, preferred_element_type=jnp.float32)
    upper = lax.dot_general(up, rows, by_columns, preferred_element_type=jnp.float32)
    return (gate / (1.0 + jnp.exp(-gate)) * upper).astype(jnp.bfloat16)


def expert_down(hidden, down):
    by_rows = (((0,), (0,)), ((), ()))
    return lax.dot_general(hidden, down, by_rows, preferred_element_type=jnp.float32).astype(jnp.bfloat16)


def plain_kernel(where, rows_ref, gate_ref, up_ref, down_ref, out_ref):
    out_ref[0] = expert_down(expert_hidden(rows_ref[0], gate_ref[0], up_ref[0]), down_ref[0])


def fused_kernel(count, where, *refs):
    at = 2 * count
    blocks, combine_ref, weights = refs[:at], refs[at], refs[at + 1 : at + 4]
    near, far = refs[at + 4 : at + 4 + count], refs[at + 4 + count : at + 4 + 2 * count]
    at += 4 + 2 * count
    picked, buffer, sems = refs[at : at + 3]
    here = picked.shape[0]
    slots, units, width = buffer.shape
    half = width // 2
    side = where[1]
    columns = [pl.ds(pl.multiple_of(turned * half, half), half) for turned in (side, 1 - side)]
    piece = units // PIECES
    middle = count // 2
    by_rows = (((0,), (0,)), ((), ()))

    def copies(expert, w):
        slot = lax.rem(3 * expert + w, slots)
        for i in range(PIECES):
            rows = pl.ds(i * piece, piece)
            yield pltpu.make_async_copy(weights[w].at[expert, rows], buffer.at[slot, rows], sems.at[slot, i])

    def start(expert, w):
        for copy in copies(expert, w):
            copy.start()

    def arrived(expert, w):
        for copy in copies(expert, w):
            copy.wait()
        return buffer[lax.rem(3 * expert + w, slots)]

    for i in range(slots):
        start(i // 3, i % 3)

    for c in range(count):
        pick = (combine_ref[c].astype(jnp.float32) > 0).astype(jnp.float32).astype(jnp.bfloat16)
        for h in range(2):
            block = blocks[2 * c + h][...]
            rows = lax.dot_general(pick, block, by_rows, preferred_element_type=jnp.float32).astype(jnp.bfloat16)
            for e in range(here):
                picked[e, c * SLOTS : (c + 1) * SLOTS, columns[h]] = rows[e * SLOTS : (e + 1) * SLOTS]

    def work(expert, _):
        hidden = expert_hidden(picked[expert], arrived(expert, 0), arrived(expert, 1))

        @pl.when(expert + slots // 3 < here)
        def _():
            start(expert + slots // 3, 1)
            start(expert + slots // 3, 2)

        picked[expert] = expert_down(hidden, arrived(expert, 2))

        @pl.when(expert + slots // 3 + 1 < here)
        def _():
            start(expert + slots // 3 + 1, 0)

        return 0

    lax.fori_loop(0, here, work, 0)

    for c in [middle] + list(range(middle)) + list(range(middle + 1, count)):
        for h, outs in ((1, far), (0, near)):
            rows = jnp.concatenate([picked[e, c * SLOTS : (c + 1) * SLOTS, columns[h]] for e in range(here)], axis=0)
            outs[c][...] = jnp.dot(combine_ref[c], rows, preferred_element_type=jnp.float32).astype(jnp.bfloat16)


def expert_specs(w_gate):
    hidden, width = w_gate.shape[1:]
    return [pl.BlockSpec((1, hidden, width), lambda e, where: (e, 0, 0))] * 3


def experts_plain(where, picked, w_gate, w_up, w_down):
    here, rows, width = picked.shape
    rows_spec = pl.BlockSpec((1, rows, width), lambda e, where: (e, 0, 0))
    return pl.pallas_call(
        plain_kernel,
        grid_spec=pltpu.PrefetchScalarGridSpec(
            num_scalar_prefetch=1,
            grid=(here,),
            in_specs=[rows_spec] + expert_specs(w_gate),
            out_specs=rows_spec,
        ),
        out_shape=jax.ShapeDtypeStruct(picked.shape, jnp.bfloat16),
        compiler_params=pltpu.CompilerParams(vmem_limit_bytes=VMEM_LIMIT),
        name="experts",
    )(where, picked, w_gate, w_up, w_down)


def experts_fused(where, found, combine, w_gate, w_up, w_down):
    count, local = len(found), found[0][0].shape[0]
    here, units, width = w_gate.shape
    rows = count * SLOTS
    whole = pl.BlockSpec(memory_space=pltpu.VMEM)
    outs = pl.pallas_call(
        functools.partial(fused_kernel, count),
        in_specs=[pl.BlockSpec(memory_space=pltpu.SMEM)]
        + [whole] * (2 * count + 1)
        + [pl.BlockSpec(memory_space=pltpu.HBM)] * 3,
        out_specs=[whole] * (2 * count),
        scratch_shapes=[pltpu.VMEM((here, rows, width), jnp.bfloat16)]
        + [pltpu.VMEM((HELD, units, width), jnp.bfloat16), pltpu.SemaphoreType.DMA((HELD, PIECES))],
        out_shape=[pltpu.VMEM((local, width // 2), jnp.bfloat16)] * (2 * count),
        compiler_params=pltpu.CompilerParams(vmem_limit_bytes=29 * MIB),
        name="experts",
    )(where, *(x for block in found for x in block), combine,
      *(pltpu.with_memory_space_constraint(w, pltpu.HBM) for w in (w_gate, w_up, w_down)))
    return outs[:count], outs[count:]


def body(
    queries,
    latent,
    residual,
    seg_lengths,
    span_order,
    expert_ids,
    route_weights,
    kv_up,
    out_proj,
    norm_gain,
    w_gate,
    w_up,
    w_down,
):
    local_rows, width = residual.shape
    span = local_rows // 2
    count = lax.axis_size("ctx")
    here = EXPERTS // count
    me, side = lax.axis_index("ctx"), lax.axis_index("exp")
    where = jnp.stack([me, side]).astype(jnp.int32)

    base = latent.shape[1]
    w_gate, w_up = w_gate.transpose(0, 2, 1), w_up.transpose(0, 2, 1)
    packed = pack(latent, expert_ids, route_weights)
    few = count <= FEW
    scalars = (sources_table(count), span_order, seg_lengths)
    beside = [(lambda gain: gain.reshape(1, width), (norm_gain,))]
    streams = [gather(x, count, beside if h == 0 else ()) for h, x in enumerate(packed)]
    gain = streams[0][1][0]
    found = list(zip(*(blocks for blocks, _ in streams)))
    partial, summand = attend(where, scalars, found, queries, kv_up, out_proj, residual, count)
    def place_rows(*blocks):
        if few:
            return route(where, blocks, here)
        facts = jnp.stack([jnp.concatenate(block, axis=0) for block in blocks])
        facts = facts[:, :, base : base + 2 * TOP].astype(jnp.float32)
        own = (me * here + jnp.arange(here, dtype=jnp.int32)).astype(jnp.float32)
        hit = facts[:, :, :TOP, None] == own
        hot = jnp.any(hit, axis=2)
        share = jnp.sum(jnp.where(hit, facts[:, :, TOP:, None], 0.0), axis=2)
        token = jnp.arange(local_rows, dtype=jnp.int32)
        before = (token[:, None] > token[None, :]).astype(jnp.bfloat16)
        rank = jnp.einsum("tu,cue->cte", before, hot.astype(jnp.bfloat16), preferred_element_type=jnp.float32)
        slot = jnp.arange(SLOTS, dtype=jnp.int32).astype(jnp.float32)
        combine = jnp.where(rank[:, :, :, None] == slot, share[:, :, :, None], 0.0)
        return combine.astype(jnp.bfloat16).reshape(count, local_rows, here * SLOTS)

    there = swap(partial)
    blocks, _ = lax.optimization_barrier((tuple(found), partial))
    combine, there = lax.optimization_barrier((place_rows(*blocks), there))
    middle, *normed = norm(where, summand, there, gain)
    got = gather_columns(*normed, count)
    if few:
        mixture = reduce(experts_fused(where, got, combine, w_gate, w_up, w_down), count)
    else:
        pick = (combine > 0).astype(jnp.bfloat16)
        near, far = (jnp.stack(x) for x in zip(*got))
        rows = jnp.concatenate([jnp.where(side == 0, near, far), jnp.where(side == 0, far, near)], axis=2)
        picked = jnp.einsum("cts,ctd->csd", pick, rows, preferred_element_type=jnp.float32).astype(jnp.bfloat16)
        picked = picked.reshape(count, here, SLOTS, width).transpose(1, 0, 2, 3).reshape(here, count * SLOTS, width)
        result = experts_plain(where, picked, w_gate, w_up, w_down)
        result = result.reshape(here, count, SLOTS, width).transpose(1, 0, 2, 3).reshape(count, here * SLOTS, width)
        total = jnp.einsum("cts,csd->ctd", combine, result, preferred_element_type=jnp.float32).astype(jnp.bfloat16)
        left, right = jnp.split(total, 2, axis=2)
        both = summed([jnp.where(side == 0, left, right), swap(jnp.where(side == 0, right, left))])
        mixture = lax.psum_scatter(both.astype(jnp.bfloat16), "ctx").astype(jnp.float32)
    return (middle.astype(jnp.float32) + mixture).astype(jnp.bfloat16)


def solution(mesh):
    in_specs = (
        P(("groups", "ctx"), "exp"),
        P(("groups", "ctx"), None),
        P(("groups", "ctx"), None),
        P("groups"),
        P("groups"),
        P(("groups", "ctx"), None),
        P(("groups", "ctx"), None),
        P(None, "exp"),
        P("exp", None),
        P(),
        P("ctx", None, "exp"),
        P("ctx", None, "exp"),
        P("ctx", "exp", None),
    )
    out_specs = P(("groups", "ctx"), "exp")
    return jax.shard_map(body, mesh=mesh, in_specs=in_specs, out_specs=out_specs, check_vma=False)
```

```python
import functools
import math

import jax
import jax.numpy as jnp
import numpy as np
from jax import lax
from jax.experimental import pallas as pl
from jax.experimental.pallas import tpu as pltpu
from jax.sharding import PartitionSpec as P

NOPE = 128
ROPE = 64
VHEAD = 128
LAT = 512
EXPERTS = 64
TOP = 6
SLOTS = 16
WIDE = 640
MIB = 1024 * 1024
VMEM_LIMIT = 50 * MIB
HELD = 7
PIECES = 4
SWAP = [(0, 1), (1, 0)]
FEW = 8


def cycle_of(count):
    fast = 2 ** (int(math.log2(count)) // 2)
    slow = count // fast
    cycle = [0]
    for i in range(slow):
        columns = range(1, fast)
        cycle += [i * fast + j for j in (columns if i % 2 == 0 else reversed(columns))]
    return cycle + [i * fast for i in reversed(range(1, slow))]


def swap(value):
    return lax.ppermute(value, "exp", SWAP)


def turn(value, count, cross=False):
    cycle = cycle_of(count)
    pairs = []
    for p in range(count):
        for core, ahead in ((0, 1), (1, -1)):
            pairs.append((cycle[p] * 2 + core, cycle[(p + ahead) % count] * 2 + (core ^ int(cross))))
    return lax.ppermute(value, ("ctx", "exp"), pairs)


def summed(pieces):
    total = pieces[0].astype(jnp.float32)
    for piece in pieces[1:]:
        total = total + piece.astype(jnp.float32)
    return total


def sources_of(me, side, count):
    if count > FEW:
        return jnp.arange(count, dtype=jnp.int32)
    cycle = cycle_of(count)
    middle = count // 2
    table = np.zeros((2 * count, count), np.int32)
    for p in range(count):
        for core, sign in ((0, 1), (1, -1)):
            ways = [sign * d for d in range(middle + 1)] + [-sign * d for d in range(1, middle)]
            table[cycle[p] * 2 + core] = [cycle[(p - way) % count] for way in ways]
    return lax.dynamic_index_in_dim(jnp.asarray(table), me * 2 + side, keepdims=False)


def gather(block, count, beside=()):
    if count > FEW:
        return list(lax.all_gather(block, "ctx")), [run(*arguments) for run, arguments in beside]
    middle = count // 2
    found, other, made = [block], [()], []
    for d in range(1, middle + 1):
        arrived, extra = turn(found[-1], count), ()
        if len(beside) >= d:
            run, arguments = beside[d - 1]
            extra = run(*lax.optimization_barrier((found[-1], arguments))[1])
        arrived, other[-1], extra = lax.optimization_barrier((arrived, other[-1], extra))
        made.append(extra)
        found.append(arrived)
        if d < middle:
            other.append(swap(arrived))
    return found + other[1:], made[: len(beside)]


def gather_columns(near, far, count):
    if count > FEW:
        return list(zip(lax.all_gather(near, "ctx"), lax.all_gather(far, "ctx")))
    middle = count // 2
    found, other = {0: [near], 1: [far]}, {0: [()], 1: [()]}
    for d in range(1, middle + 1):
        for stream in (0, 1) if d < middle else (0,):
            arrived = turn(found[stream][-1], count)
            arrived, other[stream][-1] = lax.optimization_barrier((arrived, other[stream][-1]))
            found[stream].append(arrived)
            other[stream].append(swap(arrived))
    here = [(found[0][d], found[1][d]) for d in range(middle)]
    there = [(other[1][d], other[0][d]) for d in range(1, middle)]
    return here + [(found[0][middle], other[0][middle])] + there


def reduce(parts, count):
    middle = count // 2
    given = [swap(parts[1][middle]), swap(parts[0][middle - 1])]
    running = [None, None]
    for d in range(middle, 0, -1):
        for stream in (0, 1) if d < middle else (0,):
            place = middle + d if d < middle else middle
            later = parts[1 - stream][d - 1] if d > 1 or stream == 0 else ()
            pieces = [parts[stream][place], given[stream]]
            if running[stream] is not None:
                running[stream], later = lax.optimization_barrier((running[stream], later))
                pieces.append(running[stream])
            running[stream] = turn(summed(pieces).astype(jnp.bfloat16), count, cross=d == 1 and stream == 1)
            if d > 1 or stream == 0:
                given[stream] = swap(later)
    return summed([parts[0][0], given[0], *running])


def attend_kernel(count, blocks, heads, info, *refs):
    latents, up_ref, refs = refs[: len(refs) - 13], refs[len(refs) - 13], refs[len(refs) - 12 :]
    wanted, (out_ref, base_ref) = refs[:3], refs[3:5]
    held, sems, (m_ref, l_ref, acc_ref) = refs[5:8], refs[8], refs[9:12]
    q_ref, proj_ref, residual_ref = held
    copies = [pltpu.make_async_copy(wanted[i], held[i], sems.at[i]) for i in range(3)]
    chunk = pl.program_id(0)
    sources = lambda c: info[2 + c]
    order = lambda j: info[2 + count + j]
    segs = info.shape[0] - 2 - 3 * count
    rows = q_ref.shape[0]
    span = rows // 2
    depth = q_ref.shape[1] // heads

    @pl.when(chunk == 0)
    def _():
        for copy in copies:
            copy.start()

    @pl.when(chunk == 0)
    def _():
        m_ref[...] = jnp.full_like(m_ref, -1e30)
        l_ref[...] = jnp.zeros_like(l_ref)
        acc_ref[...] = jnp.zeros_like(acc_ref)

    row = lax.broadcasted_iota(jnp.int32, (rows, 1), 0)
    first = order(2 * info[0]) * span
    second = order(2 * info[0] + 1) * span
    qpos = jnp.where(row < span, first + row, second + row - span)
    low = jnp.zeros((rows, 1), jnp.int32)
    start = jnp.int32(0)
    for m in range(segs):
        low = jnp.where(qpos >= start, start, low)
        start = start + info[2 + 3 * count + m]
    keys = blocks * rows
    lane = lax.broadcasted_iota(jnp.int32, (1, keys), 1)
    which = lane // span
    kpos = lane % span
    for j in range(blocks):
        source = sources(chunk * blocks + j)
        for i in range(2):
            kpos = jnp.where(which == 2 * j + i, order(2 * source + i) * span + lane % span, kpos)
    visible = (kpos >= low) & (kpos <= qpos)

    lat = jnp.concatenate([ref[...].reshape(-1, WIDE) for ref in latents], axis=0)

    @pl.when(chunk == 0)
    def _():
        copies[0].wait()

    keyval = jnp.dot(lat[:, :LAT], up_ref[...], preferred_element_type=jnp.float32).astype(jnp.bfloat16)
    rope = lat[:, LAT : LAT + ROPE]
    scale = 1.0 / math.sqrt(NOPE + ROPE)
    for h in range(heads):
        base = h * (NOPE + VHEAD)
        key = jnp.concatenate([keyval[:, base : base + NOPE], rope], axis=1)
        scores = lax.dot_general(q_ref[:, h * depth : (h + 1) * depth], key, (((1,), (1,)), ((), ())), preferred_element_type=jnp.float32)
        scores = jnp.where(visible, scores * scale, -1e30)
        values = keyval[:, base + NOPE : base + NOPE + VHEAD]
        if blocks == count:
            weights = jnp.where(visible, jnp.exp(scores - jnp.max(scores, axis=1, keepdims=True)), 0.0)
            mixed = jnp.dot(weights.astype(jnp.bfloat16), values, preferred_element_type=jnp.float32)
            acc_ref[h] = mixed / jnp.sum(weights, axis=1, keepdims=True)
            continue
        best = m_ref[h]
        fresh = jnp.maximum(best, jnp.max(scores, axis=1, keepdims=True))
        weights = jnp.where(visible, jnp.exp(scores - fresh), 0.0)
        shrink = jnp.exp(best - fresh)
        m_ref[h] = fresh
        l_ref[h] = l_ref[h] * shrink + jnp.sum(weights, axis=1, keepdims=True)
        mixed = jnp.dot(weights.astype(jnp.bfloat16), values, preferred_element_type=jnp.float32)
        acc_ref[h] = acc_ref[h] * shrink + mixed

    @pl.when(chunk == pl.num_programs(0) - 1)
    def _():
        totals = [1.0 if blocks == count else l_ref[h] for h in range(heads)]
        attended = [(acc_ref[h] / totals[h]).astype(jnp.bfloat16) for h in range(heads)]
        copies[1].wait()
        copies[2].wait()
        out = jnp.dot(jnp.concatenate(attended, axis=1), proj_ref[...], preferred_element_type=jnp.float32)
        out = out.astype(jnp.bfloat16)
        out_ref[...] = out
        base_ref[...] = residual_ref[...].astype(jnp.float32) + out.astype(jnp.float32)


def attend(info, found, queries, kv_up, out_proj, residual, count):
    rows, width = residual.shape
    heads = kv_up.shape[1] // (NOPE + VHEAD)
    blocks = math.gcd(count, 8)
    whole = pl.BlockSpec(memory_space=pltpu.VMEM)
    if blocks == count:
        latents, lat_spec = [half for block in found for half in block], whole
    else:
        found = [jnp.concatenate(block, axis=0) for block in found]
        latents, lat_spec = [jnp.stack(found)], pl.BlockSpec((blocks, rows, WIDE), lambda i, *_: (i, 0, 0))
    wanted = (queries, out_proj, residual)
    return pl.pallas_call(
        functools.partial(attend_kernel, count, blocks, heads),
        grid_spec=pltpu.PrefetchScalarGridSpec(
            num_scalar_prefetch=1,
            grid=(count // blocks,),
            in_specs=[lat_spec] * len(latents) + [whole] + [pl.BlockSpec(memory_space=pltpu.HBM)] * 3,
            out_specs=[whole, whole],
            scratch_shapes=[pltpu.VMEM(x.shape, x.dtype) for x in wanted]
            + [
                pltpu.SemaphoreType.DMA((3,)),
                pltpu.VMEM((heads, rows, 1), jnp.float32),
                pltpu.VMEM((heads, rows, 1), jnp.float32),
                pltpu.VMEM((heads, rows, VHEAD), jnp.float32),
            ],
        ),
        out_shape=[pltpu.VMEM((rows, width), jnp.bfloat16), pltpu.VMEM((rows, width), jnp.float32)],
        compiler_params=pltpu.CompilerParams(vmem_limit_bytes=28 * MIB),
        name="attend",
    )(info, *latents, kv_up, *(pltpu.with_memory_space_constraint(x, pltpu.HBM) for x in wanted))


def stage_kernel(source, out, sem):
    copy = pltpu.make_async_copy(source, out, sem)
    copy.start()
    copy.wait()


def stage(x):
    return pl.pallas_call(
        stage_kernel,
        in_specs=[pl.BlockSpec(memory_space=pltpu.HBM)],
        out_specs=pl.BlockSpec(memory_space=pltpu.VMEM),
        scratch_shapes=[pltpu.SemaphoreType.DMA],
        out_shape=pltpu.VMEM(x.shape, x.dtype),
        compiler_params=pltpu.CompilerParams(vmem_limit_bytes=2 * MIB),
        name="stage",
    )(pltpu.with_memory_space_constraint(x, pltpu.HBM))


def route_kernel(count, where, *refs):
    blocks, out_ref = refs[: 2 * count], refs[2 * count]
    _, rows, width = out_ref.shape
    here = width // SLOTS
    lane = lax.broadcasted_iota(jnp.int32, (rows, width), 1)
    own = (where[0] * here + lane // SLOTS).astype(jnp.float32)
    slot = (lane % SLOTS).astype(jnp.float32)
    first = lax.broadcasted_iota(jnp.int32, (rows, rows), 0)
    before = (first > lax.broadcasted_iota(jnp.int32, (rows, rows), 1)).astype(jnp.float32).astype(jnp.bfloat16)
    for c in range(count):
        facts = jnp.concatenate([blocks[2 * c + i][:, LAT:].astype(jnp.float32) for i in range(2)], axis=0)
        hot, share = jnp.zeros((rows, width), jnp.float32), jnp.zeros((rows, width), jnp.float32)
        for k in range(TOP):
            hit = facts[:, ROPE + k : ROPE + k + 1] == own
            hot = jnp.where(hit, 1.0, hot)
            share = jnp.where(hit, facts[:, ROPE + TOP + k : ROPE + TOP + k + 1], share)
        rank = jnp.dot(before, hot.astype(jnp.bfloat16), preferred_element_type=jnp.float32)
        out_ref[c] = jnp.where(rank == slot, share, 0.0).astype(jnp.bfloat16)


def route(where, found, here):
    count, (span, _) = len(found), found[0][0].shape
    whole = pl.BlockSpec(memory_space=pltpu.VMEM)
    return pl.pallas_call(
        functools.partial(route_kernel, count),
        in_specs=[pl.BlockSpec(memory_space=pltpu.SMEM)] + [whole] * (2 * count),
        out_specs=whole,
        out_shape=pltpu.VMEM((count, 2 * span, here * SLOTS), jnp.bfloat16),
        compiler_params=pltpu.CompilerParams(vmem_limit_bytes=8 * MIB),
        name="route",
    )(where, *(half for block in found for half in block))


def norm_kernel(where, base_ref, there_ref, gain_ref, middle_ref, near_ref, far_ref):
    half = middle_ref.shape[1]
    middle = (base_ref[...] + there_ref[...].astype(jnp.float32)).astype(jnp.bfloat16)
    wide = middle.astype(jnp.float32)
    inverse = lax.rsqrt(jnp.mean(wide * wide, axis=1, keepdims=True) + 1e-06)
    normed = wide * inverse * gain_ref[...].astype(jnp.float32)
    first = where[1] == 0
    near_ref[...] = jnp.where(first, normed[:, :half], normed[:, half:]).astype(jnp.bfloat16)
    far_ref[...] = jnp.where(first, normed[:, half:], normed[:, :half]).astype(jnp.bfloat16)
    middle_ref[...] = jnp.where(first, wide[:, :half], wide[:, half:]).astype(jnp.bfloat16)


def norm(where, base, there, gain):
    rows, width = base.shape
    whole = pl.BlockSpec(memory_space=pltpu.VMEM)
    return pl.pallas_call(
        norm_kernel,
        in_specs=[pl.BlockSpec(memory_space=pltpu.SMEM)] + [whole] * 3,
        out_specs=[whole] * 3,
        out_shape=[pltpu.VMEM((rows, width // 2), jnp.bfloat16)] * 3,
        compiler_params=pltpu.CompilerParams(vmem_limit_bytes=12 * MIB),
        name="norm",
    )(where, base, there, gain)


def pack_kernel(*refs):
    copies = [pltpu.make_async_copy(refs[i], refs[5 + i], refs[9].at[i]) for i in range(3)]
    for copy in copies:
        copy.start()
    for copy in copies:
        copy.wait()
    top_ref, bottom_ref, latent_ref, ids_ref, weights_ref, rows = refs[3:9]
    span = top_ref.shape[0]
    tokens = 2 * span
    rows[...] = jnp.zeros_like(rows)
    rows[0:TOP] = ids_ref[...].astype(jnp.float32)
    rows[TOP : 2 * TOP] = weights_ref[...]
    row = lax.broadcasted_iota(jnp.int32, (tokens, tokens), 0)
    same = (row == lax.broadcasted_iota(jnp.int32, (tokens, tokens), 1)).astype(jnp.float32).astype(jnp.bfloat16)
    every = jnp.concatenate([latent_ref[...], rows[...].astype(jnp.bfloat16)], axis=0)
    turned = lax.dot_general(same, every, (((1,), (1,)), ((), ())), preferred_element_type=jnp.float32)
    top_ref[...] = turned[:span].astype(jnp.bfloat16)
    bottom_ref[...] = turned[span:].astype(jnp.bfloat16)


def pack(latent, expert_ids, route_weights):
    local_rows, base = latent.shape
    arrays = (latent.T, expert_ids.T, route_weights.T)
    return pl.pallas_call(
        pack_kernel,
        in_specs=[pl.BlockSpec(memory_space=pltpu.HBM)] * 3,
        out_specs=[pl.BlockSpec(memory_space=pltpu.VMEM)] * 2,
        scratch_shapes=[pltpu.VMEM(x.shape, x.dtype) for x in arrays]
        + [pltpu.VMEM((WIDE - base, local_rows), jnp.float32), pltpu.SemaphoreType.DMA((3,))],
        out_shape=[pltpu.VMEM((local_rows // 2, WIDE), jnp.bfloat16)] * 2,
        compiler_params=pltpu.CompilerParams(vmem_limit_bytes=4 * MIB),
        name="pack",
    )(*(pltpu.with_memory_space_constraint(x, pltpu.HBM) for x in arrays))


def expert_hidden(rows, gate, up):
    by_columns = (((1,), (1,)), ((), ()))
    gate = lax.dot_general(gate, rows, by_columns, preferred_element_type=jnp.float32)
    upper = lax.dot_general(up, rows, by_columns, preferred_element_type=jnp.float32)
    return (gate / (1.0 + jnp.exp(-gate)) * upper).astype(jnp.bfloat16)


def expert_down(hidden, down):
    by_rows = (((0,), (0,)), ((), ()))
    return lax.dot_general(hidden, down, by_rows, preferred_element_type=jnp.float32).astype(jnp.bfloat16)


def plain_kernel(where, rows_ref, gate_ref, up_ref, down_ref, out_ref):
    out_ref[0] = expert_down(expert_hidden(rows_ref[0], gate_ref[0], up_ref[0]), down_ref[0])


def fused_kernel(count, where, *refs):
    at = 2 * count
    blocks, combine_ref, weights = refs[:at], refs[at], refs[at + 1 : at + 4]
    near, far = refs[at + 4 : at + 4 + count], refs[at + 4 + count : at + 4 + 2 * count]
    at += 4 + 2 * count
    picked, buffer, sems = refs[at : at + 3]
    here = picked.shape[0]
    slots, units, width = buffer.shape
    half = width // 2
    side = where[1]
    columns = [pl.ds(pl.multiple_of(turned * half, half), half) for turned in (side, 1 - side)]
    piece = units // PIECES
    middle = count // 2
    by_rows = (((0,), (0,)), ((), ()))

    def copies(expert, w):
        slot = lax.rem(3 * expert + w, slots)
        for i in range(PIECES):
            rows = pl.ds(i * piece, piece)
            yield pltpu.make_async_copy(weights[w].at[expert, rows], buffer.at[slot, rows], sems.at[slot, i])

    def start(expert, w):
        for copy in copies(expert, w):
            copy.start()

    def arrived(expert, w):
        for copy in copies(expert, w):
            copy.wait()
        return buffer[lax.rem(3 * expert + w, slots)]

    for i in range(slots):
        start(i // 3, i % 3)

    for c in range(count):
        pick = (combine_ref[c].astype(jnp.float32) > 0).astype(jnp.float32).astype(jnp.bfloat16)
        for h in range(2):
            block = blocks[2 * c + h][...]
            rows = lax.dot_general(pick, block, by_rows, preferred_element_type=jnp.float32).astype(jnp.bfloat16)
            for e in range(here):
                picked[e, c * SLOTS : (c + 1) * SLOTS, columns[h]] = rows[e * SLOTS : (e + 1) * SLOTS]

    def work(expert, _):
        hidden = expert_hidden(picked[expert], arrived(expert, 0), arrived(expert, 1))

        @pl.when(expert + slots // 3 < here)
        def _():
            start(expert + slots // 3, 1)
            start(expert + slots // 3, 2)

        picked[expert] = expert_down(hidden, arrived(expert, 2))

        @pl.when(expert + slots // 3 + 1 < here)
        def _():
            start(expert + slots // 3 + 1, 0)

        return 0

    lax.fori_loop(0, here, work, 0)

    for c in [middle] + list(range(middle)) + list(range(middle + 1, count)):
        for h, outs in ((1, far), (0, near)):
            rows = jnp.concatenate([picked[e, c * SLOTS : (c + 1) * SLOTS, columns[h]] for e in range(here)], axis=0)
            outs[c][...] = jnp.dot(combine_ref[c], rows, preferred_element_type=jnp.float32).astype(jnp.bfloat16)


def expert_specs(w_gate):
    hidden, width = w_gate.shape[1:]
    return [pl.BlockSpec((1, hidden, width), lambda e, where: (e, 0, 0))] * 3


def experts_plain(where, picked, w_gate, w_up, w_down):
    here, rows, width = picked.shape
    rows_spec = pl.BlockSpec((1, rows, width), lambda e, where: (e, 0, 0))
    return pl.pallas_call(
        plain_kernel,
        grid_spec=pltpu.PrefetchScalarGridSpec(
            num_scalar_prefetch=1,
            grid=(here,),
            in_specs=[rows_spec] + expert_specs(w_gate),
            out_specs=rows_spec,
        ),
        out_shape=jax.ShapeDtypeStruct(picked.shape, jnp.bfloat16),
        compiler_params=pltpu.CompilerParams(vmem_limit_bytes=VMEM_LIMIT),
        name="experts",
    )(where, picked, w_gate, w_up, w_down)


def experts_fused(where, found, combine, w_gate, w_up, w_down):
    count, local = len(found), found[0][0].shape[0]
    here, units, width = w_gate.shape
    rows = count * SLOTS
    whole = pl.BlockSpec(memory_space=pltpu.VMEM)
    outs = pl.pallas_call(
        functools.partial(fused_kernel, count),
        in_specs=[pl.BlockSpec(memory_space=pltpu.SMEM)]
        + [whole] * (2 * count + 1)
        + [pl.BlockSpec(memory_space=pltpu.HBM)] * 3,
        out_specs=[whole] * (2 * count),
        scratch_shapes=[pltpu.VMEM((here, rows, width), jnp.bfloat16)]
        + [pltpu.VMEM((HELD, units, width), jnp.bfloat16), pltpu.SemaphoreType.DMA((HELD, PIECES))],
        out_shape=[pltpu.VMEM((local, width // 2), jnp.bfloat16)] * (2 * count),
        compiler_params=pltpu.CompilerParams(vmem_limit_bytes=29 * MIB),
        name="experts",
    )(where, *(x for block in found for x in block), combine,
      *(pltpu.with_memory_space_constraint(w, pltpu.HBM) for w in (w_gate, w_up, w_down)))
    return outs[:count], outs[count:]


def body(
    queries,
    latent,
    residual,
    seg_lengths,
    span_order,
    expert_ids,
    route_weights,
    kv_up,
    out_proj,
    norm_gain,
    w_gate,
    w_up,
    w_down,
):
    local_rows, width = residual.shape
    span = local_rows // 2
    count = lax.axis_size("ctx")
    here = EXPERTS // count
    me, side = lax.axis_index("ctx"), lax.axis_index("exp")
    where = jnp.stack([me, side]).astype(jnp.int32)

    base = latent.shape[1]
    w_gate, w_up = w_gate.transpose(0, 2, 1), w_up.transpose(0, 2, 1)
    packed = pack(latent, expert_ids, route_weights)
    few = count <= FEW
    scalars = lambda *arrays: jnp.concatenate([where, sources_of(me, side, count), *arrays])
    beside = [
        (scalars, (span_order, seg_lengths)),
        (lambda gain: gain.reshape(1, width), (norm_gain,)),
        (stage if few else lambda x: x, (kv_up,)),
    ]
    streams = [gather(x, count, beside if h == 0 else ()) for h, x in enumerate(packed)]
    info, gain, kv_up = streams[0][1]
    found = list(zip(*(blocks for blocks, _ in streams)))
    partial, summand = attend(info, found, queries, kv_up, out_proj, residual, count)
    def place_rows(*blocks):
        if few:
            return route(where, blocks, here)
        facts = jnp.stack([jnp.concatenate(block, axis=0) for block in blocks])
        facts = facts[:, :, base : base + 2 * TOP].astype(jnp.float32)
        own = (me * here + jnp.arange(here, dtype=jnp.int32)).astype(jnp.float32)
        hit = facts[:, :, :TOP, None] == own
        hot = jnp.any(hit, axis=2)
        share = jnp.sum(jnp.where(hit, facts[:, :, TOP:, None], 0.0), axis=2)
        token = jnp.arange(local_rows, dtype=jnp.int32)
        before = (token[:, None] > token[None, :]).astype(jnp.bfloat16)
        rank = jnp.einsum("tu,cue->cte", before, hot.astype(jnp.bfloat16), preferred_element_type=jnp.float32)
        slot = jnp.arange(SLOTS, dtype=jnp.int32).astype(jnp.float32)
        combine = jnp.where(rank[:, :, :, None] == slot, share[:, :, :, None], 0.0)
        return combine.astype(jnp.bfloat16).reshape(count, local_rows, here * SLOTS)

    there = swap(partial)
    blocks, _ = lax.optimization_barrier((tuple(found), partial))
    combine, there = lax.optimization_barrier((place_rows(*blocks), there))
    middle, *normed = norm(where, summand, there, gain)
    got = gather_columns(*normed, count)
    if few:
        mixture = reduce(experts_fused(where, got, combine, w_gate, w_up, w_down), count)
    else:
        pick = (combine > 0).astype(jnp.bfloat16)
        near, far = (jnp.stack(x) for x in zip(*got))
        rows = jnp.concatenate([jnp.where(side == 0, near, far), jnp.where(side == 0, far, near)], axis=2)
        picked = jnp.einsum("cts,ctd->csd", pick, rows, preferred_element_type=jnp.float32).astype(jnp.bfloat16)
        picked = picked.reshape(count, here, SLOTS, width).transpose(1, 0, 2, 3).reshape(here, count * SLOTS, width)
        result = experts_plain(where, picked, w_gate, w_up, w_down)
        result = result.reshape(here, count, SLOTS, width).transpose(1, 0, 2, 3).reshape(count, here * SLOTS, width)
        total = jnp.einsum("cts,csd->ctd", combine, result, preferred_element_type=jnp.float32).astype(jnp.bfloat16)
        left, right = jnp.split(total, 2, axis=2)
        both = summed([jnp.where(side == 0, left, right), swap(jnp.where(side == 0, right, left))])
        mixture = lax.psum_scatter(both.astype(jnp.bfloat16), "ctx").astype(jnp.float32)
    return (middle.astype(jnp.float32) + mixture).astype(jnp.bfloat16)


def solution(mesh):
    in_specs = (
        P(("groups", "ctx"), "exp"),
        P(("groups", "ctx"), None),
        P(("groups", "ctx"), None),
        P("groups"),
        P("groups"),
        P(("groups", "ctx"), None),
        P(("groups", "ctx"), None),
        P(None, "exp"),
        P("exp", None),
        P(),
        P("ctx", None, "exp"),
        P("ctx", None, "exp"),
        P("ctx", "exp", None),
    )
    out_specs = P(("groups", "ctx"), "exp")
    return jax.shard_map(body, mesh=mesh, in_specs=in_specs, out_specs=out_specs, check_vma=False)
```

```python
import functools
import math

import jax
import jax.numpy as jnp
import numpy as np
from jax import lax
from jax.experimental import pallas as pl
from jax.experimental.pallas import tpu as pltpu
from jax.sharding import PartitionSpec as P

NOPE = 128
ROPE = 64
VHEAD = 128
LAT = 512
EXPERTS = 64
TOP = 6
SLOTS = 16
WIDE = 640
MIB = 1024 * 1024
VMEM_LIMIT = 50 * MIB
HELD = 7
PIECES = 2
SWAP = [(0, 1), (1, 0)]
FEW = 8


def cycle_of(count):
    fast = 2 ** (int(math.log2(count)) // 2)
    slow = count // fast
    cycle = [0]
    for i in range(slow):
        columns = range(1, fast)
        cycle += [i * fast + j for j in (columns if i % 2 == 0 else reversed(columns))]
    return cycle + [i * fast for i in reversed(range(1, slow))]


def swap(value):
    return lax.ppermute(value, "exp", SWAP)


def turn(value, count, cross=False):
    cycle = cycle_of(count)
    pairs = []
    for p in range(count):
        for core, ahead in ((0, 1), (1, -1)):
            pairs.append((cycle[p] * 2 + core, cycle[(p + ahead) % count] * 2 + (core ^ int(cross))))
    return lax.ppermute(value, ("ctx", "exp"), pairs)


def summed(pieces):
    total = pieces[0].astype(jnp.float32)
    for piece in pieces[1:]:
        total = total + piece.astype(jnp.float32)
    return total


def sources_of(me, side, count):
    if count > FEW:
        return jnp.arange(count, dtype=jnp.int32)
    cycle = cycle_of(count)
    middle = count // 2
    table = np.zeros((2 * count, count), np.int32)
    for p in range(count):
        for core, sign in ((0, 1), (1, -1)):
            ways = [sign * d for d in range(middle + 1)] + [-sign * d for d in range(1, middle)]
            table[cycle[p] * 2 + core] = [cycle[(p - way) % count] for way in ways]
    return lax.dynamic_index_in_dim(jnp.asarray(table), me * 2 + side, keepdims=False)


def gather(block, count, beside=()):
    if count > FEW:
        return list(lax.all_gather(block, "ctx")), [run(*arguments) for run, arguments in beside]
    middle = count // 2
    found, other, made = [block], [()], []
    for d in range(1, middle + 1):
        arrived, extra = turn(found[-1], count), ()
        if len(beside) >= d:
            run, arguments = beside[d - 1]
            extra = run(*lax.optimization_barrier((found[-1], arguments))[1])
        arrived, other[-1], extra = lax.optimization_barrier((arrived, other[-1], extra))
        made.append(extra)
        found.append(arrived)
        if d < middle:
            other.append(swap(arrived))
    return found + other[1:], made[: len(beside)]


def gather_columns(near, far, count):
    if count > FEW:
        return list(zip(lax.all_gather(near, "ctx"), lax.all_gather(far, "ctx")))
    middle = count // 2
    found, other = {0: [near], 1: [far]}, {0: [()], 1: [()]}
    for d in range(1, middle + 1):
        for stream in (0, 1) if d < middle else (0,):
            arrived = turn(found[stream][-1], count)
            arrived, other[stream][-1] = lax.optimization_barrier((arrived, other[stream][-1]))
            found[stream].append(arrived)
            other[stream].append(swap(arrived))
    here = [(found[0][d], found[1][d]) for d in range(middle)]
    there = [(other[1][d], other[0][d]) for d in range(1, middle)]
    return here + [(found[0][middle], other[0][middle])] + there


def reduce(parts, count):
    middle = count // 2
    given = [swap(parts[1][middle]), swap(parts[0][middle - 1])]
    running = [None, None]
    for d in range(middle, 0, -1):
        for stream in (0, 1) if d < middle else (0,):
            place = middle + d if d < middle else middle
            later = parts[1 - stream][d - 1] if d > 1 or stream == 0 else ()
            pieces = [parts[stream][place], given[stream]]
            if running[stream] is not None:
                running[stream], later = lax.optimization_barrier((running[stream], later))
                pieces.append(running[stream])
            running[stream] = turn(summed(pieces).astype(jnp.bfloat16), count, cross=d == 1 and stream == 1)
            if d > 1 or stream == 0:
                given[stream] = swap(later)
    return summed([parts[0][0], given[0], *running])


def attend_kernel(count, blocks, heads, info, *refs):
    latents, up_ref, refs = refs[: len(refs) - 13], refs[len(refs) - 13], refs[len(refs) - 12 :]
    wanted, (out_ref, base_ref) = refs[:3], refs[3:5]
    held, sems, (m_ref, l_ref, acc_ref) = refs[5:8], refs[8], refs[9:12]
    q_ref, proj_ref, residual_ref = held
    copies = [pltpu.make_async_copy(wanted[i], held[i], sems.at[i]) for i in range(3)]
    chunk = pl.program_id(0)
    sources = lambda c: info[2 + c]
    order = lambda j: info[2 + count + j]
    segs = info.shape[0] - 2 - 3 * count
    rows = q_ref.shape[0]
    span = rows // 2
    depth = q_ref.shape[1] // heads

    @pl.when(chunk == 0)
    def _():
        for copy in copies:
            copy.start()

    @pl.when(chunk == 0)
    def _():
        m_ref[...] = jnp.full_like(m_ref, -1e30)
        l_ref[...] = jnp.zeros_like(l_ref)
        acc_ref[...] = jnp.zeros_like(acc_ref)

    row = lax.broadcasted_iota(jnp.int32, (rows, 1), 0)
    first = order(2 * info[0]) * span
    second = order(2 * info[0] + 1) * span
    qpos = jnp.where(row < span, first + row, second + row - span)
    low = jnp.zeros((rows, 1), jnp.int32)
    start = jnp.int32(0)
    for m in range(segs):
        low = jnp.where(qpos >= start, start, low)
        start = start + info[2 + 3 * count + m]
    keys = blocks * rows
    lane = lax.broadcasted_iota(jnp.int32, (1, keys), 1)
    which = lane // span
    kpos = lane % span
    for j in range(blocks):
        source = sources(chunk * blocks + j)
        for i in range(2):
            kpos = jnp.where(which == 2 * j + i, order(2 * source + i) * span + lane % span, kpos)
    visible = (kpos >= low) & (kpos <= qpos)

    lat = jnp.concatenate([ref[...].reshape(-1, WIDE) for ref in latents], axis=0)

    @pl.when(chunk == 0)
    def _():
        copies[0].wait()

    keyval = jnp.dot(lat[:, :LAT], up_ref[...], preferred_element_type=jnp.float32).astype(jnp.bfloat16)
    rope = lat[:, LAT : LAT + ROPE]
    scale = 1.0 / math.sqrt(NOPE + ROPE)
    for h in range(heads):
        base = h * (NOPE + VHEAD)
        key = jnp.concatenate([keyval[:, base : base + NOPE], rope], axis=1)
        scores = lax.dot_general(q_ref[:, h * depth : (h + 1) * depth], key, (((1,), (1,)), ((), ())), preferred_element_type=jnp.float32)
        scores = jnp.where(visible, scores * scale, -1e30)
        values = keyval[:, base + NOPE : base + NOPE + VHEAD]
        if blocks == count:
            weights = jnp.where(visible, jnp.exp(scores - jnp.max(scores, axis=1, keepdims=True)), 0.0)
            mixed = jnp.dot(weights.astype(jnp.bfloat16), values, preferred_element_type=jnp.float32)
            acc_ref[h] = mixed / jnp.sum(weights, axis=1, keepdims=True)
            continue
        best = m_ref[h]
        fresh = jnp.maximum(best, jnp.max(scores, axis=1, keepdims=True))
        weights = jnp.where(visible, jnp.exp(scores - fresh), 0.0)
        shrink = jnp.exp(best - fresh)
        m_ref[h] = fresh
        l_ref[h] = l_ref[h] * shrink + jnp.sum(weights, axis=1, keepdims=True)
        mixed = jnp.dot(weights.astype(jnp.bfloat16), values, preferred_element_type=jnp.float32)
        acc_ref[h] = acc_ref[h] * shrink + mixed

    @pl.when(chunk == pl.num_programs(0) - 1)
    def _():
        totals = [1.0 if blocks == count else l_ref[h] for h in range(heads)]
        attended = [(acc_ref[h] / totals[h]).astype(jnp.bfloat16) for h in range(heads)]
        copies[1].wait()
        copies[2].wait()
        out = jnp.dot(jnp.concatenate(attended, axis=1), proj_ref[...], preferred_element_type=jnp.float32)
        out = out.astype(jnp.bfloat16)
        out_ref[...] = out
        base_ref[...] = residual_ref[...].astype(jnp.float32) + out.astype(jnp.float32)


def attend(info, found, queries, kv_up, out_proj, residual, count):
    rows, width = residual.shape
    heads = kv_up.shape[1] // (NOPE + VHEAD)
    blocks = math.gcd(count, 8)
    whole = pl.BlockSpec(memory_space=pltpu.VMEM)
    if blocks == count:
        latents, lat_spec = [half for block in found for half in block], whole
    else:
        found = [jnp.concatenate(block, axis=0) for block in found]
        latents, lat_spec = [jnp.stack(found)], pl.BlockSpec((blocks, rows, WIDE), lambda i, *_: (i, 0, 0))
    wanted = (queries, out_proj, residual)
    return pl.pallas_call(
        functools.partial(attend_kernel, count, blocks, heads),
        grid_spec=pltpu.PrefetchScalarGridSpec(
            num_scalar_prefetch=1,
            grid=(count // blocks,),
            in_specs=[lat_spec] * len(latents) + [whole] + [pl.BlockSpec(memory_space=pltpu.HBM)] * 3,
            out_specs=[whole, whole],
            scratch_shapes=[pltpu.VMEM(x.shape, x.dtype) for x in wanted]
            + [
                pltpu.SemaphoreType.DMA((3,)),
                pltpu.VMEM((heads, rows, 1), jnp.float32),
                pltpu.VMEM((heads, rows, 1), jnp.float32),
                pltpu.VMEM((heads, rows, VHEAD), jnp.float32),
            ],
        ),
        out_shape=[pltpu.VMEM((rows, width), jnp.bfloat16), pltpu.VMEM((rows, width), jnp.float32)],
        compiler_params=pltpu.CompilerParams(vmem_limit_bytes=28 * MIB),
        name="attend",
    )(info, *latents, kv_up, *(pltpu.with_memory_space_constraint(x, pltpu.HBM) for x in wanted))


def stage_kernel(source, out, sem):
    copy = pltpu.make_async_copy(source, out, sem)
    copy.start()
    copy.wait()


def stage(x):
    return pl.pallas_call(
        stage_kernel,
        in_specs=[pl.BlockSpec(memory_space=pltpu.HBM)],
        out_specs=pl.BlockSpec(memory_space=pltpu.VMEM),
        scratch_shapes=[pltpu.SemaphoreType.DMA],
        out_shape=pltpu.VMEM(x.shape, x.dtype),
        compiler_params=pltpu.CompilerParams(vmem_limit_bytes=2 * MIB),
        name="stage",
    )(pltpu.with_memory_space_constraint(x, pltpu.HBM))


def route_kernel(count, where, *refs):
    blocks, out_ref = refs[: 2 * count], refs[2 * count]
    _, rows, width = out_ref.shape
    here = width // SLOTS
    lane = lax.broadcasted_iota(jnp.int32, (rows, width), 1)
    own = (where[0] * here + lane // SLOTS).astype(jnp.float32)
    slot = (lane % SLOTS).astype(jnp.float32)
    first = lax.broadcasted_iota(jnp.int32, (rows, rows), 0)
    before = (first > lax.broadcasted_iota(jnp.int32, (rows, rows), 1)).astype(jnp.float32).astype(jnp.bfloat16)
    for c in range(count):
        facts = jnp.concatenate([blocks[2 * c + i][:, LAT:].astype(jnp.float32) for i in range(2)], axis=0)
        hot, share = jnp.zeros((rows, width), jnp.float32), jnp.zeros((rows, width), jnp.float32)
        for k in range(TOP):
            hit = facts[:, ROPE + k : ROPE + k + 1] == own
            hot = jnp.where(hit, 1.0, hot)
            share = jnp.where(hit, facts[:, ROPE + TOP + k : ROPE + TOP + k + 1], share)
        rank = jnp.dot(before, hot.astype(jnp.bfloat16), preferred_element_type=jnp.float32)
        out_ref[c] = jnp.where(rank == slot, share, 0.0).astype(jnp.bfloat16)


def route(where, found, here):
    count, (span, _) = len(found), found[0][0].shape
    whole = pl.BlockSpec(memory_space=pltpu.VMEM)
    return pl.pallas_call(
        functools.partial(route_kernel, count),
        in_specs=[pl.BlockSpec(memory_space=pltpu.SMEM)] + [whole] * (2 * count),
        out_specs=whole,
        out_shape=pltpu.VMEM((count, 2 * span, here * SLOTS), jnp.bfloat16),
        compiler_params=pltpu.CompilerParams(vmem_limit_bytes=8 * MIB),
        name="route",
    )(where, *(half for block in found for half in block))


def norm_kernel(where, base_ref, there_ref, gain_ref, middle_ref, near_ref, far_ref):
    half = middle_ref.shape[1]
    middle = (base_ref[...] + there_ref[...].astype(jnp.float32)).astype(jnp.bfloat16)
    wide = middle.astype(jnp.float32)
    inverse = lax.rsqrt(jnp.mean(wide * wide, axis=1, keepdims=True) + 1e-06)
    normed = wide * inverse * gain_ref[...].astype(jnp.float32)
    first = where[1] == 0
    near_ref[...] = jnp.where(first, normed[:, :half], normed[:, half:]).astype(jnp.bfloat16)
    far_ref[...] = jnp.where(first, normed[:, half:], normed[:, :half]).astype(jnp.bfloat16)
    middle_ref[...] = jnp.where(first, wide[:, :half], wide[:, half:]).astype(jnp.bfloat16)


def norm(where, base, there, gain):
    rows, width = base.shape
    whole = pl.BlockSpec(memory_space=pltpu.VMEM)
    return pl.pallas_call(
        norm_kernel,
        in_specs=[pl.BlockSpec(memory_space=pltpu.SMEM)] + [whole] * 3,
        out_specs=[whole] * 3,
        out_shape=[pltpu.VMEM((rows, width // 2), jnp.bfloat16)] * 3,
        compiler_params=pltpu.CompilerParams(vmem_limit_bytes=12 * MIB),
        name="norm",
    )(where, base, there, gain)


def pack_kernel(*refs):
    copies = [pltpu.make_async_copy(refs[i], refs[5 + i], refs[9].at[i]) for i in range(3)]
    for copy in copies:
        copy.start()
    for copy in copies:
        copy.wait()
    top_ref, bottom_ref, latent_ref, ids_ref, weights_ref, rows = refs[3:9]
    span = top_ref.shape[0]
    tokens = 2 * span
    rows[...] = jnp.zeros_like(rows)
    rows[0:TOP] = ids_ref[...].astype(jnp.float32)
    rows[TOP : 2 * TOP] = weights_ref[...]
    row = lax.broadcasted_iota(jnp.int32, (tokens, tokens), 0)
    same = (row == lax.broadcasted_iota(jnp.int32, (tokens, tokens), 1)).astype(jnp.float32).astype(jnp.bfloat16)
    every = jnp.concatenate([latent_ref[...], rows[...].astype(jnp.bfloat16)], axis=0)
    turned = lax.dot_general(same, every, (((1,), (1,)), ((), ())), preferred_element_type=jnp.float32)
    top_ref[...] = turned[:span].astype(jnp.bfloat16)
    bottom_ref[...] = turned[span:].astype(jnp.bfloat16)


def pack(latent, expert_ids, route_weights):
    local_rows, base = latent.shape
    arrays = (latent.T, expert_ids.T, route_weights.T)
    return pl.pallas_call(
        pack_kernel,
        in_specs=[pl.BlockSpec(memory_space=pltpu.HBM)] * 3,
        out_specs=[pl.BlockSpec(memory_space=pltpu.VMEM)] * 2,
        scratch_shapes=[pltpu.VMEM(x.shape, x.dtype) for x in arrays]
        + [pltpu.VMEM((WIDE - base, local_rows), jnp.float32), pltpu.SemaphoreType.DMA((3,))],
        out_shape=[pltpu.VMEM((local_rows // 2, WIDE), jnp.bfloat16)] * 2,
        compiler_params=pltpu.CompilerParams(vmem_limit_bytes=4 * MIB),
        name="pack",
    )(*(pltpu.with_memory_space_constraint(x, pltpu.HBM) for x in arrays))


def expert_hidden(rows, gate, up):
    by_columns = (((1,), (1,)), ((), ()))
    gate = lax.dot_general(gate, rows, by_columns, preferred_element_type=jnp.float32)
    upper = lax.dot_general(up, rows, by_columns, preferred_element_type=jnp.float32)
    return (gate / (1.0 + jnp.exp(-gate)) * upper).astype(jnp.bfloat16)


def expert_down(hidden, down):
    by_rows = (((0,), (0,)), ((), ()))
    return lax.dot_general(hidden, down, by_rows, preferred_element_type=jnp.float32).astype(jnp.bfloat16)


def plain_kernel(where, rows_ref, gate_ref, up_ref, down_ref, out_ref):
    out_ref[0] = expert_down(expert_hidden(rows_ref[0], gate_ref[0], up_ref[0]), down_ref[0])


def fused_kernel(count, where, *refs):
    at = 2 * count
    blocks, combine_ref, weights = refs[:at], refs[at], refs[at + 1 : at + 4]
    near, far = refs[at + 4 : at + 4 + count], refs[at + 4 + count : at + 4 + 2 * count]
    at += 4 + 2 * count
    picked, buffer, sems = refs[at : at + 3]
    here = picked.shape[0]
    slots, units, width = buffer.shape
    half = width // 2
    side = where[1]
    columns = [pl.ds(pl.multiple_of(turned * half, half), half) for turned in (side, 1 - side)]
    piece = units // PIECES
    middle = count // 2
    by_rows = (((0,), (0,)), ((), ()))

    def copies(expert, w):
        slot = lax.rem(3 * expert + w, slots)
        for i in range(PIECES):
            rows = pl.ds(i * piece, piece)
            yield pltpu.make_async_copy(weights[w].at[expert, rows], buffer.at[slot, rows], sems.at[slot, i])

    def start(expert, w):
        for copy in copies(expert, w):
            copy.start()

    def arrived(expert, w):
        for copy in copies(expert, w):
            copy.wait()
        return buffer[lax.rem(3 * expert + w, slots)]

    for i in range(slots):
        start(i // 3, i % 3)

    for c in range(count):
        pick = (combine_ref[c].astype(jnp.float32) > 0).astype(jnp.float32).astype(jnp.bfloat16)
        for h in range(2):
            block = blocks[2 * c + h][...]
            rows = lax.dot_general(pick, block, by_rows, preferred_element_type=jnp.float32).astype(jnp.bfloat16)
            for e in range(here):
                picked[e, c * SLOTS : (c + 1) * SLOTS, columns[h]] = rows[e * SLOTS : (e + 1) * SLOTS]

    def work(expert, _):
        hidden = expert_hidden(picked[expert], arrived(expert, 0), arrived(expert, 1))

        @pl.when(expert + slots // 3 < here)
        def _():
            start(expert + slots // 3, 1)
            start(expert + slots // 3, 2)

        picked[expert] = expert_down(hidden, arrived(expert, 2))

        @pl.when(expert + slots // 3 + 1 < here)
        def _():
            start(expert + slots // 3 + 1, 0)

        return 0

    lax.fori_loop(0, here, work, 0)

    for c in [middle] + list(range(middle)) + list(range(middle + 1, count)):
        for h, outs in ((1, far), (0, near)):
            rows = jnp.concatenate([picked[e, c * SLOTS : (c + 1) * SLOTS, columns[h]] for e in range(here)], axis=0)
            outs[c][...] = jnp.dot(combine_ref[c], rows, preferred_element_type=jnp.float32).astype(jnp.bfloat16)


def expert_specs(w_gate):
    hidden, width = w_gate.shape[1:]
    return [pl.BlockSpec((1, hidden, width), lambda e, where: (e, 0, 0))] * 3


def experts_plain(where, picked, w_gate, w_up, w_down):
    here, rows, width = picked.shape
    rows_spec = pl.BlockSpec((1, rows, width), lambda e, where: (e, 0, 0))
    return pl.pallas_call(
        plain_kernel,
        grid_spec=pltpu.PrefetchScalarGridSpec(
            num_scalar_prefetch=1,
            grid=(here,),
            in_specs=[rows_spec] + expert_specs(w_gate),
            out_specs=rows_spec,
        ),
        out_shape=jax.ShapeDtypeStruct(picked.shape, jnp.bfloat16),
        compiler_params=pltpu.CompilerParams(vmem_limit_bytes=VMEM_LIMIT),
        name="experts",
    )(where, picked, w_gate, w_up, w_down)


def experts_fused(where, found, combine, w_gate, w_up, w_down):
    count, local = len(found), found[0][0].shape[0]
    here, units, width = w_gate.shape
    rows = count * SLOTS
    whole = pl.BlockSpec(memory_space=pltpu.VMEM)
    outs = pl.pallas_call(
        functools.partial(fused_kernel, count),
        in_specs=[pl.BlockSpec(memory_space=pltpu.SMEM)]
        + [whole] * (2 * count + 1)
        + [pl.BlockSpec(memory_space=pltpu.HBM)] * 3,
        out_specs=[whole] * (2 * count),
        scratch_shapes=[pltpu.VMEM((here, rows, width), jnp.bfloat16)]
        + [pltpu.VMEM((HELD, units, width), jnp.bfloat16), pltpu.SemaphoreType.DMA((HELD, PIECES))],
        out_shape=[pltpu.VMEM((local, width // 2), jnp.bfloat16)] * (2 * count),
        compiler_params=pltpu.CompilerParams(vmem_limit_bytes=29 * MIB),
        name="experts",
    )(where, *(x for block in found for x in block), combine,
      *(pltpu.with_memory_space_constraint(w, pltpu.HBM) for w in (w_gate, w_up, w_down)))
    return outs[:count], outs[count:]


def body(
    queries,
    latent,
    residual,
    seg_lengths,
    span_order,
    expert_ids,
    route_weights,
    kv_up,
    out_proj,
    norm_gain,
    w_gate,
    w_up,
    w_down,
):
    local_rows, width = residual.shape
    span = local_rows // 2
    count = lax.axis_size("ctx")
    here = EXPERTS // count
    me, side = lax.axis_index("ctx"), lax.axis_index("exp")
    where = jnp.stack([me, side]).astype(jnp.int32)

    base = latent.shape[1]
    w_gate, w_up = w_gate.transpose(0, 2, 1), w_up.transpose(0, 2, 1)
    packed = pack(latent, expert_ids, route_weights)
    few = count <= FEW
    scalars = lambda *arrays: jnp.concatenate([where, sources_of(me, side, count), *arrays])
    beside = [
        (scalars, (span_order, seg_lengths)),
        (lambda gain: gain.reshape(1, width), (norm_gain,)),
        (stage if few else lambda x: x, (kv_up,)),
    ]
    streams = [gather(x, count, beside if h == 0 else ()) for h, x in enumerate(packed)]
    info, gain, kv_up = streams[0][1]
    found = list(zip(*(blocks for blocks, _ in streams)))
    partial, summand = attend(info, found, queries, kv_up, out_proj, residual, count)
    def place_rows(*blocks):
        if few:
            return route(where, blocks, here)
        facts = jnp.stack([jnp.concatenate(block, axis=0) for block in blocks])
        facts = facts[:, :, base : base + 2 * TOP].astype(jnp.float32)
        own = (me * here + jnp.arange(here, dtype=jnp.int32)).astype(jnp.float32)
        hit = facts[:, :, :TOP, None] == own
        hot = jnp.any(hit, axis=2)
        share = jnp.sum(jnp.where(hit, facts[:, :, TOP:, None], 0.0), axis=2)
        token = jnp.arange(local_rows, dtype=jnp.int32)
        before = (token[:, None] > token[None, :]).astype(jnp.bfloat16)
        rank = jnp.einsum("tu,cue->cte", before, hot.astype(jnp.bfloat16), preferred_element_type=jnp.float32)
        slot = jnp.arange(SLOTS, dtype=jnp.int32).astype(jnp.float32)
        combine = jnp.where(rank[:, :, :, None] == slot, share[:, :, :, None], 0.0)
        return combine.astype(jnp.bfloat16).reshape(count, local_rows, here * SLOTS)

    there = swap(partial)
    blocks, _ = lax.optimization_barrier((tuple(found), partial))
    combine, there = lax.optimization_barrier((place_rows(*blocks), there))
    middle, *normed = norm(where, summand, there, gain)
    got = gather_columns(*normed, count)
    if few:
        mixture = reduce(experts_fused(where, got, combine, w_gate, w_up, w_down), count)
    else:
        pick = (combine > 0).astype(jnp.bfloat16)
        near, far = (jnp.stack(x) for x in zip(*got))
        rows = jnp.concatenate([jnp.where(side == 0, near, far), jnp.where(side == 0, far, near)], axis=2)
        picked = jnp.einsum("cts,ctd->csd", pick, rows, preferred_element_type=jnp.float32).astype(jnp.bfloat16)
        picked = picked.reshape(count, here, SLOTS, width).transpose(1, 0, 2, 3).reshape(here, count * SLOTS, width)
        result = experts_plain(where, picked, w_gate, w_up, w_down)
        result = result.reshape(here, count, SLOTS, width).transpose(1, 0, 2, 3).reshape(count, here * SLOTS, width)
        total = jnp.einsum("cts,csd->ctd", combine, result, preferred_element_type=jnp.float32).astype(jnp.bfloat16)
        left, right = jnp.split(total, 2, axis=2)
        both = summed([jnp.where(side == 0, left, right), swap(jnp.where(side == 0, right, left))])
        mixture = lax.psum_scatter(both.astype(jnp.bfloat16), "ctx").astype(jnp.float32)
    return (middle.astype(jnp.float32) + mixture).astype(jnp.bfloat16)


def solution(mesh):
    in_specs = (
        P(("groups", "ctx"), "exp"),
        P(("groups", "ctx"), None),
        P(("groups", "ctx"), None),
        P("groups"),
        P("groups"),
        P(("groups", "ctx"), None),
        P(("groups", "ctx"), None),
        P(None, "exp"),
        P("exp", None),
        P(),
        P("ctx", None, "exp"),
        P("ctx", None, "exp"),
        P("ctx", "exp", None),
    )
    out_specs = P(("groups", "ctx"), "exp")
    return jax.shard_map(body, mesh=mesh, in_specs=in_specs, out_specs=out_specs, check_vma=False)
```
